32 devices in a mesh: groups: 2 (over y), dp: 4 (over x, core), tensor: 4 (over z).
Axes of the slice: x: 2, y: 2, z: 4, core: 2. Of those that a mesh axis runs over, the one named last changes fastest.
Arguments:
- inputs: bfloat16 [16384, 8192], P(('groups', 'dp', 'tensor')), parts along dimension 0, may hold values from -6 to 6
- in_proj: bfloat16 [64, 8192], replicated, as said below
- out_grads: bfloat16 [16384, 28672], P(('groups', 'dp'), 'tensor'), parts along dimension 0, may hold values from -6 to 6
- out_proj: bfloat16 [64, 28672], P(None, 'tensor'), may hold values from -0.03125 to 0.03125
- prior: float32 [8192, 4096], P(('groups', 'dp', 'tensor')), parts along dimension 0, as said below
- queries: bfloat16 [1024, 4096], P(('groups', 'dp', 'tensor')), parts along dimension 0, may hold values from -6 to 6
Outputs:
- scores: float32 [16, 512], P('groups', ('dp', 'tensor')), parts along dimension 0
The draws below stay inside these ranges and needn't reach their ends.
There are 2 independent parts, one for each index of `groups`. The reference program is written for one: setup_inputs(seed, part) draws one part's arguments, and reference() takes and returns one part's arrays. A program takes and returns all parts, laid end to end along the dimension named above; an argument that names none is the same for every part. Nothing has to cross between parts.
Inputs may be any that keep to these rules, and one draw needn't show every extreme that they name: `in_proj`: a projection from 8192 input features to 64, entries up to about ten over the square root of 8192. `prior`: symmetric and positive definite, smallest eigenvalue above 0.1, entries of order one at most on the diagonal.
All inputs are finite; a program needn't handle non-finite values.
Results may differ from the reference program's by a relative error of at most 0.0003.
Values sent between devices are 32-bit elements; how exact they have to be, the bound alone decides.
No kernel may reach another device: no remote copies, remote signals or barrier semaphores. Data moves between devices by JAX's collectives and lax.ppermute only.
A program may use at most 128 MiB of HBM per device.

```python
import math
import jax
import jax.numpy as jnp
from jax import lax

D = 8192
FF = 28672
R_IN = 64
R_OUT = 64
SEQ = 1024
ITERS = 4
K = 4096
TOKENS = 8192
NQ = 512


def draw_in_proj(key, part):
    key = jax.random.fold_in(key, 11)
    base_key, jitter_key = jax.random.split(key)
    position = jnp.arange(R_IN, dtype=jnp.float32) / max(R_IN - 1, 1)
    jitter = jnp.exp(jax.random.uniform(jitter_key, (R_IN, 1), jnp.float32, -0.2, 0.2))
    base = jnp.clip(jax.random.normal(base_key, (R_IN, D), jnp.float32), -3.0, 3.0)
    ramp = 0.6 + 1.2 * position
    return (base * ramp[:, None] * jitter / math.sqrt(D)).astype(jnp.bfloat16)


def draw_prior(key, part):
    key = jax.random.fold_in(key, 23)
    noise_key, diagonal_key = jax.random.split(key)
    noise_field = jnp.clip(jax.random.normal(noise_key, (K, K), jnp.float32), -4.0, 4.0)
    symmetric = (noise_field + noise_field.T) * (0.4 / math.sqrt(2.0 * K))
    diagonal_part = jax.random.uniform(diagonal_key, (K,), jnp.float32, 1.0, 3.0)
    return symmetric + jnp.eye(K, dtype=jnp.float32) * diagonal_part[None, :]


def levels(key, dims, pieces, low, high):
    gain, own = 1.0, jax.random.fold_in(key, 6)
    for dim, blocks in pieces:
        heights = jnp.exp(jax.random.uniform(jax.random.fold_in(own, dim), (blocks,), jnp.float32, low / len(pieces), high / len(pieces)))
        gain = gain * jnp.repeat(heights, dims[dim] // blocks).reshape([-1 if axis == dim else 1 for axis in range(len(dims))])
    return gain


def centred(key, dims, scale, limit, cuts=(), held_as=jnp.bfloat16):
    values = jax.random.normal(key, dims, jnp.float32) * scale
    if len(cuts) > 0:
        values = levels(key, dims, cuts, -0.22, 0.18) * values
    return jnp.clip(values, min=-limit, max=limit).astype(held_as)


def setup_inputs(seed: int = 0, part: int = 0) -> dict:
    key_list = jax.random.split(jax.random.key(seed), 7)
    part_keys = jax.random.split(jax.random.fold_in(key_list[6], part), 7)
    inputs = centred(part_keys[0], (TOKENS, D), 1.0, 6.0, ((0, 16),))
    in_proj = draw_in_proj(jax.random.fold_in(key_list[6], 71), part)
    out_grads = centred(part_keys[2], (TOKENS, FF), 1.0, 6.0, ((0, 4), (1, 4)))
    out_proj = centred(key_list[3], (R_OUT, FF), FF ** -0.5, 0.03125, ((1, 4),))
    prior = draw_prior(jax.random.fold_in(jax.random.fold_in(key_list[6], part), 71), part)
    queries = centred(part_keys[5], (NQ, K), 1.0, 6.0, ((0, 16),))
    return {"inputs": inputs, "in_proj": in_proj, "out_grads": out_grads, "out_proj": out_proj, "prior": prior, "queries": queries}


def reference(inputs, in_proj, out_grads, out_proj, prior, queries):
    highest = lax.Precision.HIGHEST
    in_feats = jnp.dot(inputs, in_proj.T, preferred_element_type=jnp.float32)
    out_feats = jnp.dot(out_grads, out_proj.T, preferred_element_type=jnp.float32)
    train_count = in_feats.shape[0] // SEQ
    in_tokens = in_feats.reshape(train_count, SEQ, R_IN)
    out_tokens = out_feats.reshape(train_count, SEQ, R_OUT)
    vectors = jnp.einsum("sta,stb->sab", in_tokens, out_tokens, precision=highest)
    vectors = vectors.reshape(train_count, R_IN * R_OUT) / SEQ
    fisher = prior + jnp.dot(vectors.T, vectors, precision=highest, preferred_element_type=jnp.float32) / train_count
    solution = jnp.zeros_like(vectors)
    residual = vectors
    direction = vectors
    norm_now = jnp.sum(residual * residual, axis=1)
    for iteration in range(ITERS):
        applied = jnp.dot(direction, fisher, precision=highest, preferred_element_type=jnp.float32)
        step_size = norm_now / jnp.sum(direction * applied, axis=1)
        solution = solution + step_size[:, None] * direction
        residual = residual - step_size[:, None] * applied
        norm_next = jnp.sum(residual * residual, axis=1)
        direction = residual + (norm_next / norm_now)[:, None] * direction
        norm_now = norm_next
    return jnp.dot(solution, queries.astype(jnp.float32).T, precision=highest, preferred_element_type=jnp.float32)
```

```python
import jax
import jax.numpy as jnp
from jax import lax
from jax.sharding import PartitionSpec as P

R_IN = 64
R_OUT = 64
SEQ = 1024
ITERS = 4


def on_device(inputs, in_proj, out_grads, out_proj, prior, queries):
    highest = lax.Precision.HIGHEST
    width = R_IN * R_OUT
    in_local = lax.dot_general(
        in_proj, inputs, (((1,), (1,)), ((), ())), preferred_element_type=jnp.float32
    )
    in_all = lax.all_gather(in_local, "tensor", axis=0)
    out_local = lax.dot_general(
        out_proj, out_grads, (((1,), (1,)), ((), ())), preferred_element_type=jnp.float32
    )
    tokens = out_local.shape[1]
    seq_count = tokens // SEQ
    in_tokens = in_all.transpose(1, 0, 2).reshape(R_IN, seq_count, SEQ)
    out_tokens = out_local.reshape(R_OUT, seq_count, SEQ)
    partial = jnp.einsum("ast,bst->sab", in_tokens, out_tokens, precision=highest)
    partial = partial.reshape(seq_count, width) / SEQ
    own_vectors = jnp.sum(lax.all_gather(partial, "tensor", axis=0), axis=0)
    vectors = lax.all_gather(own_vectors, "dp", axis=0, tiled=True)
    train_count = vectors.shape[0]
    row_count = prior.shape[0]
    row_start = (
        lax.axis_index("dp") * lax.axis_size("tensor") + lax.axis_index("tensor")
    ) * row_count

    def gather_rows(values):
        held = lax.all_gather(values, "tensor", axis=0)
        held = lax.all_gather(held, "dp", axis=0)
        return held.transpose(2, 0, 1, 3).reshape(values.shape[0], width)

    def own_rows(values):
        return lax.dynamic_slice_in_dim(values, row_start, row_count, 1)

    fisher_rows = (
        prior
        + lax.dot_general(
            own_rows(vectors),
            vectors,
            (((0,), (0,)), ((), ())),
            precision=highest,
            preferred_element_type=jnp.float32,
        )
        / train_count
    )

    def apply_rows(direction):
        return lax.dot_general(
            direction,
            fisher_rows,
            (((1,), (1,)), ((), ())),
            precision=highest,
            preferred_element_type=jnp.float32,
        )

    solution = jnp.zeros_like(vectors)
    residual = vectors
    direction = vectors
    norm_now = jnp.sum(residual * residual, axis=1)
    for iteration in range(ITERS):
        applied_rows = apply_rows(direction)
        if iteration == ITERS - 1:
            own = jnp.sum(own_rows(direction) * applied_rows, axis=1)
            own = jnp.broadcast_to(own[:, None], (train_count, 128))
            held = jnp.sum(lax.all_gather(own, "tensor", axis=0), axis=0)
            curvature = jnp.sum(lax.all_gather(held, "dp", axis=0), axis=0)[:, 0]
            step_size = norm_now / curvature
            solution = solution + step_size[:, None] * direction
            break
        applied = gather_rows(applied_rows)
        step_size = norm_now / jnp.sum(direction * applied, axis=1)
        solution = solution + step_size[:, None] * direction
        residual = residual - step_size[:, None] * applied
        norm_next = jnp.sum(residual * residual, axis=1)
        direction = residual + (norm_next / norm_now)[:, None] * direction
        norm_now = norm_next
    return lax.dot_general(
        solution,
        queries.astype(jnp.float32),
        (((1,), (1,)), ((), ())),
        precision=highest,
        preferred_element_type=jnp.float32,
    )


def solution(mesh):
    return jax.shard_map(
        on_device,
        mesh=mesh,
        in_specs=(
            P(("groups", "dp", "tensor"), None),
            P(),
            P(("groups", "dp"), "tensor"),
            P(None, "tensor"),
            P(("groups", "dp", "tensor"), None),
            P(("groups", "dp", "tensor"), None),
        ),
        out_specs=P("groups", ("dp", "tensor")),
        check_vma=False,
    )
```

```python
import functools

import jax
import jax.numpy as jnp
from jax import lax
from jax.experimental import pallas as pl
from jax.experimental.pallas import tpu as pltpu
from jax.sharding import PartitionSpec as P

R_IN = 64
R_OUT = 64
SEQ = 1024
ITERS = 4
LANES = 128
DIRECT_LIMIT = 16
NT = (((1,), (1,)), ((), ()))
HIGHEST = lax.Precision.HIGHEST
VMEM_SPEC = pl.BlockSpec(memory_space=pltpu.VMEM)
ANY_SPEC = pl.BlockSpec(memory_space=pl.ANY)


def exchange(value, axes, size):
    held = [value]
    for k in range(1, size):
        held.append(lax.ppermute(value, axes, [(i, i ^ k) for i in range(size)]))
    return held


def dot_nt(a, b):
    return lax.dot_general(a, b, NT, precision=HIGHEST, preferred_element_type=jnp.float32)


def row_sum(values):
    return jnp.sum(values, axis=1, keepdims=True)


def partial_kernel(size, *refs):
    blocks, out_ref, part_ref, held = refs[:size], refs[size], refs[size + 1], refs[size + 2]
    me = lax.axis_index("tensor")
    tokens = blocks[0].shape[1]
    for k, block in enumerate(blocks):
        start = pl.multiple_of((me ^ k) * tokens, LANES)
        held[:, pl.ds(start, tokens)] = block[...]
    for s in range(part_ref.shape[0]):
        span = slice(s * SEQ, (s + 1) * SEQ)
        part_ref[s] = dot_nt(held[:, span], out_ref[:, span]) * (1.0 / SEQ)


def partial_vectors(blocks, out_local):
    seq_count = out_local.shape[1] // SEQ
    return pl.pallas_call(
        functools.partial(partial_kernel, len(blocks)),
        out_shape=jax.ShapeDtypeStruct((seq_count, R_IN, R_OUT), jnp.float32),
        in_specs=[VMEM_SPEC] * (len(blocks) + 1),
        out_specs=VMEM_SPEC,
        scratch_shapes=[pltpu.VMEM(out_local.shape, jnp.float32)],
        name="partial_vectors",
    )(*blocks, out_local)


def prior_copies(prior_ref, prior_vmem, sems):
    chunk = prior_ref.shape[1] // sems.shape[0]
    copies = []
    for c in range(sems.shape[0]):
        span = pl.ds(c * chunk, chunk)
        copies.append(
            pltpu.make_async_copy(prior_ref.at[:, span], prior_vmem.at[:, span], sems.at[c])
        )
    return copies


def own_columns(ref, me, count):
    if count % LANES == 0:
        return ref[:, pl.ds(pl.multiple_of(me * count, LANES), count)]
    per = LANES // count
    held = ref[:, pl.ds(pl.multiple_of((me // per) * LANES, LANES), LANES)]
    return pltpu.roll(held, LANES - (me % per) * count, 1)[:, :count]


def apply_fisher(direction, vectors_ref, copies, prior_vmem, me):
    seqs, width = direction.shape
    rows = prior_vmem.shape[0]
    upper = direction.astype(jnp.bfloat16)
    lower = (direction - upper.astype(jnp.float32)).astype(jnp.bfloat16)
    both = jnp.concatenate([upper, lower], axis=0)
    weights = dot_nt(direction, vectors_ref[...]) * (1.0 / seqs)
    applied = jnp.dot(
        weights, own_columns(vectors_ref, me, rows), precision=HIGHEST, preferred_element_type=jnp.float32
    )
    chunk = width // len(copies)
    for c, copy in enumerate(copies):
        copy.wait()
        span = slice(c * chunk, (c + 1) * chunk)
        block = prior_vmem[:, span]
        block_upper = block.astype(jnp.bfloat16)
        block_lower = (block - block_upper.astype(jnp.float32)).astype(jnp.bfloat16)
        first = lax.dot_general(both[:, span], block_upper, NT, preferred_element_type=jnp.float32)
        second = lax.dot_general(upper[:, span], block_lower, NT, preferred_element_type=jnp.float32)
        applied = applied + (first[:seqs] + first[seqs:] + second)
    return applied


def flat_index(tensor_size):
    return lax.axis_index("dp") * tensor_size + lax.axis_index("tensor")


def start_kernel(size, tensor_size, *refs):
    pieces, prior_ref = refs[:size], refs[size]
    vectors_ref, applied_ref, norm_ref, held, prior_vmem, sems = refs[size + 1 :]
    copies = prior_copies(prior_ref, prior_vmem, sems)
    for copy in copies:
        copy.start()
    dp = lax.axis_index("dp")
    for k, piece in enumerate(pieces):
        held[dp ^ k] = piece[...]
    vectors = jnp.concatenate([held[k] for k in range(size)], axis=0)
    vectors_ref[...] = vectors
    norm_ref[...] = jnp.broadcast_to(row_sum(vectors * vectors), norm_ref.shape)
    applied_ref[...] = apply_fisher(vectors, vectors_ref, copies, prior_vmem, flat_index(tensor_size))


def start_cg(pieces, prior, tensor_size):
    seqs = len(pieces) * pieces[0].shape[0]
    rows, width = prior.shape
    shape = functools.partial(jax.ShapeDtypeStruct, dtype=jnp.float32)
    return pl.pallas_call(
        functools.partial(start_kernel, len(pieces), tensor_size),
        out_shape=(shape((seqs, width)), shape((seqs, rows)), shape((seqs, LANES))),
        in_specs=[VMEM_SPEC] * len(pieces) + [ANY_SPEC],
        out_specs=(VMEM_SPEC,) * 3,
        scratch_shapes=[
            pltpu.VMEM((len(pieces),) + pieces[0].shape, jnp.float32),
            pltpu.VMEM(prior.shape, jnp.float32),
            pltpu.SemaphoreType.DMA((4,)),
        ],
        compiler_params=pltpu.CompilerParams(vmem_limit_bytes=16 * 2**20),
        name="cg_start",
    )(*pieces, prior)


def step_kernel(size, tensor_size, first, last, *refs):
    blocks, refs = refs[:size], refs[size:]
    if first:
        prior_ref, vectors_ref, norm_ref = refs[:3]
        refs = refs[3:]
    else:
        prior_ref, vectors_ref, norm_ref, direction_ref, residual_ref, solution_ref = refs[:6]
        refs = refs[6:]
    if last:
        queries_ref, curvature_out, norm_out, solved_out, along_out = refs[:5]
        refs = refs[5:]
    else:
        applied_out, norm_out, direction_out, residual_out, solution_out = refs[:5]
        refs = refs[5:]
    held, prior_vmem, sems = refs
    copies = prior_copies(prior_ref, prior_vmem, sems)
    for copy in copies:
        copy.start()
    me = flat_index(tensor_size)
    if size == 1:
        applied = blocks[0][...]
    else:
        rows = blocks[0].shape[1]
        for k, block in enumerate(blocks):
            held[:, pl.ds(pl.multiple_of((me ^ k) * rows, LANES), rows)] = block[...]
        applied = held[...]
    direction = vectors_ref[...] if first else direction_ref[...]
    residual = direction if first else residual_ref[...]
    norm = norm_ref[...][:, :1]
    step = norm / row_sum(direction * applied)
    solution = step * direction
    if not first:
        solution = solution_ref[...] + solution
    residual = residual - step * applied
    norm_next = row_sum(residual * residual)
    direction = residual + (norm_next / norm) * direction
    norm_out[...] = jnp.broadcast_to(norm_next, norm_out.shape)
    applied_rows = apply_fisher(direction, vectors_ref, copies, prior_vmem, me)
    if last:
        held[...] = direction
        own = own_columns(held, me, applied_rows.shape[1])
        curvature_out[...] = jnp.broadcast_to(row_sum(own * applied_rows), curvature_out.shape)
        queries = queries_ref[...].astype(jnp.float32)
        solved_out[...] = dot_nt(solution, queries)
        along_out[...] = dot_nt(direction, queries)
    else:
        applied_out[...] = applied_rows
        direction_out[...] = direction
        residual_out[...] = residual
        solution_out[...] = solution


def step_cg(blocks, prior, vectors, norm, state, queries, tensor_size):
    first, last = state is None, queries is not None
    shape = functools.partial(jax.ShapeDtypeStruct, dtype=jnp.float32)
    whole, column = shape(vectors.shape), shape(norm.shape)
    seqs = vectors.shape[0]
    operands = list(blocks) + [prior, vectors, norm] + list(state or ()) + ([queries] if last else [])
    specs = [VMEM_SPEC] * len(operands)
    specs[len(blocks)] = ANY_SPEC
    if last:
        scores = shape((seqs, queries.shape[0]))
        out_shape = (column, column, scores, scores)
    else:
        out_shape = (shape((seqs, prior.shape[0])), column, whole, whole, whole)
    return pl.pallas_call(
        functools.partial(step_kernel, len(blocks), tensor_size, first, last),
        out_shape=out_shape,
        in_specs=specs,
        out_specs=(VMEM_SPEC,) * len(out_shape),
        scratch_shapes=[
            pltpu.VMEM(vectors.shape, jnp.float32),
            pltpu.VMEM(prior.shape, jnp.float32),
            pltpu.SemaphoreType.DMA((4,)),
        ],
        compiler_params=pltpu.CompilerParams(vmem_limit_bytes=16 * 2**20),
        name="cg_step",
    )(*operands)


def on_device(dp_size, tensor_size, inputs, in_proj, out_grads, out_proj, prior, queries):
    width = R_IN * R_OUT
    both, devices = ("dp", "tensor"), dp_size * tensor_size
    in_local = lax.dot_general(in_proj, inputs, NT, preferred_element_type=jnp.float32)
    in_blocks = exchange(in_local, "tensor", tensor_size)
    out_local = lax.dot_general(out_proj, out_grads, NT, preferred_element_type=jnp.float32)
    partial = partial_vectors(in_blocks, out_local).reshape(-1, width)
    own_vectors = sum(exchange(partial, "tensor", tensor_size))
    pieces = exchange(own_vectors, "dp", dp_size)

    def gather_rows(values):
        if devices <= DIRECT_LIMIT:
            return exchange(values, both, devices)
        held = lax.all_gather(lax.all_gather(values, "tensor", axis=0), "dp", axis=0)
        return [held.transpose(2, 0, 1, 3).reshape(values.shape[0], width)]

    def global_sum(values):
        if devices <= DIRECT_LIMIT:
            return sum(exchange(values, both, devices))
        return lax.psum(values, both)

    vectors, applied_rows, norm = start_cg(pieces, prior, tensor_size)
    state = None
    for iteration in range(1, ITERS - 1):
        blocks = gather_rows(applied_rows)
        applied_rows, norm, *state = step_cg(blocks, prior, vectors, norm, state, None, tensor_size)
    blocks = gather_rows(applied_rows)
    curvature, norm, solved, along = step_cg(blocks, prior, vectors, norm, state, queries, tensor_size)
    curvature = global_sum(curvature)
    return solved + (norm / curvature)[:, :1] * along


def solution(mesh):
    return jax.shard_map(
        functools.partial(on_device, mesh.shape["dp"], mesh.shape["tensor"]),
        mesh=mesh,
        in_specs=(
            P(("groups", "dp", "tensor"), None),
            P(),
            P(("groups", "dp"), "tensor"),
            P(None, "tensor"),
            P(("groups", "dp", "tensor"), None),
            P(("groups", "dp", "tensor"), None),
        ),
        out_specs=P("groups", ("dp", "tensor")),
        check_vma=False,
    )
```

```python
import functools

import jax
import jax.numpy as jnp
from jax import lax
from jax.experimental import pallas as pl
from jax.experimental.pallas import tpu as pltpu
from jax.sharding import PartitionSpec as P

R_IN = 64
R_OUT = 64
SEQ = 1024
ITERS = 4
LANES = 128
NT = (((1,), (1,)), ((), ()))
HIGHEST = lax.Precision.HIGHEST
VMEM_SPEC = pl.BlockSpec(memory_space=pltpu.VMEM)
PARAMS = pltpu.CompilerParams(vmem_limit_bytes=16 * 2**20)
F32 = functools.partial(jax.ShapeDtypeStruct, dtype=jnp.float32)


def gather(value, axes, size):
    return lax.all_to_all(jnp.broadcast_to(value[None], (size,) + value.shape), axes, 0, 0)


def dot_nt(a, b):
    return lax.dot_general(a, b, NT, precision=HIGHEST, preferred_element_type=jnp.float32)


def row_sum(values):
    return jnp.sum(values, axis=1, keepdims=True)


def partial_kernel(in_ref, out_ref, part_ref, held):
    count, _, tokens = in_ref.shape
    for k in range(count):
        held[:, k * tokens : (k + 1) * tokens] = in_ref[k]
    for s in range(part_ref.shape[0]):
        span = slice(s * SEQ, (s + 1) * SEQ)
        part_ref[s] = dot_nt(held[:, span], out_ref[:, span]) * (1.0 / SEQ)


def partial_vectors(in_all, out_local):
    seq_count = out_local.shape[1] // SEQ
    return pl.pallas_call(
        partial_kernel,
        out_shape=F32((seq_count, R_IN, R_OUT)),
        in_specs=[VMEM_SPEC] * 2,
        out_specs=VMEM_SPEC,
        scratch_shapes=[pltpu.VMEM(out_local.shape, jnp.float32)],
        compiler_params=PARAMS,
        name="partial_vectors",
    )(in_all, out_local)


def split_kernel(prior_ref, upper_ref, lower_ref):
    block = prior_ref[...]
    upper = block.astype(jnp.bfloat16)
    upper_ref[...] = upper
    lower_ref[...] = (block - upper.astype(jnp.float32)).astype(jnp.bfloat16)


def split_prior(prior):
    rows, width = prior.shape
    spec = pl.BlockSpec((rows, width // 8), lambda i: (0, i))
    return pl.pallas_call(
        split_kernel,
        grid=(8,),
        out_shape=(jax.ShapeDtypeStruct(prior.shape, jnp.bfloat16),) * 2,
        in_specs=[spec],
        out_specs=(spec, spec),
        compiler_params=PARAMS,
        name="split_prior",
    )(prior)


def own_columns(ref, me, count):
    if count % LANES == 0:
        return ref[:, pl.ds(pl.multiple_of(me * count, LANES), count)]
    per = LANES // count
    held = ref[:, pl.ds(pl.multiple_of((me // per) * LANES, LANES), LANES)]
    return pltpu.roll(held, LANES - (me % per) * count, 1)[:, :count]


def apply_fisher(direction, vectors_ref, upper_ref, lower_ref, me):
    seqs = direction.shape[0]
    upper = direction.astype(jnp.bfloat16)
    lower = (direction - upper.astype(jnp.float32)).astype(jnp.bfloat16)
    both = jnp.concatenate([upper, lower], axis=0)
    weights = dot_nt(direction, vectors_ref[...]) * (1.0 / seqs)
    own = own_columns(vectors_ref, me, upper_ref.shape[0])
    applied = jnp.dot(weights, own, precision=HIGHEST, preferred_element_type=jnp.float32)
    first = lax.dot_general(both, upper_ref[...], NT, preferred_element_type=jnp.float32)
    second = lax.dot_general(upper, lower_ref[...], NT, preferred_element_type=jnp.float32)
    return applied + (first[:seqs] + first[seqs:] + second)


def flat_index(tensor_size):
    return lax.axis_index("dp") * tensor_size + lax.axis_index("tensor")


def start_kernel(tensor_size, pieces_ref, upper_ref, lower_ref, vectors_ref, applied_ref, norm_ref):
    count, seqs, columns = pieces_ref.shape
    for i in range(count):
        dp, tensor = i // tensor_size, i % tensor_size
        vectors_ref[dp * seqs : (dp + 1) * seqs, tensor * columns : (tensor + 1) * columns] = pieces_ref[i]
    vectors = vectors_ref[...]
    norm_ref[...] = jnp.broadcast_to(row_sum(vectors * vectors), norm_ref.shape)
    applied_ref[...] = apply_fisher(vectors, vectors_ref, upper_ref, lower_ref, flat_index(tensor_size))


def start_cg(pieces, prior_pieces, tensor_size):
    seqs = pieces.shape[0] // tensor_size * pieces.shape[1]
    rows, width = prior_pieces[0].shape
    return pl.pallas_call(
        functools.partial(start_kernel, tensor_size),
        out_shape=(F32((seqs, width)), F32((seqs, rows)), F32((seqs, LANES))),
        in_specs=[VMEM_SPEC] * 3,
        out_specs=(VMEM_SPEC,) * 3,
        compiler_params=PARAMS,
        name="cg_start",
    )(pieces, *prior_pieces)


def step_kernel(tensor_size, first, last, *refs):
    blocks_ref, upper_ref, lower_ref, vectors_ref, norm_ref = refs[:5]
    refs = refs[5:]
    if not first:
        direction_ref, residual_ref, solution_ref = refs[:3]
        refs = refs[3:]
    if last:
        queries_ref, curvature_out, norm_out, solved_out, along_out, held = refs
    else:
        applied_out, norm_out, direction_out, residual_out, solution_out, held = refs
    me = flat_index(tensor_size)
    count, _, rows = blocks_ref.shape
    for i in range(count):
        held[:, i * rows : (i + 1) * rows] = blocks_ref[i]
    applied = held[...]
    direction = vectors_ref[...] if first else direction_ref[...]
    residual = direction if first else residual_ref[...]
    norm = norm_ref[...][:, :1]
    step = norm / row_sum(direction * applied)
    solution = step * direction
    if not first:
        solution = solution_ref[...] + solution
    residual = residual - step * applied
    norm_next = row_sum(residual * residual)
    direction = residual + (norm_next / norm) * direction
    norm_out[...] = jnp.broadcast_to(norm_next, norm_out.shape)
    applied_rows = apply_fisher(direction, vectors_ref, upper_ref, lower_ref, me)
    if last:
        held[...] = direction
        own = own_columns(held, me, rows)
        curvature_out[...] = jnp.broadcast_to(row_sum(own * applied_rows), curvature_out.shape)
        queries = queries_ref[...].astype(jnp.float32)
        solved_out[...] = dot_nt(solution, queries)
        along_out[...] = dot_nt(direction, queries)
    else:
        applied_out[...] = applied_rows
        direction_out[...] = direction
        residual_out[...] = residual
        solution_out[...] = solution


def step_cg(blocks, prior_pieces, vectors, norm, state, queries, tensor_size):
    first, last = state is None, queries is not None
    whole, column = F32(vectors.shape), F32(norm.shape)
    seqs = vectors.shape[0]
    operands = [blocks, *prior_pieces, vectors, norm, *(state or ())] + ([queries] if last else [])
    if last:
        scores = F32((seqs, queries.shape[0]))
        out_shape = (column, column, scores, scores)
    else:
        out_shape = (F32((seqs, blocks.shape[2])), column, whole, whole, whole)
    return pl.pallas_call(
        functools.partial(step_kernel, tensor_size, first, last),
        out_shape=out_shape,
        in_specs=[VMEM_SPEC] * len(operands),
        out_specs=(VMEM_SPEC,) * len(out_shape),
        scratch_shapes=[pltpu.VMEM(vectors.shape, jnp.float32)],
        compiler_params=PARAMS,
        name="cg_step",
    )(*operands)


def on_device(dp_size, tensor_size, inputs, in_proj, out_grads, out_proj, prior, queries):
    width = R_IN * R_OUT
    both, devices = ("dp", "tensor"), dp_size * tensor_size
    in_local = lax.dot_general(in_proj, inputs, NT, preferred_element_type=jnp.float32)
    in_all = gather(in_local, "tensor", tensor_size)
    out_local = lax.dot_general(out_proj, out_grads, NT, preferred_element_type=jnp.float32)
    partial = partial_vectors(in_all, out_local).reshape(-1, tensor_size, width // tensor_size)
    partial = lax.all_to_all(partial.transpose(1, 0, 2), "tensor", 0, 0)
    pieces = gather(jnp.sum(partial, axis=0), both, devices)
    prior_pieces = split_prior(prior)
    vectors, applied_rows, norm = start_cg(pieces, prior_pieces, tensor_size)
    state = None
    for iteration in range(1, ITERS - 1):
        blocks = gather(applied_rows, both, devices)
        applied_rows, norm, *state = step_cg(blocks, prior_pieces, vectors, norm, state, None, tensor_size)
    blocks = gather(applied_rows, both, devices)
    curvature, norm, solved, along = step_cg(blocks, prior_pieces, vectors, norm, state, queries, tensor_size)
    curvature = jnp.sum(gather(curvature, both, devices), axis=0)
    return solved + (norm / curvature)[:, :1] * along


def solution(mesh):
    return jax.shard_map(
        functools.partial(on_device, mesh.shape["dp"], mesh.shape["tensor"]),
        mesh=mesh,
        in_specs=(
            P(("groups", "dp", "tensor"), None),
            P(),
            P(("groups", "dp"), "tensor"),
            P(None, "tensor"),
            P(("groups", "dp", "tensor"), None),
            P(("groups", "dp", "tensor"), None),
        ),
        out_specs=P("groups", ("dp", "tensor")),
        check_vma=False,
    )
```

```python
import functools

import jax
import jax.numpy as jnp
from jax import lax
from jax.experimental import pallas as pl
from jax.experimental.pallas import tpu as pltpu
from jax.sharding import PartitionSpec as P

R_IN = 64
R_OUT = 64
SEQ = 1024
ITERS = 4
LANES = 128
NT = (((1,), (1,)), ((), ()))
HIGHEST = lax.Precision.HIGHEST
VMEM_SPEC = pl.BlockSpec(memory_space=pltpu.VMEM)
PARAMS = pltpu.CompilerParams(vmem_limit_bytes=16 * 2**20)
F32 = functools.partial(jax.ShapeDtypeStruct, dtype=jnp.float32)


def swap(value, axis, size, bit):
    return lax.ppermute(value, axis, [(i, i ^ bit) for i in range(size)])


def bits(size):
    return [1 << b for b in reversed(range(size.bit_length() - 1))]


def gather(value, axes, size):
    return lax.all_to_all(jnp.broadcast_to(value[None], (size,) + value.shape), axes, 0, 0)


def sum_over(value, axis, size):
    for bit in bits(size):
        value = value + swap(value, axis, size, bit)
    return value


def doubled(value, axis, size):
    held, order = value[None], [0]
    for bit in bits(size):
        held = jnp.concatenate([held, swap(held, axis, size, bit)], axis=0)
        order = order + [k ^ bit for k in order]
    return held, tuple(order)


def direct(value, axis, size):
    return [value] + [swap(value, axis, size, k) for k in reversed(range(1, size))][::-1]


def dot_nt(a, b):
    return lax.dot_general(a, b, NT, precision=HIGHEST, preferred_element_type=jnp.float32)


def row_sum(values):
    return jnp.sum(values, axis=1, keepdims=True)


def partial_kernel(in_ref, out_ref, part_ref, held):
    count, _, tokens = in_ref.shape
    for k in range(count):
        held[:, k * tokens : (k + 1) * tokens] = in_ref[k]
    for s in range(part_ref.shape[0]):
        span = slice(s * SEQ, (s + 1) * SEQ)
        part_ref[s] = dot_nt(held[:, span], out_ref[:, span]) * (1.0 / SEQ)


def partial_vectors(in_all, out_local):
    seq_count = out_local.shape[1] // SEQ
    return pl.pallas_call(
        partial_kernel,
        out_shape=F32((seq_count, R_IN, R_OUT)),
        in_specs=[VMEM_SPEC] * 2,
        out_specs=VMEM_SPEC,
        scratch_shapes=[pltpu.VMEM(out_local.shape, jnp.float32)],
        compiler_params=PARAMS,
        name="partial_vectors",
    )(in_all, out_local)


def split_kernel(prior_ref, upper_ref, lower_ref):
    block = prior_ref[...]
    upper = block.astype(jnp.bfloat16)
    upper_ref[...] = upper
    lower_ref[...] = (block - upper.astype(jnp.float32)).astype(jnp.bfloat16)


def split_prior(prior):
    rows, width = prior.shape
    spec = pl.BlockSpec((rows, width // 8), lambda i: (0, i))
    return pl.pallas_call(
        split_kernel,
        grid=(8,),
        out_shape=(jax.ShapeDtypeStruct(prior.shape, jnp.bfloat16),) * 2,
        in_specs=[spec],
        out_specs=(spec, spec),
        compiler_params=PARAMS,
        name="split_prior",
    )(prior)


def own_columns(ref, me, count):
    if count % LANES == 0:
        return ref[:, pl.ds(pl.multiple_of(me * count, LANES), count)]
    per = LANES // count
    held = ref[:, pl.ds(pl.multiple_of((me // per) * LANES, LANES), LANES)]
    return pltpu.roll(held, LANES - (me % per) * count, 1)[:, :count]


def apply_fisher(direction, vectors_ref, upper_ref, lower_ref, me):
    seqs = direction.shape[0]
    upper = direction.astype(jnp.bfloat16)
    lower = (direction - upper.astype(jnp.float32)).astype(jnp.bfloat16)
    both = jnp.concatenate([upper, lower], axis=0)
    weights = dot_nt(direction, vectors_ref[...]) * (1.0 / seqs)
    own = own_columns(vectors_ref, me, upper_ref.shape[0])
    applied = jnp.dot(weights, own, precision=HIGHEST, preferred_element_type=jnp.float32)
    first = lax.dot_general(both, upper_ref[...], NT, preferred_element_type=jnp.float32)
    second = lax.dot_general(upper, lower_ref[...], NT, preferred_element_type=jnp.float32)
    return applied + (first[:seqs] + first[seqs:] + second)


def flat_index(tensor_size):
    return lax.axis_index("dp") * tensor_size + lax.axis_index("tensor")


def start_kernel(size, tensor_size, *refs):
    pieces, (upper_ref, lower_ref, vectors_ref, applied_ref, norm_ref, held) = refs[:size], refs[size:]
    dp = lax.axis_index("dp")
    for k, piece in enumerate(pieces):
        held[dp ^ k] = piece[...]
    vectors = jnp.concatenate([held[k] for k in range(size)], axis=0)
    vectors_ref[...] = vectors
    norm_ref[...] = jnp.broadcast_to(row_sum(vectors * vectors), norm_ref.shape)
    applied_ref[...] = apply_fisher(vectors, vectors_ref, upper_ref, lower_ref, flat_index(tensor_size))


def start_cg(pieces, prior_pieces, tensor_size):
    size, seqs = len(pieces), len(pieces) * pieces[0].shape[0]
    rows, width = prior_pieces[0].shape
    return pl.pallas_call(
        functools.partial(start_kernel, size, tensor_size),
        out_shape=(F32((seqs, width)), F32((seqs, rows)), F32((seqs, LANES))),
        in_specs=[VMEM_SPEC] * (size + 2),
        out_specs=(VMEM_SPEC,) * 3,
        scratch_shapes=[pltpu.VMEM((size,) + pieces[0].shape, jnp.float32)],
        compiler_params=PARAMS,
        name="cg_start",
    )(*pieces, *prior_pieces)


def place_blocks(blocks, order, tensor_size, held):
    rows = blocks[0].shape[2]
    if rows % LANES:
        for i in range(blocks[0].shape[0]):
            held[:, i * rows : (i + 1) * rows] = blocks[0][i]
        return
    dp, tensor = lax.axis_index("dp"), lax.axis_index("tensor")
    for k, block in enumerate(blocks):
        for i, j in enumerate(order):
            start = ((dp ^ k) * tensor_size + (tensor ^ j)) * rows
            held[:, pl.ds(pl.multiple_of(start, LANES), rows)] = block[i]


def step_kernel(size, order, tensor_size, first, last, *refs):
    blocks, refs = refs[:size], refs[size:]
    upper_ref, lower_ref, vectors_ref, norm_ref = refs[:4]
    refs = refs[4:]
    if not first:
        direction_ref, residual_ref, solution_ref = refs[:3]
        refs = refs[3:]
    if last:
        queries_ref, curvature_out, norm_out, solved_out, along_out, held = refs
    else:
        applied_out, norm_out, direction_out, residual_out, solution_out, held = refs
    me = flat_index(tensor_size)
    place_blocks(blocks, order, tensor_size, held)
    applied = held[...]
    direction = vectors_ref[...] if first else direction_ref[...]
    residual = direction if first else residual_ref[...]
    norm = norm_ref[...][:, :1]
    step = norm / row_sum(direction * applied)
    solution = step * direction
    if not first:
        solution = solution_ref[...] + solution
    residual = residual - step * applied
    norm_next = row_sum(residual * residual)
    direction = residual + (norm_next / norm) * direction
    norm_out[...] = jnp.broadcast_to(norm_next, norm_out.shape)
    applied_rows = apply_fisher(direction, vectors_ref, upper_ref, lower_ref, me)
    if last:
        held[...] = direction
        own = own_columns(held, me, applied_rows.shape[1])
        curvature_out[...] = jnp.broadcast_to(row_sum(own * applied_rows), curvature_out.shape)
        queries = queries_ref[...].astype(jnp.float32)
        solved_out[...] = dot_nt(solution, queries)
        along_out[...] = dot_nt(direction, queries)
    else:
        applied_out[...] = applied_rows
        direction_out[...] = direction
        residual_out[...] = residual
        solution_out[...] = solution


def step_cg(gathered, prior_pieces, vectors, norm, state, queries, tensor_size):
    first, last = state is None, queries is not None
    blocks, order = gathered
    whole, column = F32(vectors.shape), F32(norm.shape)
    seqs = vectors.shape[0]
    operands = [*blocks, *prior_pieces, vectors, norm, *(state or ())] + ([queries] if last else [])
    if last:
        scores = F32((seqs, queries.shape[0]))
        out_shape = (column, column, scores, scores)
    else:
        out_shape = (F32((seqs, prior_pieces[0].shape[0])), column, whole, whole, whole)
    return pl.pallas_call(
        functools.partial(step_kernel, len(blocks), order, tensor_size, first, last),
        out_shape=out_shape,
        in_specs=[VMEM_SPEC] * len(operands),
        out_specs=(VMEM_SPEC,) * len(out_shape),
        scratch_shapes=[pltpu.VMEM(vectors.shape, jnp.float32)],
        compiler_params=PARAMS,
        name="cg_step",
    )(*operands)


def on_device(dp_size, tensor_size, inputs, in_proj, out_grads, out_proj, prior, queries):
    width = R_IN * R_OUT
    both, devices = ("dp", "tensor"), dp_size * tensor_size
    in_local = lax.dot_general(in_proj, inputs, NT, preferred_element_type=jnp.float32)
    in_all = gather(in_local, "tensor", tensor_size)
    out_local = lax.dot_general(out_proj, out_grads, NT, preferred_element_type=jnp.float32)
    partial = partial_vectors(in_all, out_local).reshape(-1, width)
    pieces = direct(sum_over(partial, "tensor", tensor_size), "dp", dp_size)
    prior_pieces = split_prior(prior)

    def gather_rows(values):
        if values.shape[1] % LANES:
            return [gather(values, both, devices)], None
        held, order = doubled(values, "tensor", tensor_size)
        return direct(held, "dp", dp_size), order

    vectors, applied_rows, norm = start_cg(pieces, prior_pieces, tensor_size)
    state = None
    for iteration in range(1, ITERS - 1):
        gathered = gather_rows(applied_rows)
        applied_rows, norm, *state = step_cg(gathered, prior_pieces, vectors, norm, state, None, tensor_size)
    gathered = gather_rows(applied_rows)
    curvature, norm, solved, along = step_cg(gathered, prior_pieces, vectors, norm, state, queries, tensor_size)
    curvature = sum_over(sum_over(curvature, "tensor", tensor_size), "dp", dp_size)
    return solved + (norm / curvature)[:, :1] * along


def solution(mesh):
    return jax.shard_map(
        functools.partial(on_device, mesh.shape["dp"], mesh.shape["tensor"]),
        mesh=mesh,
        in_specs=(
            P(("groups", "dp", "tensor"), None),
            P(),
            P(("groups", "dp"), "tensor"),
            P(None, "tensor"),
            P(("groups", "dp", "tensor"), None),
            P(("groups", "dp", "tensor"), None),
        ),
        out_specs=P("groups", ("dp", "tensor")),
        check_vma=False,
    )
```

```python
import functools

import jax
import jax.numpy as jnp
from jax import lax
from jax.experimental import pallas as pl
from jax.experimental.pallas import tpu as pltpu
from jax.sharding import PartitionSpec as P

R_IN = 64
R_OUT = 64
SEQ = 1024
ITERS = 4
LANES = 128
NT = (((1,), (1,)), ((), ()))
HIGHEST = lax.Precision.HIGHEST
VMEM_SPEC = pl.BlockSpec(memory_space=pltpu.VMEM)
PARAMS = pltpu.CompilerParams(vmem_limit_bytes=16 * 2**20)
F32 = functools.partial(jax.ShapeDtypeStruct, dtype=jnp.float32)


def swap(value, axis, size, bit):
    return lax.ppermute(value, axis, [(i, i ^ bit) for i in range(size)])


def bits(size):
    return [1 << b for b in reversed(range(size.bit_length() - 1))]


def gather(value, axes, size):
    return lax.all_to_all(jnp.broadcast_to(value[None], (size,) + value.shape), axes, 0, 0)


def sum_over(value, axis, size):
    for bit in bits(size):
        value = value + swap(value, axis, size, bit)
    return value


def direct(value, axis, size):
    return [value] + [swap(value, axis, size, k) for k in reversed(range(1, size))][::-1]


def dot_nt(a, b):
    return lax.dot_general(a, b, NT, precision=HIGHEST, preferred_element_type=jnp.float32)


def row_sum(values):
    return jnp.sum(values, axis=1, keepdims=True)


def in_kernel(in_ref, proj_ref, feats_ref, total):
    step = pl.program_id(0)

    @pl.when(step == 0)
    def _():
        total[...] = jnp.zeros_like(total)

    total[...] += lax.dot_general(in_ref[...], proj_ref[...], NT, preferred_element_type=jnp.float32)

    @pl.when(step == pl.num_programs(0) - 1)
    def _():
        feats_ref[...] = total[...].T


def in_features(inputs, in_proj):
    tokens, width = inputs.shape
    chunk = 1024
    return pl.pallas_call(
        in_kernel,
        grid=(width // chunk,),
        out_shape=F32((R_IN, tokens)),
        in_specs=[
            pl.BlockSpec((tokens, chunk), lambda i: (0, i)),
            pl.BlockSpec((R_IN, chunk), lambda i: (0, i)),
        ],
        out_specs=pl.BlockSpec((R_IN, tokens), lambda i: (0, 0)),
        scratch_shapes=[pltpu.VMEM((tokens, R_IN), jnp.float32)],
        compiler_params=PARAMS,
        name="in_features",
    )(inputs, in_proj)


def out_kernel(grads_ref, proj_ref, prior_ref, feats_ref, upper_ref, lower_ref):
    feats = lax.dot_general(grads_ref[...], proj_ref[...], NT, preferred_element_type=jnp.float32)
    feats_ref[...] = feats.T
    block = prior_ref[...]
    upper = block.astype(jnp.bfloat16)
    upper_ref[...] = upper
    lower_ref[...] = (block - upper.astype(jnp.float32)).astype(jnp.bfloat16)


def out_features(out_grads, out_proj, prior):
    tokens, hidden = out_grads.shape
    rows, width = prior.shape
    steps = tokens // LANES
    prior_spec = pl.BlockSpec((rows, width // steps), lambda i: (0, i))
    piece = jax.ShapeDtypeStruct(prior.shape, jnp.bfloat16)
    feats, *pieces = pl.pallas_call(
        out_kernel,
        grid=(steps,),
        out_shape=(F32((R_OUT, tokens)), piece, piece),
        in_specs=[
            pl.BlockSpec((LANES, hidden), lambda i: (i, 0)),
            pl.BlockSpec((R_OUT, hidden), lambda i: (0, 0)),
            prior_spec,
        ],
        out_specs=(pl.BlockSpec((R_OUT, LANES), lambda i: (0, i)), prior_spec, prior_spec),
        compiler_params=PARAMS,
        name="out_features",
    )(out_grads, out_proj, prior)
    return feats, pieces


def partial_kernel(size, *refs):
    blocks, (out_ref, part_ref, held) = refs[:size], refs[size:]
    me = lax.axis_index("tensor")
    tokens = blocks[0].shape[1]
    for k, block in enumerate(blocks):
        start = pl.multiple_of((me ^ k) * tokens, LANES)
        held[:, pl.ds(start, tokens)] = block[...]
    for s in range(part_ref.shape[0]):
        span = slice(s * SEQ, (s + 1) * SEQ)
        part_ref[s] = dot_nt(held[:, span], out_ref[:, span]) * (1.0 / SEQ)


def partial_vectors(blocks, out_local):
    seq_count = out_local.shape[1] // SEQ
    return pl.pallas_call(
        functools.partial(partial_kernel, len(blocks)),
        out_shape=F32((seq_count, R_IN, R_OUT)),
        in_specs=[VMEM_SPEC] * (len(blocks) + 1),
        out_specs=VMEM_SPEC,
        scratch_shapes=[pltpu.VMEM(out_local.shape, jnp.float32)],
        compiler_params=PARAMS,
        name="partial_vectors",
    )(*blocks, out_local)


def own_columns(ref, me, count):
    if count % LANES == 0:
        return ref[:, pl.ds(pl.multiple_of(me * count, LANES), count)]
    per = LANES // count
    held = ref[:, pl.ds(pl.multiple_of((me // per) * LANES, LANES), LANES)]
    return pltpu.roll(held, LANES - (me % per) * count, 1)[:, :count]


def apply_fisher(direction, vectors_ref, upper_ref, lower_ref, me):
    seqs = direction.shape[0]
    upper = direction.astype(jnp.bfloat16)
    lower = (direction - upper.astype(jnp.float32)).astype(jnp.bfloat16)
    both = jnp.concatenate([upper, lower], axis=0)
    weights = dot_nt(direction, vectors_ref[...]) * (1.0 / seqs)
    own = own_columns(vectors_ref, me, upper_ref.shape[0])
    applied = jnp.dot(weights, own, precision=HIGHEST, preferred_element_type=jnp.float32)
    first = lax.dot_general(both, upper_ref[...], NT, preferred_element_type=jnp.float32)
    second = lax.dot_general(upper, lower_ref[...], NT, preferred_element_type=jnp.float32)
    return applied + (first[:seqs] + first[seqs:] + second)


def flat_index(tensor_size):
    return lax.axis_index("dp") * tensor_size + lax.axis_index("tensor")


def start_kernel(size, tensor_size, *refs):
    pieces, (upper_ref, lower_ref, vectors_ref, applied_ref, norm_ref, held) = refs[:size], refs[size:]
    dp = lax.axis_index("dp")
    for k, piece in enumerate(pieces):
        held[dp ^ k] = piece[...]
    vectors = jnp.concatenate([held[k] for k in range(size)], axis=0)
    vectors_ref[...] = vectors
    norm_ref[...] = jnp.broadcast_to(row_sum(vectors * vectors), norm_ref.shape)
    applied_ref[...] = apply_fisher(vectors, vectors_ref, upper_ref, lower_ref, flat_index(tensor_size))


def start_cg(pieces, prior_pieces, tensor_size):
    size, seqs = len(pieces), len(pieces) * pieces[0].shape[0]
    rows, width = prior_pieces[0].shape
    return pl.pallas_call(
        functools.partial(start_kernel, size, tensor_size),
        out_shape=(F32((seqs, width)), F32((seqs, rows)), F32((seqs, LANES))),
        in_specs=[VMEM_SPEC] * (size + 2),
        out_specs=(VMEM_SPEC,) * 3,
        scratch_shapes=[pltpu.VMEM((size,) + pieces[0].shape, jnp.float32)],
        compiler_params=PARAMS,
        name="cg_start",
    )(*pieces, *prior_pieces)


def on_lanes(column):
    seqs = column.shape[0]
    row = lax.broadcasted_iota(jnp.int32, (seqs, LANES), 0)
    lane = lax.broadcasted_iota(jnp.int32, (seqs, LANES), 1)
    return jnp.sum(jnp.where(row == lane, column, 0.0), axis=0, keepdims=True)


def step_kernel(tensor_size, first, last, *refs):
    blocks_ref, upper_ref, lower_ref, vectors_ref, norm_ref = refs[:5]
    refs = refs[5:]
    if not first:
        direction_ref, residual_ref, solution_ref = refs[:3]
        refs = refs[3:]
    if last:
        queries_ref, curvature_out, norm_out, solved_out, along_out, held = refs
    else:
        applied_out, norm_out, direction_out, residual_out, solution_out, held = refs
    me = flat_index(tensor_size)
    count, _, rows = blocks_ref.shape
    for i in range(count):
        held[:, i * rows : (i + 1) * rows] = blocks_ref[i]
    applied = held[...]
    direction = vectors_ref[...] if first else direction_ref[...]
    residual = direction if first else residual_ref[...]
    norm = norm_ref[...][:, :1]
    step = norm / row_sum(direction * applied)
    solution = step * direction
    if not first:
        solution = solution_ref[...] + solution
    residual = residual - step * applied
    norm_next = row_sum(residual * residual)
    direction = residual + (norm_next / norm) * direction
    norm_out[...] = on_lanes(norm_next) if last else jnp.broadcast_to(norm_next, norm_out.shape)
    applied_rows = apply_fisher(direction, vectors_ref, upper_ref, lower_ref, me)
    if last:
        held[...] = direction
        own = own_columns(held, me, rows)
        curvature_out[...] = on_lanes(row_sum(own * applied_rows))
        queries = queries_ref[...].astype(jnp.float32)
        solved_out[...] = dot_nt(solution, queries)
        along_out[...] = dot_nt(direction, queries)
    else:
        applied_out[...] = applied_rows
        direction_out[...] = direction
        residual_out[...] = residual
        solution_out[...] = solution


def step_cg(blocks, prior_pieces, vectors, norm, state, queries, tensor_size):
    first, last = state is None, queries is not None
    whole, column = F32(vectors.shape), F32(norm.shape)
    seqs = vectors.shape[0]
    operands = [blocks, *prior_pieces, vectors, norm, *(state or ())] + ([queries] if last else [])
    if last:
        scores = F32((seqs, queries.shape[0]))
        out_shape = (F32((1, LANES)), F32((1, LANES)), scores, scores)
    else:
        out_shape = (F32((seqs, prior_pieces[0].shape[0])), column, whole, whole, whole)
    return pl.pallas_call(
        functools.partial(step_kernel, tensor_size, first, last),
        out_shape=out_shape,
        in_specs=[VMEM_SPEC] * len(operands),
        out_specs=(VMEM_SPEC,) * len(out_shape),
        scratch_shapes=[pltpu.VMEM(vectors.shape, jnp.float32)],
        compiler_params=PARAMS,
        name="cg_step",
    )(*operands)


def on_device(dp_size, tensor_size, inputs, in_proj, out_grads, out_proj, prior, queries):
    width = R_IN * R_OUT
    both, devices = ("dp", "tensor"), dp_size * tensor_size
    in_blocks = direct(in_features(inputs, in_proj), "tensor", tensor_size)
    out_local, prior_pieces = out_features(out_grads, out_proj, prior)
    partial = partial_vectors(in_blocks, out_local).reshape(-1, width)
    pieces = direct(sum_over(partial, "tensor", tensor_size), "dp", dp_size)
    vectors, applied_rows, norm = start_cg(pieces, prior_pieces, tensor_size)
    state = None
    for iteration in range(1, ITERS - 1):
        blocks = gather(applied_rows, both, devices)
        applied_rows, norm, *state = step_cg(blocks, prior_pieces, vectors, norm, state, None, tensor_size)
    blocks = gather(applied_rows, both, devices)
    curvature, norm, solved, along = step_cg(blocks, prior_pieces, vectors, norm, state, queries, tensor_size)
    curvature = jnp.sum(gather(curvature, both, devices), axis=0)
    step = (norm / curvature)[0, : solved.shape[0]]
    return solved + step[:, None] * along


def solution(mesh):
    return jax.shard_map(
        functools.partial(on_device, mesh.shape["dp"], mesh.shape["tensor"]),
        mesh=mesh,
        in_specs=(
            P(("groups", "dp", "tensor"), None),
            P(),
            P(("groups", "dp"), "tensor"),
            P(None, "tensor"),
            P(("groups", "dp", "tensor"), None),
            P(("groups", "dp", "tensor"), None),
        ),
        out_specs=P("groups", ("dp", "tensor")),
        check_vma=False,
    )
```

```python
import functools

import jax
import jax.numpy as jnp
from jax import lax
from jax.experimental import pallas as pl
from jax.experimental.pallas import tpu as pltpu
from jax.sharding import PartitionSpec as P

R_IN = 64
R_OUT = 64
SEQ = 1024
ITERS = 4
LANES = 128
NT = (((1,), (1,)), ((), ()))
HIGHEST = lax.Precision.HIGHEST
VMEM_SPEC = pl.BlockSpec(memory_space=pltpu.VMEM)
PARAMS = pltpu.CompilerParams(vmem_limit_bytes=16 * 2**20)
F32 = functools.partial(jax.ShapeDtypeStruct, dtype=jnp.float32)


def swap(value, axis, size, bit):
    return lax.ppermute(value, axis, [(i, i ^ bit) for i in range(size)])


def bits(size):
    return [1 << b for b in reversed(range(size.bit_length() - 1))]


def gather(value, axes, size):
    return lax.all_to_all(jnp.broadcast_to(value[None], (size,) + value.shape), axes, 0, 0)


def sum_over(value, axis, size):
    for bit in bits(size):
        value = value + swap(value, axis, size, bit)
    return value


def direct(value, axis, size):
    return [value] + [swap(value, axis, size, k) for k in reversed(range(1, size))][::-1]


def dot_nt(a, b):
    return lax.dot_general(a, b, NT, precision=HIGHEST, preferred_element_type=jnp.float32)


def row_sum(values):
    return jnp.sum(values, axis=1, keepdims=True)


def in_kernel(in_ref, proj_ref, feats_ref, total):
    step = pl.program_id(0)

    @pl.when(step == 0)
    def _():
        total[...] = jnp.zeros_like(total)

    total[...] += lax.dot_general(in_ref[...], proj_ref[...], NT, preferred_element_type=jnp.float32)

    @pl.when(step == pl.num_programs(0) - 1)
    def _():
        feats_ref[...] = total[...].T


def in_features(inputs, in_proj):
    tokens, width = inputs.shape
    chunk = 1024
    return pl.pallas_call(
        in_kernel,
        grid=(width // chunk,),
        out_shape=F32((R_IN, tokens)),
        in_specs=[
            pl.BlockSpec((tokens, chunk), lambda i: (0, i)),
            pl.BlockSpec((R_IN, chunk), lambda i: (0, i)),
        ],
        out_specs=pl.BlockSpec((R_IN, tokens), lambda i: (0, 0)),
        scratch_shapes=[pltpu.VMEM((tokens, R_IN), jnp.float32)],
        compiler_params=pltpu.CompilerParams(vmem_limit_bytes=60 * 2**20),
        name="in_features",
    )(inputs, in_proj)


def out_kernel(grads_ref, proj_ref, feats_ref, turned):
    @pl.when(pl.program_id(0) == 0)
    def _():
        turned[...] = proj_ref[...].T

    feats = jnp.dot(grads_ref[...], turned[...], preferred_element_type=jnp.float32)
    feats_ref[...] = feats.T


def out_features(out_grads, out_proj):
    tokens, hidden = out_grads.shape
    block = 256
    return pl.pallas_call(
        out_kernel,
        grid=(tokens // block,),
        out_shape=F32((R_OUT, tokens)),
        in_specs=[
            pl.BlockSpec((block, hidden), lambda i: (i, 0)),
            pl.BlockSpec((R_OUT, hidden), lambda i: (0, 0)),
        ],
        out_specs=pl.BlockSpec((R_OUT, block), lambda i: (0, i)),
        scratch_shapes=[pltpu.VMEM((hidden, R_OUT), jnp.bfloat16)],
        compiler_params=pltpu.CompilerParams(vmem_limit_bytes=60 * 2**20),
        name="out_features",
    )(out_grads, out_proj)


def split_kernel(prior_ref, upper_ref, lower_ref):
    block = prior_ref[...]
    upper = block.astype(jnp.bfloat16)
    upper_ref[...] = upper
    lower_ref[...] = (block - upper.astype(jnp.float32)).astype(jnp.bfloat16)


def split_prior(prior):
    rows, width = prior.shape
    spec = pl.BlockSpec((rows, width // 8), lambda i: (0, i))
    return pl.pallas_call(
        split_kernel,
        grid=(8,),
        out_shape=(jax.ShapeDtypeStruct(prior.shape, jnp.bfloat16),) * 2,
        in_specs=[spec],
        out_specs=(spec, spec),
        compiler_params=pltpu.CompilerParams(vmem_limit_bytes=56 * 2**20),
        name="split_prior",
    )(prior)


def partial_kernel(size, *refs):
    blocks, (out_ref, part_ref, held) = refs[:size], refs[size:]
    me = lax.axis_index("tensor")
    tokens = blocks[0].shape[1]
    for k, block in enumerate(blocks):
        start = pl.multiple_of((me ^ k) * tokens, LANES)
        held[:, pl.ds(start, tokens)] = block[...]
    for s in range(part_ref.shape[0]):
        span = slice(s * SEQ, (s + 1) * SEQ)
        part_ref[s] = dot_nt(held[:, span], out_ref[:, span]) * (1.0 / SEQ)


def partial_vectors(blocks, out_local):
    seq_count = out_local.shape[1] // SEQ
    return pl.pallas_call(
        functools.partial(partial_kernel, len(blocks)),
        out_shape=F32((seq_count, R_IN, R_OUT)),
        in_specs=[VMEM_SPEC] * (len(blocks) + 1),
        out_specs=VMEM_SPEC,
        scratch_shapes=[pltpu.VMEM(out_local.shape, jnp.float32)],
        compiler_params=PARAMS,
        name="partial_vectors",
    )(*blocks, out_local)


def own_columns(ref, me, count):
    if count % LANES == 0:
        return ref[:, pl.ds(pl.multiple_of(me * count, LANES), count)]
    per = LANES // count
    held = ref[:, pl.ds(pl.multiple_of((me // per) * LANES, LANES), LANES)]
    return pltpu.roll(held, LANES - (me % per) * count, 1)[:, :count]


def apply_fisher(direction, vectors_ref, upper_ref, lower_ref, me):
    seqs = direction.shape[0]
    upper = direction.astype(jnp.bfloat16)
    lower = (direction - upper.astype(jnp.float32)).astype(jnp.bfloat16)
    both = jnp.concatenate([upper, lower], axis=0)
    weights = dot_nt(direction, vectors_ref[...]) * (1.0 / seqs)
    own = own_columns(vectors_ref, me, upper_ref.shape[0])
    applied = jnp.dot(weights, own, precision=HIGHEST, preferred_element_type=jnp.float32)
    first = lax.dot_general(both, upper_ref[...], NT, preferred_element_type=jnp.float32)
    second = lax.dot_general(upper, lower_ref[...], NT, preferred_element_type=jnp.float32)
    return applied + (first[:seqs] + first[seqs:] + second)


def flat_index(tensor_size):
    return lax.axis_index("dp") * tensor_size + lax.axis_index("tensor")


def start_kernel(size, tensor_size, *refs):
    pieces, (upper_ref, lower_ref, vectors_ref, applied_ref, norm_ref, held) = refs[:size], refs[size:]
    dp = lax.axis_index("dp")
    for k, piece in enumerate(pieces):
        held[dp ^ k] = piece[...]
    vectors = jnp.concatenate([held[k] for k in range(size)], axis=0)
    vectors_ref[...] = vectors
    norm_ref[...] = jnp.broadcast_to(row_sum(vectors * vectors), norm_ref.shape)
    applied_ref[...] = apply_fisher(vectors, vectors_ref, upper_ref, lower_ref, flat_index(tensor_size))


def start_cg(pieces, prior_pieces, tensor_size):
    size, seqs = len(pieces), len(pieces) * pieces[0].shape[0]
    rows, width = prior_pieces[0].shape
    return pl.pallas_call(
        functools.partial(start_kernel, size, tensor_size),
        out_shape=(F32((seqs, width)), F32((seqs, rows)), F32((seqs, LANES))),
        in_specs=[VMEM_SPEC] * (size + 2),
        out_specs=(VMEM_SPEC,) * 3,
        scratch_shapes=[pltpu.VMEM((size,) + pieces[0].shape, jnp.float32)],
        compiler_params=PARAMS,
        name="cg_start",
    )(*pieces, *prior_pieces)


def on_lanes(column):
    seqs = column.shape[0]
    row = lax.broadcasted_iota(jnp.int32, (seqs, LANES), 0)
    lane = lax.broadcasted_iota(jnp.int32, (seqs, LANES), 1)
    return jnp.sum(jnp.where(row == lane, column, 0.0), axis=0, keepdims=True)


def step_kernel(tensor_size, first, last, *refs):
    blocks_ref, upper_ref, lower_ref, vectors_ref, norm_ref = refs[:5]
    refs = refs[5:]
    if not first:
        direction_ref, residual_ref, solution_ref = refs[:3]
        refs = refs[3:]
    if last:
        queries_ref, curvature_out, norm_out, solved_out, along_out, held = refs
    else:
        applied_out, norm_out, direction_out, residual_out, solution_out, held = refs
    me = flat_index(tensor_size)
    count, _, rows = blocks_ref.shape
    for i in range(count):
        held[:, i * rows : (i + 1) * rows] = blocks_ref[i]
    applied = held[...]
    direction = vectors_ref[...] if first else direction_ref[...]
    residual = direction if first else residual_ref[...]
    norm = norm_ref[...][:, :1]
    step = norm / row_sum(direction * applied)
    solution = step * direction
    if not first:
        solution = solution_ref[...] + solution
    residual = residual - step * applied
    norm_next = row_sum(residual * residual)
    direction = residual + (norm_next / norm) * direction
    norm_out[...] = on_lanes(norm_next) if last else jnp.broadcast_to(norm_next, norm_out.shape)
    applied_rows = apply_fisher(direction, vectors_ref, upper_ref, lower_ref, me)
    if last:
        held[...] = direction
        own = own_columns(held, me, rows)
        curvature_out[...] = on_lanes(row_sum(own * applied_rows))
        queries = queries_ref[...].astype(jnp.float32)
        solved_out[...] = dot_nt(solution, queries)
        along_out[...] = dot_nt(direction, queries)
    else:
        applied_out[...] = applied_rows
        direction_out[...] = direction
        residual_out[...] = residual
        solution_out[...] = solution


def step_cg(blocks, prior_pieces, vectors, norm, state, queries, tensor_size):
    first, last = state is None, queries is not None
    whole, column = F32(vectors.shape), F32(norm.shape)
    seqs = vectors.shape[0]
    operands = [blocks, *prior_pieces, vectors, norm, *(state or ())] + ([queries] if last else [])
    if last:
        scores = F32((seqs, queries.shape[0]))
        out_shape = (F32((1, LANES)), F32((1, LANES)), scores, scores)
    else:
        out_shape = (F32((seqs, prior_pieces[0].shape[0])), column, whole, whole, whole)
    return pl.pallas_call(
        functools.partial(step_kernel, tensor_size, first, last),
        out_shape=out_shape,
        in_specs=[VMEM_SPEC] * len(operands),
        out_specs=(VMEM_SPEC,) * len(out_shape),
        scratch_shapes=[pltpu.VMEM(vectors.shape, jnp.float32)],
        compiler_params=PARAMS,
        name="cg_step",
    )(*operands)


def on_device(dp_size, tensor_size, inputs, in_proj, out_grads, out_proj, prior, queries):
    width = R_IN * R_OUT
    both, devices = ("dp", "tensor"), dp_size * tensor_size
    in_blocks = direct(in_features(inputs, in_proj), "tensor", tensor_size)
    out_local = out_features(out_grads, out_proj)
    partial = partial_vectors(in_blocks, out_local).reshape(-1, width)
    pieces = direct(sum_over(partial, "tensor", tensor_size), "dp", dp_size)
    prior_pieces = split_prior(prior)
    vectors, applied_rows, norm = start_cg(pieces, prior_pieces, tensor_size)
    state = None
    for iteration in range(1, ITERS - 1):
        blocks = gather(applied_rows, both, devices)
        applied_rows, norm, *state = step_cg(blocks, prior_pieces, vectors, norm, state, None, tensor_size)
    blocks = gather(applied_rows, both, devices)
    curvature, norm, solved, along = step_cg(blocks, prior_pieces, vectors, norm, state, queries, tensor_size)
    curvature = jnp.sum(gather(curvature, both, devices), axis=0)
    step = (norm / curvature)[0, : solved.shape[0]]
    return solved + step[:, None] * along


def solution(mesh):
    return jax.shard_map(
        functools.partial(on_device, mesh.shape["dp"], mesh.shape["tensor"]),
        mesh=mesh,
        in_specs=(
            P(("groups", "dp", "tensor"), None),
            P(),
            P(("groups", "dp"), "tensor"),
            P(None, "tensor"),
            P(("groups", "dp", "tensor"), None),
            P(("groups", "dp", "tensor"), None),
        ),
        out_specs=P("groups", ("dp", "tensor")),
        check_vma=False,
    )
```

```python
import functools

import jax
import jax.numpy as jnp
from jax import lax
from jax.experimental import pallas as pl
from jax.experimental.pallas import tpu as pltpu
from jax.sharding import PartitionSpec as P

R_IN = 64
R_OUT = 64
SEQ = 1024
ITERS = 4
LANES = 128
NT = (((1,), (1,)), ((), ()))
HIGHEST = lax.Precision.HIGHEST
ANY_SPEC = pl.BlockSpec(memory_space=pl.ANY)
VMEM_SPEC = pl.BlockSpec(memory_space=pltpu.VMEM)
PARAMS = pltpu.CompilerParams(vmem_limit_bytes=16 * 2**20)
F32 = functools.partial(jax.ShapeDtypeStruct, dtype=jnp.float32)


def swap(value, axis, size, bit):
    return lax.ppermute(value, axis, [(i, i ^ bit) for i in range(size)])


def bits(size):
    return [1 << b for b in reversed(range(size.bit_length() - 1))]


def gather(value, axes, size):
    return lax.all_to_all(jnp.broadcast_to(value[None], (size,) + value.shape), axes, 0, 0)


def sum_over(value, axis, size):
    for bit in bits(size):
        value = value + swap(value, axis, size, bit)
    return value


def direct(value, axis, size):
    return [value] + [swap(value, axis, size, k) for k in reversed(range(1, size))][::-1]


def in_hbm(value):
    return pltpu.with_memory_space_constraint(value, pltpu.HBM)


def in_vmem(value):
    return pltpu.with_memory_space_constraint(value, pltpu.VMEM)


def dot_nt(a, b):
    return lax.dot_general(a, b, NT, precision=HIGHEST, preferred_element_type=jnp.float32)


def row_sum(values):
    return jnp.sum(values, axis=1, keepdims=True)


def in_kernel(in_ref, proj_ref, feats_ref, held, proj, sems):
    chunk = held.shape[1] // (sems.shape[0] - 1)
    spans = [pl.ds(c * chunk, chunk) for c in range(sems.shape[0] - 1)]
    first = pltpu.make_async_copy(proj_ref, proj, sems.at[len(spans)])
    copies = [
        pltpu.make_async_copy(in_ref.at[:, span], held.at[:, span], sems.at[c])
        for c, span in enumerate(spans)
    ]
    first.start()
    for copy in copies:
        copy.start()
    first.wait()
    feats = jnp.zeros((held.shape[0], proj.shape[0]), jnp.float32)
    for copy, span in zip(copies, spans):
        copy.wait()
        feats += lax.dot_general(held[:, span], proj[:, span], NT, preferred_element_type=jnp.float32)
    feats_ref[...] = feats.T


def in_features(inputs, in_proj):
    return pl.pallas_call(
        in_kernel,
        out_shape=pltpu.VMEM((R_IN, inputs.shape[0]), jnp.float32),
        in_specs=[ANY_SPEC] * 2,
        out_specs=VMEM_SPEC,
        scratch_shapes=[
            pltpu.VMEM(inputs.shape, jnp.bfloat16),
            pltpu.VMEM(in_proj.shape, jnp.bfloat16),
            pltpu.SemaphoreType.DMA((9,)),
        ],
        compiler_params=pltpu.CompilerParams(vmem_limit_bytes=16 * 2**20),
        name="in_features",
    )(in_hbm(inputs), in_hbm(in_proj))


def out_kernel(grads_ref, proj_ref, feats_ref, held, proj, turned, sems):
    tokens = held.shape[0]
    spans, start = [], 0
    while start < tokens:
        rows = 2 * LANES if tokens - start > 2 * LANES else LANES
        spans.append(pl.ds(start, rows))
        start += rows
    first = pltpu.make_async_copy(proj_ref, proj, sems.at[len(spans)])
    copies = [
        pltpu.make_async_copy(grads_ref.at[span], held.at[span], sems.at[c])
        for c, span in enumerate(spans)
    ]
    first.start()
    for copy in copies:
        copy.start()
    first.wait()
    turned[...] = proj[...].T
    for copy, span in zip(copies, spans):
        copy.wait()
        feats = jnp.dot(held[span], turned[...], preferred_element_type=jnp.float32)
        feats_ref[:, span] = feats.T


def out_features(out_grads, out_proj):
    tokens, hidden = out_grads.shape
    return pl.pallas_call(
        out_kernel,
        out_shape=pltpu.VMEM((R_OUT, tokens), jnp.float32),
        in_specs=[ANY_SPEC] * 2,
        out_specs=VMEM_SPEC,
        scratch_shapes=[
            pltpu.VMEM(out_grads.shape, jnp.bfloat16),
            pltpu.VMEM(out_proj.shape, jnp.bfloat16),
            pltpu.VMEM((hidden, R_OUT), jnp.bfloat16),
            pltpu.SemaphoreType.DMA((tokens // LANES + 1,)),
        ],
        compiler_params=pltpu.CompilerParams(vmem_limit_bytes=40 * 2**20),
        name="out_features",
    )(in_hbm(out_grads), in_hbm(out_proj))


def split_kernel(prior_ref, upper_ref, lower_ref, held, sems):
    chunk = held.shape[1] // sems.shape[0]
    spans = [pl.ds(c * chunk, chunk) for c in range(sems.shape[0])]
    copies = [
        pltpu.make_async_copy(prior_ref.at[:, span], held.at[:, span], sems.at[c])
        for c, span in enumerate(spans)
    ]
    for copy in copies:
        copy.start()
    for copy, span in zip(copies, spans):
        copy.wait()
        block = held[:, span]
        upper = block.astype(jnp.bfloat16)
        upper_ref[:, span] = upper
        lower_ref[:, span] = (block - upper.astype(jnp.float32)).astype(jnp.bfloat16)


def split_prior(prior):
    return pl.pallas_call(
        split_kernel,
        out_shape=(pltpu.VMEM(prior.shape, jnp.bfloat16),) * 2,
        in_specs=[ANY_SPEC],
        out_specs=(VMEM_SPEC,) * 2,
        scratch_shapes=[pltpu.VMEM(prior.shape, jnp.float32), pltpu.SemaphoreType.DMA((8,))],
        compiler_params=PARAMS,
        name="split_prior",
    )(in_hbm(prior))


def partial_kernel(size, *refs):
    blocks, (out_ref, part_ref, held) = refs[:size], refs[size:]
    me = lax.axis_index("tensor")
    tokens = blocks[0].shape[1]
    for k, block in enumerate(blocks):
        start = pl.multiple_of((me ^ k) * tokens, LANES)
        held[:, pl.ds(start, tokens)] = block[...]
    for s in range(part_ref.shape[0]):
        span = slice(s * SEQ, (s + 1) * SEQ)
        part_ref[s] = dot_nt(held[:, span], out_ref[:, span]) * (1.0 / SEQ)


def partial_vectors(blocks, out_local):
    seq_count = out_local.shape[1] // SEQ
    return pl.pallas_call(
        functools.partial(partial_kernel, len(blocks)),
        out_shape=F32((seq_count, R_IN, R_OUT)),
        in_specs=[VMEM_SPEC] * (len(blocks) + 1),
        out_specs=VMEM_SPEC,
        scratch_shapes=[pltpu.VMEM(out_local.shape, jnp.float32)],
        compiler_params=PARAMS,
        name="partial_vectors",
    )(*blocks, out_local)


def own_columns(ref, me, count):
    if count % LANES == 0:
        return ref[:, pl.ds(pl.multiple_of(me * count, LANES), count)]
    per = LANES // count
    held = ref[:, pl.ds(pl.multiple_of((me // per) * LANES, LANES), LANES)]
    return pltpu.roll(held, LANES - (me % per) * count, 1)[:, :count]


def apply_fisher(direction, vectors_ref, upper_ref, lower_ref, me):
    seqs = direction.shape[0]
    upper = direction.astype(jnp.bfloat16)
    lower = (direction - upper.astype(jnp.float32)).astype(jnp.bfloat16)
    both = jnp.concatenate([upper, lower], axis=0)
    weights = dot_nt(direction, vectors_ref[...]) * (1.0 / seqs)
    own = own_columns(vectors_ref, me, upper_ref.shape[0])
    applied = jnp.dot(weights, own, precision=HIGHEST, preferred_element_type=jnp.float32)
    first = lax.dot_general(both, upper_ref[...], NT, preferred_element_type=jnp.float32)
    second = lax.dot_general(upper, lower_ref[...], NT, preferred_element_type=jnp.float32)
    return applied + (first[:seqs] + first[seqs:] + second)


def flat_index(tensor_size):
    return lax.axis_index("dp") * tensor_size + lax.axis_index("tensor")


def start_kernel(size, tensor_size, *refs):
    pieces, (upper_ref, lower_ref, vectors_ref, applied_ref, norm_ref, held) = refs[:size], refs[size:]
    dp = lax.axis_index("dp")
    for k, piece in enumerate(pieces):
        held[dp ^ k] = piece[...]
    vectors = jnp.concatenate([held[k] for k in range(size)], axis=0)
    vectors_ref[...] = vectors
    norm_ref[...] = jnp.broadcast_to(row_sum(vectors * vectors), norm_ref.shape)
    applied_ref[...] = apply_fisher(vectors, vectors_ref, upper_ref, lower_ref, flat_index(tensor_size))


def start_cg(pieces, prior_pieces, tensor_size):
    size, seqs = len(pieces), len(pieces) * pieces[0].shape[0]
    rows, width = prior_pieces[0].shape
    return pl.pallas_call(
        functools.partial(start_kernel, size, tensor_size),
        out_shape=(F32((seqs, width)), F32((seqs, rows)), F32((seqs, LANES))),
        in_specs=[VMEM_SPEC] * (size + 2),
        out_specs=(VMEM_SPEC,) * 3,
        scratch_shapes=[pltpu.VMEM((size,) + pieces[0].shape, jnp.float32)],
        compiler_params=PARAMS,
        name="cg_start",
    )(*pieces, *prior_pieces)


def on_lanes(column):
    seqs = column.shape[0]
    row = lax.broadcasted_iota(jnp.int32, (seqs, LANES), 0)
    lane = lax.broadcasted_iota(jnp.int32, (seqs, LANES), 1)
    return jnp.sum(jnp.where(row == lane, column, 0.0), axis=0, keepdims=True)


def step_kernel(tensor_size, first, last, *refs):
    blocks_ref, upper_ref, lower_ref, vectors_ref, norm_ref = refs[:5]
    refs = refs[5:]
    if not first:
        direction_ref, residual_ref, solution_ref = refs[:3]
        refs = refs[3:]
    if last:
        queries_ref, curvature_out, norm_out, solved_out, along_out, held = refs
    else:
        applied_out, norm_out, direction_out, residual_out, solution_out, held = refs
    me = flat_index(tensor_size)
    count, _, rows = blocks_ref.shape
    for i in range(count):
        held[:, i * rows : (i + 1) * rows] = blocks_ref[i]
    applied = held[...]
    direction = vectors_ref[...] if first else direction_ref[...]
    residual = direction if first else residual_ref[...]
    norm = norm_ref[...][:, :1]
    step = norm / row_sum(direction * applied)
    solution = step * direction
    if not first:
        solution = solution_ref[...] + solution
    residual = residual - step * applied
    norm_next = row_sum(residual * residual)
    direction = residual + (norm_next / norm) * direction
    norm_out[...] = on_lanes(norm_next) if last else jnp.broadcast_to(norm_next, norm_out.shape)
    applied_rows = apply_fisher(direction, vectors_ref, upper_ref, lower_ref, me)
    if last:
        held[...] = direction
        own = own_columns(held, me, rows)
        curvature_out[...] = on_lanes(row_sum(own * applied_rows))
        queries = queries_ref[...].astype(jnp.float32)
        solved_out[...] = dot_nt(solution, queries)
        along_out[...] = dot_nt(direction, queries)
    else:
        applied_out[...] = applied_rows
        direction_out[...] = direction
        residual_out[...] = residual
        solution_out[...] = solution


def step_cg(blocks, prior_pieces, vectors, norm, state, queries, tensor_size):
    first, last = state is None, queries is not None
    whole, column = F32(vectors.shape), F32(norm.shape)
    seqs = vectors.shape[0]
    operands = [blocks, *prior_pieces, vectors, norm, *(state or ())] + ([queries] if last else [])
    if last:
        scores = F32((seqs, queries.shape[0]))
        out_shape = (F32((1, LANES)), F32((1, LANES)), scores, scores)
    else:
        out_shape = (F32((seqs, prior_pieces[0].shape[0])), column, whole, whole, whole)
    return pl.pallas_call(
        functools.partial(step_kernel, tensor_size, first, last),
        out_shape=out_shape,
        in_specs=[VMEM_SPEC] * len(operands),
        out_specs=(VMEM_SPEC,) * len(out_shape),
        scratch_shapes=[pltpu.VMEM(vectors.shape, jnp.float32)],
        compiler_params=PARAMS,
        name="cg_step",
    )(*operands)


def on_device(dp_size, tensor_size, inputs, in_proj, out_grads, out_proj, prior, queries):
    width = R_IN * R_OUT
    both, devices = ("dp", "tensor"), dp_size * tensor_size
    in_blocks = direct(in_features(inputs, in_proj), "tensor", tensor_size)
    out_local = out_features(out_grads, out_proj)
    partial = partial_vectors(in_blocks, out_local).reshape(-1, width)
    pieces = direct(sum_over(partial, "tensor", tensor_size), "dp", dp_size)
    prior_pieces = [in_vmem(piece) for piece in split_prior(prior)]
    vectors, applied_rows, norm = start_cg(pieces, prior_pieces, tensor_size)
    state = None
    for iteration in range(1, ITERS - 1):
        blocks = gather(applied_rows, both, devices)
        applied_rows, norm, *state = step_cg(blocks, prior_pieces, vectors, norm, state, None, tensor_size)
    blocks = gather(applied_rows, both, devices)
    curvature, norm, solved, along = step_cg(blocks, prior_pieces, vectors, norm, state, queries, tensor_size)
    curvature = jnp.sum(gather(curvature, both, devices), axis=0)
    step = (norm / curvature)[0, : solved.shape[0]]
    return solved + step[:, None] * along


def solution(mesh):
    return jax.shard_map(
        functools.partial(on_device, mesh.shape["dp"], mesh.shape["tensor"]),
        mesh=mesh,
        in_specs=(
            P(("groups", "dp", "tensor"), None),
            P(),
            P(("groups", "dp"), "tensor"),
            P(None, "tensor"),
            P(("groups", "dp", "tensor"), None),
            P(("groups", "dp", "tensor"), None),
        ),
        out_specs=P("groups", ("dp", "tensor")),
        check_vma=False,
    )
```

```python
import functools

import jax
import jax.numpy as jnp
from jax import lax
from jax.experimental import pallas as pl
from jax.experimental.pallas import tpu as pltpu
from jax.sharding import PartitionSpec as P

R_IN = 64
R_OUT = 64
SEQ = 1024
ITERS = 4
LANES = 128
NT = (((1,), (1,)), ((), ()))
HIGHEST = lax.Precision.HIGHEST
ANY_SPEC = pl.BlockSpec(memory_space=pl.ANY)
VMEM_SPEC = pl.BlockSpec(memory_space=pltpu.VMEM)
PARAMS = pltpu.CompilerParams(vmem_limit_bytes=16 * 2**20)
F32 = functools.partial(jax.ShapeDtypeStruct, dtype=jnp.float32)


def swap(value, axis, size, bit):
    return lax.ppermute(value, axis, [(i, i ^ bit) for i in range(size)])


def bits(size):
    return [1 << b for b in reversed(range(size.bit_length() - 1))]


def gather(value, axes, size):
    return lax.all_to_all(jnp.broadcast_to(value[None], (size,) + value.shape), axes, 0, 0)


def sum_over(value, axis, size):
    for bit in bits(size):
        value = value + swap(value, axis, size, bit)
    return value


def direct(value, axis, size):
    return [value] + [swap(value, axis, size, k) for k in reversed(range(1, size))][::-1]


def in_hbm(value):
    return pltpu.with_memory_space_constraint(value, pltpu.HBM)


def in_vmem(value):
    return pltpu.with_memory_space_constraint(value, pltpu.VMEM)


def dot_nt(a, b):
    return lax.dot_general(a, b, NT, precision=HIGHEST, preferred_element_type=jnp.float32)


def row_sum(values):
    return jnp.sum(values, axis=1, keepdims=True)


def row_spans(rows, sizes):
    spans, start = [], 0
    while start < rows:
        while len(sizes) > 1 and start + sizes[0] + sizes[-1] > rows:
            sizes = sizes[1:]
        spans.append(pl.ds(start, sizes[0]))
        start += sizes[0]
        sizes = sizes[1:] or sizes
    return spans


def stream_kernel(spans, rows_ref, proj_ref, feats_ref, held, proj, sems):
    first = pltpu.make_async_copy(proj_ref, proj, sems.at[len(spans)])
    copies = [
        pltpu.make_async_copy(rows_ref.at[span], held.at[span], sems.at[c])
        for c, span in enumerate(spans)
    ]
    first.start()
    for copy in copies:
        copy.start()
    first.wait()
    for copy, span in zip(copies, spans):
        copy.wait()
        feats = lax.dot_general(held[span], proj[...], NT, preferred_element_type=jnp.float32)
        feats_ref[:, span] = feats.T


def features(rows, proj, sizes, limit, name):
    spans = row_spans(rows.shape[0], sizes)
    return pl.pallas_call(
        functools.partial(stream_kernel, spans),
        out_shape=pltpu.VMEM((proj.shape[0], rows.shape[0]), jnp.float32),
        in_specs=[ANY_SPEC] * 2,
        out_specs=VMEM_SPEC,
        scratch_shapes=[
            pltpu.VMEM(rows.shape, jnp.bfloat16),
            pltpu.VMEM(proj.shape, jnp.bfloat16),
            pltpu.SemaphoreType.DMA((len(spans) + 1,)),
        ],
        compiler_params=pltpu.CompilerParams(vmem_limit_bytes=limit * 2**20),
        name=name,
    )(in_hbm(rows), in_hbm(proj))


def split_kernel(prior_ref, upper_ref, lower_ref, held, sems):
    chunk = held.shape[1] // sems.shape[0]
    spans = [pl.ds(c * chunk, chunk) for c in range(sems.shape[0])]
    copies = [
        pltpu.make_async_copy(prior_ref.at[:, span], held.at[:, span], sems.at[c])
        for c, span in enumerate(spans)
    ]
    for copy in copies:
        copy.start()
    for copy, span in zip(copies, spans):
        copy.wait()
        block = held[:, span]
        upper = block.astype(jnp.bfloat16)
        upper_ref[:, span] = upper
        lower_ref[:, span] = (block - upper.astype(jnp.float32)).astype(jnp.bfloat16)


def split_prior(prior):
    return pl.pallas_call(
        split_kernel,
        out_shape=(pltpu.VMEM(prior.shape, jnp.bfloat16),) * 2,
        in_specs=[ANY_SPEC],
        out_specs=(VMEM_SPEC,) * 2,
        scratch_shapes=[pltpu.VMEM(prior.shape, jnp.float32), pltpu.SemaphoreType.DMA((8,))],
        compiler_params=PARAMS,
        name="split_prior",
    )(in_hbm(prior))


def partial_kernel(size, *refs):
    blocks, (out_ref, part_ref, held) = refs[:size], refs[size:]
    me = lax.axis_index("tensor")
    tokens = blocks[0].shape[1]
    for k, block in enumerate(blocks):
        start = pl.multiple_of((me ^ k) * tokens, LANES)
        held[:, pl.ds(start, tokens)] = block[...]
    for s in range(part_ref.shape[0]):
        span = slice(s * SEQ, (s + 1) * SEQ)
        part_ref[s] = dot_nt(held[:, span], out_ref[:, span]) * (1.0 / SEQ)


def partial_vectors(blocks, out_local):
    seq_count = out_local.shape[1] // SEQ
    return pl.pallas_call(
        functools.partial(partial_kernel, len(blocks)),
        out_shape=F32((seq_count, R_IN, R_OUT)),
        in_specs=[VMEM_SPEC] * (len(blocks) + 1),
        out_specs=VMEM_SPEC,
        scratch_shapes=[pltpu.VMEM(out_local.shape, jnp.float32)],
        compiler_params=PARAMS,
        name="partial_vectors",
    )(*blocks, out_local)


def own_columns(ref, me, count):
    if count % LANES == 0:
        return ref[:, pl.ds(pl.multiple_of(me * count, LANES), count)]
    per = LANES // count
    held = ref[:, pl.ds(pl.multiple_of((me // per) * LANES, LANES), LANES)]
    return pltpu.roll(held, LANES - (me % per) * count, 1)[:, :count]


def pieces_of(values, count):
    held = []
    for _ in range(count):
        piece = values.astype(jnp.bfloat16)
        held.append(piece)
        values = values - piece.astype(jnp.float32)
    return jnp.concatenate(held, axis=0)


def dot_pieces(a, b, seqs):
    held = lax.dot_general(a, b, NT, preferred_element_type=jnp.float32)
    total = held[:seqs]
    for start in range(seqs, held.shape[0], seqs):
        total = total + held[start : start + seqs]
    return total


def apply_fisher(pieces, vectors_ref, vector_pieces, upper_ref, lower_ref, me):
    seqs = vectors_ref.shape[0]
    applied = dot_pieces(pieces, upper_ref[...], seqs)
    applied = applied + dot_pieces(pieces[: 2 * seqs], lower_ref[...], seqs)
    weights = dot_pieces(pieces, vector_pieces, seqs)
    weights = (weights[:, :seqs] + weights[:, seqs:]) * (1.0 / seqs)
    own = own_columns(vectors_ref, me, upper_ref.shape[0])
    return applied + jnp.dot(weights, own, precision=HIGHEST, preferred_element_type=jnp.float32)


def flat_index(tensor_size):
    return lax.axis_index("dp") * tensor_size + lax.axis_index("tensor")


def start_kernel(size, tensor_size, *refs):
    pieces, refs = refs[:size], refs[size:]
    upper_ref, lower_ref, vectors_ref, vector_pieces_ref, scale_ref, applied_ref, norm_ref, held = refs
    dp = lax.axis_index("dp")
    for k, piece in enumerate(pieces):
        held[dp ^ k] = piece[...]
    vectors = jnp.concatenate([held[k] for k in range(size)], axis=0)
    vectors_ref[...] = vectors
    split = pieces_of(vectors, 3)
    vector_pieces = split[: 2 * vectors.shape[0]]
    vector_pieces_ref[...] = vector_pieces
    norm = jnp.broadcast_to(row_sum(vectors * vectors), norm_ref.shape)
    norm_ref[...] = norm
    spread = jnp.sum(norm, axis=0, keepdims=True) * (1.0 / vectors.shape[0])
    scale_ref[...] = jnp.broadcast_to(1.0 / (1.0 + spread), scale_ref.shape)
    me = flat_index(tensor_size)
    applied_ref[...] = apply_fisher(split, vectors_ref, vector_pieces, upper_ref, lower_ref, me)


def start_cg(pieces, prior_pieces, tensor_size):
    size, seqs = len(pieces), len(pieces) * pieces[0].shape[0]
    rows, width = prior_pieces[0].shape
    vector_pieces = jax.ShapeDtypeStruct((2 * seqs, width), jnp.bfloat16)
    column = F32((seqs, LANES))
    return pl.pallas_call(
        functools.partial(start_kernel, size, tensor_size),
        out_shape=(F32((seqs, width)), vector_pieces, column, F32((seqs, rows)), column),
        in_specs=[VMEM_SPEC] * (size + 2),
        out_specs=(VMEM_SPEC,) * 5,
        scratch_shapes=[pltpu.VMEM((size,) + pieces[0].shape, jnp.float32)],
        compiler_params=PARAMS,
        name="cg_start",
    )(*pieces, *prior_pieces)


def on_lanes(column):
    seqs = column.shape[0]
    row = lax.broadcasted_iota(jnp.int32, (seqs, LANES), 0)
    lane = lax.broadcasted_iota(jnp.int32, (seqs, LANES), 1)
    return jnp.sum(jnp.where(row == lane, column, 0.0), axis=0, keepdims=True)


def step_kernel(tensor_size, first, last, *refs):
    blocks_ref, upper_ref, lower_ref, vectors_ref, vector_pieces_ref, scale_ref = refs[:6]
    norm_ref, fisher_direction_ref = refs[6:8]
    refs = refs[8:]
    if not first:
        fisher_residual_ref, direction_ref, residual_ref, solution_ref = refs[:4]
        refs = refs[4:]
    if last:
        curvature_out, norm_out, direction_out, solution_out, held = refs
    else:
        fisher_direction_out, norm_out, fisher_residual_out, direction_out, residual_out, solution_out, held = refs
    me = flat_index(tensor_size)
    count, _, rows = blocks_ref.shape
    for i in range(count):
        held[:, i * rows : (i + 1) * rows] = blocks_ref[i]
    applied = held[...]
    scale = scale_ref[...][:, :1]
    twice = apply_fisher(
        pieces_of(scale * applied, 3), vectors_ref, vector_pieces_ref[...], upper_ref, lower_ref, me
    )
    direction = vectors_ref[...] if first else direction_ref[...]
    residual = direction if first else residual_ref[...]
    norm = norm_ref[...][:, :1]
    step = norm / row_sum(direction * applied)
    solution = step * direction
    if not first:
        solution = solution_ref[...] + solution
    residual = residual - step * applied
    norm_next = row_sum(residual * residual)
    share = norm_next / norm
    direction = residual + share * direction
    fisher_direction = fisher_direction_ref[...]
    fisher_residual = (fisher_direction if first else fisher_residual_ref[...]) - (step / scale) * twice
    fisher_direction = fisher_residual + share * fisher_direction
    direction_out[...] = direction
    solution_out[...] = solution
    if last:
        own = own_columns(direction_out, me, rows)
        curvature_out[...] = on_lanes(row_sum(own * fisher_direction))
        norm_out[...] = on_lanes(norm_next)
    else:
        fisher_direction_out[...] = fisher_direction
        fisher_residual_out[...] = fisher_residual
        residual_out[...] = residual
        norm_out[...] = jnp.broadcast_to(norm_next, norm_out.shape)


def step_cg(blocks, fixed, norm, state, last, tensor_size):
    first = len(state) == 1
    whole, rows = F32(fixed[2].shape), F32(state[0].shape)
    row = F32((1, LANES))
    operands = [blocks, *fixed, norm, *state]
    out_shape = (row, row, whole, whole) if last else (rows, F32(norm.shape), rows, whole, whole, whole)
    return pl.pallas_call(
        functools.partial(step_kernel, tensor_size, first, last),
        out_shape=out_shape,
        in_specs=[VMEM_SPEC] * len(operands),
        out_specs=(VMEM_SPEC,) * len(out_shape),
        scratch_shapes=[pltpu.VMEM(whole.shape, jnp.float32)],
        compiler_params=PARAMS,
        name="cg_step",
    )(*operands)


def score_kernel(solution_ref, direction_ref, queries_ref, solved_ref, along_ref):
    seqs = solution_ref.shape[0]
    both = jnp.concatenate([solution_ref[...], direction_ref[...]], axis=0)
    scores = dot_pieces(pieces_of(both, 3), queries_ref[...], 2 * seqs)
    solved_ref[...] = scores[:seqs]
    along_ref[...] = scores[seqs:]


def score(solution, direction, queries):
    scores = F32((solution.shape[0], queries.shape[0]))
    return pl.pallas_call(
        score_kernel,
        out_shape=(scores, scores),
        in_specs=[VMEM_SPEC] * 3,
        out_specs=(VMEM_SPEC,) * 2,
        compiler_params=PARAMS,
        name="scores",
    )(solution, direction, queries)


def on_device(dp_size, tensor_size, inputs, in_proj, out_grads, out_proj, prior, queries):
    width = R_IN * R_OUT
    both, devices = ("dp", "tensor"), dp_size * tensor_size
    in_blocks = direct(features(inputs, in_proj, (256, 128), 16, "in_features"), "tensor", tensor_size)
    out_local = features(out_grads, out_proj, (512, 512, 512, 256, 128), 40, "out_features")
    partial = partial_vectors(in_blocks, out_local).reshape(-1, width)
    pieces = direct(sum_over(partial, "tensor", tensor_size), "dp", dp_size)
    prior_pieces = [in_vmem(piece) for piece in split_prior(prior)]
    vectors, vector_pieces, scale, applied_rows, norm = start_cg(pieces, prior_pieces, tensor_size)
    fixed = (*prior_pieces, vectors, vector_pieces, scale)
    state = [applied_rows]
    for iteration in range(1, ITERS - 1):
        blocks = gather(state[0], both, devices)
        applied_rows, norm, *others = step_cg(blocks, fixed, norm, state, False, tensor_size)
        state = [applied_rows, *others]
    blocks = gather(state[0], both, devices)
    curvature, norm, direction, solved = step_cg(blocks, fixed, norm, state, True, tensor_size)
    curvature = jnp.sum(gather(curvature, both, devices), axis=0)
    solved, along = score(solved, direction, queries)
    step = (norm / curvature)[0, : solved.shape[0]]
    return solved + step[:, None] * along


def solution(mesh):
    return jax.shard_map(
        functools.partial(on_device, mesh.shape["dp"], mesh.shape["tensor"]),
        mesh=mesh,
        in_specs=(
            P(("groups", "dp", "tensor"), None),
            P(),
            P(("groups", "dp"), "tensor"),
            P(None, "tensor"),
            P(("groups", "dp", "tensor"), None),
            P(("groups", "dp", "tensor"), None),
        ),
        out_specs=P("groups", ("dp", "tensor")),
        check_vma=False,
    )
```

```python
import functools

import jax
import jax.numpy as jnp
from jax import lax
from jax.experimental import pallas as pl
from jax.experimental.pallas import tpu as pltpu
from jax.sharding import PartitionSpec as P

R_IN = 64
R_OUT = 64
SEQ = 1024
ITERS = 4
LANES = 128
NT = (((1,), (1,)), ((), ()))
HIGHEST = lax.Precision.HIGHEST
ANY_SPEC = pl.BlockSpec(memory_space=pl.ANY)
VMEM_SPEC = pl.BlockSpec(memory_space=pltpu.VMEM)
PARAMS = pltpu.CompilerParams(vmem_limit_bytes=16 * 2**20)
F32 = functools.partial(jax.ShapeDtypeStruct, dtype=jnp.float32)


def swap(value, axis, size, bit):
    return lax.ppermute(value, axis, [(i, i ^ bit) for i in range(size)])


def bits(size):
    return [1 << b for b in reversed(range(size.bit_length() - 1))]


def gather(value, axes, size):
    return lax.all_to_all(jnp.broadcast_to(value[None], (size,) + value.shape), axes, 0, 0)


def sum_over(value, axis, size):
    for bit in bits(size):
        value = value + swap(value, axis, size, bit)
    return value


def direct(value, axis, size):
    return [value] + [swap(value, axis, size, k) for k in reversed(range(1, size))][::-1]


def in_hbm(value):
    return pltpu.with_memory_space_constraint(value, pltpu.HBM)


def in_vmem(value):
    return pltpu.with_memory_space_constraint(value, pltpu.VMEM)


def dot_nt(a, b):
    return lax.dot_general(a, b, NT, precision=HIGHEST, preferred_element_type=jnp.float32)


def row_sum(values):
    return jnp.sum(values, axis=1, keepdims=True)


def row_spans(rows, sizes):
    spans, start = [], 0
    while start < rows:
        while len(sizes) > 1 and start + sizes[0] + sizes[-1] > rows:
            sizes = sizes[1:]
        spans.append(pl.ds(start, sizes[0]))
        start += sizes[0]
        sizes = sizes[1:] or sizes
    return spans


def fetch(rows_ref, held, proj_ref, proj, sems, places):
    count = proj_ref.shape[0]
    first = pltpu.make_async_copy(proj_ref, proj.at[:count], sems.at[len(places)])
    copies = [
        pltpu.make_async_copy(rows_ref.at[place], held.at[place], sems.at[c])
        for c, place in enumerate(places)
    ]
    first.start()
    for copy in copies:
        copy.start()
    proj[count:] = jnp.zeros((proj.shape[0] - count, proj.shape[1]), proj.dtype)
    first.wait()
    return copies


def in_kernel(rows_ref, proj_ref, feats_ref, held, proj, sems):
    count = sems.shape[0] - 1
    chunk = held.shape[1] // count
    spans = [pl.ds(c * chunk, chunk) for c in range(count)]
    copies = fetch(rows_ref, held, proj_ref, proj, sems, [(slice(None), span) for span in spans])
    feats = None
    for copy, span in zip(copies, spans):
        copy.wait()
        part = lax.dot_general(held[:, span], proj[:, span], NT, preferred_element_type=jnp.float32)
        part = part[:, :LANES]
        feats = part if feats is None else feats + part
    feats_ref[...] = feats.T[: feats_ref.shape[0]]


def out_kernel(spans, rows_ref, proj_ref, feats_ref, held, proj, sems):
    copies = fetch(rows_ref, held, proj_ref, proj, sems, spans)
    for copy, span in zip(copies, spans):
        copy.wait()
        feats = lax.dot_general(held[span], proj[...], NT, preferred_element_type=jnp.float32)
        feats_ref[:, span] = feats[:, :LANES].T[: feats_ref.shape[0]]


def features(rows, proj, kernel, copies, limit, name):
    return pl.pallas_call(
        kernel,
        out_shape=pltpu.VMEM((proj.shape[0], rows.shape[0]), jnp.float32),
        in_specs=[ANY_SPEC] * 2,
        out_specs=VMEM_SPEC,
        scratch_shapes=[
            pltpu.VMEM(rows.shape, jnp.bfloat16),
            pltpu.VMEM((2 * LANES, proj.shape[1]), jnp.bfloat16),
            pltpu.SemaphoreType.DMA((copies + 1,)),
        ],
        compiler_params=pltpu.CompilerParams(vmem_limit_bytes=limit * 2**20),
        name=name,
    )(in_hbm(rows), in_hbm(proj))


def in_features(inputs, in_proj):
    return features(inputs, in_proj, in_kernel, 8, 20, "in_features")


def out_features(out_grads, out_proj):
    spans = row_spans(out_grads.shape[0], (512, 512, 512, 256, 128))
    kernel = functools.partial(out_kernel, spans)
    return features(out_grads, out_proj, kernel, len(spans), 44, "out_features")


def split_kernel(prior_ref, upper_ref, lower_ref, held, sems):
    chunk = held.shape[1] // sems.shape[0]
    spans = [pl.ds(c * chunk, chunk) for c in range(sems.shape[0])]
    copies = [
        pltpu.make_async_copy(prior_ref.at[:, span], held.at[:, span], sems.at[c])
        for c, span in enumerate(spans)
    ]
    for copy in copies:
        copy.start()
    for copy, span in zip(copies, spans):
        copy.wait()
        block = held[:, span]
        upper = block.astype(jnp.bfloat16)
        upper_ref[:, span] = upper
        lower_ref[:, span] = (block - upper.astype(jnp.float32)).astype(jnp.bfloat16)


def split_prior(prior):
    return pl.pallas_call(
        split_kernel,
        out_shape=(pltpu.VMEM(prior.shape, jnp.bfloat16),) * 2,
        in_specs=[ANY_SPEC],
        out_specs=(VMEM_SPEC,) * 2,
        scratch_shapes=[pltpu.VMEM(prior.shape, jnp.float32), pltpu.SemaphoreType.DMA((8,))],
        compiler_params=PARAMS,
        name="split_prior",
    )(in_hbm(prior))


def partial_kernel(size, *refs):
    blocks, (out_ref, part_ref, held) = refs[:size], refs[size:]
    me = lax.axis_index("tensor")
    tokens = blocks[0].shape[1]
    for k, block in enumerate(blocks):
        start = pl.multiple_of((me ^ k) * tokens, LANES)
        held[:, pl.ds(start, tokens)] = block[...]
    for s in range(part_ref.shape[0]):
        span = slice(s * SEQ, (s + 1) * SEQ)
        part_ref[s] = dot_nt(held[:, span], out_ref[:, span]) * (1.0 / SEQ)


def partial_vectors(blocks, out_local):
    seq_count = out_local.shape[1] // SEQ
    return pl.pallas_call(
        functools.partial(partial_kernel, len(blocks)),
        out_shape=F32((seq_count, R_IN, R_OUT)),
        in_specs=[VMEM_SPEC] * (len(blocks) + 1),
        out_specs=VMEM_SPEC,
        scratch_shapes=[pltpu.VMEM(out_local.shape, jnp.float32)],
        compiler_params=PARAMS,
        name="partial_vectors",
    )(*blocks, out_local)


def own_columns(ref, me, count):
    if count % LANES == 0:
        return ref[:, pl.ds(pl.multiple_of(me * count, LANES), count)]
    per = LANES // count
    held = ref[:, pl.ds(pl.multiple_of((me // per) * LANES, LANES), LANES)]
    return pltpu.roll(held, LANES - (me % per) * count, 1)[:, :count]


def pieces_of(values, count):
    held = []
    for _ in range(count):
        piece = values.astype(jnp.bfloat16)
        held.append(piece)
        values = values - piece.astype(jnp.float32)
    return jnp.concatenate(held, axis=0)


def dot_pieces(a, b, seqs):
    held = lax.dot_general(a, b, NT, preferred_element_type=jnp.float32)
    total = held[:seqs]
    for start in range(seqs, held.shape[0], seqs):
        total = total + held[start : start + seqs]
    return total


def apply_fisher(pieces, vectors_ref, vector_pieces, upper_ref, lower_ref, me):
    seqs = vectors_ref.shape[0]
    applied = dot_pieces(pieces, upper_ref[...], seqs)
    applied = applied + dot_pieces(pieces[: 2 * seqs], lower_ref[...], seqs)
    weights = dot_pieces(pieces, vector_pieces, seqs)
    weights = (weights[:, :seqs] + weights[:, seqs:]) * (1.0 / seqs)
    own = own_columns(vectors_ref, me, upper_ref.shape[0])
    return applied + jnp.dot(weights, own, precision=HIGHEST, preferred_element_type=jnp.float32)


def flat_index(tensor_size):
    return lax.axis_index("dp") * tensor_size + lax.axis_index("tensor")


def start_kernel(size, tensor_size, *refs):
    pieces, refs = refs[:size], refs[size:]
    upper_ref, lower_ref, vectors_ref, vector_pieces_ref, scale_ref, applied_ref, norm_ref, held = refs
    dp = lax.axis_index("dp")
    for k, piece in enumerate(pieces):
        held[dp ^ k] = piece[...]
    vectors = jnp.concatenate([held[k] for k in range(size)], axis=0)
    vectors_ref[...] = vectors
    split = pieces_of(vectors, 3)
    vector_pieces = split[: 2 * vectors.shape[0]]
    vector_pieces_ref[...] = vector_pieces
    norm = jnp.broadcast_to(row_sum(vectors * vectors), norm_ref.shape)
    norm_ref[...] = norm
    spread = jnp.sum(norm, axis=0, keepdims=True) * (1.0 / vectors.shape[0])
    scale_ref[...] = jnp.broadcast_to(1.0 / (1.0 + spread), scale_ref.shape)
    me = flat_index(tensor_size)
    applied_ref[...] = apply_fisher(split, vectors_ref, vector_pieces, upper_ref, lower_ref, me)


def start_cg(pieces, prior_pieces, tensor_size):
    size, seqs = len(pieces), len(pieces) * pieces[0].shape[0]
    rows, width = prior_pieces[0].shape
    vector_pieces = jax.ShapeDtypeStruct((2 * seqs, width), jnp.bfloat16)
    column = F32((seqs, LANES))
    return pl.pallas_call(
        functools.partial(start_kernel, size, tensor_size),
        out_shape=(F32((seqs, width)), vector_pieces, column, F32((seqs, rows)), column),
        in_specs=[VMEM_SPEC] * (size + 2),
        out_specs=(VMEM_SPEC,) * 5,
        scratch_shapes=[pltpu.VMEM((size,) + pieces[0].shape, jnp.float32)],
        compiler_params=PARAMS,
        name="cg_start",
    )(*pieces, *prior_pieces)


def on_lanes(column):
    seqs = column.shape[0]
    row = lax.broadcasted_iota(jnp.int32, (seqs, LANES), 0)
    lane = lax.broadcasted_iota(jnp.int32, (seqs, LANES), 1)
    return jnp.sum(jnp.where(row == lane, column, 0.0), axis=0, keepdims=True)


def step_kernel(tensor_size, first, last, *refs):
    blocks_ref, upper_ref, lower_ref, vectors_ref, vector_pieces_ref, scale_ref = refs[:6]
    norm_ref, fisher_direction_ref = refs[6:8]
    refs = refs[8:]
    if not first:
        fisher_residual_ref, direction_ref, residual_ref, solution_ref = refs[:4]
        refs = refs[4:]
    if last:
        curvature_out, norm_out, direction_out, solution_out, held = refs
    else:
        fisher_direction_out, norm_out, fisher_residual_out, direction_out, residual_out, solution_out, held = refs
    me = flat_index(tensor_size)
    count, _, rows = blocks_ref.shape
    for i in range(count):
        held[:, i * rows : (i + 1) * rows] = blocks_ref[i]
    applied = held[...]
    scale = scale_ref[...][:, :1]
    twice = apply_fisher(
        pieces_of(scale * applied, 3), vectors_ref, vector_pieces_ref[...], upper_ref, lower_ref, me
    )
    direction = vectors_ref[...] if first else direction_ref[...]
    residual = direction if first else residual_ref[...]
    norm = norm_ref[...][:, :1]
    step = norm / row_sum(direction * applied)
    solution = step * direction
    if not first:
        solution = solution_ref[...] + solution
    residual = residual - step * applied
    norm_next = row_sum(residual * residual)
    share = norm_next / norm
    direction = residual + share * direction
    fisher_direction = fisher_direction_ref[...]
    fisher_residual = (fisher_direction if first else fisher_residual_ref[...]) - (step / scale) * twice
    fisher_direction = fisher_residual + share * fisher_direction
    direction_out[...] = direction
    solution_out[...] = solution
    if last:
        own = own_columns(direction_out, me, rows)
        curvature_out[...] = jnp.broadcast_to(on_lanes(row_sum(own * fisher_direction))[None], curvature_out.shape)
        norm_out[...] = on_lanes(norm_next)
    else:
        fisher_direction_out[...] = fisher_direction
        fisher_residual_out[...] = fisher_residual
        residual_out[...] = residual
        norm_out[...] = jnp.broadcast_to(norm_next, norm_out.shape)


def step_cg(blocks, fixed, norm, state, last, tensor_size):
    first = len(state) == 1
    whole, rows = F32(fixed[2].shape), F32(state[0].shape)
    row, repeated = F32((1, LANES)), F32((blocks.shape[0], 1, LANES))
    operands = [blocks, *fixed, norm, *state]
    out_shape = (repeated, row, whole, whole) if last else (rows, F32(norm.shape), rows, whole, whole, whole)
    return pl.pallas_call(
        functools.partial(step_kernel, tensor_size, first, last),
        out_shape=out_shape,
        in_specs=[VMEM_SPEC] * len(operands),
        out_specs=(VMEM_SPEC,) * len(out_shape),
        scratch_shapes=[pltpu.VMEM(whole.shape, jnp.float32)],
        compiler_params=PARAMS,
        name="cg_step",
    )(*operands)


def score_kernel(solution_ref, direction_ref, queries_ref, solved_ref, along_ref):
    seqs = solution_ref.shape[0]
    both = jnp.concatenate([solution_ref[...], direction_ref[...]], axis=0)
    scores = dot_pieces(pieces_of(both, 3), queries_ref[...], 2 * seqs)
    solved_ref[...] = scores[:seqs]
    along_ref[...] = scores[seqs:]


def score(solution, direction, queries):
    scores = F32((solution.shape[0], queries.shape[0]))
    return pl.pallas_call(
        score_kernel,
        out_shape=(scores, scores),
        in_specs=[VMEM_SPEC] * 3,
        out_specs=(VMEM_SPEC,) * 2,
        compiler_params=PARAMS,
        name="scores",
    )(solution, direction, queries)


def on_device(dp_size, tensor_size, inputs, in_proj, out_grads, out_proj, prior, queries):
    width = R_IN * R_OUT
    both, devices = ("dp", "tensor"), dp_size * tensor_size
    in_blocks = direct(in_features(inputs, in_proj), "tensor", tensor_size)
    out_local = out_features(out_grads, out_proj)
    partial = partial_vectors(in_blocks, out_local).reshape(-1, width)
    pieces = direct(sum_over(partial, "tensor", tensor_size), "dp", dp_size)
    prior_pieces = [in_vmem(piece) for piece in split_prior(prior)]
    vectors, vector_pieces, scale, applied_rows, norm = start_cg(pieces, prior_pieces, tensor_size)
    fixed = (*prior_pieces, vectors, vector_pieces, scale)
    state = [applied_rows]
    for iteration in range(1, ITERS - 1):
        blocks = gather(state[0], both, devices)
        applied_rows, norm, *others = step_cg(blocks, fixed, norm, state, False, tensor_size)
        state = [applied_rows, *others]
    blocks = gather(state[0], both, devices)
    curvature, norm, direction, solved = step_cg(blocks, fixed, norm, state, True, tensor_size)
    curvature = jnp.sum(lax.all_to_all(curvature, both, 0, 0), axis=0)
    solved, along = score(solved, direction, queries)
    step = (norm / curvature)[0, : solved.shape[0]]
    return solved + step[:, None] * along


def solution(mesh):
    return jax.shard_map(
        functools.partial(on_device, mesh.shape["dp"], mesh.shape["tensor"]),
        mesh=mesh,
        in_specs=(
            P(("groups", "dp", "tensor"), None),
            P(),
            P(("groups", "dp"), "tensor"),
            P(None, "tensor"),
            P(("groups", "dp", "tensor"), None),
            P(("groups", "dp", "tensor"), None),
        ),
        out_specs=P("groups", ("dp", "tensor")),
        check_vma=False,
    )
```

```python
import functools

import jax
import jax.numpy as jnp
from jax import lax
from jax.experimental import pallas as pl
from jax.experimental.pallas import tpu as pltpu
from jax.sharding import PartitionSpec as P

R_IN = 64
R_OUT = 64
SEQ = 1024
ITERS = 4
LANES = 128
NT = (((1,), (1,)), ((), ()))
HIGHEST = lax.Precision.HIGHEST
ANY_SPEC = pl.BlockSpec(memory_space=pl.ANY)
VMEM_SPEC = pl.BlockSpec(memory_space=pltpu.VMEM)
PARAMS = pltpu.CompilerParams(vmem_limit_bytes=16 * 2**20)
F32 = functools.partial(jax.ShapeDtypeStruct, dtype=jnp.float32)


def swap(value, axis, size, bit):
    return lax.ppermute(value, axis, [(i, i ^ bit) for i in range(size)])


def bits(size):
    return [1 << b for b in reversed(range(size.bit_length() - 1))]


def gather(value, axes, size):
    return lax.all_to_all(jnp.broadcast_to(value[None], (size,) + value.shape), axes, 0, 0)


def sum_over(value, axis, size):
    for bit in bits(size):
        value = value + swap(value, axis, size, bit)
    return value


def direct(value, axis, size):
    return [value] + [swap(value, axis, size, k) for k in reversed(range(1, size))][::-1]


def in_hbm(value):
    return pltpu.with_memory_space_constraint(value, pltpu.HBM)


def in_vmem(value):
    return pltpu.with_memory_space_constraint(value, pltpu.VMEM)


def dot_nt(a, b):
    return lax.dot_general(a, b, NT, precision=HIGHEST, preferred_element_type=jnp.float32)


def row_sum(values):
    return jnp.sum(values, axis=1, keepdims=True)


def row_spans(rows, sizes):
    spans, start = [], 0
    while start < rows:
        while len(sizes) > 1 and start + sizes[0] + sizes[-1] > rows:
            sizes = sizes[1:]
        spans.append(pl.ds(start, sizes[0]))
        start += sizes[0]
        sizes = sizes[1:] or sizes
    return spans


def stream_kernel(spans, rows_ref, proj_ref, feats_ref, held, proj, sems):
    first = pltpu.make_async_copy(proj_ref, proj, sems.at[len(spans)])
    copies = [
        pltpu.make_async_copy(rows_ref.at[span], held.at[span], sems.at[c])
        for c, span in enumerate(spans)
    ]
    first.start()
    for copy in copies:
        copy.start()
    first.wait()
    for copy, span in zip(copies, spans):
        copy.wait()
        feats_ref[:, span] = lax.dot_general(proj[...], held[span], NT, preferred_element_type=jnp.float32)


def features(rows, proj, sizes, limit, name):
    spans = row_spans(rows.shape[0], sizes)
    return pl.pallas_call(
        functools.partial(stream_kernel, spans),
        out_shape=pltpu.VMEM((proj.shape[0], rows.shape[0]), jnp.float32),
        in_specs=[ANY_SPEC] * 2,
        out_specs=VMEM_SPEC,
        scratch_shapes=[
            pltpu.VMEM(rows.shape, jnp.bfloat16),
            pltpu.VMEM(proj.shape, jnp.bfloat16),
            pltpu.SemaphoreType.DMA((len(spans) + 1,)),
        ],
        compiler_params=pltpu.CompilerParams(vmem_limit_bytes=limit * 2**20),
        name=name,
    )(in_hbm(rows), in_hbm(proj))


def split_kernel(prior_ref, upper_ref, lower_ref, held, sems):
    chunk = held.shape[1] // sems.shape[0]
    spans = [pl.ds(c * chunk, chunk) for c in range(sems.shape[0])]
    copies = [
        pltpu.make_async_copy(prior_ref.at[:, span], held.at[:, span], sems.at[c])
        for c, span in enumerate(spans)
    ]
    for copy in copies:
        copy.start()
    for copy, span in zip(copies, spans):
        copy.wait()
        block = held[:, span]
        upper = block.astype(jnp.bfloat16)
        upper_ref[:, span] = upper
        lower_ref[:, span] = (block - upper.astype(jnp.float32)).astype(jnp.bfloat16)


def split_prior(prior):
    return pl.pallas_call(
        split_kernel,
        out_shape=(pltpu.VMEM(prior.shape, jnp.bfloat16),) * 2,
        in_specs=[ANY_SPEC],
        out_specs=(VMEM_SPEC,) * 2,
        scratch_shapes=[pltpu.VMEM(prior.shape, jnp.float32), pltpu.SemaphoreType.DMA((8,))],
        compiler_params=PARAMS,
        name="split_prior",
    )(in_hbm(prior))


def partial_kernel(size, *refs):
    blocks, (out_ref, part_ref, held) = refs[:size], refs[size:]
    me = lax.axis_index("tensor")
    tokens = blocks[0].shape[1]
    for k, block in enumerate(blocks):
        start = pl.multiple_of((me ^ k) * tokens, LANES)
        held[:, pl.ds(start, tokens)] = block[...]
    for s in range(part_ref.shape[0]):
        span = slice(s * SEQ, (s + 1) * SEQ)
        part_ref[s] = dot_nt(held[:, span], out_ref[:, span]) * (1.0 / SEQ)


def partial_vectors(blocks, out_local):
    seq_count = out_local.shape[1] // SEQ
    return pl.pallas_call(
        functools.partial(partial_kernel, len(blocks)),
        out_shape=F32((seq_count, R_IN, R_OUT)),
        in_specs=[VMEM_SPEC] * (len(blocks) + 1),
        out_specs=VMEM_SPEC,
        scratch_shapes=[pltpu.VMEM(out_local.shape, jnp.float32)],
        compiler_params=PARAMS,
        name="partial_vectors",
    )(*blocks, out_local)


def own_columns(ref, me, count):
    if count % LANES == 0:
        return ref[:, pl.ds(pl.multiple_of(me * count, LANES), count)]
    per = LANES // count
    held = ref[:, pl.ds(pl.multiple_of((me // per) * LANES, LANES), LANES)]
    return pltpu.roll(held, LANES - (me % per) * count, 1)[:, :count]


def pieces_of(values, count):
    held = []
    for _ in range(count):
        piece = values.astype(jnp.bfloat16)
        held.append(piece)
        values = values - piece.astype(jnp.float32)
    return jnp.concatenate(held, axis=0)


def dot_pieces(a, b, seqs):
    held = lax.dot_general(a, b, NT, preferred_element_type=jnp.float32)
    total = held[:seqs]
    for start in range(seqs, held.shape[0], seqs):
        total = total + held[start : start + seqs]
    return total


def apply_fisher(pieces, vectors_ref, vector_pieces, upper_ref, lower_ref, me):
    seqs = vectors_ref.shape[0]
    applied = dot_pieces(pieces, upper_ref[...], seqs)
    applied = applied + dot_pieces(pieces[: 2 * seqs], lower_ref[...], seqs)
    weights = dot_pieces(pieces, vector_pieces, seqs)
    weights = (weights[:, :seqs] + weights[:, seqs:]) * (1.0 / seqs)
    own = own_columns(vectors_ref, me, upper_ref.shape[0])
    return applied + jnp.dot(weights, own, precision=HIGHEST, preferred_element_type=jnp.float32)


def flat_index(tensor_size):
    return lax.axis_index("dp") * tensor_size + lax.axis_index("tensor")


def start_kernel(size, tensor_size, *refs):
    pieces, refs = refs[:size], refs[size:]
    upper_ref, lower_ref, vectors_ref, vector_pieces_ref, scale_ref, applied_ref, norm_ref, held = refs
    dp = lax.axis_index("dp")
    for k, piece in enumerate(pieces):
        held[dp ^ k] = piece[...]
    vectors = jnp.concatenate([held[k] for k in range(size)], axis=0)
    vectors_ref[...] = vectors
    split = pieces_of(vectors, 3)
    vector_pieces = split[: 2 * vectors.shape[0]]
    vector_pieces_ref[...] = vector_pieces
    norm = jnp.broadcast_to(row_sum(vectors * vectors), norm_ref.shape)
    norm_ref[...] = norm
    spread = jnp.sum(norm, axis=0, keepdims=True) * (1.0 / vectors.shape[0])
    scale_ref[...] = jnp.broadcast_to(1.0 / (1.0 + spread), scale_ref.shape)
    me = flat_index(tensor_size)
    applied_ref[...] = apply_fisher(split, vectors_ref, vector_pieces, upper_ref, lower_ref, me)


def start_cg(pieces, prior_pieces, tensor_size):
    size, seqs = len(pieces), len(pieces) * pieces[0].shape[0]
    rows, width = prior_pieces[0].shape
    vector_pieces = jax.ShapeDtypeStruct((2 * seqs, width), jnp.bfloat16)
    column = F32((seqs, LANES))
    return pl.pallas_call(
        functools.partial(start_kernel, size, tensor_size),
        out_shape=(F32((seqs, width)), vector_pieces, column, F32((seqs, rows)), column),
        in_specs=[VMEM_SPEC] * (size + 2),
        out_specs=(VMEM_SPEC,) * 5,
        scratch_shapes=[pltpu.VMEM((size,) + pieces[0].shape, jnp.float32)],
        compiler_params=PARAMS,
        name="cg_start",
    )(*pieces, *prior_pieces)


def on_lanes(column):
    seqs = column.shape[0]
    row = lax.broadcasted_iota(jnp.int32, (seqs, LANES), 0)
    lane = lax.broadcasted_iota(jnp.int32, (seqs, LANES), 1)
    return jnp.sum(jnp.where(row == lane, column, 0.0), axis=0, keepdims=True)


def step_kernel(tensor_size, first, last, *refs):
    blocks_ref, upper_ref, lower_ref, vectors_ref, vector_pieces_ref, scale_ref = refs[:6]
    norm_ref, fisher_direction_ref = refs[6:8]
    refs = refs[8:]
    if not first:
        fisher_residual_ref, direction_ref, residual_ref, solution_ref = refs[:4]
        refs = refs[4:]
    if last:
        curvature_out, norm_out, direction_out, solution_out, held = refs
    else:
        fisher_direction_out, norm_out, fisher_residual_out, direction_out, residual_out, solution_out, held = refs
    me = flat_index(tensor_size)
    count, _, rows = blocks_ref.shape
    for i in range(count):
        held[:, i * rows : (i + 1) * rows] = blocks_ref[i]
    applied = held[...]
    scale = scale_ref[...][:, :1]
    twice = apply_fisher(
        pieces_of(scale * applied, 3), vectors_ref, vector_pieces_ref[...], upper_ref, lower_ref, me
    )
    direction = vectors_ref[...] if first else direction_ref[...]
    residual = direction if first else residual_ref[...]
    norm = norm_ref[...][:, :1]
    step = norm / row_sum(direction * applied)
    solution = step * direction
    if not first:
        solution = solution_ref[...] + solution
    residual = residual - step * applied
    norm_next = row_sum(residual * residual)
    share = norm_next / norm
    direction = residual + share * direction
    fisher_direction = fisher_direction_ref[...]
    fisher_residual = (fisher_direction if first else fisher_residual_ref[...]) - (step / scale) * twice
    fisher_direction = fisher_residual + share * fisher_direction
    direction_out[...] = direction
    solution_out[...] = solution
    if last:
        own = own_columns(direction_out, me, rows)
        curvature_out[...] = on_lanes(row_sum(own * fisher_direction))
        norm_out[...] = on_lanes(norm_next)
    else:
        fisher_direction_out[...] = fisher_direction
        fisher_residual_out[...] = fisher_residual
        residual_out[...] = residual
        norm_out[...] = jnp.broadcast_to(norm_next, norm_out.shape)


def step_cg(blocks, fixed, norm, state, last, tensor_size):
    first = len(state) == 1
    whole, rows = F32(fixed[2].shape), F32(state[0].shape)
    row = F32((1, LANES))
    operands = [blocks, *fixed, norm, *state]
    out_shape = (row, row, whole, whole) if last else (rows, F32(norm.shape), rows, whole, whole, whole)
    return pl.pallas_call(
        functools.partial(step_kernel, tensor_size, first, last),
        out_shape=out_shape,
        in_specs=[VMEM_SPEC] * len(operands),
        out_specs=(VMEM_SPEC,) * len(out_shape),
        scratch_shapes=[pltpu.VMEM(whole.shape, jnp.float32)],
        compiler_params=PARAMS,
        name="cg_step",
    )(*operands)


def score_kernel(solution_ref, direction_ref, queries_ref, solved_ref, along_ref):
    seqs = solution_ref.shape[0]
    both = jnp.concatenate([solution_ref[...], direction_ref[...]], axis=0)
    scores = dot_pieces(pieces_of(both, 3), queries_ref[...], 2 * seqs)
    solved_ref[...] = scores[:seqs]
    along_ref[...] = scores[seqs:]


def score(solution, direction, queries):
    scores = F32((solution.shape[0], queries.shape[0]))
    return pl.pallas_call(
        score_kernel,
        out_shape=(scores, scores),
        in_specs=[VMEM_SPEC] * 3,
        out_specs=(VMEM_SPEC,) * 2,
        compiler_params=PARAMS,
        name="scores",
    )(solution, direction, queries)


def on_device(dp_size, tensor_size, inputs, in_proj, out_grads, out_proj, prior, queries):
    width = R_IN * R_OUT
    both, devices = ("dp", "tensor"), dp_size * tensor_size
    in_blocks = direct(features(inputs, in_proj, (256, 128), 16, "in_features"), "tensor", tensor_size)
    out_local = features(out_grads, out_proj, (256,) * 7 + (128,), 40, "out_features")
    partial = partial_vectors(in_blocks, out_local).reshape(-1, width)
    pieces = direct(sum_over(partial, "tensor", tensor_size), "dp", dp_size)
    prior_pieces = [in_vmem(piece) for piece in split_prior(prior)]
    vectors, vector_pieces, scale, applied_rows, norm = start_cg(pieces, prior_pieces, tensor_size)
    fixed = (*prior_pieces, vectors, vector_pieces, scale)
    state = [applied_rows]
    for iteration in range(1, ITERS - 1):
        blocks = gather(state[0], both, devices)
        applied_rows, norm, *others = step_cg(blocks, fixed, norm, state, False, tensor_size)
        state = [applied_rows, *others]
    blocks = gather(state[0], both, devices)
    curvature, norm, direction, solved = step_cg(blocks, fixed, norm, state, True, tensor_size)
    curvature = jnp.sum(gather(curvature, both, devices), axis=0)
    solved, along = score(solved, direction, queries)
    step = (norm / curvature)[0, : solved.shape[0]]
    return solved + step[:, None] * along


def solution(mesh):
    return jax.shard_map(
        functools.partial(on_device, mesh.shape["dp"], mesh.shape["tensor"]),
        mesh=mesh,
        in_specs=(
            P(("groups", "dp", "tensor"), None),
            P(),
            P(("groups", "dp"), "tensor"),
            P(None, "tensor"),
            P(("groups", "dp", "tensor"), None),
            P(("groups", "dp", "tensor"), None),
        ),
        out_specs=P("groups", ("dp", "tensor")),
        check_vma=False,
    )
```

```python
import functools

import jax
import jax.numpy as jnp
from jax import lax
from jax.experimental import pallas as pl
from jax.experimental.pallas import tpu as pltpu
from jax.sharding import PartitionSpec as P

R_IN = 64
R_OUT = 64
SEQ = 1024
ITERS = 4
LANES = 128
FEW = 4
NT = (((1,), (1,)), ((), ()))
HIGHEST = lax.Precision.HIGHEST
ANY_SPEC = pl.BlockSpec(memory_space=pl.ANY)
VMEM_SPEC = pl.BlockSpec(memory_space=pltpu.VMEM)
PARAMS = pltpu.CompilerParams(vmem_limit_bytes=16 * 2**20)
F32 = functools.partial(jax.ShapeDtypeStruct, dtype=jnp.float32)


def swap(value, axis, size, bit):
    return lax.ppermute(value, axis, [(i, i ^ bit) for i in range(size)])


def bits(size):
    return [1 << b for b in reversed(range(size.bit_length() - 1))]


def gather(value, axes, size):
    return lax.all_to_all(jnp.broadcast_to(value[None], (size,) + value.shape), axes, 0, 0)


def order_of(size):
    return (0, 2, 3, 1) if size == 4 else tuple(range(size))


def direct(value, axis, size):
    return [value] + [swap(value, axis, size, k) for k in order_of(size)[1:]]


def sum_over(value, axis, size):
    if size > FEW:
        for bit in bits(size):
            value = value + swap(value, axis, size, bit)
        return value
    blocks = direct(value, axis, size)
    while len(blocks) > 1:
        blocks = [a + b for a, b in zip(blocks[::2], blocks[1::2])]
    return blocks[0]


def in_hbm(value):
    return pltpu.with_memory_space_constraint(value, pltpu.HBM)


def in_vmem(value):
    return pltpu.with_memory_space_constraint(value, pltpu.VMEM)


def dot_nt(a, b):
    return lax.dot_general(a, b, NT, precision=HIGHEST, preferred_element_type=jnp.float32)


def row_sum(values):
    return jnp.sum(values, axis=1, keepdims=True)


def row_spans(rows, sizes):
    spans, start = [], 0
    while start < rows:
        while len(sizes) > 1 and start + sizes[0] + sizes[-1] > rows:
            sizes = sizes[1:]
        spans.append(pl.ds(start, sizes[0]))
        start += sizes[0]
        sizes = sizes[1:] or sizes
    return spans


def stream_kernel(spans, rows_ref, proj_ref, feats_ref, held, proj, turned, sems):
    first = pltpu.make_async_copy(proj_ref, proj, sems.at[len(spans)])
    copies = [
        pltpu.make_async_copy(rows_ref.at[span], held.at[span], sems.at[c])
        for c, span in enumerate(spans)
    ]
    first.start()
    for copy in copies:
        copy.start()
    first.wait()
    turned[...] = proj[...].T
    for copy, span in zip(copies, spans):
        copy.wait()
        feats = jnp.dot(held[span], turned[...], preferred_element_type=jnp.float32)
        feats_ref[:, span] = feats.T


def features(rows, proj, sizes, limit, name):
    spans = row_spans(rows.shape[0], sizes)
    return pl.pallas_call(
        functools.partial(stream_kernel, spans),
        out_shape=pltpu.VMEM((proj.shape[0], rows.shape[0]), jnp.float32),
        in_specs=[ANY_SPEC] * 2,
        out_specs=VMEM_SPEC,
        scratch_shapes=[
            pltpu.VMEM(rows.shape, jnp.bfloat16),
            pltpu.VMEM(proj.shape, jnp.bfloat16),
            pltpu.VMEM(proj.shape[::-1], jnp.bfloat16),
            pltpu.SemaphoreType.DMA((len(spans) + 1,)),
        ],
        compiler_params=pltpu.CompilerParams(vmem_limit_bytes=limit * 2**20),
        name=name,
    )(in_hbm(rows), in_hbm(proj))


def split_kernel(prior_ref, upper_ref, lower_ref, held, sems):
    chunk = held.shape[1] // sems.shape[0]
    spans = [pl.ds(c * chunk, chunk) for c in range(sems.shape[0])]
    copies = [
        pltpu.make_async_copy(prior_ref.at[:, span], held.at[:, span], sems.at[c])
        for c, span in enumerate(spans)
    ]
    for copy in copies:
        copy.start()
    for copy, span in zip(copies, spans):
        copy.wait()
        block = held[:, span]
        upper = block.astype(jnp.bfloat16)
        upper_ref[:, span] = upper
        lower_ref[:, span] = (block - upper.astype(jnp.float32)).astype(jnp.bfloat16)


def split_prior(prior):
    return pl.pallas_call(
        split_kernel,
        out_shape=(pltpu.VMEM(prior.shape, jnp.bfloat16),) * 2,
        in_specs=[ANY_SPEC],
        out_specs=(VMEM_SPEC,) * 2,
        scratch_shapes=[pltpu.VMEM(prior.shape, jnp.float32), pltpu.SemaphoreType.DMA((8,))],
        compiler_params=PARAMS,
        name="split_prior",
    )(in_hbm(prior))


def partial_kernel(size, *refs):
    blocks, (out_ref, part_ref, held) = refs[:size], refs[size:]
    me = lax.axis_index("tensor")
    tokens = blocks[0].shape[1]
    for k, block in zip(order_of(size), blocks):
        start = pl.multiple_of((me ^ k) * tokens, LANES)
        held[:, pl.ds(start, tokens)] = block[...]
    for s in range(part_ref.shape[0]):
        span = slice(s * SEQ, (s + 1) * SEQ)
        part_ref[s] = dot_nt(held[:, span], out_ref[:, span]) * (1.0 / SEQ)


def partial_vectors(blocks, out_local):
    seq_count = out_local.shape[1] // SEQ
    return pl.pallas_call(
        functools.partial(partial_kernel, len(blocks)),
        out_shape=F32((seq_count, R_IN, R_OUT)),
        in_specs=[VMEM_SPEC] * (len(blocks) + 1),
        out_specs=VMEM_SPEC,
        scratch_shapes=[pltpu.VMEM(out_local.shape, jnp.float32)],
        compiler_params=PARAMS,
        name="partial_vectors",
    )(*blocks, out_local)


def own_columns(ref, me, count):
    if count % LANES == 0:
        return ref[:, pl.ds(pl.multiple_of(me * count, LANES), count)]
    per = LANES // count
    held = ref[:, pl.ds(pl.multiple_of((me // per) * LANES, LANES), LANES)]
    return pltpu.roll(held, LANES - (me % per) * count, 1)[:, :count]


def pieces_of(values, count):
    held = []
    for _ in range(count):
        piece = values.astype(jnp.bfloat16)
        held.append(piece)
        values = values - piece.astype(jnp.float32)
    return jnp.concatenate(held, axis=0)


def dot_pieces(a, b, seqs):
    held = lax.dot_general(a, b, NT, preferred_element_type=jnp.float32)
    total = held[:seqs]
    for start in range(seqs, held.shape[0], seqs):
        total = total + held[start : start + seqs]
    return total


def apply_fisher(pieces, vectors_ref, vector_pieces, upper_ref, lower_ref, me):
    seqs = vectors_ref.shape[0]
    applied = dot_pieces(pieces, upper_ref[...], seqs)
    applied = applied + dot_pieces(pieces[: 2 * seqs], lower_ref[...], seqs)
    weights = dot_pieces(pieces, vector_pieces, seqs)
    weights = (weights[:, :seqs] + weights[:, seqs:]) * (1.0 / seqs)
    own = own_columns(vectors_ref, me, upper_ref.shape[0])
    return applied + jnp.dot(weights, own, precision=HIGHEST, preferred_element_type=jnp.float32)


def flat_index(tensor_size):
    return lax.axis_index("dp") * tensor_size + lax.axis_index("tensor")


def start_kernel(size, tensor_size, *refs):
    pieces, refs = refs[:size], refs[size:]
    upper_ref, lower_ref, vectors_ref, vector_pieces_ref, scale_ref, applied_ref, norm_ref, held = refs
    dp = lax.axis_index("dp")
    for k, piece in zip(order_of(size), pieces):
        held[dp ^ k] = piece[...]
    vectors = jnp.concatenate([held[k] for k in range(size)], axis=0)
    vectors_ref[...] = vectors
    split = pieces_of(vectors, 3)
    vector_pieces = split[: 2 * vectors.shape[0]]
    vector_pieces_ref[...] = vector_pieces
    norm = jnp.broadcast_to(row_sum(vectors * vectors), norm_ref.shape)
    norm_ref[...] = norm
    spread = jnp.sum(norm, axis=0, keepdims=True) * (1.0 / vectors.shape[0])
    scale_ref[...] = jnp.broadcast_to(1.0 / (1.0 + spread), scale_ref.shape)
    me = flat_index(tensor_size)
    applied_ref[...] = apply_fisher(split, vectors_ref, vector_pieces, upper_ref, lower_ref, me)


def start_cg(pieces, prior_pieces, tensor_size):
    size, seqs = len(pieces), len(pieces) * pieces[0].shape[0]
    rows, width = prior_pieces[0].shape
    vector_pieces = jax.ShapeDtypeStruct((2 * seqs, width), jnp.bfloat16)
    column = F32((seqs, LANES))
    return pl.pallas_call(
        functools.partial(start_kernel, size, tensor_size),
        out_shape=(F32((seqs, width)), vector_pieces, column, F32((seqs, rows)), column),
        in_specs=[VMEM_SPEC] * (size + 2),
        out_specs=(VMEM_SPEC,) * 5,
        scratch_shapes=[pltpu.VMEM((size,) + pieces[0].shape, jnp.float32)],
        compiler_params=PARAMS,
        name="cg_start",
    )(*pieces, *prior_pieces)


def place_blocks(blocks, sizes, held):
    if len(blocks) == 1:
        count, _, rows = blocks[0].shape
        for i in range(count):
            held[:, i * rows : (i + 1) * rows] = blocks[0][i]
        return
    dp, tensor = lax.axis_index("dp"), lax.axis_index("tensor")
    rows = blocks[0].shape[2]
    for k, block in zip(order_of(sizes[0]), blocks):
        for i, j in enumerate(order_of(sizes[1])):
            start = ((dp ^ k) * sizes[1] + (tensor ^ j)) * rows
            held[:, pl.ds(pl.multiple_of(start, LANES), rows)] = block[i]


def step_kernel(count, sizes, first, last, *refs):
    blocks, refs = refs[:count], refs[count:]
    upper_ref, lower_ref, vectors_ref, vector_pieces_ref, scale_ref = refs[:5]
    norm_ref, fisher_direction_ref = refs[5:7]
    refs = refs[7:]
    if not first:
        fisher_residual_ref, direction_ref, residual_ref, solution_ref = refs[:4]
        refs = refs[4:]
    if last:
        curvature_out, norm_out, direction_out, solution_out, held = refs
    else:
        fisher_direction_out, norm_out, fisher_residual_out, direction_out, residual_out, solution_out, held = refs
    me = flat_index(sizes[1])
    place_blocks(blocks, sizes, held)
    applied = held[...]
    scale = scale_ref[...][:, :1]
    twice = apply_fisher(
        pieces_of(scale * applied, 3), vectors_ref, vector_pieces_ref[...], upper_ref, lower_ref, me
    )
    direction = vectors_ref[...] if first else direction_ref[...]
    residual = direction if first else residual_ref[...]
    norm = norm_ref[...][:, :1]
    step = norm / row_sum(direction * applied)
    solution = step * direction
    if not first:
        solution = solution_ref[...] + solution
    residual = residual - step * applied
    norm_next = row_sum(residual * residual)
    share = norm_next / norm
    direction = residual + share * direction
    fisher_direction = fisher_direction_ref[...]
    fisher_residual = (fisher_direction if first else fisher_residual_ref[...]) - (step / scale) * twice
    fisher_direction = fisher_residual + share * fisher_direction
    direction_out[...] = direction
    solution_out[...] = solution
    norm_out[...] = jnp.broadcast_to(norm_next, norm_out.shape)
    if last:
        own = own_columns(direction_out, me, fisher_direction.shape[1])
        curvature_out[...] = jnp.broadcast_to(row_sum(own * fisher_direction), curvature_out.shape)
    else:
        fisher_direction_out[...] = fisher_direction
        fisher_residual_out[...] = fisher_residual
        residual_out[...] = residual


def step_cg(blocks, fixed, norm, state, last, sizes):
    first = len(state) == 1
    whole, rows = F32(fixed[2].shape), F32(state[0].shape)
    column = F32(norm.shape)
    operands = [*blocks, *fixed, norm, *state]
    out_shape = (column, column, whole, whole) if last else (rows, column, rows, whole, whole, whole)
    return pl.pallas_call(
        functools.partial(step_kernel, len(blocks), sizes, first, last),
        out_shape=out_shape,
        in_specs=[VMEM_SPEC] * len(operands),
        out_specs=(VMEM_SPEC,) * len(out_shape),
        scratch_shapes=[pltpu.VMEM(whole.shape, jnp.float32)],
        compiler_params=PARAMS,
        name="cg_step",
    )(*operands)


def score_kernel(solution_ref, direction_ref, queries_ref, solved_ref, along_ref):
    seqs = solution_ref.shape[0]
    both = jnp.concatenate([solution_ref[...], direction_ref[...]], axis=0)
    scores = dot_pieces(pieces_of(both, 3), queries_ref[...], 2 * seqs)
    solved_ref[...] = scores[:seqs]
    along_ref[...] = scores[seqs:]


def score(solution, direction, queries):
    scores = F32((solution.shape[0], queries.shape[0]))
    return pl.pallas_call(
        score_kernel,
        out_shape=(scores, scores),
        in_specs=[VMEM_SPEC] * 3,
        out_specs=(VMEM_SPEC,) * 2,
        compiler_params=PARAMS,
        name="scores",
    )(solution, direction, queries)


def on_device(dp_size, tensor_size, inputs, in_proj, out_grads, out_proj, prior, queries):
    width = R_IN * R_OUT
    both, devices, sizes = ("dp", "tensor"), dp_size * tensor_size, (dp_size, tensor_size)
    in_blocks = direct(features(inputs, in_proj, (256, 128), 20, "in_features"), "tensor", tensor_size)
    out_local = features(out_grads, out_proj, (256,) * 7 + (128,), 44, "out_features")
    partial = partial_vectors(in_blocks, out_local).reshape(-1, width)
    pieces = direct(sum_over(partial, "tensor", tensor_size), "dp", dp_size)
    prior_pieces = [in_vmem(piece) for piece in split_prior(prior)]
    few = max(sizes) <= FEW and prior.shape[0] % LANES == 0

    def gather_rows(values):
        if not few:
            return [gather(values, both, devices)]
        return direct(jnp.stack(direct(values, "tensor", tensor_size)), "dp", dp_size)

    vectors, vector_pieces, scale, applied_rows, norm = start_cg(pieces, prior_pieces, tensor_size)
    fixed = (*prior_pieces, vectors, vector_pieces, scale)
    state = [applied_rows]
    for iteration in range(1, ITERS - 1):
        blocks = gather_rows(state[0])
        applied_rows, norm, *others = step_cg(blocks, fixed, norm, state, False, sizes)
        state = [applied_rows, *others]
    blocks = gather_rows(state[0])
    curvature, norm, direction, solved = step_cg(blocks, fixed, norm, state, True, sizes)
    if few:
        curvature = sum_over(sum_over(curvature, "tensor", tensor_size), "dp", dp_size)
    else:
        curvature = jnp.sum(gather(curvature, both, devices), axis=0)
    solved, along = score(solved, direction, queries)
    return solved + (norm / curvature)[:, :1] * along


def solution(mesh):
    return jax.shard_map(
        functools.partial(on_device, mesh.shape["dp"], mesh.shape["tensor"]),
        mesh=mesh,
        in_specs=(
            P(("groups", "dp", "tensor"), None),
            P(),
            P(("groups", "dp"), "tensor"),
            P(None, "tensor"),
            P(("groups", "dp", "tensor"), None),
            P(("groups", "dp", "tensor"), None),
        ),
        out_specs=P("groups", ("dp", "tensor")),
        check_vma=False,
    )
```

```python
import functools

import jax
import jax.numpy as jnp
from jax import lax
from jax.experimental import pallas as pl
from jax.experimental.pallas import tpu as pltpu
from jax.sharding import PartitionSpec as P

R_IN = 64
R_OUT = 64
SEQ = 1024
ITERS = 4
LANES = 128
NT = (((1,), (1,)), ((), ()))
HIGHEST = lax.Precision.HIGHEST
ANY_SPEC = pl.BlockSpec(memory_space=pl.ANY)
VMEM_SPEC = pl.BlockSpec(memory_space=pltpu.VMEM)
PARAMS = pltpu.CompilerParams(vmem_limit_bytes=16 * 2**20)
F32 = functools.partial(jax.ShapeDtypeStruct, dtype=jnp.float32)


def swap(value, axis, size, bit):
    return lax.ppermute(value, axis, [(i, i ^ bit) for i in range(size)])


def bits(size):
    return [1 << b for b in reversed(range(size.bit_length() - 1))]


def gather(value, axes, size):
    return lax.all_to_all(jnp.broadcast_to(value[None], (size,) + value.shape), axes, 0, 0)


def order_of(size):
    return (0, 2, 3, 1) if size == 4 else tuple(range(size))


def direct(value, axis, size):
    return [value] + [swap(value, axis, size, k) for k in order_of(size)[1:]]


def sum_over(value, axis, size):
    for bit in bits(size):
        value = value + swap(value, axis, size, bit)
    return value


def in_hbm(value):
    return pltpu.with_memory_space_constraint(value, pltpu.HBM)


def in_vmem(value):
    return pltpu.with_memory_space_constraint(value, pltpu.VMEM)


def dot_nt(a, b):
    return lax.dot_general(a, b, NT, precision=HIGHEST, preferred_element_type=jnp.float32)


def row_sum(values):
    return jnp.sum(values, axis=1, keepdims=True)


def row_spans(rows, sizes):
    spans, start = [], 0
    while start < rows:
        while len(sizes) > 1 and start + sizes[0] + sizes[-1] > rows:
            sizes = sizes[1:]
        spans.append(pl.ds(start, sizes[0]))
        start += sizes[0]
        sizes = sizes[1:] or sizes
    return spans


def stream_kernel(spans, rows_ref, proj_ref, feats_ref, held, proj, turned, sems):
    count, half = proj_ref.shape[0], proj.shape[1]
    firsts = [
        pltpu.make_async_copy(
            proj_ref.at[:, pl.ds(h * half, half)], proj.at[pl.ds(h * count, count)], sems.at[len(spans) + h]
        )
        for h in range(2)
    ]
    copies = [
        pltpu.make_async_copy(rows_ref.at[span], held.at[span], sems.at[c])
        for c, span in enumerate(spans)
    ]
    for copy in firsts + copies:
        copy.start()
    for copy in firsts:
        copy.wait()
    turned[...] = proj[...].T
    for copy, span in zip(copies, spans):
        copy.wait()
        left = jnp.dot(held[span, :half], turned[...], preferred_element_type=jnp.float32)
        right = jnp.dot(held[span, half:], turned[...], preferred_element_type=jnp.float32)
        feats_ref[:, span] = left.T[:count] + right.T[count:]


def features(rows, proj, sizes, limit, name):
    spans = row_spans(rows.shape[0], sizes)
    return pl.pallas_call(
        functools.partial(stream_kernel, spans),
        out_shape=pltpu.VMEM((proj.shape[0], rows.shape[0]), jnp.float32),
        in_specs=[ANY_SPEC] * 2,
        out_specs=VMEM_SPEC,
        scratch_shapes=[
            pltpu.VMEM(rows.shape, jnp.bfloat16),
            pltpu.VMEM((2 * proj.shape[0], proj.shape[1] // 2), jnp.bfloat16),
            pltpu.VMEM((proj.shape[1] // 2, 2 * proj.shape[0]), jnp.bfloat16),
            pltpu.SemaphoreType.DMA((len(spans) + 2,)),
        ],
        compiler_params=pltpu.CompilerParams(vmem_limit_bytes=limit * 2**20),
        name=name,
    )(in_hbm(rows), in_hbm(proj))


def split_kernel(prior_ref, upper_ref, lower_ref, held, sems):
    chunk = held.shape[1] // sems.shape[0]
    spans = [pl.ds(c * chunk, chunk) for c in range(sems.shape[0])]
    copies = [
        pltpu.make_async_copy(prior_ref.at[:, span], held.at[:, span], sems.at[c])
        for c, span in enumerate(spans)
    ]
    for copy in copies:
        copy.start()
    for copy, span in zip(copies, spans):
        copy.wait()
        block = held[:, span]
        upper = block.astype(jnp.bfloat16)
        upper_ref[:, span] = upper
        lower_ref[:, span] = (block - upper.astype(jnp.float32)).astype(jnp.bfloat16)


def split_prior(prior):
    return pl.pallas_call(
        split_kernel,
        out_shape=(pltpu.VMEM(prior.shape, jnp.bfloat16),) * 2,
        in_specs=[ANY_SPEC],
        out_specs=(VMEM_SPEC,) * 2,
        scratch_shapes=[pltpu.VMEM(prior.shape, jnp.float32), pltpu.SemaphoreType.DMA((8,))],
        compiler_params=PARAMS,
        name="split_prior",
    )(in_hbm(prior))


def partial_kernel(size, *refs):
    blocks, (out_ref, part_ref, held) = refs[:size], refs[size:]
    me = lax.axis_index("tensor")
    tokens = blocks[0].shape[1]
    for k, block in zip(order_of(size), blocks):
        start = pl.multiple_of((me ^ k) * tokens, LANES)
        held[:, pl.ds(start, tokens)] = block[...]
    for s in range(part_ref.shape[0]):
        span = slice(s * SEQ, (s + 1) * SEQ)
        part_ref[s] = dot_nt(held[:, span], out_ref[:, span]) * (1.0 / SEQ)


def partial_vectors(blocks, out_local):
    seq_count = out_local.shape[1] // SEQ
    return pl.pallas_call(
        functools.partial(partial_kernel, len(blocks)),
        out_shape=F32((seq_count, R_IN, R_OUT)),
        in_specs=[VMEM_SPEC] * (len(blocks) + 1),
        out_specs=VMEM_SPEC,
        scratch_shapes=[pltpu.VMEM(out_local.shape, jnp.float32)],
        compiler_params=PARAMS,
        name="partial_vectors",
    )(*blocks, out_local)


def own_columns(ref, me, count):
    if count % LANES == 0:
        return ref[:, pl.ds(pl.multiple_of(me * count, LANES), count)]
    per = LANES // count
    held = ref[:, pl.ds(pl.multiple_of((me // per) * LANES, LANES), LANES)]
    return pltpu.roll(held, LANES - (me % per) * count, 1)[:, :count]


def pieces_of(values, count):
    held = []
    for _ in range(count):
        piece = values.astype(jnp.bfloat16)
        held.append(piece)
        values = values - piece.astype(jnp.float32)
    return jnp.concatenate(held, axis=0)


def dot_pieces(a, b, seqs):
    held = lax.dot_general(a, b, NT, preferred_element_type=jnp.float32)
    total = held[:seqs]
    for start in range(seqs, held.shape[0], seqs):
        total = total + held[start : start + seqs]
    return total


def apply_fisher(pieces, vectors_ref, vector_pieces, upper_ref, lower_ref, me):
    seqs = vectors_ref.shape[0]
    applied = dot_pieces(pieces, upper_ref[...], seqs)
    applied = applied + dot_pieces(pieces[: 2 * seqs], lower_ref[...], seqs)
    weights = dot_pieces(pieces, vector_pieces, seqs)
    weights = (weights[:, :seqs] + weights[:, seqs:]) * (1.0 / seqs)
    own = own_columns(vectors_ref, me, upper_ref.shape[0])
    return applied + jnp.dot(weights, own, precision=HIGHEST, preferred_element_type=jnp.float32)


def flat_index(tensor_size):
    return lax.axis_index("dp") * tensor_size + lax.axis_index("tensor")


def start_kernel(size, tensor_size, *refs):
    pieces, refs = refs[:size], refs[size:]
    upper_ref, lower_ref, vectors_ref, vector_pieces_ref, scale_ref, applied_ref, norm_ref, held = refs
    dp = lax.axis_index("dp")
    for k, piece in zip(order_of(size), pieces):
        held[dp ^ k] = piece[...]
    vectors = jnp.concatenate([held[k] for k in range(size)], axis=0)
    vectors_ref[...] = vectors
    split = pieces_of(vectors, 3)
    vector_pieces = split[: 2 * vectors.shape[0]]
    vector_pieces_ref[...] = vector_pieces
    norm = jnp.broadcast_to(row_sum(vectors * vectors), norm_ref.shape)
    norm_ref[...] = norm
    spread = jnp.sum(norm, axis=0, keepdims=True) * (1.0 / vectors.shape[0])
    scale_ref[...] = jnp.broadcast_to(1.0 / (1.0 + spread), scale_ref.shape)
    me = flat_index(tensor_size)
    applied_ref[...] = apply_fisher(split, vectors_ref, vector_pieces, upper_ref, lower_ref, me)


def start_cg(pieces, prior_pieces, tensor_size):
    size, seqs = len(pieces), len(pieces) * pieces[0].shape[0]
    rows, width = prior_pieces[0].shape
    vector_pieces = jax.ShapeDtypeStruct((2 * seqs, width), jnp.bfloat16)
    column = F32((seqs, LANES))
    return pl.pallas_call(
        functools.partial(start_kernel, size, tensor_size),
        out_shape=(F32((seqs, width)), vector_pieces, column, F32((seqs, rows)), column),
        in_specs=[VMEM_SPEC] * (size + 2),
        out_specs=(VMEM_SPEC,) * 5,
        scratch_shapes=[pltpu.VMEM((size,) + pieces[0].shape, jnp.float32)],
        compiler_params=PARAMS,
        name="cg_start",
    )(*pieces, *prior_pieces)


def step_kernel(tensor_size, first, last, *refs):
    blocks_ref, upper_ref, lower_ref, vectors_ref, vector_pieces_ref, scale_ref = refs[:6]
    norm_ref, fisher_direction_ref = refs[6:8]
    refs = refs[8:]
    if not first:
        fisher_residual_ref, direction_ref, residual_ref, solution_ref = refs[:4]
        refs = refs[4:]
    if last:
        curvature_out, norm_out, direction_out, solution_out, held = refs
    else:
        fisher_direction_out, norm_out, fisher_residual_out, direction_out, residual_out, solution_out, held = refs
    me = flat_index(tensor_size)
    count, _, rows = blocks_ref.shape
    for i in range(count):
        held[:, i * rows : (i + 1) * rows] = blocks_ref[i]
    applied = held[...]
    scale = scale_ref[...][:, :1]
    twice = apply_fisher(
        pieces_of(scale * applied, 3), vectors_ref, vector_pieces_ref[...], upper_ref, lower_ref, me
    )
    direction = vectors_ref[...] if first else direction_ref[...]
    residual = direction if first else residual_ref[...]
    norm = norm_ref[...][:, :1]
    step = norm / row_sum(direction * applied)
    solution = step * direction
    if not first:
        solution = solution_ref[...] + solution
    residual = residual - step * applied
    norm_next = row_sum(residual * residual)
    share = norm_next / norm
    direction = residual + share * direction
    fisher_direction = fisher_direction_ref[...]
    fisher_residual = (fisher_direction if first else fisher_residual_ref[...]) - (step / scale) * twice
    fisher_direction = fisher_residual + share * fisher_direction
    direction_out[...] = direction
    solution_out[...] = solution
    norm_out[...] = jnp.broadcast_to(norm_next, norm_out.shape)
    if last:
        own = own_columns(direction_out, me, rows)
        curvature_out[...] = jnp.broadcast_to(row_sum(own * fisher_direction), curvature_out.shape)
    else:
        fisher_direction_out[...] = fisher_direction
        fisher_residual_out[...] = fisher_residual
        residual_out[...] = residual


def step_cg(blocks, fixed, norm, state, last, tensor_size):
    first = len(state) == 1
    whole, rows = F32(fixed[2].shape), F32(state[0].shape)
    column = F32(norm.shape)
    operands = [blocks, *fixed, norm, *state]
    out_shape = (column, column, whole, whole) if last else (rows, column, rows, whole, whole, whole)
    return pl.pallas_call(
        functools.partial(step_kernel, tensor_size, first, last),
        out_shape=out_shape,
        in_specs=[VMEM_SPEC] * len(operands),
        out_specs=(VMEM_SPEC,) * len(out_shape),
        scratch_shapes=[pltpu.VMEM(whole.shape, jnp.float32)],
        compiler_params=PARAMS,
        name="cg_step",
    )(*operands)


def score_kernel(solution_ref, direction_ref, queries_ref, solved_ref, along_ref):
    seqs = solution_ref.shape[0]
    both = jnp.concatenate([solution_ref[...], direction_ref[...]], axis=0)
    scores = dot_pieces(pieces_of(both, 3), queries_ref[...], 2 * seqs)
    solved_ref[...] = scores[:seqs]
    along_ref[...] = scores[seqs:]


def score(solution, direction, queries):
    scores = F32((solution.shape[0], queries.shape[0]))
    return pl.pallas_call(
        score_kernel,
        out_shape=(scores, scores),
        in_specs=[VMEM_SPEC] * 3,
        out_specs=(VMEM_SPEC,) * 2,
        compiler_params=PARAMS,
        name="scores",
    )(solution, direction, queries)


def on_device(dp_size, tensor_size, inputs, in_proj, out_grads, out_proj, prior, queries):
    width = R_IN * R_OUT
    both, devices = ("dp", "tensor"), dp_size * tensor_size
    in_blocks = direct(features(inputs, in_proj, (128,), 20, "in_features"), "tensor", tensor_size)
    out_local = features(out_grads, out_proj, (256,) * 7 + (128,), 44, "out_features")
    partial = partial_vectors(in_blocks, out_local).reshape(-1, width)
    pieces = direct(sum_over(partial, "tensor", tensor_size), "dp", dp_size)
    prior_pieces = [in_vmem(piece) for piece in split_prior(prior)]
    vectors, vector_pieces, scale, applied_rows, norm = start_cg(pieces, prior_pieces, tensor_size)
    fixed = (*prior_pieces, vectors, vector_pieces, scale)
    state = [applied_rows]
    for iteration in range(1, ITERS - 1):
        blocks = gather(state[0], both, devices)
        applied_rows, norm, *others = step_cg(blocks, fixed, norm, state, False, tensor_size)
        state = [applied_rows, *others]
    blocks = gather(state[0], both, devices)
    curvature, norm, direction, solved = step_cg(blocks, fixed, norm, state, True, tensor_size)
    curvature = jnp.sum(gather(curvature, both, devices), axis=0)
    solved, along = score(solved, direction, queries)
    return solved + (norm / curvature)[:, :1] * along


def solution(mesh):
    return jax.shard_map(
        functools.partial(on_device, mesh.shape["dp"], mesh.shape["tensor"]),
        mesh=mesh,
        in_specs=(
            P(("groups", "dp", "tensor"), None),
            P(),
            P(("groups", "dp"), "tensor"),
            P(None, "tensor"),
            P(("groups", "dp", "tensor"), None),
            P(("groups", "dp", "tensor"), None),
        ),
        out_specs=P("groups", ("dp", "tensor")),
        check_vma=False,
    )
```

```python
import functools

import jax
import jax.numpy as jnp
from jax import lax
from jax.experimental import pallas as pl
from jax.experimental.pallas import tpu as pltpu
from jax.sharding import PartitionSpec as P

R_IN = 64
R_OUT = 64
SEQ = 1024
ITERS = 4
LANES = 128
DEPTH = 4
NT = (((1,), (1,)), ((), ()))
HIGHEST = lax.Precision.HIGHEST
ANY_SPEC = pl.BlockSpec(memory_space=pl.ANY)
VMEM_SPEC = pl.BlockSpec(memory_space=pltpu.VMEM)
PARAMS = pltpu.CompilerParams(vmem_limit_bytes=16 * 2**20)
F32 = functools.partial(jax.ShapeDtypeStruct, dtype=jnp.float32)


def swap(value, axis, size, bit):
    return lax.ppermute(value, axis, [(i, i ^ bit) for i in range(size)])


def bits(size):
    return [1 << b for b in reversed(range(size.bit_length() - 1))]


def gather(value, axes, size):
    return lax.all_to_all(jnp.broadcast_to(value[None], (size,) + value.shape), axes, 0, 0)


def order_of(size):
    return (0, 2, 3, 1) if size == 4 else tuple(range(size))


def direct(value, axis, size):
    return [value] + [swap(value, axis, size, k) for k in order_of(size)[1:]]


def in_hbm(value):
    return pltpu.with_memory_space_constraint(value, pltpu.HBM)


def in_vmem(value):
    return pltpu.with_memory_space_constraint(value, pltpu.VMEM)


def dot_nt(a, b):
    return lax.dot_general(a, b, NT, precision=HIGHEST, preferred_element_type=jnp.float32)


def row_sum(values):
    return jnp.sum(values, axis=1, keepdims=True)


def row_spans(rows, sizes):
    spans, start = [], 0
    while start < rows:
        while len(sizes) > 1 and start + sizes[0] + sizes[-1] > rows:
            sizes = sizes[1:]
        spans.append(pl.ds(start, sizes[0]))
        start += sizes[0]
        sizes = sizes[1:] or sizes
    return spans


def stream_kernel(spans, rows_ref, proj_ref, feats_ref, held, proj, turned, sems):
    count, half = proj_ref.shape[0], proj.shape[1]
    firsts = [
        pltpu.make_async_copy(
            proj_ref.at[:, pl.ds(h * half, half)], proj.at[pl.ds(h * count, count)], sems.at[len(spans) + h]
        )
        for h in range(2)
    ]
    copies = [
        pltpu.make_async_copy(rows_ref.at[span], held.at[span], sems.at[c])
        for c, span in enumerate(spans)
    ]
    for copy in firsts + copies[:DEPTH]:
        copy.start()
    for copy in firsts:
        copy.wait()
    turned[...] = proj[...].T
    for c, span in enumerate(spans):
        copies[c].wait()
        if c + DEPTH < len(spans):
            copies[c + DEPTH].start()
        left = jnp.dot(held[span, :half], turned[...], preferred_element_type=jnp.float32)
        right = jnp.dot(held[span, half:], turned[...], preferred_element_type=jnp.float32)
        feats_ref[:, span] = left.T[:count] + right.T[count:]


def features(rows, proj, sizes, limit, name):
    spans = row_spans(rows.shape[0], sizes)
    return pl.pallas_call(
        functools.partial(stream_kernel, spans),
        out_shape=pltpu.VMEM((proj.shape[0], rows.shape[0]), jnp.float32),
        in_specs=[ANY_SPEC] * 2,
        out_specs=VMEM_SPEC,
        scratch_shapes=[
            pltpu.VMEM(rows.shape, jnp.bfloat16),
            pltpu.VMEM((2 * proj.shape[0], proj.shape[1] // 2), jnp.bfloat16),
            pltpu.VMEM((proj.shape[1] // 2, 2 * proj.shape[0]), jnp.bfloat16),
            pltpu.SemaphoreType.DMA((len(spans) + 2,)),
        ],
        compiler_params=pltpu.CompilerParams(vmem_limit_bytes=limit * 2**20),
        name=name,
    )(in_hbm(rows), in_hbm(proj))


def split_kernel(prior_ref, upper_ref, lower_ref, held, sems):
    chunk = held.shape[1] // sems.shape[0]
    spans = [pl.ds(c * chunk, chunk) for c in range(sems.shape[0])]
    copies = [
        pltpu.make_async_copy(prior_ref.at[:, span], held.at[:, span], sems.at[c])
        for c, span in enumerate(spans)
    ]
    for copy in copies:
        copy.start()
    for copy, span in zip(copies, spans):
        copy.wait()
        block = held[:, span]
        upper = block.astype(jnp.bfloat16)
        upper_ref[:, span] = upper
        lower_ref[:, span] = (block - upper.astype(jnp.float32)).astype(jnp.bfloat16)


def split_prior(prior):
    return pl.pallas_call(
        split_kernel,
        out_shape=(pltpu.VMEM(prior.shape, jnp.bfloat16),) * 2,
        in_specs=[ANY_SPEC],
        out_specs=(VMEM_SPEC,) * 2,
        scratch_shapes=[pltpu.VMEM(prior.shape, jnp.float32), pltpu.SemaphoreType.DMA((8,))],
        compiler_params=PARAMS,
        name="split_prior",
    )(in_hbm(prior))


def partial_kernel(size, *refs):
    blocks, (out_ref, part_ref, held) = refs[:size], refs[size:]
    me = lax.axis_index("tensor")
    tokens = blocks[0].shape[1]
    for k, block in zip(order_of(size), blocks):
        start = pl.multiple_of((me ^ k) * tokens, LANES)
        held[:, pl.ds(start, tokens)] = block[...]
    for s in range(part_ref.shape[0]):
        span = slice(s * SEQ, (s + 1) * SEQ)
        part_ref[s] = dot_nt(held[:, span], out_ref[:, span]) * (1.0 / SEQ)


def partial_vectors(blocks, out_local):
    seq_count = out_local.shape[1] // SEQ
    return pl.pallas_call(
        functools.partial(partial_kernel, len(blocks)),
        out_shape=F32((seq_count, R_IN, R_OUT)),
        in_specs=[VMEM_SPEC] * (len(blocks) + 1),
        out_specs=VMEM_SPEC,
        scratch_shapes=[pltpu.VMEM(out_local.shape, jnp.float32)],
        compiler_params=PARAMS,
        name="partial_vectors",
    )(*blocks, out_local)


def own_columns(ref, me, count):
    if count % LANES == 0:
        return ref[:, pl.ds(pl.multiple_of(me * count, LANES), count)]
    per = LANES // count
    held = ref[:, pl.ds(pl.multiple_of((me // per) * LANES, LANES), LANES)]
    return pltpu.roll(held, LANES - (me % per) * count, 1)[:, :count]


def pieces_of(values, count):
    held = []
    for _ in range(count):
        piece = values.astype(jnp.bfloat16)
        held.append(piece)
        values = values - piece.astype(jnp.float32)
    return jnp.concatenate(held, axis=0)


def dot_pieces(a, b, seqs):
    held = lax.dot_general(a, b, NT, preferred_element_type=jnp.float32)
    total = held[:seqs]
    for start in range(seqs, held.shape[0], seqs):
        total = total + held[start : start + seqs]
    return total


def apply_fisher(pieces, vectors_ref, vector_pieces, upper_ref, lower_ref, me):
    seqs = vectors_ref.shape[0]
    applied = dot_pieces(pieces, upper_ref[...], seqs)
    applied = applied + dot_pieces(pieces[: 2 * seqs], lower_ref[...], seqs)
    weights = dot_pieces(pieces, vector_pieces, seqs)
    weights = (weights[:, :seqs] + weights[:, seqs:]) * (1.0 / seqs)
    own = own_columns(vectors_ref, me, upper_ref.shape[0])
    return applied + jnp.dot(weights, own, precision=HIGHEST, preferred_element_type=jnp.float32)


def flat_index(tensor_size):
    return lax.axis_index("dp") * tensor_size + lax.axis_index("tensor")


def start_kernel(size, tensor_size, *refs):
    pieces, refs = refs[:size], refs[size:]
    upper_ref, lower_ref, vectors_ref, vector_pieces_ref, scale_ref, applied_ref, norm_ref, held = refs
    dp = lax.axis_index("dp")
    for k, piece in zip(order_of(size), pieces):
        held[dp ^ k] = piece[...]
    vectors = jnp.concatenate([held[k] for k in range(size)], axis=0)
    vectors_ref[...] = vectors
    split = pieces_of(vectors, 3)
    vector_pieces = split[: 2 * vectors.shape[0]]
    vector_pieces_ref[...] = vector_pieces
    norm = jnp.broadcast_to(row_sum(vectors * vectors), norm_ref.shape)
    norm_ref[...] = norm
    spread = jnp.sum(norm, axis=0, keepdims=True) * (1.0 / vectors.shape[0])
    scale_ref[...] = jnp.broadcast_to(1.0 / (1.0 + spread), scale_ref.shape)
    me = flat_index(tensor_size)
    applied_ref[...] = apply_fisher(split, vectors_ref, vector_pieces, upper_ref, lower_ref, me)


def start_cg(pieces, prior_pieces, tensor_size):
    size, seqs = len(pieces), len(pieces) * pieces[0].shape[0]
    rows, width = prior_pieces[0].shape
    vector_pieces = jax.ShapeDtypeStruct((2 * seqs, width), jnp.bfloat16)
    column = F32((seqs, LANES))
    return pl.pallas_call(
        functools.partial(start_kernel, size, tensor_size),
        out_shape=(F32((seqs, width)), vector_pieces, column, F32((seqs, rows)), column),
        in_specs=[VMEM_SPEC] * (size + 2),
        out_specs=(VMEM_SPEC,) * 5,
        scratch_shapes=[pltpu.VMEM((size,) + pieces[0].shape, jnp.float32)],
        compiler_params=PARAMS,
        name="cg_start",
    )(*pieces, *prior_pieces)


def step_kernel(tensor_size, first, last, *refs):
    blocks_ref, upper_ref, lower_ref, vectors_ref, vector_pieces_ref, scale_ref = refs[:6]
    norm_ref, fisher_direction_ref = refs[6:8]
    refs = refs[8:]
    if not first:
        fisher_residual_ref, direction_ref, residual_ref, solution_ref = refs[:4]
        refs = refs[4:]
    if last:
        queries_ref, curvature_out, norm_out, solved_out, along_out, held = refs
    else:
        fisher_direction_out, norm_out, fisher_residual_out, direction_out, residual_out, solution_out, held = refs
    me = flat_index(tensor_size)
    count, _, rows = blocks_ref.shape
    for i in range(count):
        held[:, i * rows : (i + 1) * rows] = blocks_ref[i]
    applied = held[...]
    scale = scale_ref[...][:, :1]
    twice = apply_fisher(
        pieces_of(scale * applied, 3), vectors_ref, vector_pieces_ref[...], upper_ref, lower_ref, me
    )
    direction = vectors_ref[...] if first else direction_ref[...]
    residual = direction if first else residual_ref[...]
    norm = norm_ref[...][:, :1]
    step = norm / row_sum(direction * applied)
    solution = step * direction
    if not first:
        solution = solution_ref[...] + solution
    residual = residual - step * applied
    norm_next = row_sum(residual * residual)
    share = norm_next / norm
    direction = residual + share * direction
    fisher_direction = fisher_direction_ref[...]
    fisher_residual = (fisher_direction if first else fisher_residual_ref[...]) - (step / scale) * twice
    fisher_direction = fisher_residual + share * fisher_direction
    norm_out[...] = jnp.broadcast_to(norm_next, norm_out.shape)
    if last:
        held[...] = direction
        own = own_columns(held, me, rows)
        curvature_out[...] = jnp.broadcast_to(row_sum(own * fisher_direction), curvature_out.shape)
        seqs = direction.shape[0]
        solved = jnp.concatenate([solution, direction], axis=0)
        scores = dot_pieces(pieces_of(solved, 3), queries_ref[...], 2 * seqs)
        solved_out[...] = scores[:seqs]
        along_out[...] = scores[seqs:]
    else:
        fisher_direction_out[...] = fisher_direction
        fisher_residual_out[...] = fisher_residual
        residual_out[...] = residual
        direction_out[...] = direction
        solution_out[...] = solution


def step_cg(blocks, fixed, norm, state, queries, tensor_size):
    first, last = len(state) == 1, queries is not None
    whole, rows = F32(fixed[2].shape), F32(state[0].shape)
    column = F32(norm.shape)
    operands = [blocks, *fixed, norm, *state]
    out_shape = (rows, column, rows, whole, whole, whole)
    if last:
        operands.append(queries)
        scores = F32((whole.shape[0], queries.shape[0]))
        out_shape = (column, column, scores, scores)
    return pl.pallas_call(
        functools.partial(step_kernel, tensor_size, first, last),
        out_shape=out_shape,
        in_specs=[VMEM_SPEC] * len(operands),
        out_specs=(VMEM_SPEC,) * len(out_shape),
        scratch_shapes=[pltpu.VMEM(whole.shape, jnp.float32)],
        compiler_params=PARAMS,
        name="cg_step",
    )(*operands)


def on_device(dp_size, tensor_size, inputs, in_proj, out_grads, out_proj, prior, queries):
    width = R_IN * R_OUT
    both, devices = ("dp", "tensor"), dp_size * tensor_size
    in_blocks = direct(features(inputs, in_proj, (128,), 20, "in_features"), "tensor", tensor_size)
    out_local = features(out_grads, out_proj, (128, 128) + (256,) * 6 + (128,), 44, "out_features")
    partial = partial_vectors(in_blocks, out_local).reshape(-1, width)
    first, *rest = bits(tensor_size)
    prior, partial = lax.optimization_barrier((prior, partial))
    partial = partial + swap(partial, "tensor", tensor_size, first)
    partial, prior_pieces = lax.optimization_barrier((partial, split_prior(prior)))
    for bit in rest:
        partial = partial + swap(partial, "tensor", tensor_size, bit)
    pieces = direct(partial, "dp", dp_size)
    prior_pieces = [in_vmem(piece) for piece in prior_pieces]
    vectors, vector_pieces, scale, applied_rows, norm = start_cg(pieces, prior_pieces, tensor_size)
    fixed = (*prior_pieces, vectors, vector_pieces, scale)
    state = [applied_rows]
    for iteration in range(1, ITERS - 1):
        blocks = gather(state[0], both, devices)
        applied_rows, norm, *others = step_cg(blocks, fixed, norm, state, None, tensor_size)
        state = [applied_rows, *others]
    blocks = gather(state[0], both, devices)
    curvature, norm, solved, along = step_cg(blocks, fixed, norm, state, queries, tensor_size)
    curvature = jnp.sum(gather(curvature, both, devices), axis=0)
    return solved + (norm / curvature)[:, :1] * along


def solution(mesh):
    return jax.shard_map(
        functools.partial(on_device, mesh.shape["dp"], mesh.shape["tensor"]),
        mesh=mesh,
        in_specs=(
            P(("groups", "dp", "tensor"), None),
            P(),
            P(("groups", "dp"), "tensor"),
            P(None, "tensor"),
            P(("groups", "dp", "tensor"), None),
            P(("groups", "dp", "tensor"), None),
        ),
        out_specs=P("groups", ("dp", "tensor")),
        check_vma=False,
    )
```

```python
import functools

import jax
import jax.numpy as jnp
from jax import lax
from jax.experimental import pallas as pl
from jax.experimental.pallas import tpu as pltpu
from jax.sharding import PartitionSpec as P

R_IN = 64
R_OUT = 64
SEQ = 1024
ITERS = 4
LANES = 128
NT = (((1,), (1,)), ((), ()))
HIGHEST = lax.Precision.HIGHEST
ANY_SPEC = pl.BlockSpec(memory_space=pl.ANY)
VMEM_SPEC = pl.BlockSpec(memory_space=pltpu.VMEM)
PARAMS = pltpu.CompilerParams(vmem_limit_bytes=16 * 2**20)
F32 = functools.partial(jax.ShapeDtypeStruct, dtype=jnp.float32)


def swap(value, axis, size, bit):
    return lax.ppermute(value, axis, [(i, i ^ bit) for i in range(size)])


def bits(size):
    return [1 << b for b in reversed(range(size.bit_length() - 1))]


def gather(value, axes, size):
    return lax.all_to_all(jnp.broadcast_to(value[None], (size,) + value.shape), axes, 0, 0)


def order_of(size):
    return (0, 2, 3, 1) if size == 4 else tuple(range(size))


def direct(value, axis, size, order):
    return [value] + [swap(value, axis, size, k) for k in order[1:]]


def in_hbm(value):
    return pltpu.with_memory_space_constraint(value, pltpu.HBM)


def in_vmem(value):
    return pltpu.with_memory_space_constraint(value, pltpu.VMEM)


def dot_nt(a, b):
    return lax.dot_general(a, b, NT, precision=HIGHEST, preferred_element_type=jnp.float32)


def row_sum(values):
    return jnp.sum(values, axis=1, keepdims=True)


def stream_kernel(block, rows_ref, proj_ref, feats_ref, held, proj, turned, sems):
    count, half = proj_ref.shape[0], proj.shape[1]
    steps = held.shape[0] // block
    firsts = [
        pltpu.make_async_copy(
            proj_ref.at[:, pl.ds(h * half, half)], proj.at[pl.ds(h * count, count)], sems.at[steps + h]
        )
        for h in range(2)
    ]

    def fetch(step):
        span = pl.ds(pl.multiple_of(step * block, block), block)
        return pltpu.make_async_copy(rows_ref.at[span], held.at[span], sems.at[step])

    for copy in firsts:
        copy.start()
    for step in range(steps):
        fetch(step).start()
    for copy in firsts:
        copy.wait()
    turned[...] = proj[...].T

    @pl.loop(0, steps)
    def _(step):
        fetch(step).wait()
        span = pl.ds(pl.multiple_of(step * block, block), block)
        left = jnp.dot(held[span, :half], turned[...], preferred_element_type=jnp.float32)
        right = jnp.dot(held[span, half:], turned[...], preferred_element_type=jnp.float32)
        feats_ref[:, span] = left.T[:count] + right.T[count:]


def features(rows, proj, block, limit, name):
    count, width = proj.shape
    return pl.pallas_call(
        functools.partial(stream_kernel, block),
        out_shape=pltpu.VMEM((count, rows.shape[0]), jnp.float32),
        in_specs=[ANY_SPEC] * 2,
        out_specs=VMEM_SPEC,
        scratch_shapes=[
            pltpu.VMEM(rows.shape, jnp.bfloat16),
            pltpu.VMEM((2 * count, width // 2), jnp.bfloat16),
            pltpu.VMEM((width // 2, 2 * count), jnp.bfloat16),
            pltpu.SemaphoreType.DMA((rows.shape[0] // block + 2,)),
        ],
        compiler_params=pltpu.CompilerParams(vmem_limit_bytes=limit * 2**20),
        name=name,
    )(in_hbm(rows), in_hbm(proj))


def split_kernel(prior_ref, upper_ref, lower_ref, held, sems):
    chunk = held.shape[1] // sems.shape[0]
    spans = [pl.ds(c * chunk, chunk) for c in range(sems.shape[0])]
    copies = [
        pltpu.make_async_copy(prior_ref.at[:, span], held.at[:, span], sems.at[c])
        for c, span in enumerate(spans)
    ]
    for copy in copies:
        copy.start()
    for copy, span in zip(copies, spans):
        copy.wait()
        block = held[:, span]
        upper = block.astype(jnp.bfloat16)
        upper_ref[:, span] = upper
        lower_ref[:, span] = (block - upper.astype(jnp.float32)).astype(jnp.bfloat16)


def split_prior(prior):
    return pl.pallas_call(
        split_kernel,
        out_shape=(pltpu.VMEM(prior.shape, jnp.bfloat16),) * 2,
        in_specs=[ANY_SPEC],
        out_specs=(VMEM_SPEC,) * 2,
        scratch_shapes=[pltpu.VMEM(prior.shape, jnp.float32), pltpu.SemaphoreType.DMA((8,))],
        compiler_params=PARAMS,
        name="split_prior",
    )(in_hbm(prior))


def partial_kernel(size, *refs):
    blocks, (out_ref, part_ref, held) = refs[:size], refs[size:]
    me = lax.axis_index("tensor")
    tokens = blocks[0].shape[1]
    for k, block in zip(order_of(size), blocks):
        start = pl.multiple_of((me ^ k) * tokens, LANES)
        held[:, pl.ds(start, tokens)] = block[...]
    for s in range(part_ref.shape[0]):
        span = slice(s * SEQ, (s + 1) * SEQ)
        part_ref[s] = dot_nt(held[:, span], out_ref[:, span]) * (1.0 / SEQ)


def partial_vectors(blocks, out_local):
    seq_count = out_local.shape[1] // SEQ
    return pl.pallas_call(
        functools.partial(partial_kernel, len(blocks)),
        out_shape=F32((seq_count, R_IN, R_OUT)),
        in_specs=[VMEM_SPEC] * (len(blocks) + 1),
        out_specs=VMEM_SPEC,
        scratch_shapes=[pltpu.VMEM(out_local.shape, jnp.float32)],
        compiler_params=PARAMS,
        name="partial_vectors",
    )(*blocks, out_local)


def own_columns(ref, me, count):
    if count % LANES == 0:
        return ref[:, pl.ds(pl.multiple_of(me * count, LANES), count)]
    per = LANES // count
    held = ref[:, pl.ds(pl.multiple_of((me // per) * LANES, LANES), LANES)]
    return pltpu.roll(held, LANES - (me % per) * count, 1)[:, :count]


def pieces_of(values, count):
    held = []
    for _ in range(count):
        piece = values.astype(jnp.bfloat16)
        held.append(piece)
        values = values - piece.astype(jnp.float32)
    return jnp.concatenate(held, axis=0)


def dot_pieces(a, b, seqs):
    held = lax.dot_general(a, b, NT, preferred_element_type=jnp.float32)
    total = held[:seqs]
    for start in range(seqs, held.shape[0], seqs):
        total = total + held[start : start + seqs]
    return total


def apply_fisher(pieces, vectors_ref, vector_pieces, upper_ref, lower_ref, me):
    seqs = vectors_ref.shape[0]
    applied = dot_pieces(pieces, upper_ref[...], seqs)
    applied = applied + dot_pieces(pieces[: 2 * seqs], lower_ref[...], seqs)
    weights = dot_pieces(pieces, vector_pieces, seqs)
    weights = (weights[:, :seqs] + weights[:, seqs:]) * (1.0 / seqs)
    own = own_columns(vectors_ref, me, upper_ref.shape[0])
    return applied + jnp.dot(weights, own, precision=HIGHEST, preferred_element_type=jnp.float32)


def flat_index(tensor_size):
    return lax.axis_index("dp") * tensor_size + lax.axis_index("tensor")


def start_kernel(size, tensor_size, *refs):
    pieces, refs = refs[:size], refs[size:]
    upper_ref, lower_ref, vectors_ref, vector_pieces_ref, scale_ref, applied_ref, norm_ref, held = refs
    dp = lax.axis_index("dp")
    for k, piece in enumerate(pieces):
        held[dp ^ k] = piece[...]
    vectors = jnp.concatenate([held[k] for k in range(size)], axis=0)
    vectors_ref[...] = vectors
    split = pieces_of(vectors, 3)
    vector_pieces = split[: 2 * vectors.shape[0]]
    vector_pieces_ref[...] = vector_pieces
    norm = jnp.broadcast_to(row_sum(vectors * vectors), norm_ref.shape)
    norm_ref[...] = norm
    spread = jnp.sum(norm, axis=0, keepdims=True) * (1.0 / vectors.shape[0])
    scale_ref[...] = jnp.broadcast_to(1.0 / (1.0 + spread), scale_ref.shape)
    me = flat_index(tensor_size)
    applied_ref[...] = apply_fisher(split, vectors_ref, vector_pieces, upper_ref, lower_ref, me)


def start_cg(pieces, prior_pieces, tensor_size):
    size, seqs = len(pieces), len(pieces) * pieces[0].shape[0]
    rows, width = prior_pieces[0].shape
    vector_pieces = jax.ShapeDtypeStruct((2 * seqs, width), jnp.bfloat16)
    column = F32((seqs, LANES))
    return pl.pallas_call(
        functools.partial(start_kernel, size, tensor_size),
        out_shape=(F32((seqs, width)), vector_pieces, column, F32((seqs, rows)), column),
        in_specs=[VMEM_SPEC] * (size + 2),
        out_specs=(VMEM_SPEC,) * 5,
        scratch_shapes=[pltpu.VMEM((size,) + pieces[0].shape, jnp.float32)],
        compiler_params=PARAMS,
        name="cg_start",
    )(*pieces, *prior_pieces)


def step_kernel(tensor_size, first, last, *refs):
    blocks_ref, upper_ref, lower_ref, vectors_ref, vector_pieces_ref, scale_ref = refs[:6]
    norm_ref, fisher_direction_ref = refs[6:8]
    refs = refs[8:]
    if not first:
        fisher_residual_ref, direction_ref, residual_ref, solution_ref = refs[:4]
        refs = refs[4:]
    if last:
        queries_ref, curvature_out, norm_out, solved_out, along_out, held = refs
    else:
        fisher_direction_out, norm_out, fisher_residual_out, direction_out, residual_out, solution_out, held = refs
    me = flat_index(tensor_size)
    count, _, rows = blocks_ref.shape
    for i in range(count):
        held[:, i * rows : (i + 1) * rows] = blocks_ref[i]
    applied = held[...]
    scale = scale_ref[...][:, :1]
    twice = apply_fisher(
        pieces_of(scale * applied, 3), vectors_ref, vector_pieces_ref[...], upper_ref, lower_ref, me
    )
    direction = vectors_ref[...] if first else direction_ref[...]
    residual = direction if first else residual_ref[...]
    norm = norm_ref[...][:, :1]
    step = norm / row_sum(direction * applied)
    solution = step * direction
    if not first:
        solution = solution_ref[...] + solution
    residual = residual - step * applied
    norm_next = row_sum(residual * residual)
    share = norm_next / norm
    direction = residual + share * direction
    fisher_direction = fisher_direction_ref[...]
    fisher_residual = (fisher_direction if first else fisher_residual_ref[...]) - (step / scale) * twice
    fisher_direction = fisher_residual + share * fisher_direction
    norm_out[...] = jnp.broadcast_to(norm_next, norm_out.shape)
    if last:
        held[...] = direction
        own = own_columns(held, me, rows)
        curvature_out[...] = jnp.broadcast_to(row_sum(own * fisher_direction), curvature_out.shape)
        seqs = direction.shape[0]
        solved = jnp.concatenate([solution, direction], axis=0)
        scores = dot_pieces(pieces_of(solved, 3), queries_ref[...], 2 * seqs)
        solved_out[...] = scores[:seqs]
        along_out[...] = scores[seqs:]
    else:
        fisher_direction_out[...] = fisher_direction
        fisher_residual_out[...] = fisher_residual
        residual_out[...] = residual
        direction_out[...] = direction
        solution_out[...] = solution


def step_cg(blocks, fixed, norm, state, queries, tensor_size):
    first, last = len(state) == 1, queries is not None
    whole, rows = F32(fixed[2].shape), F32(state[0].shape)
    column = F32(norm.shape)
    operands = [blocks, *fixed, norm, *state]
    out_shape = (rows, column, rows, whole, whole, whole)
    if last:
        operands.append(queries)
        scores = F32((whole.shape[0], queries.shape[0]))
        out_shape = (column, column, scores, scores)
    return pl.pallas_call(
        functools.partial(step_kernel, tensor_size, first, last),
        out_shape=out_shape,
        in_specs=[VMEM_SPEC] * len(operands),
        out_specs=(VMEM_SPEC,) * len(out_shape),
        scratch_shapes=[pltpu.VMEM(whole.shape, jnp.float32)],
        compiler_params=PARAMS,
        name="cg_step",
    )(*operands)


def on_device(dp_size, tensor_size, inputs, in_proj, out_grads, out_proj, prior, queries):
    width = R_IN * R_OUT
    both, devices = ("dp", "tensor"), dp_size * tensor_size
    in_blocks = direct(features(inputs, in_proj, LANES, 20, "in_features"), "tensor", tensor_size, order_of(tensor_size))
    out_local = features(out_grads, out_proj, 2 * LANES, 44, "out_features")
    partial = partial_vectors(in_blocks, out_local).reshape(-1, width)
    first, *rest = bits(tensor_size)
    prior, partial = lax.optimization_barrier((prior, partial))
    partial = partial + swap(partial, "tensor", tensor_size, first)
    partial, prior_pieces = lax.optimization_barrier((partial, split_prior(prior)))
    for bit in rest:
        partial = partial + swap(partial, "tensor", tensor_size, bit)
    pieces = direct(partial, "dp", dp_size, range(dp_size))
    prior_pieces = [in_vmem(piece) for piece in prior_pieces]
    vectors, vector_pieces, scale, applied_rows, norm = start_cg(pieces, prior_pieces, tensor_size)
    fixed = (*prior_pieces, vectors, vector_pieces, scale)
    state = [applied_rows]
    for iteration in range(1, ITERS - 1):
        blocks = gather(state[0], both, devices)
        applied_rows, norm, *others = step_cg(blocks, fixed, norm, state, None, tensor_size)
        state = [applied_rows, *others]
    blocks = gather(state[0], both, devices)
    curvature, norm, solved, along = step_cg(blocks, fixed, norm, state, queries, tensor_size)
    curvature = jnp.sum(gather(curvature, both, devices), axis=0)
    return solved + (norm / curvature)[:, :1] * along


def solution(mesh):
    return jax.shard_map(
        functools.partial(on_device, mesh.shape["dp"], mesh.shape["tensor"]),
        mesh=mesh,
        in_specs=(
            P(("groups", "dp", "tensor"), None),
            P(),
            P(("groups", "dp"), "tensor"),
            P(None, "tensor"),
            P(("groups", "dp", "tensor"), None),
            P(("groups", "dp", "tensor"), None),
        ),
        out_specs=P("groups", ("dp", "tensor")),
        check_vma=False,
    )
```

```python
import functools

import jax
import jax.numpy as jnp
from jax import lax
from jax.experimental import pallas as pl
from jax.experimental.pallas import tpu as pltpu
from jax.sharding import PartitionSpec as P

R_IN = 64
R_OUT = 64
SEQ = 1024
ITERS = 4
LANES = 128
NT = (((1,), (1,)), ((), ()))
HIGHEST = lax.Precision.HIGHEST
ANY_SPEC = pl.BlockSpec(memory_space=pl.ANY)
VMEM_SPEC = pl.BlockSpec(memory_space=pltpu.VMEM)
PARAMS = pltpu.CompilerParams(vmem_limit_bytes=16 * 2**20)
F32 = functools.partial(jax.ShapeDtypeStruct, dtype=jnp.float32)


def swap(value, axis, size, bit):
    return lax.ppermute(value, axis, [(i, i ^ bit) for i in range(size)])


def bits(size):
    return [1 << b for b in reversed(range(size.bit_length() - 1))]


def group_order(sizes):
    dp_size, tensor_size = sizes
    first = min(1, dp_size - 1) * tensor_size + (tensor_size - 1) // 2
    return [first] + [i for i in range(dp_size * tensor_size) if i != first]


def gather(value, sizes):
    order = group_order(sizes)
    value = jnp.broadcast_to(value[None], (len(order),) + value.shape)
    return lax.all_to_all(value, ("dp", "tensor"), 0, 0, axis_index_groups=[order])


def order_of(size):
    return (0, 2, 3, 1) if size == 4 else tuple(range(size))


def direct(value, axis, size, order):
    return [value] + [swap(value, axis, size, k) for k in order[1:]]


def in_hbm(value):
    return pltpu.with_memory_space_constraint(value, pltpu.HBM)


def in_vmem(value):
    return pltpu.with_memory_space_constraint(value, pltpu.VMEM)


def dot_nt(a, b):
    return lax.dot_general(a, b, NT, precision=HIGHEST, preferred_element_type=jnp.float32)


def row_sum(values):
    return jnp.sum(values, axis=1, keepdims=True)


def stream_kernel(block, rows_ref, proj_ref, feats_ref, held, proj, turned, sems):
    count, half = proj_ref.shape[0], proj.shape[1]
    steps = held.shape[0] // block
    firsts = [
        pltpu.make_async_copy(
            proj_ref.at[:, pl.ds(h * half, half)], proj.at[pl.ds(h * count, count)], sems.at[steps + h]
        )
        for h in range(2)
    ]

    def fetch(step):
        span = pl.ds(pl.multiple_of(step * block, block), block)
        return pltpu.make_async_copy(rows_ref.at[span], held.at[span], sems.at[step])

    for copy in firsts:
        copy.start()
    for step in range(steps):
        fetch(step).start()
    for copy in firsts:
        copy.wait()
    turned[...] = proj[...].T

    @pl.loop(0, steps)
    def _(step):
        fetch(step).wait()
        span = pl.ds(pl.multiple_of(step * block, block), block)
        left = jnp.dot(held[span, :half], turned[...], preferred_element_type=jnp.float32)
        right = jnp.dot(held[span, half:], turned[...], preferred_element_type=jnp.float32)
        feats_ref[:, span] = left.T[:count] + right.T[count:]


def features(rows, proj, block, limit, name):
    count, width = proj.shape
    return pl.pallas_call(
        functools.partial(stream_kernel, block),
        out_shape=pltpu.VMEM((count, rows.shape[0]), jnp.float32),
        in_specs=[ANY_SPEC] * 2,
        out_specs=VMEM_SPEC,
        scratch_shapes=[
            pltpu.VMEM(rows.shape, jnp.bfloat16),
            pltpu.VMEM((2 * count, width // 2), jnp.bfloat16),
            pltpu.VMEM((width // 2, 2 * count), jnp.bfloat16),
            pltpu.SemaphoreType.DMA((rows.shape[0] // block + 2,)),
        ],
        compiler_params=pltpu.CompilerParams(vmem_limit_bytes=limit * 2**20),
        name=name,
    )(in_hbm(rows), in_hbm(proj))


def split_kernel(prior_ref, upper_ref, lower_ref, held, sems):
    chunk = held.shape[1] // sems.shape[0]
    spans = [pl.ds(c * chunk, chunk) for c in range(sems.shape[0])]
    copies = [
        pltpu.make_async_copy(prior_ref.at[:, span], held.at[:, span], sems.at[c])
        for c, span in enumerate(spans)
    ]
    for copy in copies:
        copy.start()
    for copy, span in zip(copies, spans):
        copy.wait()
        block = held[:, span]
        upper = block.astype(jnp.bfloat16)
        upper_ref[:, span] = upper
        lower_ref[:, span] = (block - upper.astype(jnp.float32)).astype(jnp.bfloat16)


def split_prior(prior):
    return pl.pallas_call(
        split_kernel,
        out_shape=(pltpu.VMEM(prior.shape, jnp.bfloat16),) * 2,
        in_specs=[ANY_SPEC],
        out_specs=(VMEM_SPEC,) * 2,
        scratch_shapes=[pltpu.VMEM(prior.shape, jnp.float32), pltpu.SemaphoreType.DMA((8,))],
        compiler_params=PARAMS,
        name="split_prior",
    )(in_hbm(prior))


def partial_kernel(size, *refs):
    blocks, (out_ref, part_ref, held) = refs[:size], refs[size:]
    me = lax.axis_index("tensor")
    tokens = blocks[0].shape[1]
    for k, block in zip(order_of(size), blocks):
        start = pl.multiple_of((me ^ k) * tokens, LANES)
        held[:, pl.ds(start, tokens)] = block[...]
    for s in range(part_ref.shape[0]):
        span = slice(s * SEQ, (s + 1) * SEQ)
        part_ref[s] = dot_nt(held[:, span], out_ref[:, span]) * (1.0 / SEQ)


def partial_vectors(blocks, out_local):
    seq_count = out_local.shape[1] // SEQ
    return pl.pallas_call(
        functools.partial(partial_kernel, len(blocks)),
        out_shape=F32((seq_count, R_IN, R_OUT)),
        in_specs=[VMEM_SPEC] * (len(blocks) + 1),
        out_specs=VMEM_SPEC,
        scratch_shapes=[pltpu.VMEM(out_local.shape, jnp.float32)],
        compiler_params=PARAMS,
        name="partial_vectors",
    )(*blocks, out_local)


def own_columns(ref, me, count):
    if count % LANES == 0:
        return ref[:, pl.ds(pl.multiple_of(me * count, LANES), count)]
    per = LANES // count
    held = ref[:, pl.ds(pl.multiple_of((me // per) * LANES, LANES), LANES)]
    return pltpu.roll(held, LANES - (me % per) * count, 1)[:, :count]


def pieces_of(values, count):
    held = []
    for _ in range(count):
        piece = values.astype(jnp.bfloat16)
        held.append(piece)
        values = values - piece.astype(jnp.float32)
    return jnp.concatenate(held, axis=0)


def dot_pieces(a, b, seqs):
    held = lax.dot_general(a, b, NT, preferred_element_type=jnp.float32)
    total = held[:seqs]
    for start in range(seqs, held.shape[0], seqs):
        total = total + held[start : start + seqs]
    return total


def apply_fisher(pieces, vectors_ref, vector_pieces, upper_ref, lower_ref, me):
    seqs = vectors_ref.shape[0]
    applied = dot_pieces(pieces, upper_ref[...], seqs)
    applied = applied + dot_pieces(pieces[: 2 * seqs], lower_ref[...], seqs)
    weights = dot_pieces(pieces, vector_pieces, seqs)
    weights = (weights[:, :seqs] + weights[:, seqs:]) * (1.0 / seqs)
    own = own_columns(vectors_ref, me, upper_ref.shape[0])
    return applied + jnp.dot(weights, own, precision=HIGHEST, preferred_element_type=jnp.float32)


def flat_index(tensor_size):
    return lax.axis_index("dp") * tensor_size + lax.axis_index("tensor")


def start_kernel(size, tensor_size, *refs):
    pieces, refs = refs[:size], refs[size:]
    upper_ref, lower_ref, vectors_ref, vector_pieces_ref, scale_ref, applied_ref, norm_ref, held = refs
    dp = lax.axis_index("dp")
    for k, piece in enumerate(pieces):
        held[dp ^ k] = piece[...]
    vectors = jnp.concatenate([held[k] for k in range(size)], axis=0)
    vectors_ref[...] = vectors
    split = pieces_of(vectors, 3)
    vector_pieces = split[: 2 * vectors.shape[0]]
    vector_pieces_ref[...] = vector_pieces
    norm = jnp.broadcast_to(row_sum(vectors * vectors), norm_ref.shape)
    norm_ref[...] = norm
    spread = jnp.sum(norm, axis=0, keepdims=True) * (1.0 / vectors.shape[0])
    scale_ref[...] = jnp.broadcast_to(1.0 / (1.0 + spread), scale_ref.shape)
    me = flat_index(tensor_size)
    applied_ref[...] = apply_fisher(split, vectors_ref, vector_pieces, upper_ref, lower_ref, me)


def start_cg(pieces, prior_pieces, tensor_size):
    size, seqs = len(pieces), len(pieces) * pieces[0].shape[0]
    rows, width = prior_pieces[0].shape
    vector_pieces = jax.ShapeDtypeStruct((2 * seqs, width), jnp.bfloat16)
    column = F32((seqs, LANES))
    return pl.pallas_call(
        functools.partial(start_kernel, size, tensor_size),
        out_shape=(F32((seqs, width)), vector_pieces, column, F32((seqs, rows)), column),
        in_specs=[VMEM_SPEC] * (size + 2),
        out_specs=(VMEM_SPEC,) * 5,
        scratch_shapes=[pltpu.VMEM((size,) + pieces[0].shape, jnp.float32)],
        compiler_params=PARAMS,
        name="cg_start",
    )(*pieces, *prior_pieces)


def step_kernel(sizes, first, last, *refs):
    blocks_ref, upper_ref, lower_ref, vectors_ref, vector_pieces_ref, scale_ref = refs[:6]
    norm_ref, fisher_direction_ref = refs[6:8]
    refs = refs[8:]
    if not first:
        fisher_residual_ref, direction_ref, residual_ref, solution_ref = refs[:4]
        refs = refs[4:]
    if last:
        queries_ref, curvature_out, norm_out, solved_out, along_out, held = refs
    else:
        fisher_direction_out, norm_out, fisher_residual_out, direction_out, residual_out, solution_out, held = refs
    me = flat_index(sizes[1])
    rows = blocks_ref.shape[2]
    for i, k in enumerate(group_order(sizes)):
        held[:, k * rows : (k + 1) * rows] = blocks_ref[i]
    applied = held[...]
    scale = scale_ref[...][:, :1]
    twice = apply_fisher(
        pieces_of(scale * applied, 3), vectors_ref, vector_pieces_ref[...], upper_ref, lower_ref, me
    )
    direction = vectors_ref[...] if first else direction_ref[...]
    residual = direction if first else residual_ref[...]
    norm = norm_ref[...][:, :1]
    step = norm / row_sum(direction * applied)
    solution = step * direction
    if not first:
        solution = solution_ref[...] + solution
    residual = residual - step * applied
    norm_next = row_sum(residual * residual)
    share = norm_next / norm
    direction = residual + share * direction
    fisher_direction = fisher_direction_ref[...]
    fisher_residual = (fisher_direction if first else fisher_residual_ref[...]) - (step / scale) * twice
    fisher_direction = fisher_residual + share * fisher_direction
    norm_out[...] = jnp.broadcast_to(norm_next, norm_out.shape)
    if last:
        held[...] = direction
        own = own_columns(held, me, rows)
        curvature_out[...] = jnp.broadcast_to(row_sum(own * fisher_direction), curvature_out.shape)
        seqs = direction.shape[0]
        solved = jnp.concatenate([solution, direction], axis=0)
        scores = dot_pieces(pieces_of(solved, 3), queries_ref[...], 2 * seqs)
        solved_out[...] = scores[:seqs]
        along_out[...] = scores[seqs:]
    else:
        fisher_direction_out[...] = fisher_direction
        fisher_residual_out[...] = fisher_residual
        residual_out[...] = residual
        direction_out[...] = direction
        solution_out[...] = solution


def step_cg(blocks, fixed, norm, state, queries, sizes):
    first, last = len(state) == 1, queries is not None
    whole, rows = F32(fixed[2].shape), F32(state[0].shape)
    column = F32(norm.shape)
    operands = [blocks, *fixed, norm, *state]
    out_shape = (rows, column, rows, whole, whole, whole)
    if last:
        operands.append(queries)
        scores = F32((whole.shape[0], queries.shape[0]))
        out_shape = (column, column, scores, scores)
    return pl.pallas_call(
        functools.partial(step_kernel, sizes, first, last),
        out_shape=out_shape,
        in_specs=[VMEM_SPEC] * len(operands),
        out_specs=(VMEM_SPEC,) * len(out_shape),
        scratch_shapes=[pltpu.VMEM(whole.shape, jnp.float32)],
        compiler_params=PARAMS,
        name="cg_step",
    )(*operands)


def on_device(dp_size, tensor_size, inputs, in_proj, out_grads, out_proj, prior, queries):
    width = R_IN * R_OUT
    sizes = dp_size, tensor_size
    in_blocks = direct(features(inputs, in_proj, LANES, 20, "in_features"), "tensor", tensor_size, order_of(tensor_size))
    out_local = features(out_grads, out_proj, 2 * LANES, 44, "out_features")
    partial = partial_vectors(in_blocks, out_local).reshape(-1, width)
    first, *rest = bits(tensor_size)
    prior, partial = lax.optimization_barrier((prior, partial))
    partial = partial + swap(partial, "tensor", tensor_size, first)
    partial, prior_pieces = lax.optimization_barrier((partial, split_prior(prior)))
    for bit in rest:
        partial = partial + swap(partial, "tensor", tensor_size, bit)
    pieces = direct(partial, "dp", dp_size, range(dp_size))
    prior_pieces = [in_vmem(piece) for piece in prior_pieces]
    vectors, vector_pieces, scale, applied_rows, norm = start_cg(pieces, prior_pieces, tensor_size)
    fixed = (*prior_pieces, vectors, vector_pieces, scale)
    state = [applied_rows]
    for iteration in range(1, ITERS - 1):
        blocks = gather(state[0], sizes)
        applied_rows, norm, *others = step_cg(blocks, fixed, norm, state, None, sizes)
        state = [applied_rows, *others]
    blocks = gather(state[0], sizes)
    curvature, norm, solved, along = step_cg(blocks, fixed, norm, state, queries, sizes)
    curvature = jnp.sum(gather(curvature, sizes), axis=0)
    return solved + (norm / curvature)[:, :1] * along


def solution(mesh):
    return jax.shard_map(
        functools.partial(on_device, mesh.shape["dp"], mesh.shape["tensor"]),
        mesh=mesh,
        in_specs=(
            P(("groups", "dp", "tensor"), None),
            P(),
            P(("groups", "dp"), "tensor"),
            P(None, "tensor"),
            P(("groups", "dp", "tensor"), None),
            P(("groups", "dp", "tensor"), None),
        ),
        out_specs=P("groups", ("dp", "tensor")),
        check_vma=False,
    )
```

```python
import functools

import jax
import jax.numpy as jnp
from jax import lax
from jax.experimental import pallas as pl
from jax.experimental.pallas import tpu as pltpu
from jax.sharding import PartitionSpec as P

R_IN = 64
R_OUT = 64
SEQ = 1024
ITERS = 4
LANES = 128
NT = (((1,), (1,)), ((), ()))
HIGHEST = lax.Precision.HIGHEST
ANY_SPEC = pl.BlockSpec(memory_space=pl.ANY)
VMEM_SPEC = pl.BlockSpec(memory_space=pltpu.VMEM)
PARAMS = pltpu.CompilerParams(vmem_limit_bytes=16 * 2**20)
F32 = functools.partial(jax.ShapeDtypeStruct, dtype=jnp.float32)


def swap(value, axis, size, bit):
    return lax.ppermute(value, axis, [(i, i ^ bit) for i in range(size)])


def bits(size):
    return [1 << b for b in reversed(range(size.bit_length() - 1))]


def group_order(sizes):
    dp_size, tensor_size = sizes
    order = [min(1, dp_size - 1) * tensor_size + (tensor_size - 1) // 2]
    for t in range((tensor_size + 1) // 2):
        for dp in range(dp_size):
            across = (dp + dp_size // 2) % dp_size
            order += [dp * tensor_size + tensor_size - 1 - t, across * tensor_size + t]
    return list(dict.fromkeys(order))


def gather(value, axes, order):
    value = jnp.broadcast_to(value[None], (len(order),) + value.shape)
    return lax.all_to_all(value, axes, 0, 0, axis_index_groups=[order])


def order_of(size):
    return (0, 2, 3, 1) if size == 4 else tuple(range(size))


def direct(value, axis, size, order):
    return [value] + [swap(value, axis, size, k) for k in order[1:]]


def in_hbm(value):
    return pltpu.with_memory_space_constraint(value, pltpu.HBM)


def in_vmem(value):
    return pltpu.with_memory_space_constraint(value, pltpu.VMEM)


def dot_nt(a, b):
    return lax.dot_general(a, b, NT, precision=HIGHEST, preferred_element_type=jnp.float32)


def row_sum(values):
    return jnp.sum(values, axis=1, keepdims=True)


def stream_kernel(block, rows_ref, proj_ref, feats_ref, held, proj, turned, sems):
    count, half = proj_ref.shape[0], proj.shape[1]
    steps = held.shape[0] // block
    firsts = [
        pltpu.make_async_copy(
            proj_ref.at[:, pl.ds(h * half, half)], proj.at[pl.ds(h * count, count)], sems.at[steps + h]
        )
        for h in range(2)
    ]

    def fetch(step):
        span = pl.ds(pl.multiple_of(step * block, block), block)
        return pltpu.make_async_copy(rows_ref.at[span], held.at[span], sems.at[step])

    for copy in firsts:
        copy.start()
    for step in range(steps):
        fetch(step).start()
    for copy in firsts:
        copy.wait()
    turned[...] = proj[...].T

    @pl.loop(0, steps)
    def _(step):
        fetch(step).wait()
        span = pl.ds(pl.multiple_of(step * block, block), block)
        left = jnp.dot(held[span, :half], turned[...], preferred_element_type=jnp.float32)
        right = jnp.dot(held[span, half:], turned[...], preferred_element_type=jnp.float32)
        feats_ref[:, span] = left.T[:count] + right.T[count:]


def features(rows, proj, block, limit, name):
    count, width = proj.shape
    return pl.pallas_call(
        functools.partial(stream_kernel, block),
        out_shape=pltpu.VMEM((count, rows.shape[0]), jnp.float32),
        in_specs=[ANY_SPEC] * 2,
        out_specs=VMEM_SPEC,
        scratch_shapes=[
            pltpu.VMEM(rows.shape, jnp.bfloat16),
            pltpu.VMEM((2 * count, width // 2), jnp.bfloat16),
            pltpu.VMEM((width // 2, 2 * count), jnp.bfloat16),
            pltpu.SemaphoreType.DMA((rows.shape[0] // block + 2,)),
        ],
        compiler_params=pltpu.CompilerParams(vmem_limit_bytes=limit * 2**20),
        name=name,
    )(in_hbm(rows), in_hbm(proj))


def split_kernel(prior_ref, upper_ref, lower_ref, held, sems):
    chunk = held.shape[1] // sems.shape[0]
    spans = [pl.ds(c * chunk, chunk) for c in range(sems.shape[0])]
    copies = [
        pltpu.make_async_copy(prior_ref.at[:, span], held.at[:, span], sems.at[c])
        for c, span in enumerate(spans)
    ]
    for copy in copies:
        copy.start()
    for copy, span in zip(copies, spans):
        copy.wait()
        block = held[:, span]
        upper = block.astype(jnp.bfloat16)
        upper_ref[:, span] = upper
        lower_ref[:, span] = (block - upper.astype(jnp.float32)).astype(jnp.bfloat16)


def split_prior(prior):
    return pl.pallas_call(
        split_kernel,
        out_shape=(pltpu.VMEM(prior.shape, jnp.bfloat16),) * 2,
        in_specs=[ANY_SPEC],
        out_specs=(VMEM_SPEC,) * 2,
        scratch_shapes=[pltpu.VMEM(prior.shape, jnp.float32), pltpu.SemaphoreType.DMA((8,))],
        compiler_params=PARAMS,
        name="split_prior",
    )(in_hbm(prior))


def partial_kernel(size, *refs):
    blocks, (out_ref, part_ref, held) = refs[:size], refs[size:]
    me = lax.axis_index("tensor")
    tokens = blocks[0].shape[1]
    for k, block in zip(order_of(size), blocks):
        start = pl.multiple_of((me ^ k) * tokens, LANES)
        held[:, pl.ds(start, tokens)] = block[...]
    for s in range(part_ref.shape[0]):
        span = slice(s * SEQ, (s + 1) * SEQ)
        part_ref[s] = dot_nt(held[:, span], out_ref[:, span]) * (1.0 / SEQ)


def partial_vectors(blocks, out_local):
    seq_count = out_local.shape[1] // SEQ
    return pl.pallas_call(
        functools.partial(partial_kernel, len(blocks)),
        out_shape=F32((seq_count, R_IN, R_OUT)),
        in_specs=[VMEM_SPEC] * (len(blocks) + 1),
        out_specs=VMEM_SPEC,
        scratch_shapes=[pltpu.VMEM(out_local.shape, jnp.float32)],
        compiler_params=PARAMS,
        name="partial_vectors",
    )(*blocks, out_local)


def own_columns(ref, me, count):
    if count % LANES == 0:
        return ref[:, pl.ds(pl.multiple_of(me * count, LANES), count)]
    per = LANES // count
    held = ref[:, pl.ds(pl.multiple_of((me // per) * LANES, LANES), LANES)]
    return pltpu.roll(held, LANES - (me % per) * count, 1)[:, :count]


def pieces_of(values, count):
    held = []
    for _ in range(count):
        piece = values.astype(jnp.bfloat16)
        held.append(piece)
        values = values - piece.astype(jnp.float32)
    return jnp.concatenate(held, axis=0)


def dot_pieces(a, b, seqs):
    held = lax.dot_general(a, b, NT, preferred_element_type=jnp.float32)
    total = held[:seqs]
    for start in range(seqs, held.shape[0], seqs):
        total = total + held[start : start + seqs]
    return total


def apply_fisher(pieces, vectors_ref, vector_pieces, upper_ref, lower_ref, me):
    seqs = vectors_ref.shape[0]
    applied = dot_pieces(pieces, upper_ref[...], seqs)
    applied = applied + dot_pieces(pieces[: 2 * seqs], lower_ref[...], seqs)
    weights = dot_pieces(pieces, vector_pieces, seqs)
    weights = (weights[:, :seqs] + weights[:, seqs:]) * (1.0 / seqs)
    own = own_columns(vectors_ref, me, upper_ref.shape[0])
    return applied + jnp.dot(weights, own, precision=HIGHEST, preferred_element_type=jnp.float32)


def flat_index(tensor_size):
    return lax.axis_index("dp") * tensor_size + lax.axis_index("tensor")


def start_kernel(order, tensor_size, *refs):
    pieces_ref, upper_ref, lower_ref, vectors_ref, vector_pieces_ref, scale_ref, applied_ref, norm_ref = refs
    vectors = jnp.concatenate([pieces_ref[order.index(k)] for k in range(len(order))], axis=0)
    vectors_ref[...] = vectors
    split = pieces_of(vectors, 3)
    vector_pieces = split[: 2 * vectors.shape[0]]
    vector_pieces_ref[...] = vector_pieces
    norm = jnp.broadcast_to(row_sum(vectors * vectors), norm_ref.shape)
    norm_ref[...] = norm
    spread = jnp.sum(norm, axis=0, keepdims=True) * (1.0 / vectors.shape[0])
    scale_ref[...] = jnp.broadcast_to(1.0 / (1.0 + spread), scale_ref.shape)
    me = flat_index(tensor_size)
    applied_ref[...] = apply_fisher(split, vectors_ref, vector_pieces, upper_ref, lower_ref, me)


def start_cg(pieces, prior_pieces, order, tensor_size):
    seqs = len(order) * pieces.shape[1]
    rows, width = prior_pieces[0].shape
    vector_pieces = jax.ShapeDtypeStruct((2 * seqs, width), jnp.bfloat16)
    column = F32((seqs, LANES))
    return pl.pallas_call(
        functools.partial(start_kernel, order, tensor_size),
        out_shape=(F32((seqs, width)), vector_pieces, column, F32((seqs, rows)), column),
        in_specs=[VMEM_SPEC] * 3,
        out_specs=(VMEM_SPEC,) * 5,
        compiler_params=PARAMS,
        name="cg_start",
    )(pieces, *prior_pieces)


def step_kernel(sizes, first, last, *refs):
    blocks_ref, upper_ref, lower_ref, vectors_ref, vector_pieces_ref, scale_ref = refs[:6]
    norm_ref, fisher_direction_ref = refs[6:8]
    refs = refs[8:]
    if not first:
        fisher_residual_ref, direction_ref, residual_ref, solution_ref = refs[:4]
        refs = refs[4:]
    if last:
        queries_ref, curvature_out, norm_out, solved_out, along_out, held = refs
    else:
        fisher_direction_out, norm_out, fisher_residual_out, direction_out, residual_out, solution_out, held = refs
    me = flat_index(sizes[1])
    rows = blocks_ref.shape[2]
    for i, k in enumerate(group_order(sizes)):
        held[:, k * rows : (k + 1) * rows] = blocks_ref[i]
    applied = held[...]
    scale = scale_ref[...][:, :1]
    twice = apply_fisher(
        pieces_of(scale * applied, 3), vectors_ref, vector_pieces_ref[...], upper_ref, lower_ref, me
    )
    direction = vectors_ref[...] if first else direction_ref[...]
    residual = direction if first else residual_ref[...]
    norm = norm_ref[...][:, :1]
    step = norm / row_sum(direction * applied)
    solution = step * direction
    if not first:
        solution = solution_ref[...] + solution
    residual = residual - step * applied
    norm_next = row_sum(residual * residual)
    share = norm_next / norm
    direction = residual + share * direction
    fisher_direction = fisher_direction_ref[...]
    fisher_residual = (fisher_direction if first else fisher_residual_ref[...]) - (step / scale) * twice
    fisher_direction = fisher_residual + share * fisher_direction
    norm_out[...] = jnp.broadcast_to(norm_next, norm_out.shape)
    if last:
        held[...] = direction
        own = own_columns(held, me, rows)
        curvature_out[...] = jnp.broadcast_to(row_sum(own * fisher_direction), curvature_out.shape)
        seqs = direction.shape[0]
        solved = jnp.concatenate([solution, direction], axis=0)
        scores = dot_pieces(pieces_of(solved, 3), queries_ref[...], 2 * seqs)
        solved_out[...] = scores[:seqs]
        along_out[...] = scores[seqs:]
    else:
        fisher_direction_out[...] = fisher_direction
        fisher_residual_out[...] = fisher_residual
        residual_out[...] = residual
        direction_out[...] = direction
        solution_out[...] = solution


def step_cg(blocks, fixed, norm, state, queries, sizes):
    first, last = len(state) == 1, queries is not None
    whole, rows = F32(fixed[2].shape), F32(state[0].shape)
    column = F32(norm.shape)
    operands = [blocks, *fixed, norm, *state]
    out_shape = (rows, column, rows, whole, whole, whole)
    if last:
        operands.append(queries)
        scores = F32((whole.shape[0], queries.shape[0]))
        out_shape = (column, column, scores, scores)
    return pl.pallas_call(
        functools.partial(step_kernel, sizes, first, last),
        out_shape=out_shape,
        in_specs=[VMEM_SPEC] * len(operands),
        out_specs=(VMEM_SPEC,) * len(out_shape),
        scratch_shapes=[pltpu.VMEM(whole.shape, jnp.float32)],
        compiler_params=PARAMS,
        name="cg_step",
    )(*operands)


def on_device(dp_size, tensor_size, inputs, in_proj, out_grads, out_proj, prior, queries):
    width = R_IN * R_OUT
    both, sizes = ("dp", "tensor"), (dp_size, tensor_size)
    order, dp_order = group_order(sizes), group_order((dp_size, 1))
    in_blocks = direct(features(inputs, in_proj, LANES, 20, "in_features"), "tensor", tensor_size, order_of(tensor_size))
    out_local = features(out_grads, out_proj, 2 * LANES, 44, "out_features")
    partial = partial_vectors(in_blocks, out_local).reshape(-1, width)
    first, *rest = bits(tensor_size)
    prior, partial = lax.optimization_barrier((prior, partial))
    partial = partial + swap(partial, "tensor", tensor_size, first)
    partial, prior_pieces = lax.optimization_barrier((partial, split_prior(prior)))
    for bit in rest:
        partial = partial + swap(partial, "tensor", tensor_size, bit)
    pieces = gather(partial, "dp", dp_order)
    prior_pieces = [in_vmem(piece) for piece in prior_pieces]
    vectors, vector_pieces, scale, applied_rows, norm = start_cg(pieces, prior_pieces, dp_order, tensor_size)
    fixed = (*prior_pieces, vectors, vector_pieces, scale)
    state = [applied_rows]
    for iteration in range(1, ITERS - 1):
        blocks = gather(state[0], both, order)
        applied_rows, norm, *others = step_cg(blocks, fixed, norm, state, None, sizes)
        state = [applied_rows, *others]
    blocks = gather(state[0], both, order)
    curvature, norm, solved, along = step_cg(blocks, fixed, norm, state, queries, sizes)
    curvature = jnp.sum(gather(curvature, both, order), axis=0)
    return solved + (norm / curvature)[:, :1] * along


def solution(mesh):
    return jax.shard_map(
        functools.partial(on_device, mesh.shape["dp"], mesh.shape["tensor"]),
        mesh=mesh,
        in_specs=(
            P(("groups", "dp", "tensor"), None),
            P(),
            P(("groups", "dp"), "tensor"),
            P(None, "tensor"),
            P(("groups", "dp", "tensor"), None),
            P(("groups", "dp", "tensor"), None),
        ),
        out_specs=P("groups", ("dp", "tensor")),
        check_vma=False,
    )
```

```python
import functools

import jax
import jax.numpy as jnp
from jax import lax
from jax.experimental import pallas as pl
from jax.experimental.pallas import tpu as pltpu
from jax.sharding import PartitionSpec as P

R_IN = 64
R_OUT = 64
SEQ = 1024
ITERS = 4
LANES = 128
HEAD = 2 * LANES
NT = (((1,), (1,)), ((), ()))
HIGHEST = lax.Precision.HIGHEST
ANY_SPEC = pl.BlockSpec(memory_space=pl.ANY)
VMEM_SPEC = pl.BlockSpec(memory_space=pltpu.VMEM)
PARAMS = pltpu.CompilerParams(vmem_limit_bytes=16 * 2**20)
F32 = functools.partial(jax.ShapeDtypeStruct, dtype=jnp.float32)


def swap(value, axis, size, bit):
    return lax.ppermute(value, axis, [(i, i ^ bit) for i in range(size)])


def bits(size):
    return [1 << b for b in reversed(range(size.bit_length() - 1))]


def group_order(sizes):
    dp_size, tensor_size = sizes
    first = min(1, dp_size - 1) * tensor_size + (tensor_size - 1) // 2
    return [first] + [i for i in range(dp_size * tensor_size) if i != first]


def gather(value, sizes):
    order = group_order(sizes)
    value = jnp.broadcast_to(value[None], (len(order),) + value.shape)
    return lax.all_to_all(value, ("dp", "tensor"), 0, 0, axis_index_groups=[order])


def order_of(size):
    return (0, 2, 3, 1) if size == 4 else tuple(range(size))


def direct(value, axis, size, order):
    return [value] + [swap(value, axis, size, k) for k in order[1:]]


def in_hbm(value):
    return pltpu.with_memory_space_constraint(value, pltpu.HBM)


def in_vmem(value):
    return pltpu.with_memory_space_constraint(value, pltpu.VMEM)


def dot_nt(a, b):
    return lax.dot_general(a, b, NT, precision=HIGHEST, preferred_element_type=jnp.float32)


def row_sum(values):
    return jnp.sum(values, axis=1, keepdims=True)


def fetch(rows_ref, held, sems, step, block):
    span = pl.ds(pl.multiple_of(step * block, block), block)
    return pltpu.make_async_copy(rows_ref.at[span], held.at[span], sems.at[step])


def fetch_halves(proj_ref, proj, sems):
    count, half = proj_ref.shape[0], proj.shape[1]
    return [
        pltpu.make_async_copy(
            proj_ref.at[:, pl.ds(h * half, half)], proj.at[pl.ds(h * count, count)], sems.at[h]
        )
        for h in range(2)
    ]


def project(rows, turned, count):
    half = turned.shape[0]
    left = jnp.dot(rows[:, :half], turned[...], preferred_element_type=jnp.float32)
    right = jnp.dot(rows[:, half:], turned[...], preferred_element_type=jnp.float32)
    return left.T[:count] + right.T[count:]


def in_kernel(rows_ref, proj_ref, grads_ref, next_proj_ref, feats_ref, head_ref, next_turned_ref, *scratch):
    held, proj, turned, next_proj, row_sems, proj_sems, next_sems, head_sem = scratch
    steps = held.shape[0] // LANES
    firsts = fetch_halves(proj_ref, proj, proj_sems)
    nexts = fetch_halves(next_proj_ref, next_proj, next_sems)
    head = pltpu.make_async_copy(grads_ref.at[pl.ds(0, HEAD)], head_ref, head_sem)
    for copy in firsts:
        copy.start()
    fetch(rows_ref, held, row_sems, 0, LANES).start()
    for copy in nexts:
        copy.start()
    for step in range(1, steps):
        fetch(rows_ref, held, row_sems, step, LANES).start()
    head.start()
    for copy in firsts:
        copy.wait()
    turned[...] = proj[...].T
    for copy in nexts:
        copy.wait()
    part = next_proj.shape[1] // steps

    @pl.loop(0, steps)
    def _(step):
        fetch(rows_ref, held, row_sems, step, LANES).wait()
        span = pl.ds(pl.multiple_of(step * LANES, LANES), LANES)
        feats_ref[:, span] = project(held.at[span], turned, proj_ref.shape[0])
        span = pl.ds(pl.multiple_of(step * part, LANES), part)
        next_turned_ref[span, :] = next_proj[:, span].T

    head.wait()


def in_features(inputs, in_proj, out_grads, out_proj):
    count, width = in_proj.shape
    next_count, next_width = out_proj.shape
    return pl.pallas_call(
        in_kernel,
        out_shape=(
            pltpu.VMEM((count, inputs.shape[0]), jnp.float32),
            pltpu.VMEM((HEAD, next_width), jnp.bfloat16),
            pltpu.VMEM((next_width // 2, 2 * next_count), jnp.bfloat16),
        ),
        in_specs=[ANY_SPEC] * 4,
        out_specs=(VMEM_SPEC,) * 3,
        scratch_shapes=[
            pltpu.VMEM(inputs.shape, jnp.bfloat16),
            pltpu.VMEM((2 * count, width // 2), jnp.bfloat16),
            pltpu.VMEM((width // 2, 2 * count), jnp.bfloat16),
            pltpu.VMEM((2 * next_count, next_width // 2), jnp.bfloat16),
            pltpu.SemaphoreType.DMA((inputs.shape[0] // LANES,)),
            pltpu.SemaphoreType.DMA((2,)),
            pltpu.SemaphoreType.DMA((2,)),
            pltpu.SemaphoreType.DMA,
        ],
        compiler_params=pltpu.CompilerParams(vmem_limit_bytes=24 * 2**20),
        name="in_features",
    )(in_hbm(inputs), in_hbm(in_proj), in_hbm(out_grads), in_hbm(out_proj))


def out_kernel(rows_ref, head_ref, turned_ref, feats_ref, held, sems):
    count, steps = feats_ref.shape[0], held.shape[0] // HEAD
    for step in range(1, steps):
        fetch(rows_ref, held, sems, step, HEAD).start()
    feats_ref[:, :HEAD] = project(head_ref, turned_ref, count)

    @pl.loop(1, steps)
    def _(step):
        fetch(rows_ref, held, sems, step, HEAD).wait()
        span = pl.ds(pl.multiple_of(step * HEAD, HEAD), HEAD)
        feats_ref[:, span] = project(held.at[span], turned_ref, count)


def out_features(out_grads, head, turned):
    tokens = out_grads.shape[0]
    return pl.pallas_call(
        out_kernel,
        out_shape=pltpu.VMEM((R_OUT, tokens), jnp.float32),
        in_specs=[ANY_SPEC, VMEM_SPEC, VMEM_SPEC],
        out_specs=VMEM_SPEC,
        scratch_shapes=[
            pltpu.VMEM(out_grads.shape, jnp.bfloat16),
            pltpu.SemaphoreType.DMA((tokens // HEAD,)),
        ],
        compiler_params=pltpu.CompilerParams(vmem_limit_bytes=40 * 2**20),
        name="out_features",
    )(in_hbm(out_grads), in_vmem(head), in_vmem(turned))


def split_kernel(prior_ref, upper_ref, lower_ref, held, sems):
    chunk = held.shape[1] // sems.shape[0]
    spans = [pl.ds(c * chunk, chunk) for c in range(sems.shape[0])]
    copies = [
        pltpu.make_async_copy(prior_ref.at[:, span], held.at[:, span], sems.at[c])
        for c, span in enumerate(spans)
    ]
    for copy in copies:
        copy.start()
    for copy, span in zip(copies, spans):
        copy.wait()
        block = held[:, span]
        upper = block.astype(jnp.bfloat16)
        upper_ref[:, span] = upper
        lower_ref[:, span] = (block - upper.astype(jnp.float32)).astype(jnp.bfloat16)


def split_prior(prior):
    return pl.pallas_call(
        split_kernel,
        out_shape=(pltpu.VMEM(prior.shape, jnp.bfloat16),) * 2,
        in_specs=[ANY_SPEC],
        out_specs=(VMEM_SPEC,) * 2,
        scratch_shapes=[pltpu.VMEM(prior.shape, jnp.float32), pltpu.SemaphoreType.DMA((8,))],
        compiler_params=PARAMS,
        name="split_prior",
    )(in_hbm(prior))


def partial_kernel(size, *refs):
    blocks, (out_ref, part_ref, held) = refs[:size], refs[size:]
    me = lax.axis_index("tensor")
    tokens = blocks[0].shape[1]
    for k, block in zip(order_of(size), blocks):
        start = pl.multiple_of((me ^ k) * tokens, LANES)
        held[:, pl.ds(start, tokens)] = block[...]
    for s in range(part_ref.shape[0]):
        span = slice(s * SEQ, (s + 1) * SEQ)
        outs = pieces_of(out_ref[:, span], 2)
        sums = dot_pieces(pieces_of(held[:, span], 2), outs, R_IN)
        part_ref[s] = (sums[:, :R_OUT] + sums[:, R_OUT:]) * (1.0 / SEQ)


def partial_vectors(blocks, out_local):
    seq_count = out_local.shape[1] // SEQ
    return pl.pallas_call(
        functools.partial(partial_kernel, len(blocks)),
        out_shape=F32((seq_count, R_IN, R_OUT)),
        in_specs=[VMEM_SPEC] * (len(blocks) + 1),
        out_specs=VMEM_SPEC,
        scratch_shapes=[pltpu.VMEM(out_local.shape, jnp.float32)],
        compiler_params=PARAMS,
        name="partial_vectors",
    )(*blocks, out_local)


def own_columns(ref, me, count):
    if count % LANES == 0:
        return ref[:, pl.ds(pl.multiple_of(me * count, LANES), count)]
    per = LANES // count
    held = ref[:, pl.ds(pl.multiple_of((me // per) * LANES, LANES), LANES)]
    return pltpu.roll(held, LANES - (me % per) * count, 1)[:, :count]


def pieces_of(values, count):
    held = []
    for _ in range(count):
        piece = values.astype(jnp.bfloat16)
        held.append(piece)
        values = values - piece.astype(jnp.float32)
    return jnp.concatenate(held, axis=0)


def dot_pieces(a, b, seqs):
    held = lax.dot_general(a, b, NT, preferred_element_type=jnp.float32)
    total = held[:seqs]
    for start in range(seqs, held.shape[0], seqs):
        total = total + held[start : start + seqs]
    return total


def apply_fisher(pieces, vectors_ref, vector_pieces, upper_ref, lower_ref, me):
    seqs = vectors_ref.shape[0]
    applied = dot_pieces(pieces, upper_ref[...], seqs)
    applied = applied + dot_pieces(pieces[: 2 * seqs], lower_ref[...], seqs)
    weights = dot_pieces(pieces, vector_pieces, seqs)
    weights = (weights[:, :seqs] + weights[:, seqs:]) * (1.0 / seqs)
    own = own_columns(vectors_ref, me, upper_ref.shape[0])
    return applied + jnp.dot(weights, own, precision=HIGHEST, preferred_element_type=jnp.float32)


def flat_index(tensor_size):
    return lax.axis_index("dp") * tensor_size + lax.axis_index("tensor")


def start_kernel(size, tensor_size, *refs):
    pieces, refs = refs[:size], refs[size:]
    upper_ref, lower_ref, vectors_ref, vector_pieces_ref, scale_ref, applied_ref, norm_ref, held = refs
    dp = lax.axis_index("dp")
    for k, piece in enumerate(pieces):
        held[dp ^ k] = piece[...]
    vectors = jnp.concatenate([held[k] for k in range(size)], axis=0)
    vectors_ref[...] = vectors
    split = pieces_of(vectors, 3)
    vector_pieces = split[: 2 * vectors.shape[0]]
    vector_pieces_ref[...] = vector_pieces
    norm = jnp.broadcast_to(row_sum(vectors * vectors), norm_ref.shape)
    norm_ref[...] = norm
    spread = jnp.sum(norm, axis=0, keepdims=True) * (1.0 / vectors.shape[0])
    scale_ref[...] = jnp.broadcast_to(1.0 / (1.0 + spread), scale_ref.shape)
    me = flat_index(tensor_size)
    applied_ref[...] = apply_fisher(split, vectors_ref, vector_pieces, upper_ref, lower_ref, me)


def start_cg(pieces, prior_pieces, tensor_size):
    size, seqs = len(pieces), len(pieces) * pieces[0].shape[0]
    rows, width = prior_pieces[0].shape
    vector_pieces = jax.ShapeDtypeStruct((2 * seqs, width), jnp.bfloat16)
    column = F32((seqs, LANES))
    return pl.pallas_call(
        functools.partial(start_kernel, size, tensor_size),
        out_shape=(F32((seqs, width)), vector_pieces, column, F32((seqs, rows)), column),
        in_specs=[VMEM_SPEC] * (size + 2),
        out_specs=(VMEM_SPEC,) * 5,
        scratch_shapes=[pltpu.VMEM((size,) + pieces[0].shape, jnp.float32)],
        compiler_params=PARAMS,
        name="cg_start",
    )(*pieces, *prior_pieces)


def step_kernel(sizes, first, last, *refs):
    blocks_ref, upper_ref, lower_ref, vectors_ref, vector_pieces_ref, scale_ref = refs[:6]
    norm_ref, fisher_direction_ref = refs[6:8]
    refs = refs[8:]
    if not first:
        fisher_residual_ref, direction_ref, residual_ref, solution_ref = refs[:4]
        refs = refs[4:]
    if last:
        queries_ref, curvature_out, norm_out, solved_out, along_out, held = refs
    else:
        fisher_direction_out, norm_out, fisher_residual_out, direction_out, residual_out, solution_out, held = refs
    me = flat_index(sizes[1])
    rows = blocks_ref.shape[2]
    for i, k in enumerate(group_order(sizes)):
        held[:, k * rows : (k + 1) * rows] = blocks_ref[i]
    applied = held[...]
    scale = scale_ref[...][:, :1]
    twice = apply_fisher(
        pieces_of(scale * applied, 3), vectors_ref, vector_pieces_ref[...], upper_ref, lower_ref, me
    )
    direction = vectors_ref[...] if first else direction_ref[...]
    residual = direction if first else residual_ref[...]
    norm = norm_ref[...][:, :1]
    step = norm / row_sum(direction * applied)
    solution = step * direction
    if not first:
        solution = solution_ref[...] + solution
    residual = residual - step * applied
    norm_next = row_sum(residual * residual)
    share = norm_next / norm
    direction = residual + share * direction
    fisher_direction = fisher_direction_ref[...]
    fisher_residual = (fisher_direction if first else fisher_residual_ref[...]) - (step / scale) * twice
    fisher_direction = fisher_residual + share * fisher_direction
    norm_out[...] = jnp.broadcast_to(norm_next, norm_out.shape)
    if last:
        held[...] = direction
        own = own_columns(held, me, rows)
        curvature_out[...] = jnp.broadcast_to(row_sum(own * fisher_direction), curvature_out.shape)
        seqs = direction.shape[0]
        solved = jnp.concatenate([solution, direction], axis=0)
        scores = dot_pieces(pieces_of(solved, 3), queries_ref[...], 2 * seqs)
        solved_out[...] = scores[:seqs]
        along_out[...] = scores[seqs:]
    else:
        fisher_direction_out[...] = fisher_direction
        fisher_residual_out[...] = fisher_residual
        residual_out[...] = residual
        direction_out[...] = direction
        solution_out[...] = solution


def step_cg(blocks, fixed, norm, state, queries, sizes):
    first, last = len(state) == 1, queries is not None
    whole, rows = F32(fixed[2].shape), F32(state[0].shape)
    column = F32(norm.shape)
    operands = [blocks, *fixed, norm, *state]
    out_shape = (rows, column, rows, whole, whole, whole)
    if last:
        operands.append(queries)
        scores = F32((whole.shape[0], queries.shape[0]))
        out_shape = (column, column, scores, scores)
    return pl.pallas_call(
        functools.partial(step_kernel, sizes, first, last),
        out_shape=out_shape,
        in_specs=[VMEM_SPEC] * len(operands),
        out_specs=(VMEM_SPEC,) * len(out_shape),
        scratch_shapes=[pltpu.VMEM(whole.shape, jnp.float32)],
        compiler_params=PARAMS,
        name="cg_step",
    )(*operands)


def combine_kernel(curvature_ref, norm_ref, solved_ref, along_ref, scores_ref):
    step = norm_ref[...] / jnp.sum(curvature_ref[...], axis=0)
    scores_ref[...] = solved_ref[...] + step[:, :1] * along_ref[...]


def combine(curvature, norm, solved, along):
    return pl.pallas_call(
        combine_kernel,
        out_shape=F32(solved.shape),
        in_specs=[VMEM_SPEC] * 4,
        out_specs=VMEM_SPEC,
        compiler_params=PARAMS,
        name="combine",
    )(curvature, norm, solved, along)


def on_device(dp_size, tensor_size, inputs, in_proj, out_grads, out_proj, prior, queries):
    width = R_IN * R_OUT
    sizes = dp_size, tensor_size
    in_local, head, turned = in_features(inputs, in_proj, out_grads, out_proj)
    in_blocks = direct(in_local, "tensor", tensor_size, order_of(tensor_size))
    out_local = out_features(out_grads, head, turned)
    partial = partial_vectors(in_blocks, out_local).reshape(-1, width)
    first, *rest = bits(tensor_size)
    prior, partial = lax.optimization_barrier((prior, partial))
    partial = partial + swap(partial, "tensor", tensor_size, first)
    partial, prior_pieces = lax.optimization_barrier((partial, split_prior(prior)))
    for bit in rest:
        partial = partial + swap(partial, "tensor", tensor_size, bit)
    pieces = direct(partial, "dp", dp_size, range(dp_size))
    prior_pieces = [in_vmem(piece) for piece in prior_pieces]
    vectors, vector_pieces, scale, applied_rows, norm = start_cg(pieces, prior_pieces, tensor_size)
    fixed = (*prior_pieces, vectors, vector_pieces, scale)
    state = [applied_rows]
    for iteration in range(1, ITERS - 1):
        blocks = gather(state[0], sizes)
        applied_rows, norm, *others = step_cg(blocks, fixed, norm, state, None, sizes)
        state = [applied_rows, *others]
    blocks = gather(state[0], sizes)
    curvature, norm, solved, along = step_cg(blocks, fixed, norm, state, queries, sizes)
    return combine(gather(curvature, sizes), norm, solved, along)


def solution(mesh):
    return jax.shard_map(
        functools.partial(on_device, mesh.shape["dp"], mesh.shape["tensor"]),
        mesh=mesh,
        in_specs=(
            P(("groups", "dp", "tensor"), None),
            P(),
            P(("groups", "dp"), "tensor"),
            P(None, "tensor"),
            P(("groups", "dp", "tensor"), None),
            P(("groups", "dp", "tensor"), None),
        ),
        out_specs=P("groups", ("dp", "tensor")),
        check_vma=False,
    )
```

```python
import functools

import jax
import jax.numpy as jnp
from jax import lax
from jax.experimental import pallas as pl
from jax.experimental.pallas import tpu as pltpu
from jax.sharding import PartitionSpec as P

R_IN = 64
R_OUT = 64
SEQ = 1024
ITERS = 4
LANES = 128
NT = (((1,), (1,)), ((), ()))
HIGHEST = lax.Precision.HIGHEST
ANY_SPEC = pl.BlockSpec(memory_space=pl.ANY)
VMEM_SPEC = pl.BlockSpec(memory_space=pltpu.VMEM)
PARAMS = pltpu.CompilerParams(vmem_limit_bytes=16 * 2**20)
F32 = functools.partial(jax.ShapeDtypeStruct, dtype=jnp.float32)


def swap(value, axis, size, bit):
    return lax.ppermute(value, axis, [(i, i ^ bit) for i in range(size)])


def bits(size):
    return [1 << b for b in reversed(range(size.bit_length() - 1))]


def group_order(sizes):
    dp_size, tensor_size = sizes
    first = min(1, dp_size - 1) * tensor_size + (tensor_size - 1) // 2
    return [first] + [i for i in range(dp_size * tensor_size) if i != first]


def gather(value, sizes):
    order = group_order(sizes)
    value = jnp.broadcast_to(value[None], (len(order),) + value.shape)
    return lax.all_to_all(value, ("dp", "tensor"), 0, 0, axis_index_groups=[order])


def order_of(size):
    return (0, 1, 3, 2) if size == 4 else tuple(range(size))


def direct(value, axis, size, order):
    return [value] + [swap(value, axis, size, k) for k in order[1:]]


def in_hbm(value):
    return pltpu.with_memory_space_constraint(value, pltpu.HBM)


def in_vmem(value):
    return pltpu.with_memory_space_constraint(value, pltpu.VMEM)


def dot_nt(a, b):
    return lax.dot_general(a, b, NT, precision=HIGHEST, preferred_element_type=jnp.float32)


def row_sum(values):
    return jnp.sum(values, axis=1, keepdims=True)


def stream_kernel(block, rows_ref, proj_ref, feats_ref, held, proj, turned, sems):
    count, half = proj_ref.shape[0], proj.shape[1]
    steps, tail = held.shape[0] // block, block // LANES
    firsts = [
        pltpu.make_async_copy(
            proj_ref.at[:, pl.ds(h * half, half)], proj.at[pl.ds(h * count, count)], sems.at[h]
        )
        for h in range(2)
    ]

    def span_of(step, size):
        return pl.ds(pl.multiple_of(step * size, size), size)

    def fetch(step, size):
        sem = step + 2 if size == block else step - (steps - 1) * tail + steps + 1
        span = span_of(step, size)
        return pltpu.make_async_copy(rows_ref.at[span], held.at[span], sems.at[sem])

    def project(step, size):
        fetch(step, size).wait()
        span = span_of(step, size)
        left = jnp.dot(held[span, :half], turned[...], preferred_element_type=jnp.float32)
        right = jnp.dot(held[span, half:], turned[...], preferred_element_type=jnp.float32)
        feats_ref[:, span] = left.T[:count] + right.T[count:]

    for copy in firsts:
        copy.start()
    for step in range(steps - 1):
        fetch(step, block).start()
    for step in range((steps - 1) * tail, steps * tail):
        fetch(step, LANES).start()
    for copy in firsts:
        copy.wait()
    turned[...] = proj[...].T

    @pl.loop(0, steps - 1)
    def _(step):
        project(step, block)

    @pl.loop((steps - 1) * tail, steps * tail)
    def _(step):
        project(step, LANES)


def features(rows, proj, block, limit, name):
    count, width = proj.shape
    return pl.pallas_call(
        functools.partial(stream_kernel, block),
        out_shape=pltpu.VMEM((count, rows.shape[0]), jnp.float32),
        in_specs=[ANY_SPEC] * 2,
        out_specs=VMEM_SPEC,
        scratch_shapes=[
            pltpu.VMEM(rows.shape, jnp.bfloat16),
            pltpu.VMEM((2 * count, width // 2), jnp.bfloat16),
            pltpu.VMEM((width // 2, 2 * count), jnp.bfloat16),
            pltpu.SemaphoreType.DMA((rows.shape[0] // block + block // LANES + 1,)),
        ],
        compiler_params=pltpu.CompilerParams(vmem_limit_bytes=limit * 2**20),
        name=name,
    )(in_hbm(rows), in_hbm(proj))


def split_kernel(prior_ref, upper_ref, lower_ref, held, sems):
    chunk = held.shape[1] // sems.shape[0]
    spans = [pl.ds(c * chunk, chunk) for c in range(sems.shape[0])]
    copies = [
        pltpu.make_async_copy(prior_ref.at[:, span], held.at[:, span], sems.at[c])
        for c, span in enumerate(spans)
    ]
    for copy in copies:
        copy.start()
    for copy, span in zip(copies, spans):
        copy.wait()
        block = held[:, span]
        upper = block.astype(jnp.bfloat16)
        upper_ref[:, span] = upper
        lower_ref[:, span] = (block - upper.astype(jnp.float32)).astype(jnp.bfloat16)


def split_prior(prior):
    return pl.pallas_call(
        split_kernel,
        out_shape=(pltpu.VMEM(prior.shape, jnp.bfloat16),) * 2,
        in_specs=[ANY_SPEC],
        out_specs=(VMEM_SPEC,) * 2,
        scratch_shapes=[pltpu.VMEM(prior.shape, jnp.float32), pltpu.SemaphoreType.DMA((8,))],
        compiler_params=PARAMS,
        name="split_prior",
    )(in_hbm(prior))


def partial_kernel(size, *refs):
    blocks, (out_ref, part_ref, held) = refs[:size], refs[size:]
    me = lax.axis_index("tensor")
    tokens = blocks[0].shape[1]
    for k, block in zip(order_of(size), blocks):
        start = pl.multiple_of((me ^ k) * tokens, LANES)
        held[:, pl.ds(start, tokens)] = block[...]
    for s in range(part_ref.shape[0]):
        span = slice(s * SEQ, (s + 1) * SEQ)
        outs = pieces_of(out_ref[:, span], 2)
        sums = dot_pieces(pieces_of(held[:, span], 2), outs, R_IN)
        part_ref[s] = (sums[:, :R_OUT] + sums[:, R_OUT:]) * (1.0 / SEQ)


def partial_vectors(blocks, out_local):
    seq_count = out_local.shape[1] // SEQ
    return pl.pallas_call(
        functools.partial(partial_kernel, len(blocks)),
        out_shape=F32((seq_count, R_IN, R_OUT)),
        in_specs=[VMEM_SPEC] * (len(blocks) + 1),
        out_specs=VMEM_SPEC,
        scratch_shapes=[pltpu.VMEM(out_local.shape, jnp.float32)],
        compiler_params=PARAMS,
        name="partial_vectors",
    )(*blocks, out_local)


def own_columns(ref, me, count):
    if count % LANES == 0:
        return ref[:, pl.ds(pl.multiple_of(me * count, LANES), count)]
    per = LANES // count
    held = ref[:, pl.ds(pl.multiple_of((me // per) * LANES, LANES), LANES)]
    return pltpu.roll(held, LANES - (me % per) * count, 1)[:, :count]


def pieces_of(values, count):
    held = []
    for _ in range(count):
        piece = values.astype(jnp.bfloat16)
        held.append(piece)
        values = values - piece.astype(jnp.float32)
    return jnp.concatenate(held, axis=0)


def dot_pieces(a, b, seqs):
    held = lax.dot_general(a, b, NT, preferred_element_type=jnp.float32)
    total = held[:seqs]
    for start in range(seqs, held.shape[0], seqs):
        total = total + held[start : start + seqs]
    return total


def apply_fisher(pieces, vectors_ref, vector_pieces, upper_ref, lower_ref, me):
    seqs = vectors_ref.shape[0]
    applied = dot_pieces(pieces, upper_ref[...], seqs)
    applied = applied + dot_pieces(pieces, lower_ref[...], seqs)
    weights = dot_pieces(pieces, vector_pieces, seqs)
    weights = (weights[:, :seqs] + weights[:, seqs:]) * (1.0 / seqs)
    own = own_columns(vectors_ref, me, upper_ref.shape[0])
    return applied + jnp.dot(weights, own, precision=HIGHEST, preferred_element_type=jnp.float32)


def flat_index(tensor_size):
    return lax.axis_index("dp") * tensor_size + lax.axis_index("tensor")


def start_kernel(size, tensor_size, *refs):
    pieces, refs = refs[:size], refs[size:]
    upper_ref, lower_ref, vectors_ref, vector_pieces_ref, scale_ref, applied_ref, norm_ref, held = refs
    dp = lax.axis_index("dp")
    for k, piece in enumerate(pieces):
        held[dp ^ k] = piece[...]
    vectors = jnp.concatenate([held[k] for k in range(size)], axis=0)
    vectors_ref[...] = vectors
    split = pieces_of(vectors, 2)
    vector_pieces_ref[...] = split
    norm = jnp.broadcast_to(row_sum(vectors * vectors), norm_ref.shape)
    norm_ref[...] = norm
    spread = jnp.sum(norm, axis=0, keepdims=True) * (1.0 / vectors.shape[0])
    scale_ref[...] = jnp.broadcast_to(1.0 / (1.0 + spread), scale_ref.shape)
    me = flat_index(tensor_size)
    applied_ref[...] = apply_fisher(split, vectors_ref, split, upper_ref, lower_ref, me)


def start_cg(pieces, prior_pieces, tensor_size):
    size, seqs = len(pieces), len(pieces) * pieces[0].shape[0]
    rows, width = prior_pieces[0].shape
    vector_pieces = jax.ShapeDtypeStruct((2 * seqs, width), jnp.bfloat16)
    column = F32((seqs, LANES))
    return pl.pallas_call(
        functools.partial(start_kernel, size, tensor_size),
        out_shape=(F32((seqs, width)), vector_pieces, column, F32((seqs, rows)), column),
        in_specs=[VMEM_SPEC] * (size + 2),
        out_specs=(VMEM_SPEC,) * 5,
        scratch_shapes=[pltpu.VMEM((size,) + pieces[0].shape, jnp.float32)],
        compiler_params=PARAMS,
        name="cg_start",
    )(*pieces, *prior_pieces)


def step_kernel(sizes, first, last, *refs):
    blocks_ref, upper_ref, lower_ref, vectors_ref, vector_pieces_ref, scale_ref = refs[:6]
    norm_ref, fisher_direction_ref = refs[6:8]
    refs = refs[8:]
    if not first:
        fisher_residual_ref, direction_ref, residual_ref, solution_ref = refs[:4]
        refs = refs[4:]
    if last:
        queries_ref, curvature_out, norm_out, solved_out, along_out, held = refs
    else:
        fisher_direction_out, norm_out, fisher_residual_out, direction_out, residual_out, solution_out, held = refs
    me = flat_index(sizes[1])
    rows = blocks_ref.shape[2]
    for i, k in enumerate(group_order(sizes)):
        held[:, k * rows : (k + 1) * rows] = blocks_ref[i]
    applied = held[...]
    scale = scale_ref[...][:, :1]
    twice = apply_fisher(
        pieces_of(scale * applied, 2), vectors_ref, vector_pieces_ref[...], upper_ref, lower_ref, me
    )
    direction = vectors_ref[...] if first else direction_ref[...]
    residual = direction if first else residual_ref[...]
    norm = norm_ref[...][:, :1]
    step = norm / row_sum(direction * applied)
    solution = step * direction
    if not first:
        solution = solution_ref[...] + solution
    residual = residual - step * applied
    norm_next = row_sum(residual * residual)
    share = norm_next / norm
    direction = residual + share * direction
    fisher_direction = fisher_direction_ref[...]
    fisher_residual = (fisher_direction if first else fisher_residual_ref[...]) - (step / scale) * twice
    fisher_direction = fisher_residual + share * fisher_direction
    norm_out[...] = jnp.broadcast_to(norm_next, norm_out.shape)
    if last:
        held[...] = direction
        own = own_columns(held, me, rows)
        curvature_out[...] = jnp.broadcast_to(row_sum(own * fisher_direction), curvature_out.shape)
        seqs = direction.shape[0]
        solved = jnp.concatenate([solution, direction], axis=0)
        scores = dot_pieces(pieces_of(solved, 3), queries_ref[...], 2 * seqs)
        solved_out[...] = scores[:seqs]
        along_out[...] = scores[seqs:]
    else:
        fisher_direction_out[...] = fisher_direction
        fisher_residual_out[...] = fisher_residual
        residual_out[...] = residual
        direction_out[...] = direction
        solution_out[...] = solution


def step_cg(blocks, fixed, norm, state, queries, sizes):
    first, last = len(state) == 1, queries is not None
    whole, rows = F32(fixed[2].shape), F32(state[0].shape)
    column = F32(norm.shape)
    operands = [blocks, *fixed, norm, *state]
    out_shape = (rows, column, rows, whole, whole, whole)
    if last:
        operands.append(queries)
        scores = F32((whole.shape[0], queries.shape[0]))
        out_shape = (column, column, scores, scores)
    return pl.pallas_call(
        functools.partial(step_kernel, sizes, first, last),
        out_shape=out_shape,
        in_specs=[VMEM_SPEC] * len(operands),
        out_specs=(VMEM_SPEC,) * len(out_shape),
        scratch_shapes=[pltpu.VMEM(whole.shape, jnp.float32)],
        compiler_params=PARAMS,
        name="cg_step",
    )(*operands)


def combine_kernel(curvature_ref, norm_ref, solved_ref, along_ref, scores_ref):
    step = norm_ref[...] / jnp.sum(curvature_ref[...], axis=0)
    scores_ref[...] = solved_ref[...] + step[:, :1] * along_ref[...]


def combine(curvature, norm, solved, along):
    return pl.pallas_call(
        combine_kernel,
        out_shape=F32(solved.shape),
        in_specs=[VMEM_SPEC] * 4,
        out_specs=VMEM_SPEC,
        compiler_params=PARAMS,
        name="combine",
    )(curvature, norm, solved, along)


def on_device(dp_size, tensor_size, inputs, in_proj, out_grads, out_proj, prior, queries):
    width = R_IN * R_OUT
    sizes = dp_size, tensor_size
    in_blocks = direct(features(inputs, in_proj, LANES, 20, "in_features"), "tensor", tensor_size, order_of(tensor_size))
    out_local = features(out_grads, out_proj, 2 * LANES, 44, "out_features")
    partial = partial_vectors(in_blocks, out_local).reshape(-1, width)
    first, *rest = bits(tensor_size)
    prior, partial = lax.optimization_barrier((prior, partial))
    partial = partial + swap(partial, "tensor", tensor_size, first)
    partial, prior_pieces = lax.optimization_barrier((partial, split_prior(prior)))
    for bit in rest:
        partial = partial + swap(partial, "tensor", tensor_size, bit)
    pieces = direct(partial, "dp", dp_size, range(dp_size))
    prior_pieces = [in_vmem(piece) for piece in prior_pieces]
    vectors, vector_pieces, scale, applied_rows, norm = start_cg(pieces, prior_pieces, tensor_size)
    fixed = (*prior_pieces, vectors, vector_pieces, scale)
    state = [applied_rows]
    for iteration in range(1, ITERS - 1):
        blocks = gather(state[0], sizes)
        applied_rows, norm, *others = step_cg(blocks, fixed, norm, state, None, sizes)
        state = [applied_rows, *others]
    blocks = gather(state[0], sizes)
    curvature, norm, solved, along = step_cg(blocks, fixed, norm, state, queries, sizes)
    return combine(gather(curvature, sizes), norm, solved, along)


def solution(mesh):
    return jax.shard_map(
        functools.partial(on_device, mesh.shape["dp"], mesh.shape["tensor"]),
        mesh=mesh,
        in_specs=(
            P(("groups", "dp", "tensor"), None),
            P(),
            P(("groups", "dp"), "tensor"),
            P(None, "tensor"),
            P(("groups", "dp", "tensor"), None),
            P(("groups", "dp", "tensor"), None),
        ),
        out_specs=P("groups", ("dp", "tensor")),
        check_vma=False,
    )
```

```python
import functools

import jax
import jax.numpy as jnp
from jax import lax
from jax.experimental import pallas as pl
from jax.experimental.pallas import tpu as pltpu
from jax.sharding import PartitionSpec as P

R_IN = 64
R_OUT = 64
SEQ = 1024
ITERS = 4
LANES = 128
FEW = 4
NT = (((1,), (1,)), ((), ()))
HIGHEST = lax.Precision.HIGHEST
ANY_SPEC = pl.BlockSpec(memory_space=pl.ANY)
VMEM_SPEC = pl.BlockSpec(memory_space=pltpu.VMEM)
PARAMS = pltpu.CompilerParams(vmem_limit_bytes=16 * 2**20)
F32 = functools.partial(jax.ShapeDtypeStruct, dtype=jnp.float32)


def swap(value, axis, size, bit):
    return lax.ppermute(value, axis, [(i, i ^ bit) for i in range(size)])


def bits(size):
    return [1 << b for b in reversed(range(size.bit_length() - 1))]


def group_order(sizes):
    dp_size, tensor_size = sizes
    first = min(1, dp_size - 1) * tensor_size + (tensor_size - 1) // 2
    return [first] + [i for i in range(dp_size * tensor_size) if i != first]


def gather(value, sizes):
    order = group_order(sizes)
    value = jnp.broadcast_to(value[None], (len(order),) + value.shape)
    return lax.all_to_all(value, ("dp", "tensor"), 0, 0, axis_index_groups=[order])


def order_of(size):
    return (0, 2, 3, 1) if size == 4 else tuple(range(size))


def direct(value, axis, size, order):
    return [value] + [swap(value, axis, size, k) for k in order[1:]]


def sum_over(value, axis, size):
    if size > FEW:
        for bit in bits(size):
            value = value + swap(value, axis, size, bit)
        return value
    blocks = direct(value, axis, size, order_of(size))
    while len(blocks) > 1:
        blocks = [a + b for a, b in zip(blocks[::2], blocks[1::2])]
    return blocks[0]


def in_hbm(value):
    return pltpu.with_memory_space_constraint(value, pltpu.HBM)


def in_vmem(value):
    return pltpu.with_memory_space_constraint(value, pltpu.VMEM)


def dot_nt(a, b):
    return lax.dot_general(a, b, NT, precision=HIGHEST, preferred_element_type=jnp.float32)


def row_sum(values):
    return jnp.sum(values, axis=1, keepdims=True)


def stream_kernel(block, rows_ref, proj_ref, feats_ref, held, proj, turned, sems):
    count, half = proj_ref.shape[0], proj.shape[1]
    steps = held.shape[0] // block
    firsts = [
        pltpu.make_async_copy(
            proj_ref.at[:, pl.ds(h * half, half)], proj.at[pl.ds(h * count, count)], sems.at[steps + h]
        )
        for h in range(2)
    ]

    def fetch(step):
        span = pl.ds(pl.multiple_of(step * block, block), block)
        return pltpu.make_async_copy(rows_ref.at[span], held.at[span], sems.at[step])

    for copy in firsts:
        copy.start()
    for step in range(steps):
        fetch(step).start()
    for copy in firsts:
        copy.wait()
    turned[...] = proj[...].T

    @pl.loop(0, steps)
    def _(step):
        fetch(step).wait()
        span = pl.ds(pl.multiple_of(step * block, block), block)
        left = jnp.dot(held[span, :half], turned[...], preferred_element_type=jnp.float32)
        right = jnp.dot(held[span, half:], turned[...], preferred_element_type=jnp.float32)
        feats_ref[:, span] = left.T[:count] + right.T[count:]


def features(rows, proj, block, limit, name):
    count, width = proj.shape
    return pl.pallas_call(
        functools.partial(stream_kernel, block),
        out_shape=pltpu.VMEM((count, rows.shape[0]), jnp.float32),
        in_specs=[ANY_SPEC] * 2,
        out_specs=VMEM_SPEC,
        scratch_shapes=[
            pltpu.VMEM(rows.shape, jnp.bfloat16),
            pltpu.VMEM((2 * count, width // 2), jnp.bfloat16),
            pltpu.VMEM((width // 2, 2 * count), jnp.bfloat16),
            pltpu.SemaphoreType.DMA((rows.shape[0] // block + 2,)),
        ],
        compiler_params=pltpu.CompilerParams(vmem_limit_bytes=limit * 2**20),
        name=name,
    )(in_hbm(rows), in_hbm(proj))


def split_kernel(prior_ref, upper_ref, lower_ref, held, sems):
    chunk = held.shape[1] // sems.shape[0]
    spans = [pl.ds(c * chunk, chunk) for c in range(sems.shape[0])]
    copies = [
        pltpu.make_async_copy(prior_ref.at[:, span], held.at[:, span], sems.at[c])
        for c, span in enumerate(spans)
    ]
    for copy in copies:
        copy.start()
    for copy, span in zip(copies, spans):
        copy.wait()
        block = held[:, span]
        upper = block.astype(jnp.bfloat16)
        upper_ref[:, span] = upper
        lower_ref[:, span] = (block - upper.astype(jnp.float32)).astype(jnp.bfloat16)


def split_prior(prior):
    return pl.pallas_call(
        split_kernel,
        out_shape=(pltpu.VMEM(prior.shape, jnp.bfloat16),) * 2,
        in_specs=[ANY_SPEC],
        out_specs=(VMEM_SPEC,) * 2,
        scratch_shapes=[pltpu.VMEM(prior.shape, jnp.float32), pltpu.SemaphoreType.DMA((8,))],
        compiler_params=PARAMS,
        name="split_prior",
    )(in_hbm(prior))


def partial_kernel(size, *refs):
    blocks, (out_ref, part_ref, held) = refs[:size], refs[size:]
    me = lax.axis_index("tensor")
    tokens = blocks[0].shape[1]
    for k, block in zip(order_of(size), blocks):
        start = pl.multiple_of((me ^ k) * tokens, LANES)
        held[:, pl.ds(start, tokens)] = block[...]
    for s in range(part_ref.shape[0]):
        span = slice(s * SEQ, (s + 1) * SEQ)
        outs = pieces_of(out_ref[:, span], 2)
        sums = dot_pieces(pieces_of(held[:, span], 2), outs, R_IN)
        part_ref[s] = (sums[:, :R_OUT] + sums[:, R_OUT:]) * (1.0 / SEQ)


def partial_vectors(blocks, out_local):
    seq_count = out_local.shape[1] // SEQ
    return pl.pallas_call(
        functools.partial(partial_kernel, len(blocks)),
        out_shape=F32((seq_count, R_IN, R_OUT)),
        in_specs=[VMEM_SPEC] * (len(blocks) + 1),
        out_specs=VMEM_SPEC,
        scratch_shapes=[pltpu.VMEM(out_local.shape, jnp.float32)],
        compiler_params=PARAMS,
        name="partial_vectors",
    )(*blocks, out_local)


def own_columns(ref, me, count):
    if count % LANES == 0:
        return ref[:, pl.ds(pl.multiple_of(me * count, LANES), count)]
    per = LANES // count
    held = ref[:, pl.ds(pl.multiple_of((me // per) * LANES, LANES), LANES)]
    return pltpu.roll(held, LANES - (me % per) * count, 1)[:, :count]


def pieces_of(values, count):
    held = []
    for _ in range(count):
        piece = values.astype(jnp.bfloat16)
        held.append(piece)
        values = values - piece.astype(jnp.float32)
    return jnp.concatenate(held, axis=0)


def dot_pieces(a, b, seqs):
    held = lax.dot_general(a, b, NT, preferred_element_type=jnp.float32)
    total = held[:seqs]
    for start in range(seqs, held.shape[0], seqs):
        total = total + held[start : start + seqs]
    return total


def apply_fisher(pieces, vectors_ref, vector_pieces, upper_ref, lower_ref, me):
    seqs = vectors_ref.shape[0]
    applied = dot_pieces(pieces, upper_ref[...], seqs)
    applied = applied + dot_pieces(pieces[: 2 * seqs], lower_ref[...], seqs)
    weights = dot_pieces(pieces, vector_pieces, seqs)
    weights = (weights[:, :seqs] + weights[:, seqs:]) * (1.0 / seqs)
    own = own_columns(vectors_ref, me, upper_ref.shape[0])
    return applied + jnp.dot(weights, own, precision=HIGHEST, preferred_element_type=jnp.float32)


def flat_index(tensor_size):
    return lax.axis_index("dp") * tensor_size + lax.axis_index("tensor")


def start_kernel(size, tensor_size, *refs):
    pieces, refs = refs[:size], refs[size:]
    upper_ref, lower_ref, vectors_ref, vector_pieces_ref, scale_ref, applied_ref, norm_ref, held = refs
    dp = lax.axis_index("dp")
    for k, piece in enumerate(pieces):
        held[dp ^ k] = piece[...]
    vectors = jnp.concatenate([held[k] for k in range(size)], axis=0)
    vectors_ref[...] = vectors
    split = pieces_of(vectors, 3)
    vector_pieces = split[: 2 * vectors.shape[0]]
    vector_pieces_ref[...] = vector_pieces
    norm = jnp.broadcast_to(row_sum(vectors * vectors), norm_ref.shape)
    norm_ref[...] = norm
    spread = jnp.sum(norm, axis=0, keepdims=True) * (1.0 / vectors.shape[0])
    scale_ref[...] = jnp.broadcast_to(1.0 / (1.0 + spread), scale_ref.shape)
    me = flat_index(tensor_size)
    applied_ref[...] = apply_fisher(split, vectors_ref, vector_pieces, upper_ref, lower_ref, me)


def start_cg(pieces, prior_pieces, tensor_size):
    size, seqs = len(pieces), len(pieces) * pieces[0].shape[0]
    rows, width = prior_pieces[0].shape
    vector_pieces = jax.ShapeDtypeStruct((2 * seqs, width), jnp.bfloat16)
    column = F32((seqs, LANES))
    return pl.pallas_call(
        functools.partial(start_kernel, size, tensor_size),
        out_shape=(F32((seqs, width)), vector_pieces, column, F32((seqs, rows)), column),
        in_specs=[VMEM_SPEC] * (size + 2),
        out_specs=(VMEM_SPEC,) * 5,
        scratch_shapes=[pltpu.VMEM((size,) + pieces[0].shape, jnp.float32)],
        compiler_params=PARAMS,
        name="cg_start",
    )(*pieces, *prior_pieces)


def step_kernel(sizes, first, last, *refs):
    blocks_ref, upper_ref, lower_ref, vectors_ref, vector_pieces_ref, scale_ref = refs[:6]
    norm_ref, fisher_direction_ref = refs[6:8]
    refs = refs[8:]
    if not first:
        fisher_residual_ref, direction_ref, residual_ref, solution_ref = refs[:4]
        refs = refs[4:]
    if last:
        queries_ref, curvature_out, norm_out, solved_out, along_out, held = refs
    else:
        fisher_direction_out, norm_out, fisher_residual_out, direction_out, residual_out, solution_out, held = refs
    me = flat_index(sizes[1])
    rows = blocks_ref.shape[2]
    for i, k in enumerate(group_order(sizes)):
        held[:, k * rows : (k + 1) * rows] = blocks_ref[i]
    applied = held[...]
    scale = scale_ref[...][:, :1]
    twice = apply_fisher(
        pieces_of(scale * applied, 3), vectors_ref, vector_pieces_ref[...], upper_ref, lower_ref, me
    )
    direction = vectors_ref[...] if first else direction_ref[...]
    residual = direction if first else residual_ref[...]
    norm = norm_ref[...][:, :1]
    step = norm / row_sum(direction * applied)
    solution = step * direction
    if not first:
        solution = solution_ref[...] + solution
    residual = residual - step * applied
    norm_next = row_sum(residual * residual)
    share = norm_next / norm
    direction = residual + share * direction
    fisher_direction = fisher_direction_ref[...]
    fisher_residual = (fisher_direction if first else fisher_residual_ref[...]) - (step / scale) * twice
    fisher_direction = fisher_residual + share * fisher_direction
    norm_out[...] = jnp.broadcast_to(norm_next, norm_out.shape)
    if last:
        held[...] = direction
        own = own_columns(held, me, rows)
        curvature_out[...] = jnp.broadcast_to(row_sum(own * fisher_direction), curvature_out.shape)
        seqs = direction.shape[0]
        solved = jnp.concatenate([solution, direction], axis=0)
        scores = dot_pieces(pieces_of(solved, 3), queries_ref[...], 2 * seqs)
        solved_out[...] = scores[:seqs]
        along_out[...] = scores[seqs:]
    else:
        fisher_direction_out[...] = fisher_direction
        fisher_residual_out[...] = fisher_residual
        residual_out[...] = residual
        direction_out[...] = direction
        solution_out[...] = solution


def step_cg(blocks, fixed, norm, state, queries, sizes):
    first, last = len(state) == 1, queries is not None
    whole, rows = F32(fixed[2].shape), F32(state[0].shape)
    column = F32(norm.shape)
    operands = [blocks, *fixed, norm, *state]
    out_shape = (rows, column, rows, whole, whole, whole)
    if last:
        operands.append(queries)
        scores = F32((whole.shape[0], queries.shape[0]))
        out_shape = (column, column, scores, scores)
    return pl.pallas_call(
        functools.partial(step_kernel, sizes, first, last),
        out_shape=out_shape,
        in_specs=[VMEM_SPEC] * len(operands),
        out_specs=(VMEM_SPEC,) * len(out_shape),
        scratch_shapes=[pltpu.VMEM(whole.shape, jnp.float32)],
        compiler_params=PARAMS,
        name="cg_step",
    )(*operands)


def combine_kernel(curvature_ref, norm_ref, solved_ref, along_ref, scores_ref):
    step = norm_ref[...] / jnp.sum(curvature_ref[...], axis=0)
    scores_ref[...] = solved_ref[...] + step[:, :1] * along_ref[...]


def combine(curvature, norm, solved, along):
    return pl.pallas_call(
        combine_kernel,
        out_shape=F32(solved.shape),
        in_specs=[VMEM_SPEC] * 4,
        out_specs=VMEM_SPEC,
        compiler_params=PARAMS,
        name="combine",
    )(curvature, norm, solved, along)


def on_device(dp_size, tensor_size, inputs, in_proj, out_grads, out_proj, prior, queries):
    width = R_IN * R_OUT
    sizes = dp_size, tensor_size
    in_blocks = direct(features(inputs, in_proj, LANES, 20, "in_features"), "tensor", tensor_size, order_of(tensor_size))
    out_local = features(out_grads, out_proj, 2 * LANES, 44, "out_features")
    partial = partial_vectors(in_blocks, out_local).reshape(-1, width)
    prior, partial = lax.optimization_barrier((prior, partial))
    own_vectors = sum_over(partial, "tensor", tensor_size)
    own_vectors, prior_pieces = lax.optimization_barrier((own_vectors, split_prior(prior)))
    pieces = direct(own_vectors, "dp", dp_size, range(dp_size))
    prior_pieces = [in_vmem(piece) for piece in prior_pieces]
    vectors, vector_pieces, scale, applied_rows, norm = start_cg(pieces, prior_pieces, tensor_size)
    fixed = (*prior_pieces, vectors, vector_pieces, scale)
    state = [applied_rows]
    for iteration in range(1, ITERS - 1):
        blocks = gather(state[0], sizes)
        applied_rows, norm, *others = step_cg(blocks, fixed, norm, state, None, sizes)
        state = [applied_rows, *others]
    blocks = gather(state[0], sizes)
    curvature, norm, solved, along = step_cg(blocks, fixed, norm, state, queries, sizes)
    return combine(gather(curvature, sizes), norm, solved, along)


def solution(mesh):
    return jax.shard_map(
        functools.partial(on_device, mesh.shape["dp"], mesh.shape["tensor"]),
        mesh=mesh,
        in_specs=(
            P(("groups", "dp", "tensor"), None),
            P(),
            P(("groups", "dp"), "tensor"),
            P(None, "tensor"),
            P(("groups", "dp", "tensor"), None),
            P(("groups", "dp", "tensor"), None),
        ),
        out_specs=P("groups", ("dp", "tensor")),
        check_vma=False,
    )
```

```python
import functools

import jax
import jax.numpy as jnp
from jax import lax
from jax.experimental import pallas as pl
from jax.experimental.pallas import tpu as pltpu
from jax.sharding import PartitionSpec as P

R_IN = 64
R_OUT = 64
SEQ = 1024
ITERS = 4
LANES = 128
FEW = 4
NT = (((1,), (1,)), ((), ()))
HIGHEST = lax.Precision.HIGHEST
ANY_SPEC = pl.BlockSpec(memory_space=pl.ANY)
VMEM_SPEC = pl.BlockSpec(memory_space=pltpu.VMEM)
PARAMS = pltpu.CompilerParams(vmem_limit_bytes=16 * 2**20)
F32 = functools.partial(jax.ShapeDtypeStruct, dtype=jnp.float32)


def swap(value, axis, size, bit):
    return lax.ppermute(value, axis, [(i, i ^ bit) for i in range(size)])


def bits(size):
    return [1 << b for b in reversed(range(size.bit_length() - 1))]


def group_order(sizes):
    dp_size, tensor_size = sizes
    first = min(1, dp_size - 1) * tensor_size + (tensor_size - 1) // 2
    return [first] + [i for i in range(dp_size * tensor_size) if i != first]


def gather(value, sizes):
    order = group_order(sizes)
    value = jnp.broadcast_to(value[None], (len(order),) + value.shape)
    return lax.all_to_all(value, ("dp", "tensor"), 0, 0, axis_index_groups=[order])


def order_of(size):
    return (0, 2, 3, 1) if size == 4 else tuple(range(size))


def direct(value, axis, size, order):
    return [value] + [swap(value, axis, size, k) for k in order[1:]]


def sum_over(value, axis, size):
    if size > FEW:
        for bit in bits(size):
            value = value + swap(value, axis, size, bit)
        return value
    blocks = direct(value, axis, size, order_of(size))
    while len(blocks) > 1:
        blocks = [a + b for a, b in zip(blocks[::2], blocks[1::2])]
    return blocks[0]


def in_hbm(value):
    return pltpu.with_memory_space_constraint(value, pltpu.HBM)


def in_vmem(value):
    return pltpu.with_memory_space_constraint(value, pltpu.VMEM)


def dot_nt(a, b):
    return lax.dot_general(a, b, NT, precision=HIGHEST, preferred_element_type=jnp.float32)


def row_sum(values):
    return jnp.sum(values, axis=1, keepdims=True)


def stream_kernel(block, rows_ref, proj_ref, feats_ref, held, proj, turned, sems):
    count, half = proj_ref.shape[0], proj.shape[1]
    steps = held.shape[0] // block
    firsts = [
        pltpu.make_async_copy(
            proj_ref.at[:, pl.ds(h * half, half)], proj.at[pl.ds(h * count, count)], sems.at[h]
        )
        for h in range(2)
    ]

    def fetch(step):
        part = block // 4
        copies = []
        for q in range(4):
            span = pl.ds(pl.multiple_of(step * block + q * part, part), part)
            copies.append(
                pltpu.make_async_copy(rows_ref.at[span], held.at[span], sems.at[step * 4 + q + 2])
            )
        return copies

    for copy in firsts:
        copy.start()
    for step in range(steps):
        for copy in fetch(step):
            copy.start()
    for copy in firsts:
        copy.wait()
    turned[...] = proj[...].T

    @pl.loop(0, steps)
    def _(step):
        for copy in fetch(step):
            copy.wait()
        span = pl.ds(pl.multiple_of(step * block, block), block)
        left = jnp.dot(held[span, :half], turned[...], preferred_element_type=jnp.float32)
        right = jnp.dot(held[span, half:], turned[...], preferred_element_type=jnp.float32)
        feats_ref[:, span] = left.T[:count] + right.T[count:]


def features(rows, proj, block, limit, name):
    count, width = proj.shape
    return pl.pallas_call(
        functools.partial(stream_kernel, block),
        out_shape=pltpu.VMEM((count, rows.shape[0]), jnp.float32),
        in_specs=[ANY_SPEC] * 2,
        out_specs=VMEM_SPEC,
        scratch_shapes=[
            pltpu.VMEM(rows.shape, jnp.bfloat16),
            pltpu.VMEM((2 * count, width // 2), jnp.bfloat16),
            pltpu.VMEM((width // 2, 2 * count), jnp.bfloat16),
            pltpu.SemaphoreType.DMA((rows.shape[0] // block * 4 + 2,)),
        ],
        compiler_params=pltpu.CompilerParams(vmem_limit_bytes=limit * 2**20),
        name=name,
    )(in_hbm(rows), in_hbm(proj))


def split_kernel(prior_ref, upper_ref, lower_ref, held, sems):
    chunk = held.shape[1] // sems.shape[0]
    spans = [pl.ds(c * chunk, chunk) for c in range(sems.shape[0])]
    copies = [
        pltpu.make_async_copy(prior_ref.at[:, span], held.at[:, span], sems.at[c])
        for c, span in enumerate(spans)
    ]
    for copy in copies:
        copy.start()
    for copy, span in zip(copies, spans):
        copy.wait()
        block = held[:, span]
        upper = block.astype(jnp.bfloat16)
        upper_ref[:, span] = upper
        lower_ref[:, span] = (block - upper.astype(jnp.float32)).astype(jnp.bfloat16)


def split_prior(prior):
    return pl.pallas_call(
        split_kernel,
        out_shape=(pltpu.VMEM(prior.shape, jnp.bfloat16),) * 2,
        in_specs=[ANY_SPEC],
        out_specs=(VMEM_SPEC,) * 2,
        scratch_shapes=[pltpu.VMEM(prior.shape, jnp.float32), pltpu.SemaphoreType.DMA((8,))],
        compiler_params=PARAMS,
        name="split_prior",
    )(in_hbm(prior))


def partial_kernel(size, *refs):
    blocks, (out_ref, part_ref, held) = refs[:size], refs[size:]
    me = lax.axis_index("tensor")
    tokens = blocks[0].shape[1]
    for k, block in zip(order_of(size), blocks):
        start = pl.multiple_of((me ^ k) * tokens, LANES)
        held[:, pl.ds(start, tokens)] = block[...]
    for s in range(part_ref.shape[0]):
        span = slice(s * SEQ, (s + 1) * SEQ)
        outs = pieces_of(out_ref[:, span], 2)
        sums = dot_pieces(pieces_of(held[:, span], 2), outs, R_IN)
        part_ref[s] = (sums[:, :R_OUT] + sums[:, R_OUT:]) * (1.0 / SEQ)


def partial_vectors(blocks, out_local):
    seq_count = out_local.shape[1] // SEQ
    return pl.pallas_call(
        functools.partial(partial_kernel, len(blocks)),
        out_shape=F32((seq_count, R_IN, R_OUT)),
        in_specs=[VMEM_SPEC] * (len(blocks) + 1),
        out_specs=VMEM_SPEC,
        scratch_shapes=[pltpu.VMEM(out_local.shape, jnp.float32)],
        compiler_params=PARAMS,
        name="partial_vectors",
    )(*blocks, out_local)


def own_columns(ref, me, count):
    if count % LANES == 0:
        return ref[:, pl.ds(pl.multiple_of(me * count, LANES), count)]
    per = LANES // count
    held = ref[:, pl.ds(pl.multiple_of((me // per) * LANES, LANES), LANES)]
    return pltpu.roll(held, LANES - (me % per) * count, 1)[:, :count]


def pieces_of(values, count):
    held = []
    for _ in range(count):
        piece = values.astype(jnp.bfloat16)
        held.append(piece)
        values = values - piece.astype(jnp.float32)
    return jnp.concatenate(held, axis=0)


def dot_pieces(a, b, seqs):
    held = lax.dot_general(a, b, NT, preferred_element_type=jnp.float32)
    total = held[:seqs]
    for start in range(seqs, held.shape[0], seqs):
        total = total + held[start : start + seqs]
    return total


def apply_fisher(pieces, vectors_ref, vector_pieces, upper_ref, lower_ref, me):
    seqs = vectors_ref.shape[0]
    applied = dot_pieces(pieces, upper_ref[...], seqs)
    applied = applied + dot_pieces(pieces[: 2 * seqs], lower_ref[...], seqs)
    weights = dot_pieces(pieces, vector_pieces, seqs)
    weights = (weights[:, :seqs] + weights[:, seqs:]) * (1.0 / seqs)
    own = own_columns(vectors_ref, me, upper_ref.shape[0])
    return applied + jnp.dot(weights, own, precision=HIGHEST, preferred_element_type=jnp.float32)


def flat_index(tensor_size):
    return lax.axis_index("dp") * tensor_size + lax.axis_index("tensor")


def start_kernel(size, tensor_size, *refs):
    pieces, refs = refs[:size], refs[size:]
    upper_ref, lower_ref, vectors_ref, vector_pieces_ref, scale_ref, applied_ref, norm_ref, held = refs
    dp = lax.axis_index("dp")
    for k, piece in enumerate(pieces):
        held[dp ^ k] = piece[...]
    vectors = jnp.concatenate([held[k] for k in range(size)], axis=0)
    vectors_ref[...] = vectors
    split = pieces_of(vectors, 3)
    vector_pieces = split[: 2 * vectors.shape[0]]
    vector_pieces_ref[...] = vector_pieces
    norm = jnp.broadcast_to(row_sum(vectors * vectors), norm_ref.shape)
    norm_ref[...] = norm
    spread = jnp.sum(norm, axis=0, keepdims=True) * (1.0 / vectors.shape[0])
    scale_ref[...] = jnp.broadcast_to(1.0 / (1.0 + spread), scale_ref.shape)
    me = flat_index(tensor_size)
    applied_ref[...] = apply_fisher(split, vectors_ref, vector_pieces, upper_ref, lower_ref, me)


def start_cg(pieces, prior_pieces, tensor_size):
    size, seqs = len(pieces), len(pieces) * pieces[0].shape[0]
    rows, width = prior_pieces[0].shape
    vector_pieces = jax.ShapeDtypeStruct((2 * seqs, width), jnp.bfloat16)
    column = F32((seqs, LANES))
    return pl.pallas_call(
        functools.partial(start_kernel, size, tensor_size),
        out_shape=(F32((seqs, width)), vector_pieces, column, F32((seqs, rows)), column),
        in_specs=[VMEM_SPEC] * (size + 2),
        out_specs=(VMEM_SPEC,) * 5,
        scratch_shapes=[pltpu.VMEM((size,) + pieces[0].shape, jnp.float32)],
        compiler_params=PARAMS,
        name="cg_start",
    )(*pieces, *prior_pieces)


def step_kernel(sizes, first, last, *refs):
    blocks_ref, upper_ref, lower_ref, vectors_ref, vector_pieces_ref, scale_ref = refs[:6]
    norm_ref, fisher_direction_ref = refs[6:8]
    refs = refs[8:]
    if not first:
        fisher_residual_ref, direction_ref, residual_ref, solution_ref = refs[:4]
        refs = refs[4:]
    if last:
        queries_ref, curvature_out, norm_out, solved_out, along_out, held = refs
    else:
        fisher_direction_out, norm_out, fisher_residual_out, direction_out, residual_out, solution_out, held = refs
    me = flat_index(sizes[1])
    rows = blocks_ref.shape[2]
    for i, k in enumerate(group_order(sizes)):
        held[:, k * rows : (k + 1) * rows] = blocks_ref[i]
    applied = held[...]
    scale = scale_ref[...][:, :1]
    twice = apply_fisher(
        pieces_of(scale * applied, 3), vectors_ref, vector_pieces_ref[...], upper_ref, lower_ref, me
    )
    direction = vectors_ref[...] if first else direction_ref[...]
    residual = direction if first else residual_ref[...]
    norm = norm_ref[...][:, :1]
    step = norm / row_sum(direction * applied)
    solution = step * direction
    if not first:
        solution = solution_ref[...] + solution
    residual = residual - step * applied
    norm_next = row_sum(residual * residual)
    share = norm_next / norm
    direction = residual + share * direction
    fisher_direction = fisher_direction_ref[...]
    fisher_residual = (fisher_direction if first else fisher_residual_ref[...]) - (step / scale) * twice
    fisher_direction = fisher_residual + share * fisher_direction
    norm_out[...] = jnp.broadcast_to(norm_next, norm_out.shape)
    if last:
        held[...] = direction
        own = own_columns(held, me, rows)
        curvature_out[...] = jnp.broadcast_to(row_sum(own * fisher_direction), curvature_out.shape)
        seqs = direction.shape[0]
        solved = jnp.concatenate([solution, direction], axis=0)
        scores = dot_pieces(pieces_of(solved, 3), queries_ref[...], 2 * seqs)
        solved_out[...] = scores[:seqs]
        along_out[...] = scores[seqs:]
    else:
        fisher_direction_out[...] = fisher_direction
        fisher_residual_out[...] = fisher_residual
        residual_out[...] = residual
        direction_out[...] = direction
        solution_out[...] = solution


def step_cg(blocks, fixed, norm, state, queries, sizes):
    first, last = len(state) == 1, queries is not None
    whole, rows = F32(fixed[2].shape), F32(state[0].shape)
    column = F32(norm.shape)
    operands = [blocks, *fixed, norm, *state]
    out_shape = (rows, column, rows, whole, whole, whole)
    if last:
        operands.append(queries)
        scores = F32((whole.shape[0], queries.shape[0]))
        out_shape = (column, column, scores, scores)
    return pl.pallas_call(
        functools.partial(step_kernel, sizes, first, last),
        out_shape=out_shape,
        in_specs=[VMEM_SPEC] * len(operands),
        out_specs=(VMEM_SPEC,) * len(out_shape),
        scratch_shapes=[pltpu.VMEM(whole.shape, jnp.float32)],
        compiler_params=PARAMS,
        name="cg_step",
    )(*operands)


def combine_kernel(curvature_ref, norm_ref, solved_ref, along_ref, scores_ref):
    step = norm_ref[...] / jnp.sum(curvature_ref[...], axis=0)
    scores_ref[...] = solved_ref[...] + step[:, :1] * along_ref[...]


def combine(curvature, norm, solved, along):
    return pl.pallas_call(
        combine_kernel,
        out_shape=F32(solved.shape),
        in_specs=[VMEM_SPEC] * 4,
        out_specs=VMEM_SPEC,
        compiler_params=PARAMS,
        name="combine",
    )(curvature, norm, solved, along)


def on_device(dp_size, tensor_size, inputs, in_proj, out_grads, out_proj, prior, queries):
    width = R_IN * R_OUT
    sizes = dp_size, tensor_size
    in_blocks = direct(features(inputs, in_proj, LANES, 20, "in_features"), "tensor", tensor_size, order_of(tensor_size))
    out_local = features(out_grads, out_proj, 2 * LANES, 44, "out_features")
    partial = partial_vectors(in_blocks, out_local).reshape(-1, width)
    prior, partial = lax.optimization_barrier((prior, partial))
    own_vectors = sum_over(partial, "tensor", tensor_size)
    own_vectors, prior_pieces = lax.optimization_barrier((own_vectors, split_prior(prior)))
    pieces = direct(own_vectors, "dp", dp_size, range(dp_size))
    prior_pieces = [in_vmem(piece) for piece in prior_pieces]
    vectors, vector_pieces, scale, applied_rows, norm = start_cg(pieces, prior_pieces, tensor_size)
    fixed = (*prior_pieces, vectors, vector_pieces, scale)
    state = [applied_rows]
    for iteration in range(1, ITERS - 1):
        blocks = gather(state[0], sizes)
        applied_rows, norm, *others = step_cg(blocks, fixed, norm, state, None, sizes)
        state = [applied_rows, *others]
    blocks = gather(state[0], sizes)
    curvature, norm, solved, along = step_cg(blocks, fixed, norm, state, queries, sizes)
    return combine(gather(curvature, sizes), norm, solved, along)


def solution(mesh):
    return jax.shard_map(
        functools.partial(on_device, mesh.shape["dp"], mesh.shape["tensor"]),
        mesh=mesh,
        in_specs=(
            P(("groups", "dp", "tensor"), None),
            P(),
            P(("groups", "dp"), "tensor"),
            P(None, "tensor"),
            P(("groups", "dp", "tensor"), None),
            P(("groups", "dp", "tensor"), None),
        ),
        out_specs=P("groups", ("dp", "tensor")),
        check_vma=False,
    )
```

```python
import functools

import jax
import jax.numpy as jnp
from jax import lax
from jax.experimental import pallas as pl
from jax.experimental.pallas import tpu as pltpu
from jax.sharding import PartitionSpec as P

R_IN = 64
R_OUT = 64
SEQ = 1024
ITERS = 4
LANES = 128
FEW = 4
NT = (((1,), (1,)), ((), ()))
HIGHEST = lax.Precision.HIGHEST
ANY_SPEC = pl.BlockSpec(memory_space=pl.ANY)
VMEM_SPEC = pl.BlockSpec(memory_space=pltpu.VMEM)
PARAMS = pltpu.CompilerParams(vmem_limit_bytes=16 * 2**20)
F32 = functools.partial(jax.ShapeDtypeStruct, dtype=jnp.float32)


def swap(value, axis, size, bit):
    return lax.ppermute(value, axis, [(i, i ^ bit) for i in range(size)])


def bits(size):
    return [1 << b for b in reversed(range(size.bit_length() - 1))]


def group_order(sizes):
    dp_size, tensor_size = sizes
    first = min(1, dp_size - 1) * tensor_size + (tensor_size - 1) // 2
    return [first] + [i for i in range(dp_size * tensor_size) if i != first]


def gather(value, sizes):
    order = group_order(sizes)
    value = jnp.broadcast_to(value[None], (len(order),) + value.shape)
    return lax.all_to_all(value, ("dp", "tensor"), 0, 0, axis_index_groups=[order])


def order_of(size):
    return (0, 2, 3, 1) if size == 4 else tuple(range(size))


def direct(value, axis, size, order):
    return [value] + [swap(value, axis, size, k) for k in order[1:]]


def shifted(value, axis, size):
    last, first_ones, last_ones = size - 1, [], []
    for k in reversed(range(1, size)):
        pairs = [((i + k) % size, i) for i in range(size)]
        kept = [pair for pair in pairs if pair[1] != last or k == 1]
        first_ones.append(lax.ppermute(value, axis, kept))
        if k > 1:
            last_ones.append(lax.ppermute(value, axis, pairs[last:]))
    return [value, *reversed(last_ones), *reversed(first_ones)]


def sum_over(value, axis, size):
    if size > FEW:
        for bit in bits(size):
            value = value + swap(value, axis, size, bit)
        return value
    blocks = direct(value, axis, size, order_of(size))
    while len(blocks) > 1:
        blocks = [a + b for a, b in zip(blocks[::2], blocks[1::2])]
    return blocks[0]


def in_hbm(value):
    return pltpu.with_memory_space_constraint(value, pltpu.HBM)


def in_vmem(value):
    return pltpu.with_memory_space_constraint(value, pltpu.VMEM)


def dot_nt(a, b):
    return lax.dot_general(a, b, NT, precision=HIGHEST, preferred_element_type=jnp.float32)


def row_sum(values):
    return jnp.sum(values, axis=1, keepdims=True)


def stream_kernel(block, rows_ref, proj_ref, feats_ref, held, proj, turned, sems):
    count, half = proj_ref.shape[0], proj.shape[1]
    steps = held.shape[0] // block
    firsts = [
        pltpu.make_async_copy(
            proj_ref.at[:, pl.ds(h * half, half)], proj.at[pl.ds(h * count, count)], sems.at[steps + h]
        )
        for h in range(2)
    ]

    def fetch(step):
        span = pl.ds(pl.multiple_of(step * block, block), block)
        return pltpu.make_async_copy(rows_ref.at[span], held.at[span], sems.at[step])

    for copy in firsts:
        copy.start()
    for step in range(steps):
        fetch(step).start()
    for copy in firsts:
        copy.wait()
    turned[...] = proj[...].T

    @pl.loop(0, steps)
    def _(step):
        fetch(step).wait()
        span = pl.ds(pl.multiple_of(step * block, block), block)
        left = jnp.dot(held[span, :half], turned[...], preferred_element_type=jnp.float32)
        right = jnp.dot(held[span, half:], turned[...], preferred_element_type=jnp.float32)
        feats_ref[:, span] = left.T[:count] + right.T[count:]


def features(rows, proj, block, limit, name):
    count, width = proj.shape
    return pl.pallas_call(
        functools.partial(stream_kernel, block),
        out_shape=pltpu.VMEM((count, rows.shape[0]), jnp.float32),
        in_specs=[ANY_SPEC] * 2,
        out_specs=VMEM_SPEC,
        scratch_shapes=[
            pltpu.VMEM(rows.shape, jnp.bfloat16),
            pltpu.VMEM((2 * count, width // 2), jnp.bfloat16),
            pltpu.VMEM((width // 2, 2 * count), jnp.bfloat16),
            pltpu.SemaphoreType.DMA((rows.shape[0] // block + 2,)),
        ],
        compiler_params=pltpu.CompilerParams(vmem_limit_bytes=limit * 2**20),
        name=name,
    )(in_hbm(rows), in_hbm(proj))


def split_kernel(prior_ref, upper_ref, lower_ref, held, sems):
    chunk = held.shape[1] // sems.shape[0]
    spans = [pl.ds(c * chunk, chunk) for c in range(sems.shape[0])]
    copies = [
        pltpu.make_async_copy(prior_ref.at[:, span], held.at[:, span], sems.at[c])
        for c, span in enumerate(spans)
    ]
    for copy in copies:
        copy.start()
    for copy, span in zip(copies, spans):
        copy.wait()
        block = held[:, span]
        upper = block.astype(jnp.bfloat16)
        upper_ref[:, span] = upper
        lower_ref[:, span] = (block - upper.astype(jnp.float32)).astype(jnp.bfloat16)


def split_prior(prior):
    return pl.pallas_call(
        split_kernel,
        out_shape=(pltpu.VMEM(prior.shape, jnp.bfloat16),) * 2,
        in_specs=[ANY_SPEC],
        out_specs=(VMEM_SPEC,) * 2,
        scratch_shapes=[pltpu.VMEM(prior.shape, jnp.float32), pltpu.SemaphoreType.DMA((8,))],
        compiler_params=PARAMS,
        name="split_prior",
    )(in_hbm(prior))


def partial_kernel(size, few, *refs):
    blocks, (out_ref, part_ref, held) = refs[:-3], refs[-3:]
    me = lax.axis_index("tensor")
    tokens = blocks[0].shape[1]

    def place(k, block):
        source = lax.rem(me + k, size) if few else me ^ k
        held[:, pl.ds(pl.multiple_of(source * tokens, LANES), tokens)] = block

    place(0, blocks[0][...])
    rest = blocks[1:]
    if few:
        extra, rest = rest[: size - 2], rest[size - 2 :]
    for k, block in enumerate(rest, 1):
        block = block[...]
        if few and k > 1:
            block = block + extra[k - 2][...]
        place(k, block)
    for s in range(part_ref.shape[0]):
        span = slice(s * SEQ, (s + 1) * SEQ)
        outs = pieces_of(out_ref[:, span], 2)
        sums = dot_pieces(pieces_of(held[:, span], 2), outs, R_IN)
        part_ref[s] = (sums[:, :R_OUT] + sums[:, R_OUT:]) * (1.0 / SEQ)


def partial_vectors(blocks, out_local, size, few):
    seq_count = out_local.shape[1] // SEQ
    return pl.pallas_call(
        functools.partial(partial_kernel, size, few),
        out_shape=F32((seq_count, R_IN, R_OUT)),
        in_specs=[VMEM_SPEC] * (len(blocks) + 1),
        out_specs=VMEM_SPEC,
        scratch_shapes=[pltpu.VMEM(out_local.shape, jnp.float32)],
        compiler_params=PARAMS,
        name="partial_vectors",
    )(*blocks, out_local)


def own_columns(ref, me, count):
    if count % LANES == 0:
        return ref[:, pl.ds(pl.multiple_of(me * count, LANES), count)]
    per = LANES // count
    held = ref[:, pl.ds(pl.multiple_of((me // per) * LANES, LANES), LANES)]
    return pltpu.roll(held, LANES - (me % per) * count, 1)[:, :count]


def pieces_of(values, count):
    held = []
    for _ in range(count):
        piece = values.astype(jnp.bfloat16)
        held.append(piece)
        values = values - piece.astype(jnp.float32)
    return jnp.concatenate(held, axis=0)


def dot_pieces(a, b, seqs):
    held = lax.dot_general(a, b, NT, preferred_element_type=jnp.float32)
    total = held[:seqs]
    for start in range(seqs, held.shape[0], seqs):
        total = total + held[start : start + seqs]
    return total


def apply_fisher(pieces, vectors_ref, vector_pieces, upper_ref, lower_ref, me):
    seqs = vectors_ref.shape[0]
    applied = dot_pieces(pieces, upper_ref[...], seqs)
    applied = applied + dot_pieces(pieces[: 2 * seqs], lower_ref[...], seqs)
    weights = dot_pieces(pieces, vector_pieces, seqs)
    weights = (weights[:, :seqs] + weights[:, seqs:]) * (1.0 / seqs)
    own = own_columns(vectors_ref, me, upper_ref.shape[0])
    return applied + jnp.dot(weights, own, precision=HIGHEST, preferred_element_type=jnp.float32)


def flat_index(tensor_size):
    return lax.axis_index("dp") * tensor_size + lax.axis_index("tensor")


def start_kernel(size, tensor_size, *refs):
    pieces, refs = refs[:size], refs[size:]
    upper_ref, lower_ref, vectors_ref, vector_pieces_ref, scale_ref, applied_ref, norm_ref, held = refs
    dp = lax.axis_index("dp")
    for k, piece in enumerate(pieces):
        held[dp ^ k] = piece[...]
    vectors = jnp.concatenate([held[k] for k in range(size)], axis=0)
    vectors_ref[...] = vectors
    split = pieces_of(vectors, 3)
    vector_pieces = split[: 2 * vectors.shape[0]]
    vector_pieces_ref[...] = vector_pieces
    norm = jnp.broadcast_to(row_sum(vectors * vectors), norm_ref.shape)
    norm_ref[...] = norm
    spread = jnp.sum(norm, axis=0, keepdims=True) * (1.0 / vectors.shape[0])
    scale_ref[...] = jnp.broadcast_to(1.0 / (1.0 + spread), scale_ref.shape)
    me = flat_index(tensor_size)
    applied_ref[...] = apply_fisher(split, vectors_ref, vector_pieces, upper_ref, lower_ref, me)


def start_cg(pieces, prior_pieces, tensor_size):
    size, seqs = len(pieces), len(pieces) * pieces[0].shape[0]
    rows, width = prior_pieces[0].shape
    vector_pieces = jax.ShapeDtypeStruct((2 * seqs, width), jnp.bfloat16)
    column = F32((seqs, LANES))
    return pl.pallas_call(
        functools.partial(start_kernel, size, tensor_size),
        out_shape=(F32((seqs, width)), vector_pieces, column, F32((seqs, rows)), column),
        in_specs=[VMEM_SPEC] * (size + 2),
        out_specs=(VMEM_SPEC,) * 5,
        scratch_shapes=[pltpu.VMEM((size,) + pieces[0].shape, jnp.float32)],
        compiler_params=PARAMS,
        name="cg_start",
    )(*pieces, *prior_pieces)


def step_kernel(sizes, first, last, *refs):
    blocks_ref, upper_ref, lower_ref, vectors_ref, vector_pieces_ref, scale_ref = refs[:6]
    norm_ref, fisher_direction_ref = refs[6:8]
    refs = refs[8:]
    if not first:
        fisher_residual_ref, direction_ref, residual_ref, solution_ref = refs[:4]
        refs = refs[4:]
    if last:
        queries_ref, curvature_out, norm_out, solved_out, along_out, held = refs
    else:
        fisher_direction_out, norm_out, fisher_residual_out, direction_out, residual_out, solution_out, held = refs
    me = flat_index(sizes[1])
    rows = blocks_ref.shape[2]
    for i, k in enumerate(group_order(sizes)):
        held[:, k * rows : (k + 1) * rows] = blocks_ref[i]
    applied = held[...]
    scale = scale_ref[...][:, :1]
    twice = apply_fisher(
        pieces_of(scale * applied, 3), vectors_ref, vector_pieces_ref[...], upper_ref, lower_ref, me
    )
    direction = vectors_ref[...] if first else direction_ref[...]
    residual = direction if first else residual_ref[...]
    norm = norm_ref[...][:, :1]
    step = norm / row_sum(direction * applied)
    solution = step * direction
    if not first:
        solution = solution_ref[...] + solution
    residual = residual - step * applied
    norm_next = row_sum(residual * residual)
    share = norm_next / norm
    direction = residual + share * direction
    fisher_direction = fisher_direction_ref[...]
    fisher_residual = (fisher_direction if first else fisher_residual_ref[...]) - (step / scale) * twice
    fisher_direction = fisher_residual + share * fisher_direction
    norm_out[...] = jnp.broadcast_to(norm_next, norm_out.shape)
    if last:
        held[...] = direction
        own = own_columns(held, me, rows)
        curvature_out[...] = jnp.broadcast_to(row_sum(own * fisher_direction), curvature_out.shape)
        seqs = direction.shape[0]
        solved = jnp.concatenate([solution, direction], axis=0)
        scores = dot_pieces(pieces_of(solved, 3), queries_ref[...], 2 * seqs)
        solved_out[...] = scores[:seqs]
        along_out[...] = scores[seqs:]
    else:
        fisher_direction_out[...] = fisher_direction
        fisher_residual_out[...] = fisher_residual
        residual_out[...] = residual
        direction_out[...] = direction
        solution_out[...] = solution


def step_cg(blocks, fixed, norm, state, queries, sizes):
    first, last = len(state) == 1, queries is not None
    whole, rows = F32(fixed[2].shape), F32(state[0].shape)
    column = F32(norm.shape)
    operands = [blocks, *fixed, norm, *state]
    out_shape = (rows, column, rows, whole, whole, whole)
    if last:
        operands.append(queries)
        scores = F32((whole.shape[0], queries.shape[0]))
        out_shape = (column, column, scores, scores)
    return pl.pallas_call(
        functools.partial(step_kernel, sizes, first, last),
        out_shape=out_shape,
        in_specs=[VMEM_SPEC] * len(operands),
        out_specs=(VMEM_SPEC,) * len(out_shape),
        scratch_shapes=[pltpu.VMEM(whole.shape, jnp.float32)],
        compiler_params=PARAMS,
        name="cg_step",
    )(*operands)


def combine_kernel(curvature_ref, norm_ref, solved_ref, along_ref, scores_ref):
    step = norm_ref[...] / jnp.sum(curvature_ref[...], axis=0)
    scores_ref[...] = solved_ref[...] + step[:, :1] * along_ref[...]


def combine(curvature, norm, solved, along):
    return pl.pallas_call(
        combine_kernel,
        out_shape=F32(solved.shape),
        in_specs=[VMEM_SPEC] * 4,
        out_specs=VMEM_SPEC,
        compiler_params=PARAMS,
        name="combine",
    )(curvature, norm, solved, along)


def on_device(dp_size, tensor_size, inputs, in_proj, out_grads, out_proj, prior, queries):
    width = R_IN * R_OUT
    sizes = dp_size, tensor_size
    in_local = features(inputs, in_proj, LANES, 20, "in_features")
    few = tensor_size <= FEW
    in_blocks = shifted(in_local, "tensor", tensor_size) if few else direct(in_local, "tensor", tensor_size, range(tensor_size))
    out_local = features(out_grads, out_proj, 2 * LANES, 44, "out_features")
    partial = partial_vectors(in_blocks, out_local, tensor_size, few).reshape(-1, width)
    prior, partial = lax.optimization_barrier((prior, partial))
    own_vectors = sum_over(partial, "tensor", tensor_size)
    own_vectors, prior_pieces = lax.optimization_barrier((own_vectors, split_prior(prior)))
    pieces = direct(own_vectors, "dp", dp_size, range(dp_size))
    prior_pieces = [in_vmem(piece) for piece in prior_pieces]
    vectors, vector_pieces, scale, applied_rows, norm = start_cg(pieces, prior_pieces, tensor_size)
    fixed = (*prior_pieces, vectors, vector_pieces, scale)
    state = [applied_rows]
    for iteration in range(1, ITERS - 1):
        blocks = gather(state[0], sizes)
        applied_rows, norm, *others = step_cg(blocks, fixed, norm, state, None, sizes)
        state = [applied_rows, *others]
    blocks = gather(state[0], sizes)
    curvature, norm, solved, along = step_cg(blocks, fixed, norm, state, queries, sizes)
    return combine(gather(curvature, sizes), norm, solved, along)


def solution(mesh):
    return jax.shard_map(
        functools.partial(on_device, mesh.shape["dp"], mesh.shape["tensor"]),
        mesh=mesh,
        in_specs=(
            P(("groups", "dp", "tensor"), None),
            P(),
            P(("groups", "dp"), "tensor"),
            P(None, "tensor"),
            P(("groups", "dp", "tensor"), None),
            P(("groups", "dp", "tensor"), None),
        ),
        out_specs=P("groups", ("dp", "tensor")),
        check_vma=False,
    )
```

```python
import functools

import jax
import jax.numpy as jnp
from jax import lax
from jax.experimental import pallas as pl
from jax.experimental.pallas import tpu as pltpu
from jax.sharding import PartitionSpec as P

R_IN = 64
R_OUT = 64
SEQ = 1024
ITERS = 4
LANES = 128
FEW = 4
NT = (((1,), (1,)), ((), ()))
HIGHEST = lax.Precision.HIGHEST
ANY_SPEC = pl.BlockSpec(memory_space=pl.ANY)
VMEM_SPEC = pl.BlockSpec(memory_space=pltpu.VMEM)
PARAMS = pltpu.CompilerParams(vmem_limit_bytes=16 * 2**20)
F32 = functools.partial(jax.ShapeDtypeStruct, dtype=jnp.float32)


def swap(value, axis, size, bit):
    return lax.ppermute(value, axis, [(i, i ^ bit) for i in range(size)])


def bits(size):
    return [1 << b for b in reversed(range(size.bit_length() - 1))]


def group_order(sizes):
    dp_size, tensor_size = sizes
    first = min(1, dp_size - 1) * tensor_size + (tensor_size - 1) // 2
    return [first] + [i for i in range(dp_size * tensor_size) if i != first]


def gather(value, sizes):
    order = group_order(sizes)
    value = jnp.broadcast_to(value[None], (len(order),) + value.shape)
    return lax.all_to_all(value, ("dp", "tensor"), 0, 0, axis_index_groups=[order])


def order_of(size):
    return (0, 2, 3, 1) if size == 4 else tuple(range(size))


def direct(value, axis, size, order):
    return [value] + [swap(value, axis, size, k) for k in order[1:]]


def sum_over(value, axis, size):
    if size > FEW:
        for bit in bits(size):
            value = value + swap(value, axis, size, bit)
        return value
    blocks = direct(value, axis, size, order_of(size))
    while len(blocks) > 1:
        blocks = [a + b for a, b in zip(blocks[::2], blocks[1::2])]
    return blocks[0]


def in_hbm(value):
    return pltpu.with_memory_space_constraint(value, pltpu.HBM)


def in_vmem(value):
    return pltpu.with_memory_space_constraint(value, pltpu.VMEM)


def dot_nt(a, b):
    return lax.dot_general(a, b, NT, precision=HIGHEST, preferred_element_type=jnp.float32)


def row_sum(values):
    return jnp.sum(values, axis=1, keepdims=True)


def stream_kernel(block, rows_ref, proj_ref, feats_ref, held, proj, turned, sems):
    count, half = proj_ref.shape[0], proj.shape[1]
    steps = held.shape[0] // block
    firsts = [
        pltpu.make_async_copy(
            proj_ref.at[:, pl.ds(h * half, half)], proj.at[pl.ds(h * count, count)], sems.at[steps + h]
        )
        for h in range(2)
    ]

    def fetch(step):
        span = pl.ds(pl.multiple_of(step * block, block), block)
        return pltpu.make_async_copy(rows_ref.at[span], held.at[span], sems.at[step])

    for copy in firsts:
        copy.start()
    for step in range(steps):
        fetch(step).start()
    for copy in firsts:
        copy.wait()
    turned[...] = proj[...].T

    @pl.loop(0, steps)
    def _(step):
        fetch(step).wait()
        span = pl.ds(pl.multiple_of(step * block, block), block)
        left = jnp.dot(held[span, :half], turned[...], preferred_element_type=jnp.float32)
        right = jnp.dot(held[span, half:], turned[...], preferred_element_type=jnp.float32)
        feats_ref[:, span] = left.T[:count] + right.T[count:]


def features(rows, proj, block, limit, name):
    count, width = proj.shape
    return pl.pallas_call(
        functools.partial(stream_kernel, block),
        out_shape=pltpu.VMEM((count, rows.shape[0]), jnp.float32),
        in_specs=[ANY_SPEC] * 2,
        out_specs=VMEM_SPEC,
        scratch_shapes=[
            pltpu.VMEM(rows.shape, jnp.bfloat16),
            pltpu.VMEM((2 * count, width // 2), jnp.bfloat16),
            pltpu.VMEM((width // 2, 2 * count), jnp.bfloat16),
            pltpu.SemaphoreType.DMA((rows.shape[0] // block + 2,)),
        ],
        compiler_params=pltpu.CompilerParams(vmem_limit_bytes=limit * 2**20),
        name=name,
    )(in_hbm(rows), in_hbm(proj))


def split_kernel(prior_ref, queries_ref, upper_ref, lower_ref, turned_ref, held, sems):
    chunk = held.shape[1] // sems.shape[0]
    spans = [pl.ds(c * chunk, chunk) for c in range(sems.shape[0])]
    copies = [
        pltpu.make_async_copy(prior_ref.at[:, span], held.at[:, span], sems.at[c])
        for c, span in enumerate(spans)
    ]
    for copy in copies:
        copy.start()
    turned_ref[...] = queries_ref[...].T
    for copy, span in zip(copies, spans):
        copy.wait()
        block = held[:, span]
        upper = block.astype(jnp.bfloat16)
        upper_ref[:, span] = upper
        lower_ref[:, span] = (block - upper.astype(jnp.float32)).astype(jnp.bfloat16)


def split_prior(prior, queries):
    return pl.pallas_call(
        split_kernel,
        out_shape=(
            pltpu.VMEM(prior.shape, jnp.bfloat16),
            pltpu.VMEM(prior.shape, jnp.bfloat16),
            pltpu.VMEM(queries.shape[::-1], jnp.bfloat16),
        ),
        in_specs=[ANY_SPEC, VMEM_SPEC],
        out_specs=(VMEM_SPEC,) * 3,
        scratch_shapes=[pltpu.VMEM(prior.shape, jnp.float32), pltpu.SemaphoreType.DMA((8,))],
        compiler_params=PARAMS,
        name="split_prior",
    )(in_hbm(prior), queries)


def partial_kernel(size, *refs):
    blocks, (out_ref, part_ref, held) = refs[:size], refs[size:]
    me = lax.axis_index("tensor")
    tokens = blocks[0].shape[1]
    for k, block in zip(order_of(size), blocks):
        start = pl.multiple_of((me ^ k) * tokens, LANES)
        held[:, pl.ds(start, tokens)] = block[...]
    for s in range(part_ref.shape[0]):
        span = slice(s * SEQ, (s + 1) * SEQ)
        outs = pieces_of(out_ref[:, span], 2)
        sums = dot_pieces(pieces_of(held[:, span], 2), outs, R_IN)
        part_ref[s] = (sums[:, :R_OUT] + sums[:, R_OUT:]) * (1.0 / SEQ)


def partial_vectors(blocks, out_local):
    seq_count = out_local.shape[1] // SEQ
    return pl.pallas_call(
        functools.partial(partial_kernel, len(blocks)),
        out_shape=F32((seq_count, R_IN, R_OUT)),
        in_specs=[VMEM_SPEC] * (len(blocks) + 1),
        out_specs=VMEM_SPEC,
        scratch_shapes=[pltpu.VMEM(out_local.shape, jnp.float32)],
        compiler_params=PARAMS,
        name="partial_vectors",
    )(*blocks, out_local)


def own_columns(ref, me, count):
    if count % LANES == 0:
        return ref[:, pl.ds(pl.multiple_of(me * count, LANES), count)]
    per = LANES // count
    held = ref[:, pl.ds(pl.multiple_of((me // per) * LANES, LANES), LANES)]
    return pltpu.roll(held, LANES - (me % per) * count, 1)[:, :count]


def pieces_of(values, count):
    held = []
    for _ in range(count):
        piece = values.astype(jnp.bfloat16)
        held.append(piece)
        values = values - piece.astype(jnp.float32)
    return jnp.concatenate(held, axis=0)


def dot_pieces(a, b, seqs):
    held = lax.dot_general(a, b, NT, preferred_element_type=jnp.float32)
    total = held[:seqs]
    for start in range(seqs, held.shape[0], seqs):
        total = total + held[start : start + seqs]
    return total


def apply_fisher(x, vectors_ref, upper_ref, lower_ref, me):
    seqs = vectors_ref.shape[0]
    pieces = pieces_of(x, 3)
    applied = dot_pieces(pieces, upper_ref[...], seqs)
    applied = applied + dot_pieces(pieces[: 2 * seqs], lower_ref[...], seqs)
    own = own_columns(vectors_ref, me, upper_ref.shape[0])
    for s in range(seqs):
        weight = row_sum(x * vectors_ref[s : s + 1, :]) * (1.0 / seqs)
        applied = applied + weight * own[s : s + 1, :]
    return applied


def flat_index(tensor_size):
    return lax.axis_index("dp") * tensor_size + lax.axis_index("tensor")


def start_kernel(size, tensor_size, *refs):
    pieces, refs = refs[:size], refs[size:]
    upper_ref, lower_ref, vectors_ref, scale_ref, applied_ref, norm_ref, held = refs
    dp = lax.axis_index("dp")
    for k, piece in enumerate(pieces):
        held[dp ^ k] = piece[...]
    vectors = jnp.concatenate([held[k] for k in range(size)], axis=0)
    vectors_ref[...] = vectors
    norm = jnp.broadcast_to(row_sum(vectors * vectors), norm_ref.shape)
    norm_ref[...] = norm
    spread = jnp.sum(norm, axis=0, keepdims=True) * (1.0 / vectors.shape[0])
    scale_ref[...] = jnp.broadcast_to(1.0 / (1.0 + spread), scale_ref.shape)
    me = flat_index(tensor_size)
    applied_ref[...] = apply_fisher(vectors, vectors_ref, upper_ref, lower_ref, me)


def start_cg(pieces, prior_pieces, tensor_size):
    size, seqs = len(pieces), len(pieces) * pieces[0].shape[0]
    rows, width = prior_pieces[0].shape
    column = F32((seqs, LANES))
    return pl.pallas_call(
        functools.partial(start_kernel, size, tensor_size),
        out_shape=(F32((seqs, width)), column, F32((seqs, rows)), column),
        in_specs=[VMEM_SPEC] * (size + 2),
        out_specs=(VMEM_SPEC,) * 4,
        scratch_shapes=[pltpu.VMEM((size,) + pieces[0].shape, jnp.float32)],
        compiler_params=PARAMS,
        name="cg_start",
    )(*pieces, *prior_pieces)


def step_kernel(sizes, first, last, *refs):
    blocks_ref, upper_ref, lower_ref, vectors_ref, scale_ref, norm_ref, fisher_direction_ref = refs[:7]
    refs = refs[7:]
    if not first:
        fisher_residual_ref, direction_ref, residual_ref, solution_ref = refs[:4]
        refs = refs[4:]
    if last:
        queries_ref, curvature_out, norm_out, solved_out, along_out, held = refs
    else:
        fisher_direction_out, norm_out, fisher_residual_out, direction_out, residual_out, solution_out, held = refs
    me = flat_index(sizes[1])
    rows = blocks_ref.shape[2]
    for i, k in enumerate(group_order(sizes)):
        held[:, k * rows : (k + 1) * rows] = blocks_ref[i]
    applied = held[...]
    scale = scale_ref[...][:, :1]
    twice = apply_fisher(scale * applied, vectors_ref, upper_ref, lower_ref, me)
    direction = vectors_ref[...] if first else direction_ref[...]
    residual = direction if first else residual_ref[...]
    norm = norm_ref[...][:, :1]
    step = norm / row_sum(direction * applied)
    solution = step * direction
    if not first:
        solution = solution_ref[...] + solution
    residual = residual - step * applied
    norm_next = row_sum(residual * residual)
    share = norm_next / norm
    direction = residual + share * direction
    fisher_direction = fisher_direction_ref[...]
    fisher_residual = (fisher_direction if first else fisher_residual_ref[...]) - (step / scale) * twice
    fisher_direction = fisher_residual + share * fisher_direction
    norm_out[...] = jnp.broadcast_to(norm_next, norm_out.shape)
    if last:
        held[...] = direction
        own = own_columns(held, me, rows)
        curvature_out[...] = jnp.broadcast_to(row_sum(own * fisher_direction), curvature_out.shape)
        seqs = direction.shape[0]
        solved = jnp.concatenate([solution, direction], axis=0)
        parts = jnp.dot(pieces_of(solved, 3), queries_ref[...], preferred_element_type=jnp.float32)
        scores = parts[: 2 * seqs] + parts[2 * seqs : 4 * seqs] + parts[4 * seqs :]
        solved_out[...] = scores[:seqs]
        along_out[...] = scores[seqs:]
    else:
        fisher_direction_out[...] = fisher_direction
        fisher_residual_out[...] = fisher_residual
        residual_out[...] = residual
        direction_out[...] = direction
        solution_out[...] = solution


def step_cg(blocks, fixed, norm, state, queries, sizes):
    first, last = len(state) == 1, queries is not None
    whole, rows = F32(fixed[2].shape), F32(state[0].shape)
    column = F32(norm.shape)
    operands = [blocks, *fixed, norm, *state]
    out_shape = (rows, column, rows, whole, whole, whole)
    if last:
        operands.append(queries)
        scores = F32((whole.shape[0], queries.shape[1]))
        out_shape = (column, column, scores, scores)
    return pl.pallas_call(
        functools.partial(step_kernel, sizes, first, last),
        out_shape=out_shape,
        in_specs=[VMEM_SPEC] * len(operands),
        out_specs=(VMEM_SPEC,) * len(out_shape),
        scratch_shapes=[pltpu.VMEM(whole.shape, jnp.float32)],
        compiler_params=PARAMS,
        name="cg_step",
    )(*operands)


def combine_kernel(curvature_ref, norm_ref, solved_ref, along_ref, scores_ref):
    step = norm_ref[...] / jnp.sum(curvature_ref[...], axis=0)
    scores_ref[...] = solved_ref[...] + step[:, :1] * along_ref[...]


def combine(curvature, norm, solved, along):
    return pl.pallas_call(
        combine_kernel,
        out_shape=F32(solved.shape),
        in_specs=[VMEM_SPEC] * 4,
        out_specs=VMEM_SPEC,
        compiler_params=PARAMS,
        name="combine",
    )(curvature, norm, solved, along)


def on_device(dp_size, tensor_size, inputs, in_proj, out_grads, out_proj, prior, queries):
    width = R_IN * R_OUT
    sizes = dp_size, tensor_size
    in_blocks = direct(features(inputs, in_proj, LANES, 20, "in_features"), "tensor", tensor_size, order_of(tensor_size))
    out_local = features(out_grads, out_proj, 2 * LANES, 44, "out_features")
    partial = partial_vectors(in_blocks, out_local).reshape(-1, width)
    prior, partial = lax.optimization_barrier((prior, partial))
    own_vectors = sum_over(partial, "tensor", tensor_size)
    own_vectors, prior_pieces = lax.optimization_barrier((own_vectors, split_prior(prior, queries)))
    pieces = direct(own_vectors, "dp", dp_size, range(dp_size))
    *prior_pieces, queries = [in_vmem(piece) for piece in prior_pieces]
    vectors, scale, applied_rows, norm = start_cg(pieces, prior_pieces, tensor_size)
    fixed = (*prior_pieces, vectors, scale)
    state = [applied_rows]
    for iteration in range(1, ITERS - 1):
        blocks = gather(state[0], sizes)
        applied_rows, norm, *others = step_cg(blocks, fixed, norm, state, None, sizes)
        state = [applied_rows, *others]
    blocks = gather(state[0], sizes)
    curvature, norm, solved, along = step_cg(blocks, fixed, norm, state, queries, sizes)
    return combine(gather(curvature, sizes), norm, solved, along)


def solution(mesh):
    return jax.shard_map(
        functools.partial(on_device, mesh.shape["dp"], mesh.shape["tensor"]),
        mesh=mesh,
        in_specs=(
            P(("groups", "dp", "tensor"), None),
            P(),
            P(("groups", "dp"), "tensor"),
            P(None, "tensor"),
            P(("groups", "dp", "tensor"), None),
            P(("groups", "dp", "tensor"), None),
        ),
        out_specs=P("groups", ("dp", "tensor")),
        check_vma=False,
    )
```

```python
import functools

import jax
import jax.numpy as jnp
from jax import lax
from jax.experimental import pallas as pl
from jax.experimental.pallas import tpu as pltpu
from jax.sharding import PartitionSpec as P

R_IN = 64
R_OUT = 64
SEQ = 1024
ITERS = 4
LANES = 128
FEW = 4
DEPTH = 3
NT = (((1,), (1,)), ((), ()))
HIGHEST = lax.Precision.HIGHEST
ANY_SPEC = pl.BlockSpec(memory_space=pl.ANY)
VMEM_SPEC = pl.BlockSpec(memory_space=pltpu.VMEM)
PARAMS = pltpu.CompilerParams(vmem_limit_bytes=16 * 2**20)
F32 = functools.partial(jax.ShapeDtypeStruct, dtype=jnp.float32)


def swap(value, axis, size, bit):
    return lax.ppermute(value, axis, [(i, i ^ bit) for i in range(size)])


def bits(size):
    return [1 << b for b in reversed(range(size.bit_length() - 1))]


def group_order(sizes):
    dp_size, tensor_size = sizes
    first = (dp_size - 1) * tensor_size + (tensor_size - 1) // 2
    return [first] + [i for i in range(dp_size * tensor_size) if i != first]


def gather(value, sizes):
    order = group_order(sizes)
    value = jnp.broadcast_to(value[None], (len(order),) + value.shape)
    return lax.all_to_all(value, ("dp", "tensor"), 0, 0, axis_index_groups=[order])


def order_of(size):
    return (0, 2, 3, 1) if size == 4 else tuple(range(size))


def direct(value, axis, size, order):
    return [value] + [swap(value, axis, size, k) for k in order[1:]]


def sum_over(value, axis, size):
    if size > FEW:
        for bit in bits(size):
            value = value + swap(value, axis, size, bit)
        return value
    blocks = direct(value, axis, size, order_of(size))
    while len(blocks) > 1:
        blocks = [a + b for a, b in zip(blocks[::2], blocks[1::2])]
    return blocks[0]


def in_hbm(value):
    return pltpu.with_memory_space_constraint(value, pltpu.HBM)


def in_vmem(value):
    return pltpu.with_memory_space_constraint(value, pltpu.VMEM)


def dot_nt(a, b):
    return lax.dot_general(a, b, NT, precision=HIGHEST, preferred_element_type=jnp.float32)


def row_sum(values):
    return jnp.sum(values, axis=1, keepdims=True)


def stream_kernel(block, rows_ref, proj_ref, feats_ref, held, proj, turned, sems):
    count, half = proj_ref.shape[0], proj.shape[1]
    steps = held.shape[0] // block
    firsts = [
        pltpu.make_async_copy(
            proj_ref.at[:, pl.ds(h * half, half)], proj.at[pl.ds(h * count, count)], sems.at[steps + h]
        )
        for h in range(2)
    ]

    def fetch(step):
        span = pl.ds(pl.multiple_of(step * block, block), block)
        return pltpu.make_async_copy(rows_ref.at[span], held.at[span], sems.at[step])

    for copy in firsts:
        copy.start()
    for step in range(min(DEPTH, steps)):
        fetch(step).start()
    for copy in firsts:
        copy.wait()
    turned[...] = proj[...].T

    @pl.loop(0, steps)
    def _(step):
        fetch(step).wait()

        @pl.when(step + DEPTH < steps)
        def _():
            fetch(step + DEPTH).start()

        span = pl.ds(pl.multiple_of(step * block, block), block)
        left = jnp.dot(held[span, :half], turned[...], preferred_element_type=jnp.float32)
        right = jnp.dot(held[span, half:], turned[...], preferred_element_type=jnp.float32)
        feats_ref[:, span] = left.T[:count] + right.T[count:]


def features(rows, proj, block, limit, name):
    count, width = proj.shape
    return pl.pallas_call(
        functools.partial(stream_kernel, block),
        out_shape=pltpu.VMEM((count, rows.shape[0]), jnp.float32),
        in_specs=[ANY_SPEC] * 2,
        out_specs=VMEM_SPEC,
        scratch_shapes=[
            pltpu.VMEM(rows.shape, jnp.bfloat16),
            pltpu.VMEM((2 * count, width // 2), jnp.bfloat16),
            pltpu.VMEM((width // 2, 2 * count), jnp.bfloat16),
            pltpu.SemaphoreType.DMA((rows.shape[0] // block + 2,)),
        ],
        compiler_params=pltpu.CompilerParams(vmem_limit_bytes=limit * 2**20),
        name=name,
    )(in_hbm(rows), in_hbm(proj))


def split_kernel(prior_ref, queries_ref, upper_ref, lower_ref, turned_ref, held, sems):
    chunk = held.shape[1] // sems.shape[0]
    spans = [pl.ds(c * chunk, chunk) for c in range(sems.shape[0])]
    copies = [
        pltpu.make_async_copy(prior_ref.at[:, span], held.at[:, span], sems.at[c])
        for c, span in enumerate(spans)
    ]
    for copy in copies:
        copy.start()
    turned_ref[...] = queries_ref[...].T
    for copy, span in zip(copies, spans):
        copy.wait()
        block = held[:, span]
        upper = block.astype(jnp.bfloat16)
        upper_ref[:, span] = upper
        lower_ref[:, span] = (block - upper.astype(jnp.float32)).astype(jnp.bfloat16)


def split_prior(prior, queries):
    return pl.pallas_call(
        split_kernel,
        out_shape=(
            pltpu.VMEM(prior.shape, jnp.bfloat16),
            pltpu.VMEM(prior.shape, jnp.bfloat16),
            pltpu.VMEM(queries.shape[::-1], jnp.bfloat16),
        ),
        in_specs=[ANY_SPEC, VMEM_SPEC],
        out_specs=(VMEM_SPEC,) * 3,
        scratch_shapes=[pltpu.VMEM(prior.shape, jnp.float32), pltpu.SemaphoreType.DMA((8,))],
        compiler_params=PARAMS,
        name="split_prior",
    )(in_hbm(prior), queries)


def partial_kernel(size, *refs):
    blocks, (out_ref, part_ref, held) = refs[:size], refs[size:]
    me = lax.axis_index("tensor")
    tokens = blocks[0].shape[1]
    for k, block in zip(order_of(size), blocks):
        start = pl.multiple_of((me ^ k) * tokens, LANES)
        held[:, pl.ds(start, tokens)] = block[...]
    for s in range(part_ref.shape[0]):
        span = slice(s * SEQ, (s + 1) * SEQ)
        outs = pieces_of(out_ref[:, span], 2)
        sums = dot_pieces(pieces_of(held[:, span], 2), outs, R_IN)
        part_ref[s] = (sums[:, :R_OUT] + sums[:, R_OUT:]) * (1.0 / SEQ)


def partial_vectors(blocks, out_local):
    seq_count = out_local.shape[1] // SEQ
    return pl.pallas_call(
        functools.partial(partial_kernel, len(blocks)),
        out_shape=F32((seq_count, R_IN, R_OUT)),
        in_specs=[VMEM_SPEC] * (len(blocks) + 1),
        out_specs=VMEM_SPEC,
        scratch_shapes=[pltpu.VMEM(out_local.shape, jnp.float32)],
        compiler_params=PARAMS,
        name="partial_vectors",
    )(*blocks, out_local)


def own_columns(ref, me, count):
    if count % LANES == 0:
        return ref[:, pl.ds(pl.multiple_of(me * count, LANES), count)]
    per = LANES // count
    held = ref[:, pl.ds(pl.multiple_of((me // per) * LANES, LANES), LANES)]
    return pltpu.roll(held, LANES - (me % per) * count, 1)[:, :count]


def pieces_of(values, count):
    held = []
    for _ in range(count):
        piece = values.astype(jnp.bfloat16)
        held.append(piece)
        values = values - piece.astype(jnp.float32)
    return jnp.concatenate(held, axis=0)


def dot_pieces(a, b, seqs):
    held = lax.dot_general(a, b, NT, preferred_element_type=jnp.float32)
    total = held[:seqs]
    for start in range(seqs, held.shape[0], seqs):
        total = total + held[start : start + seqs]
    return total


def apply_fisher(x, vectors_ref, upper_ref, lower_ref, me):
    seqs = vectors_ref.shape[0]
    pieces = pieces_of(x, 3)
    applied = dot_pieces(pieces, upper_ref[...], seqs)
    applied = applied + dot_pieces(pieces[: 2 * seqs], lower_ref[...], seqs)
    own = own_columns(vectors_ref, me, upper_ref.shape[0])
    for s in range(seqs):
        weight = row_sum(x * vectors_ref[s : s + 1, :]) * (1.0 / seqs)
        applied = applied + weight * own[s : s + 1, :]
    return applied


def flat_index(tensor_size):
    return lax.axis_index("dp") * tensor_size + lax.axis_index("tensor")


def start_kernel(size, tensor_size, *refs):
    pieces, refs = refs[:size], refs[size:]
    upper_ref, lower_ref, vectors_ref, scale_ref, applied_ref, norm_ref, held = refs
    dp = lax.axis_index("dp")
    for k, piece in enumerate(pieces):
        held[dp ^ k] = piece[...]
    vectors = jnp.concatenate([held[k] for k in range(size)], axis=0)
    vectors_ref[...] = vectors
    norm = jnp.broadcast_to(row_sum(vectors * vectors), norm_ref.shape)
    norm_ref[...] = norm
    spread = jnp.sum(norm, axis=0, keepdims=True) * (1.0 / vectors.shape[0])
    scale_ref[...] = jnp.broadcast_to(1.0 / (1.0 + spread), scale_ref.shape)
    me = flat_index(tensor_size)
    applied_ref[...] = apply_fisher(vectors, vectors_ref, upper_ref, lower_ref, me)


def start_cg(pieces, prior_pieces, tensor_size):
    size, seqs = len(pieces), len(pieces) * pieces[0].shape[0]
    rows, width = prior_pieces[0].shape
    column = F32((seqs, LANES))
    return pl.pallas_call(
        functools.partial(start_kernel, size, tensor_size),
        out_shape=(F32((seqs, width)), column, F32((seqs, rows)), column),
        in_specs=[VMEM_SPEC] * (size + 2),
        out_specs=(VMEM_SPEC,) * 4,
        scratch_shapes=[pltpu.VMEM((size,) + pieces[0].shape, jnp.float32)],
        compiler_params=PARAMS,
        name="cg_start",
    )(*pieces, *prior_pieces)


def step_kernel(sizes, first, last, *refs):
    blocks_ref, upper_ref, lower_ref, vectors_ref, scale_ref, norm_ref, fisher_direction_ref = refs[:7]
    refs = refs[7:]
    if not first:
        fisher_residual_ref, direction_ref, residual_ref, solution_ref = refs[:4]
        refs = refs[4:]
    if last:
        queries_ref, curvature_out, norm_out, solved_out, along_out, held = refs
    else:
        fisher_direction_out, norm_out, fisher_residual_out, direction_out, residual_out, solution_out, held = refs
    me = flat_index(sizes[1])
    rows = blocks_ref.shape[2]
    for i, k in enumerate(group_order(sizes)):
        held[:, k * rows : (k + 1) * rows] = blocks_ref[i]
    applied = held[...]
    scale = scale_ref[...][:, :1]
    twice = apply_fisher(scale * applied, vectors_ref, upper_ref, lower_ref, me)
    direction = vectors_ref[...] if first else direction_ref[...]
    residual = direction if first else residual_ref[...]
    norm = norm_ref[...][:, :1]
    step = norm / row_sum(direction * applied)
    solution = step * direction
    if not first:
        solution = solution_ref[...] + solution
    residual = residual - step * applied
    norm_next = row_sum(residual * residual)
    share = norm_next / norm
    direction = residual + share * direction
    fisher_direction = fisher_direction_ref[...]
    fisher_residual = (fisher_direction if first else fisher_residual_ref[...]) - (step / scale) * twice
    fisher_direction = fisher_residual + share * fisher_direction
    norm_out[...] = jnp.broadcast_to(norm_next, norm_out.shape)
    if last:
        held[...] = direction
        own = own_columns(held, me, rows)
        curvature_out[...] = jnp.broadcast_to(row_sum(own * fisher_direction), curvature_out.shape)
        seqs = direction.shape[0]
        solved = jnp.concatenate([solution, direction], axis=0)
        parts = jnp.dot(pieces_of(solved, 3), queries_ref[...], preferred_element_type=jnp.float32)
        scores = parts[: 2 * seqs] + parts[2 * seqs : 4 * seqs] + parts[4 * seqs :]
        solved_out[...] = scores[:seqs]
        along_out[...] = scores[seqs:]
    else:
        fisher_direction_out[...] = fisher_direction
        fisher_residual_out[...] = fisher_residual
        residual_out[...] = residual
        direction_out[...] = direction
        solution_out[...] = solution


def step_cg(blocks, fixed, norm, state, queries, sizes):
    first, last = len(state) == 1, queries is not None
    whole, rows = F32(fixed[2].shape), F32(state[0].shape)
    column = F32(norm.shape)
    operands = [blocks, *fixed, norm, *state]
    out_shape = (rows, column, rows, whole, whole, whole)
    if last:
        operands.append(queries)
        scores = F32((whole.shape[0], queries.shape[1]))
        out_shape = (column, column, scores, scores)
    return pl.pallas_call(
        functools.partial(step_kernel, sizes, first, last),
        out_shape=out_shape,
        in_specs=[VMEM_SPEC] * len(operands),
        out_specs=(VMEM_SPEC,) * len(out_shape),
        scratch_shapes=[pltpu.VMEM(whole.shape, jnp.float32)],
        compiler_params=PARAMS,
        name="cg_step",
    )(*operands)


def combine_kernel(curvature_ref, norm_ref, solved_ref, along_ref, scores_ref):
    step = norm_ref[...] / jnp.sum(curvature_ref[...], axis=0)
    scores_ref[...] = solved_ref[...] + step[:, :1] * along_ref[...]


def combine(curvature, norm, solved, along):
    return pl.pallas_call(
        combine_kernel,
        out_shape=F32(solved.shape),
        in_specs=[VMEM_SPEC] * 4,
        out_specs=VMEM_SPEC,
        compiler_params=PARAMS,
        name="combine",
    )(curvature, norm, solved, along)


def on_device(dp_size, tensor_size, inputs, in_proj, out_grads, out_proj, prior, queries):
    width = R_IN * R_OUT
    sizes = dp_size, tensor_size
    in_blocks = direct(features(inputs, in_proj, LANES, 20, "in_features"), "tensor", tensor_size, order_of(tensor_size))
    out_local = features(out_grads, out_proj, 2 * LANES, 44, "out_features")
    partial = partial_vectors(in_blocks, out_local).reshape(-1, width)
    prior, partial = lax.optimization_barrier((prior, partial))
    own_vectors = sum_over(partial, "tensor", tensor_size)
    own_vectors, prior_pieces = lax.optimization_barrier((own_vectors, split_prior(prior, queries)))
    pieces = direct(own_vectors, "dp", dp_size, range(dp_size))
    *prior_pieces, queries = [in_vmem(piece) for piece in prior_pieces]
    vectors, scale, applied_rows, norm = start_cg(pieces, prior_pieces, tensor_size)
    fixed = (*prior_pieces, vectors, scale)
    state = [applied_rows]
    for iteration in range(1, ITERS - 1):
        blocks = gather(state[0], sizes)
        applied_rows, norm, *others = step_cg(blocks, fixed, norm, state, None, sizes)
        state = [applied_rows, *others]
    blocks = gather(state[0], sizes)
    curvature, norm, solved, along = step_cg(blocks, fixed, norm, state, queries, sizes)
    return combine(gather(curvature, sizes), norm, solved, along)


def solution(mesh):
    return jax.shard_map(
        functools.partial(on_device, mesh.shape["dp"], mesh.shape["tensor"]),
        mesh=mesh,
        in_specs=(
            P(("groups", "dp", "tensor"), None),
            P(),
            P(("groups", "dp"), "tensor"),
            P(None, "tensor"),
            P(("groups", "dp", "tensor"), None),
            P(("groups", "dp", "tensor"), None),
        ),
        out_specs=P("groups", ("dp", "tensor")),
        check_vma=False,
    )
```

```python
import functools

import jax
import jax.numpy as jnp
from jax import lax
from jax.experimental import pallas as pl
from jax.experimental.pallas import tpu as pltpu
from jax.sharding import PartitionSpec as P

R_IN = 64
R_OUT = 64
SEQ = 1024
ITERS = 4
LANES = 128
FEW = 4
DEPTH = 3
NT = (((1,), (1,)), ((), ()))
HIGHEST = lax.Precision.HIGHEST
ANY_SPEC = pl.BlockSpec(memory_space=pl.ANY)
VMEM_SPEC = pl.BlockSpec(memory_space=pltpu.VMEM)
PARAMS = pltpu.CompilerParams(vmem_limit_bytes=16 * 2**20)
F32 = functools.partial(jax.ShapeDtypeStruct, dtype=jnp.float32)


def swap(value, axis, size, bit):
    return lax.ppermute(value, axis, [(i, i ^ bit) for i in range(size)])


def bits(size):
    return [1 << b for b in reversed(range(size.bit_length() - 1))]


def group_order(sizes):
    dp_size, tensor_size = sizes
    first = (dp_size - 1) * tensor_size + (tensor_size - 1) // 2
    return [first] + [i for i in range(dp_size * tensor_size) if i != first]


def gather(value, sizes):
    order = group_order(sizes)
    value = jnp.broadcast_to(value[None], (len(order),) + value.shape)
    return lax.all_to_all(value, ("dp", "tensor"), 0, 0, axis_index_groups=[order])


def order_of(size):
    return (0, 2, 3, 1) if size == 4 else tuple(range(size))


def direct(value, axis, size, order):
    return [value] + [swap(value, axis, size, k) for k in order[1:]]


def sum_over(value, axis, size):
    if size > FEW:
        for bit in bits(size):
            value = value + swap(value, axis, size, bit)
        return value
    blocks = direct(value, axis, size, order_of(size))
    while len(blocks) > 1:
        blocks = [a + b for a, b in zip(blocks[::2], blocks[1::2])]
    return blocks[0]


def in_hbm(value):
    return pltpu.with_memory_space_constraint(value, pltpu.HBM)


def in_vmem(value):
    return pltpu.with_memory_space_constraint(value, pltpu.VMEM)


def dot_nt(a, b):
    return lax.dot_general(a, b, NT, precision=HIGHEST, preferred_element_type=jnp.float32)


def row_sum(values):
    return jnp.sum(values, axis=1, keepdims=True)


def stream_kernel(block, by_row, rows_ref, proj_ref, feats_ref, held, proj, turned, sems):
    count, half = proj_ref.shape[0], proj.shape[1]
    steps = held.shape[0] // block
    firsts = [
        pltpu.make_async_copy(
            proj_ref.at[:, pl.ds(h * half, half)], proj.at[pl.ds(h * count, count)], sems.at[steps + h]
        )
        for h in range(2)
    ]

    def fetch(step):
        span = pl.ds(pl.multiple_of(step * block, block), block)
        return pltpu.make_async_copy(rows_ref.at[span], held.at[span], sems.at[step])

    for copy in firsts:
        copy.start()
    for step in range(min(DEPTH, steps)):
        fetch(step).start()
    for copy in firsts:
        copy.wait()
    turned[...] = proj[...].T

    @pl.loop(0, steps)
    def _(step):
        fetch(step).wait()

        @pl.when(step + DEPTH < steps)
        def _():
            fetch(step + DEPTH).start()

        span = pl.ds(pl.multiple_of(step * block, block), block)
        left = jnp.dot(held[span, :half], turned[...], preferred_element_type=jnp.float32)
        right = jnp.dot(held[span, half:], turned[...], preferred_element_type=jnp.float32)
        lane = lax.broadcasted_iota(jnp.int32, left.shape, 1)
        both = jnp.where(lane < count, left, right)
        if by_row:
            feats_ref[span, :] = both
        else:
            both = both.T
            feats_ref[:, span] = both[:count] + both[count:]


def features(rows, proj, block, by_row, limit, name):
    count, width = proj.shape
    shape = (rows.shape[0], 2 * count) if by_row else (count, rows.shape[0])
    return pl.pallas_call(
        functools.partial(stream_kernel, block, by_row),
        out_shape=pltpu.VMEM(shape, jnp.float32),
        in_specs=[ANY_SPEC] * 2,
        out_specs=VMEM_SPEC,
        scratch_shapes=[
            pltpu.VMEM(rows.shape, jnp.bfloat16),
            pltpu.VMEM((2 * count, width // 2), jnp.bfloat16),
            pltpu.VMEM((width // 2, 2 * count), jnp.bfloat16),
            pltpu.SemaphoreType.DMA((rows.shape[0] // block + 2,)),
        ],
        compiler_params=pltpu.CompilerParams(vmem_limit_bytes=limit * 2**20),
        name=name,
    )(in_hbm(rows), in_hbm(proj))


def split_kernel(prior_ref, queries_ref, upper_ref, lower_ref, turned_ref, held, sems):
    chunk = held.shape[1] // sems.shape[0]
    spans = [pl.ds(c * chunk, chunk) for c in range(sems.shape[0])]
    copies = [
        pltpu.make_async_copy(prior_ref.at[:, span], held.at[:, span], sems.at[c])
        for c, span in enumerate(spans)
    ]
    for copy in copies:
        copy.start()
    turned_ref[...] = queries_ref[...].T
    for copy, span in zip(copies, spans):
        copy.wait()
        block = held[:, span]
        upper = block.astype(jnp.bfloat16)
        upper_ref[:, span] = upper
        lower_ref[:, span] = (block - upper.astype(jnp.float32)).astype(jnp.bfloat16)


def split_prior(prior, queries):
    return pl.pallas_call(
        split_kernel,
        out_shape=(
            pltpu.VMEM(prior.shape, jnp.bfloat16),
            pltpu.VMEM(prior.shape, jnp.bfloat16),
            pltpu.VMEM(queries.shape[::-1], jnp.bfloat16),
        ),
        in_specs=[ANY_SPEC, VMEM_SPEC],
        out_specs=(VMEM_SPEC,) * 3,
        scratch_shapes=[pltpu.VMEM(prior.shape, jnp.float32), pltpu.SemaphoreType.DMA((8,))],
        compiler_params=PARAMS,
        name="split_prior",
    )(in_hbm(prior), queries)


def partial_kernel(size, *refs):
    blocks, (out_ref, part_ref, held) = refs[:size], refs[size:]
    me = lax.axis_index("tensor")
    tokens = blocks[0].shape[1]
    for k, block in zip(order_of(size), blocks):
        start = pl.multiple_of((me ^ k) * tokens, LANES)
        held[:, pl.ds(start, tokens)] = block[...]
    for s in range(part_ref.shape[0]):
        span = slice(s * SEQ, (s + 1) * SEQ)
        ins, sums = pieces_of(held[:, span], 2), 0.0
        outs = out_ref[span, :]
        for _ in range(2):
            piece = outs.astype(jnp.bfloat16)
            outs = outs - piece.astype(jnp.float32)
            sums = sums + jnp.dot(ins, piece, preferred_element_type=jnp.float32)
        sums = sums[:R_IN] + sums[R_IN:]
        part_ref[s] = (sums[:, :R_OUT] + sums[:, R_OUT:]) * (1.0 / SEQ)


def partial_vectors(blocks, out_local):
    seq_count = out_local.shape[0] // SEQ
    return pl.pallas_call(
        functools.partial(partial_kernel, len(blocks)),
        out_shape=F32((seq_count, R_IN, R_OUT)),
        in_specs=[VMEM_SPEC] * (len(blocks) + 1),
        out_specs=VMEM_SPEC,
        scratch_shapes=[pltpu.VMEM((R_IN, out_local.shape[0]), jnp.float32)],
        compiler_params=PARAMS,
        name="partial_vectors",
    )(*blocks, out_local)


def own_columns(ref, me, count):
    if count % LANES == 0:
        return ref[:, pl.ds(pl.multiple_of(me * count, LANES), count)]
    per = LANES // count
    held = ref[:, pl.ds(pl.multiple_of((me // per) * LANES, LANES), LANES)]
    return pltpu.roll(held, LANES - (me % per) * count, 1)[:, :count]


def pieces_of(values, count):
    held = []
    for _ in range(count):
        piece = values.astype(jnp.bfloat16)
        held.append(piece)
        values = values - piece.astype(jnp.float32)
    return jnp.concatenate(held, axis=0)


def dot_pieces(a, b, seqs):
    held = lax.dot_general(a, b, NT, preferred_element_type=jnp.float32)
    total = held[:seqs]
    for start in range(seqs, held.shape[0], seqs):
        total = total + held[start : start + seqs]
    return total


def apply_fisher(x, vectors_ref, upper_ref, lower_ref, me):
    seqs = vectors_ref.shape[0]
    pieces = pieces_of(x, 3)
    applied = dot_pieces(pieces, upper_ref[...], seqs)
    applied = applied + dot_pieces(pieces[: 2 * seqs], lower_ref[...], seqs)
    own = own_columns(vectors_ref, me, upper_ref.shape[0])
    for s in range(seqs):
        weight = row_sum(x * vectors_ref[s : s + 1, :]) * (1.0 / seqs)
        applied = applied + weight * own[s : s + 1, :]
    return applied


def flat_index(tensor_size):
    return lax.axis_index("dp") * tensor_size + lax.axis_index("tensor")


def start_kernel(size, tensor_size, *refs):
    pieces, refs = refs[:size], refs[size:]
    upper_ref, lower_ref, vectors_ref, scale_ref, applied_ref, norm_ref, held = refs
    dp = lax.axis_index("dp")
    for k, piece in enumerate(pieces):
        held[dp ^ k] = piece[...]
    vectors = jnp.concatenate([held[k] for k in range(size)], axis=0)
    vectors_ref[...] = vectors
    norm = jnp.broadcast_to(row_sum(vectors * vectors), norm_ref.shape)
    norm_ref[...] = norm
    spread = jnp.sum(norm, axis=0, keepdims=True) * (1.0 / vectors.shape[0])
    scale_ref[...] = jnp.broadcast_to(1.0 / (1.0 + spread), scale_ref.shape)
    me = flat_index(tensor_size)
    applied_ref[...] = apply_fisher(vectors, vectors_ref, upper_ref, lower_ref, me)


def start_cg(pieces, prior_pieces, tensor_size):
    size, seqs = len(pieces), len(pieces) * pieces[0].shape[0]
    rows, width = prior_pieces[0].shape
    column = F32((seqs, LANES))
    return pl.pallas_call(
        functools.partial(start_kernel, size, tensor_size),
        out_shape=(F32((seqs, width)), column, F32((seqs, rows)), column),
        in_specs=[VMEM_SPEC] * (size + 2),
        out_specs=(VMEM_SPEC,) * 4,
        scratch_shapes=[pltpu.VMEM((size,) + pieces[0].shape, jnp.float32)],
        compiler_params=PARAMS,
        name="cg_start",
    )(*pieces, *prior_pieces)


def step_kernel(sizes, first, last, *refs):
    blocks_ref, upper_ref, lower_ref, vectors_ref, scale_ref, norm_ref, fisher_direction_ref = refs[:7]
    refs = refs[7:]
    if not first:
        fisher_residual_ref, direction_ref, residual_ref, solution_ref = refs[:4]
        refs = refs[4:]
    if last:
        queries_ref, curvature_out, norm_out, solved_out, along_out, held = refs
    else:
        fisher_direction_out, norm_out, fisher_residual_out, direction_out, residual_out, solution_out, held = refs
    me = flat_index(sizes[1])
    rows = blocks_ref.shape[2]
    for i, k in enumerate(group_order(sizes)):
        held[:, k * rows : (k + 1) * rows] = blocks_ref[i]
    applied = held[...]
    scale = scale_ref[...][:, :1]
    twice = apply_fisher(scale * applied, vectors_ref, upper_ref, lower_ref, me)
    direction = vectors_ref[...] if first else direction_ref[...]
    residual = direction if first else residual_ref[...]
    norm = norm_ref[...][:, :1]
    step = norm / row_sum(direction * applied)
    solution = step * direction
    if not first:
        solution = solution_ref[...] + solution
    residual = residual - step * applied
    norm_next = row_sum(residual * residual)
    share = norm_next / norm
    direction = residual + share * direction
    fisher_direction = fisher_direction_ref[...]
    fisher_residual = (fisher_direction if first else fisher_residual_ref[...]) - (step / scale) * twice
    fisher_direction = fisher_residual + share * fisher_direction
    norm_out[...] = jnp.broadcast_to(norm_next, norm_out.shape)
    if last:
        held[...] = direction
        own = own_columns(held, me, rows)
        curvature_out[...] = jnp.broadcast_to(row_sum(own * fisher_direction), curvature_out.shape)
        seqs = direction.shape[0]
        solved = jnp.concatenate([solution, direction], axis=0)
        parts = jnp.dot(pieces_of(solved, 3), queries_ref[...], preferred_element_type=jnp.float32)
        scores = parts[: 2 * seqs] + parts[2 * seqs : 4 * seqs] + parts[4 * seqs :]
        solved_out[...] = scores[:seqs]
        along_out[...] = scores[seqs:]
    else:
        fisher_direction_out[...] = fisher_direction
        fisher_residual_out[...] = fisher_residual
        residual_out[...] = residual
        direction_out[...] = direction
        solution_out[...] = solution


def step_cg(blocks, fixed, norm, state, queries, sizes):
    first, last = len(state) == 1, queries is not None
    whole, rows = F32(fixed[2].shape), F32(state[0].shape)
    column = F32(norm.shape)
    operands = [blocks, *fixed, norm, *state]
    out_shape = (rows, column, rows, whole, whole, whole)
    if last:
        operands.append(queries)
        scores = F32((whole.shape[0], queries.shape[1]))
        out_shape = (column, column, scores, scores)
    return pl.pallas_call(
        functools.partial(step_kernel, sizes, first, last),
        out_shape=out_shape,
        in_specs=[VMEM_SPEC] * len(operands),
        out_specs=(VMEM_SPEC,) * len(out_shape),
        scratch_shapes=[pltpu.VMEM(whole.shape, jnp.float32)],
        compiler_params=PARAMS,
        name="cg_step",
    )(*operands)


def combine_kernel(curvature_ref, norm_ref, solved_ref, along_ref, scores_ref):
    step = norm_ref[...] / jnp.sum(curvature_ref[...], axis=0)
    scores_ref[...] = solved_ref[...] + step[:, :1] * along_ref[...]


def combine(curvature, norm, solved, along):
    return pl.pallas_call(
        combine_kernel,
        out_shape=F32(solved.shape),
        in_specs=[VMEM_SPEC] * 4,
        out_specs=VMEM_SPEC,
        compiler_params=PARAMS,
        name="combine",
    )(curvature, norm, solved, along)


def on_device(dp_size, tensor_size, inputs, in_proj, out_grads, out_proj, prior, queries):
    width = R_IN * R_OUT
    sizes = dp_size, tensor_size
    in_blocks = direct(features(inputs, in_proj, LANES, False, 20, "in_features"), "tensor", tensor_size, order_of(tensor_size))
    out_local = features(out_grads, out_proj, 2 * LANES, True, 44, "out_features")
    partial = partial_vectors(in_blocks, out_local).reshape(-1, width)
    prior, partial = lax.optimization_barrier((prior, partial))
    own_vectors = sum_over(partial, "tensor", tensor_size)
    own_vectors, prior_pieces = lax.optimization_barrier((own_vectors, split_prior(prior, queries)))
    pieces = direct(own_vectors, "dp", dp_size, range(dp_size))
    *prior_pieces, queries = [in_vmem(piece) for piece in prior_pieces]
    vectors, scale, applied_rows, norm = start_cg(pieces, prior_pieces, tensor_size)
    fixed = (*prior_pieces, vectors, scale)
    state = [applied_rows]
    for iteration in range(1, ITERS - 1):
        blocks = gather(state[0], sizes)
        applied_rows, norm, *others = step_cg(blocks, fixed, norm, state, None, sizes)
        state = [applied_rows, *others]
    blocks = gather(state[0], sizes)
    curvature, norm, solved, along = step_cg(blocks, fixed, norm, state, queries, sizes)
    return combine(gather(curvature, sizes), norm, solved, along)


def solution(mesh):
    return jax.shard_map(
        functools.partial(on_device, mesh.shape["dp"], mesh.shape["tensor"]),
        mesh=mesh,
        in_specs=(
            P(("groups", "dp", "tensor"), None),
            P(),
            P(("groups", "dp"), "tensor"),
            P(None, "tensor"),
            P(("groups", "dp", "tensor"), None),
            P(("groups", "dp", "tensor"), None),
        ),
        out_specs=P("groups", ("dp", "tensor")),
        check_vma=False,
    )
```

```python
import functools

import jax
import jax.numpy as jnp
from jax import lax
from jax.experimental import pallas as pl
from jax.experimental.pallas import tpu as pltpu
from jax.sharding import PartitionSpec as P

R_IN = 64
R_OUT = 64
SEQ = 1024
ITERS = 4
LANES = 128
FEW = 4
DEPTH = 3
NT = (((1,), (1,)), ((), ()))
HIGHEST = lax.Precision.HIGHEST
ANY_SPEC = pl.BlockSpec(memory_space=pl.ANY)
VMEM_SPEC = pl.BlockSpec(memory_space=pltpu.VMEM)
PARAMS = pltpu.CompilerParams(vmem_limit_bytes=16 * 2**20)
F32 = functools.partial(jax.ShapeDtypeStruct, dtype=jnp.float32)


def swap(value, axis, size, bit):
    return lax.ppermute(value, axis, [(i, i ^ bit) for i in range(size)])


def bits(size):
    return [1 << b for b in reversed(range(size.bit_length() - 1))]


def group_order(sizes):
    dp_size, tensor_size = sizes
    first = (dp_size - 1) * tensor_size + (tensor_size - 1) // 2
    return [first] + [i for i in range(dp_size * tensor_size) if i != first]


def gather(value, sizes):
    order = group_order(sizes)
    value = jnp.broadcast_to(value[None], (len(order),) + value.shape)
    return lax.all_to_all(value, ("dp", "tensor"), 0, 0, axis_index_groups=[order])


def order_of(size):
    return (0, 2, 3, 1) if size == 4 else tuple(range(size))


def direct(value, axis, size, order):
    return [value] + [swap(value, axis, size, k) for k in order[1:]]


def sum_over(value, axis, size):
    if size > FEW:
        for bit in bits(size):
            value = value + swap(value, axis, size, bit)
        return value
    blocks = direct(value, axis, size, order_of(size))
    while len(blocks) > 1:
        blocks = [a + b for a, b in zip(blocks[::2], blocks[1::2])]
    return blocks[0]


def in_hbm(value):
    return pltpu.with_memory_space_constraint(value, pltpu.HBM)


def in_vmem(value):
    return pltpu.with_memory_space_constraint(value, pltpu.VMEM)


def dot_nt(a, b):
    return lax.dot_general(a, b, NT, precision=HIGHEST, preferred_element_type=jnp.float32)


def row_sum(values):
    return jnp.sum(values, axis=1, keepdims=True)


def stream_kernel(block, by_row, rows_ref, proj_ref, feats_ref, held, proj, turned, sems):
    count, half = proj_ref.shape[0], proj.shape[1]
    steps = held.shape[0] // block
    firsts = [
        pltpu.make_async_copy(
            proj_ref.at[:, pl.ds(h * half, half)], proj.at[pl.ds(h * count, count)], sems.at[steps + h]
        )
        for h in range(2)
    ]

    def fetch(step):
        span = pl.ds(pl.multiple_of(step * block, block), block)
        return pltpu.make_async_copy(rows_ref.at[span], held.at[span], sems.at[step])

    for copy in firsts:
        copy.start()
    for step in range(min(DEPTH, steps)):
        fetch(step).start()
    for copy in firsts:
        copy.wait()
    turned[...] = proj[...].T

    @pl.loop(0, steps)
    def _(step):
        fetch(step).wait()

        @pl.when(step + DEPTH < steps)
        def _():
            fetch(step + DEPTH).start()

        span = pl.ds(pl.multiple_of(step * block, block), block)
        left = jnp.dot(held[span, :half], turned[...], preferred_element_type=jnp.float32)
        right = jnp.dot(held[span, half:], turned[...], preferred_element_type=jnp.float32)
        lane = lax.broadcasted_iota(jnp.int32, left.shape, 1)
        both = jnp.where(lane < count, left, right)
        if by_row:
            feats_ref[span, :] = both
        else:
            both = both.T
            feats_ref[:, span] = both[:count] + both[count:]


def features(rows, proj, block, by_row, limit, name):
    count, width = proj.shape
    shape = (rows.shape[0], 2 * count) if by_row else (count, rows.shape[0])
    return pl.pallas_call(
        functools.partial(stream_kernel, block, by_row),
        out_shape=pltpu.VMEM(shape, jnp.float32),
        in_specs=[ANY_SPEC] * 2,
        out_specs=VMEM_SPEC,
        scratch_shapes=[
            pltpu.VMEM(rows.shape, jnp.bfloat16),
            pltpu.VMEM((2 * count, width // 2), jnp.bfloat16),
            pltpu.VMEM((width // 2, 2 * count), jnp.bfloat16),
            pltpu.SemaphoreType.DMA((rows.shape[0] // block + 2,)),
        ],
        compiler_params=pltpu.CompilerParams(vmem_limit_bytes=limit * 2**20),
        name=name,
    )(in_hbm(rows), in_hbm(proj))


def split_kernel(prior_ref, queries_ref, upper_ref, lower_ref, turned_ref, held, sems):
    chunk = held.shape[1] // sems.shape[0]
    spans = [pl.ds(c * chunk, chunk) for c in range(sems.shape[0])]
    copies = [
        pltpu.make_async_copy(prior_ref.at[:, span], held.at[:, span], sems.at[c])
        for c, span in enumerate(spans)
    ]
    for copy in copies:
        copy.start()
    turned_ref[...] = queries_ref[...].T
    for copy, span in zip(copies, spans):
        copy.wait()
        block = held[:, span]
        upper = block.astype(jnp.bfloat16)
        upper_ref[:, span] = upper
        lower_ref[:, span] = (block - upper.astype(jnp.float32)).astype(jnp.bfloat16)


def split_prior(prior, queries):
    return pl.pallas_call(
        split_kernel,
        out_shape=(
            pltpu.VMEM(prior.shape, jnp.bfloat16),
            pltpu.VMEM(prior.shape, jnp.bfloat16),
            pltpu.VMEM(queries.shape[::-1], jnp.bfloat16),
        ),
        in_specs=[ANY_SPEC, VMEM_SPEC],
        out_specs=(VMEM_SPEC,) * 3,
        scratch_shapes=[pltpu.VMEM(prior.shape, jnp.float32), pltpu.SemaphoreType.DMA((8,))],
        compiler_params=PARAMS,
        name="split_prior",
    )(in_hbm(prior), queries)


def partial_kernel(size, *refs):
    blocks, (out_ref, part_ref, held) = refs[:size], refs[size:]
    me = lax.axis_index("tensor")
    tokens = blocks[0].shape[1]
    for k, block in zip(order_of(size), blocks):
        start = pl.multiple_of((me ^ k) * tokens, LANES)
        held[:, pl.ds(start, tokens)] = block[...]
    for s in range(part_ref.shape[0]):
        span = slice(s * SEQ, (s + 1) * SEQ)
        ins, sums = pieces_of(held[:, span], 2), 0.0
        outs = out_ref[span, :]
        for _ in range(2):
            piece = outs.astype(jnp.bfloat16)
            outs = outs - piece.astype(jnp.float32)
            sums = sums + jnp.dot(ins, piece, preferred_element_type=jnp.float32)
        sums = sums[:R_IN] + sums[R_IN:]
        part_ref[s] = (sums[:, :R_OUT] + sums[:, R_OUT:]) * (1.0 / SEQ)


def partial_vectors(blocks, out_local):
    seq_count = out_local.shape[0] // SEQ
    return pl.pallas_call(
        functools.partial(partial_kernel, len(blocks)),
        out_shape=F32((seq_count, R_IN, R_OUT)),
        in_specs=[VMEM_SPEC] * (len(blocks) + 1),
        out_specs=VMEM_SPEC,
        scratch_shapes=[pltpu.VMEM((R_IN, out_local.shape[0]), jnp.float32)],
        compiler_params=PARAMS,
        name="partial_vectors",
    )(*blocks, out_local)


def own_columns(ref, me, count):
    if count % LANES == 0:
        return ref[:, pl.ds(pl.multiple_of(me * count, LANES), count)]
    per = LANES // count
    held = ref[:, pl.ds(pl.multiple_of((me // per) * LANES, LANES), LANES)]
    return pltpu.roll(held, LANES - (me % per) * count, 1)[:, :count]


def pieces_of(values, count):
    held = []
    for _ in range(count):
        piece = values.astype(jnp.bfloat16)
        held.append(piece)
        values = values - piece.astype(jnp.float32)
    return jnp.concatenate(held, axis=0)


def dot_pieces(a, b, seqs):
    held = lax.dot_general(a, b, NT, preferred_element_type=jnp.float32)
    total = held[:seqs]
    for start in range(seqs, held.shape[0], seqs):
        total = total + held[start : start + seqs]
    return total


def apply_fisher(x, vectors_ref, upper_ref, lower_ref, me):
    seqs = vectors_ref.shape[0]
    pieces = pieces_of(x, 3)
    applied = dot_pieces(pieces, upper_ref[...], seqs)
    applied = applied + dot_pieces(pieces[: 2 * seqs], lower_ref[...], seqs)
    own = own_columns(vectors_ref, me, upper_ref.shape[0])
    for s in range(seqs):
        weight = row_sum(x * vectors_ref[s : s + 1, :]) * (1.0 / seqs)
        applied = applied + weight * own[s : s + 1, :]
    return applied


def flat_index(tensor_size):
    return lax.axis_index("dp") * tensor_size + lax.axis_index("tensor")


def start_kernel(size, tensor_size, *refs):
    pieces, refs = refs[:size], refs[size:]
    upper_ref, lower_ref, vectors_ref, scale_ref, applied_ref, norm_ref, held = refs
    dp = lax.axis_index("dp")
    for k, piece in enumerate(pieces):
        held[dp ^ k] = piece[...]
    vectors = jnp.concatenate([held[k] for k in range(size)], axis=0)
    vectors_ref[...] = vectors
    norm = jnp.broadcast_to(row_sum(vectors * vectors), norm_ref.shape)
    norm_ref[...] = norm
    spread = jnp.sum(norm, axis=0, keepdims=True) * (1.0 / vectors.shape[0])
    scale_ref[...] = jnp.broadcast_to(1.0 / (1.0 + spread), scale_ref.shape)
    me = flat_index(tensor_size)
    applied_ref[...] = apply_fisher(vectors, vectors_ref, upper_ref, lower_ref, me)


def start_cg(pieces, prior_pieces, tensor_size):
    size, seqs = len(pieces), len(pieces) * pieces[0].shape[0]
    rows, width = prior_pieces[0].shape
    column = F32((seqs, LANES))
    return pl.pallas_call(
        functools.partial(start_kernel, size, tensor_size),
        out_shape=(F32((seqs, width)), column, F32((seqs, rows)), column),
        in_specs=[VMEM_SPEC] * (size + 2),
        out_specs=(VMEM_SPEC,) * 4,
        scratch_shapes=[pltpu.VMEM((size,) + pieces[0].shape, jnp.float32)],
        compiler_params=PARAMS,
        name="cg_start",
    )(*pieces, *prior_pieces)


def diagonal(shape):
    return lax.broadcasted_iota(jnp.int32, shape, 0) == lax.broadcasted_iota(jnp.int32, shape, 1)


def on_lanes(column):
    here = diagonal((column.shape[0], LANES))
    return jnp.sum(jnp.where(here, column, 0.0), axis=0, keepdims=True)


def step_kernel(sizes, first, last, *refs):
    blocks_ref, upper_ref, lower_ref, vectors_ref, scale_ref, norm_ref, fisher_direction_ref = refs[:7]
    refs = refs[7:]
    if not first:
        fisher_residual_ref, direction_ref, residual_ref, solution_ref = refs[:4]
        refs = refs[4:]
    if last:
        queries_ref, curvature_out, norm_out, solved_out, along_out, held = refs
    else:
        fisher_direction_out, norm_out, fisher_residual_out, direction_out, residual_out, solution_out, held = refs
    me = flat_index(sizes[1])
    rows = blocks_ref.shape[2]
    for i, k in enumerate(group_order(sizes)):
        held[:, k * rows : (k + 1) * rows] = blocks_ref[i]
    applied = held[...]
    scale = scale_ref[...][:, :1]
    twice = apply_fisher(scale * applied, vectors_ref, upper_ref, lower_ref, me)
    direction = vectors_ref[...] if first else direction_ref[...]
    residual = direction if first else residual_ref[...]
    norm = norm_ref[...][:, :1]
    step = norm / row_sum(direction * applied)
    solution = step * direction
    if not first:
        solution = solution_ref[...] + solution
    residual = residual - step * applied
    norm_next = row_sum(residual * residual)
    share = norm_next / norm
    direction = residual + share * direction
    fisher_direction = fisher_direction_ref[...]
    fisher_residual = (fisher_direction if first else fisher_residual_ref[...]) - (step / scale) * twice
    fisher_direction = fisher_residual + share * fisher_direction
    norm_out[...] = on_lanes(norm_next) if last else jnp.broadcast_to(norm_next, norm_out.shape)
    if last:
        held[...] = direction
        own = own_columns(held, me, rows)
        curvature_out[...] = on_lanes(row_sum(own * fisher_direction))
        seqs = direction.shape[0]
        solved = jnp.concatenate([solution, direction], axis=0)
        parts = jnp.dot(pieces_of(solved, 3), queries_ref[...], preferred_element_type=jnp.float32)
        scores = parts[: 2 * seqs] + parts[2 * seqs : 4 * seqs] + parts[4 * seqs :]
        solved_out[...] = scores[:seqs]
        along_out[...] = scores[seqs:]
    else:
        fisher_direction_out[...] = fisher_direction
        fisher_residual_out[...] = fisher_residual
        residual_out[...] = residual
        direction_out[...] = direction
        solution_out[...] = solution


def step_cg(blocks, fixed, norm, state, queries, sizes):
    first, last = len(state) == 1, queries is not None
    whole, rows = F32(fixed[2].shape), F32(state[0].shape)
    column = F32(norm.shape)
    operands = [blocks, *fixed, norm, *state]
    out_shape = (rows, column, rows, whole, whole, whole)
    if last:
        operands.append(queries)
        scores = F32((whole.shape[0], queries.shape[1]))
        out_shape = (F32((1, LANES)), F32((1, LANES)), scores, scores)
    return pl.pallas_call(
        functools.partial(step_kernel, sizes, first, last),
        out_shape=out_shape,
        in_specs=[VMEM_SPEC] * len(operands),
        out_specs=(VMEM_SPEC,) * len(out_shape),
        scratch_shapes=[pltpu.VMEM(whole.shape, jnp.float32)],
        compiler_params=PARAMS,
        name="cg_step",
    )(*operands)


def combine_kernel(curvature_ref, norm_ref, solved_ref, along_ref, scores_ref):
    step = norm_ref[...] / jnp.sum(curvature_ref[...], axis=0)
    here = diagonal((solved_ref.shape[0], LANES))
    step = row_sum(jnp.where(here, step, 0.0))
    scores_ref[...] = solved_ref[...] + step * along_ref[...]


def combine(curvature, norm, solved, along):
    return pl.pallas_call(
        combine_kernel,
        out_shape=F32(solved.shape),
        in_specs=[VMEM_SPEC] * 4,
        out_specs=VMEM_SPEC,
        compiler_params=PARAMS,
        name="combine",
    )(curvature, norm, solved, along)


def on_device(dp_size, tensor_size, inputs, in_proj, out_grads, out_proj, prior, queries):
    width = R_IN * R_OUT
    sizes = dp_size, tensor_size
    in_blocks = direct(features(inputs, in_proj, LANES, False, 20, "in_features"), "tensor", tensor_size, order_of(tensor_size))
    out_local = features(out_grads, out_proj, 2 * LANES, True, 44, "out_features")
    partial = partial_vectors(in_blocks, out_local).reshape(-1, width)
    prior, partial = lax.optimization_barrier((prior, partial))
    own_vectors = sum_over(partial, "tensor", tensor_size)
    own_vectors, prior_pieces = lax.optimization_barrier((own_vectors, split_prior(prior, queries)))
    pieces = direct(own_vectors, "dp", dp_size, range(dp_size))
    *prior_pieces, queries = [in_vmem(piece) for piece in prior_pieces]
    vectors, scale, applied_rows, norm = start_cg(pieces, prior_pieces, tensor_size)
    fixed = (*prior_pieces, vectors, scale)
    state = [applied_rows]
    for iteration in range(1, ITERS - 1):
        blocks = gather(state[0], sizes)
        applied_rows, norm, *others = step_cg(blocks, fixed, norm, state, None, sizes)
        state = [applied_rows, *others]
    blocks = gather(state[0], sizes)
    curvature, norm, solved, along = step_cg(blocks, fixed, norm, state, queries, sizes)
    return combine(gather(curvature, sizes), norm, solved, along)


def solution(mesh):
    return jax.shard_map(
        functools.partial(on_device, mesh.shape["dp"], mesh.shape["tensor"]),
        mesh=mesh,
        in_specs=(
            P(("groups", "dp", "tensor"), None),
            P(),
            P(("groups", "dp"), "tensor"),
            P(None, "tensor"),
            P(("groups", "dp", "tensor"), None),
            P(("groups", "dp", "tensor"), None),
        ),
        out_specs=P("groups", ("dp", "tensor")),
        check_vma=False,
    )
```

```python
import functools

import jax
import jax.numpy as jnp
from jax import lax
from jax.experimental import pallas as pl
from jax.experimental.pallas import tpu as pltpu
from jax.sharding import PartitionSpec as P

R_IN = 64
R_OUT = 64
SEQ = 1024
ITERS = 4
LANES = 128
FEW = 4
DEPTH = 6
NT = (((1,), (1,)), ((), ()))
HIGHEST = lax.Precision.HIGHEST
ANY_SPEC = pl.BlockSpec(memory_space=pl.ANY)
VMEM_SPEC = pl.BlockSpec(memory_space=pltpu.VMEM)
PARAMS = pltpu.CompilerParams(vmem_limit_bytes=16 * 2**20)
F32 = functools.partial(jax.ShapeDtypeStruct, dtype=jnp.float32)


def swap(value, axis, size, bit):
    return lax.ppermute(value, axis, [(i, i ^ bit) for i in range(size)])


def bits(size):
    return [1 << b for b in reversed(range(size.bit_length() - 1))]


def group_order(sizes):
    dp_size, tensor_size = sizes
    first = (dp_size - 1) * tensor_size + (tensor_size - 1) // 2
    return [first] + [i for i in range(dp_size * tensor_size) if i != first]


def gather(value, sizes):
    order = group_order(sizes)
    value = jnp.broadcast_to(value[None], (len(order),) + value.shape)
    return lax.all_to_all(value, ("dp", "tensor"), 0, 0, axis_index_groups=[order])


def order_of(size):
    return (0, 2, 3, 1) if size == 4 else tuple(range(size))


def direct(value, axis, size, order):
    return [value] + [swap(value, axis, size, k) for k in order[1:]]


def sum_over(value, axis, size):
    if size > FEW:
        for bit in bits(size):
            value = value + swap(value, axis, size, bit)
        return value
    blocks = direct(value, axis, size, order_of(size))
    while len(blocks) > 1:
        blocks = [a + b for a, b in zip(blocks[::2], blocks[1::2])]
    return blocks[0]


def in_hbm(value):
    return pltpu.with_memory_space_constraint(value, pltpu.HBM)


def in_vmem(value):
    return pltpu.with_memory_space_constraint(value, pltpu.VMEM)


def dot_nt(a, b):
    return lax.dot_general(a, b, NT, precision=HIGHEST, preferred_element_type=jnp.float32)


def row_sum(values):
    return jnp.sum(values, axis=1, keepdims=True)


def stream_kernel(block, by_row, rows_ref, proj_ref, feats_ref, held, proj, turned, sems):
    count, half = proj_ref.shape[0], proj.shape[1]
    steps = held.shape[0] // block
    firsts = [
        pltpu.make_async_copy(
            proj_ref.at[:, pl.ds(h * half, half)], proj.at[pl.ds(h * count, count)], sems.at[steps + h]
        )
        for h in range(2)
    ]

    def fetch(step):
        span = pl.ds(pl.multiple_of(step * block, block), block)
        return pltpu.make_async_copy(rows_ref.at[span], held.at[span], sems.at[step])

    for copy in firsts:
        copy.start()
    for step in range(min(DEPTH, steps)):
        fetch(step).start()
    for copy in firsts:
        copy.wait()
    turned[...] = proj[...].T

    @pl.loop(0, steps)
    def _(step):
        fetch(step).wait()

        @pl.when(step + DEPTH < steps)
        def _():
            fetch(step + DEPTH).start()

        span = pl.ds(pl.multiple_of(step * block, block), block)
        left = jnp.dot(held[span, :half], turned[...], preferred_element_type=jnp.float32)
        right = jnp.dot(held[span, half:], turned[...], preferred_element_type=jnp.float32)
        lane = lax.broadcasted_iota(jnp.int32, left.shape, 1)
        both = jnp.where(lane < count, left, right)
        if by_row:
            feats_ref[span, :] = both
        else:
            both = both.T
            feats_ref[:, span] = both[:count] + both[count:]


def features(rows, proj, block, by_row, limit, name):
    count, width = proj.shape
    shape = (rows.shape[0], 2 * count) if by_row else (count, rows.shape[0])
    return pl.pallas_call(
        functools.partial(stream_kernel, block, by_row),
        out_shape=pltpu.VMEM(shape, jnp.float32),
        in_specs=[ANY_SPEC] * 2,
        out_specs=VMEM_SPEC,
        scratch_shapes=[
            pltpu.VMEM(rows.shape, jnp.bfloat16),
            pltpu.VMEM((2 * count, width // 2), jnp.bfloat16),
            pltpu.VMEM((width // 2, 2 * count), jnp.bfloat16),
            pltpu.SemaphoreType.DMA((rows.shape[0] // block + 2,)),
        ],
        compiler_params=pltpu.CompilerParams(vmem_limit_bytes=limit * 2**20),
        name=name,
    )(in_hbm(rows), in_hbm(proj))


def split_kernel(prior_ref, queries_ref, upper_ref, lower_ref, turned_ref, held, sems):
    chunk = held.shape[1] // sems.shape[0]
    spans = [pl.ds(c * chunk, chunk) for c in range(sems.shape[0])]
    copies = [
        pltpu.make_async_copy(prior_ref.at[:, span], held.at[:, span], sems.at[c])
        for c, span in enumerate(spans)
    ]
    for copy in copies:
        copy.start()
    turned_ref[...] = queries_ref[...].T
    for copy, span in zip(copies, spans):
        copy.wait()
        block = held[:, span]
        upper = block.astype(jnp.bfloat16)
        upper_ref[:, span] = upper
        lower_ref[:, span] = (block - upper.astype(jnp.float32)).astype(jnp.bfloat16)


def split_prior(prior, queries):
    return pl.pallas_call(
        split_kernel,
        out_shape=(
            pltpu.VMEM(prior.shape, jnp.bfloat16),
            pltpu.VMEM(prior.shape, jnp.bfloat16),
            pltpu.VMEM(queries.shape[::-1], jnp.bfloat16),
        ),
        in_specs=[ANY_SPEC, VMEM_SPEC],
        out_specs=(VMEM_SPEC,) * 3,
        scratch_shapes=[pltpu.VMEM(prior.shape, jnp.float32), pltpu.SemaphoreType.DMA((8,))],
        compiler_params=PARAMS,
        name="split_prior",
    )(in_hbm(prior), queries)


def partial_kernel(size, *refs):
    blocks, (out_ref, part_ref, held) = refs[:size], refs[size:]
    me = lax.axis_index("tensor")
    tokens = blocks[0].shape[1]
    for k, block in zip(order_of(size), blocks):
        start = pl.multiple_of((me ^ k) * tokens, LANES)
        held[:, pl.ds(start, tokens)] = block[...]
    for s in range(part_ref.shape[0]):
        span = slice(s * SEQ, (s + 1) * SEQ)
        ins, sums = pieces_of(held[:, span], 2), 0.0
        outs = out_ref[span, :]
        for _ in range(2):
            piece = outs.astype(jnp.bfloat16)
            outs = outs - piece.astype(jnp.float32)
            sums = sums + jnp.dot(ins, piece, preferred_element_type=jnp.float32)
        sums = sums[:R_IN] + sums[R_IN:]
        part_ref[s] = (sums[:, :R_OUT] + sums[:, R_OUT:]) * (1.0 / SEQ)


def partial_vectors(blocks, out_local):
    seq_count = out_local.shape[0] // SEQ
    return pl.pallas_call(
        functools.partial(partial_kernel, len(blocks)),
        out_shape=F32((seq_count, R_IN, R_OUT)),
        in_specs=[VMEM_SPEC] * (len(blocks) + 1),
        out_specs=VMEM_SPEC,
        scratch_shapes=[pltpu.VMEM((R_IN, out_local.shape[0]), jnp.float32)],
        compiler_params=PARAMS,
        name="partial_vectors",
    )(*blocks, out_local)


def own_columns(ref, me, count):
    if count % LANES == 0:
        return ref[:, pl.ds(pl.multiple_of(me * count, LANES), count)]
    per = LANES // count
    held = ref[:, pl.ds(pl.multiple_of((me // per) * LANES, LANES), LANES)]
    return pltpu.roll(held, LANES - (me % per) * count, 1)[:, :count]


def pieces_of(values, count):
    held = []
    for _ in range(count):
        piece = values.astype(jnp.bfloat16)
        held.append(piece)
        values = values - piece.astype(jnp.float32)
    return jnp.concatenate(held, axis=0)


def dot_pieces(a, b, seqs):
    held = lax.dot_general(a, b, NT, preferred_element_type=jnp.float32)
    total = held[:seqs]
    for start in range(seqs, held.shape[0], seqs):
        total = total + held[start : start + seqs]
    return total


def apply_fisher(x, vectors_ref, upper_ref, lower_ref, me):
    seqs = vectors_ref.shape[0]
    pieces = pieces_of(x, 3)
    applied = dot_pieces(pieces, upper_ref[...], seqs)
    applied = applied + dot_pieces(pieces[: 2 * seqs], lower_ref[...], seqs)
    own = own_columns(vectors_ref, me, upper_ref.shape[0])
    for s in range(seqs):
        weight = row_sum(x * vectors_ref[s : s + 1, :]) * (1.0 / seqs)
        applied = applied + weight * own[s : s + 1, :]
    return applied


def flat_index(tensor_size):
    return lax.axis_index("dp") * tensor_size + lax.axis_index("tensor")


def start_kernel(size, tensor_size, *refs):
    pieces, refs = refs[:size], refs[size:]
    upper_ref, lower_ref, vectors_ref, scale_ref, applied_ref, norm_ref, held = refs
    dp = lax.axis_index("dp")
    for k, piece in enumerate(pieces):
        held[dp ^ k] = piece[...]
    vectors = jnp.concatenate([held[k] for k in range(size)], axis=0)
    vectors_ref[...] = vectors
    norm = jnp.broadcast_to(row_sum(vectors * vectors), norm_ref.shape)
    norm_ref[...] = norm
    spread = jnp.sum(norm, axis=0, keepdims=True) * (1.0 / vectors.shape[0])
    scale_ref[...] = jnp.broadcast_to(1.0 / (1.0 + spread), scale_ref.shape)
    me = flat_index(tensor_size)
    applied_ref[...] = apply_fisher(vectors, vectors_ref, upper_ref, lower_ref, me)


def start_cg(pieces, prior_pieces, tensor_size):
    size, seqs = len(pieces), len(pieces) * pieces[0].shape[0]
    rows, width = prior_pieces[0].shape
    column = F32((seqs, LANES))
    return pl.pallas_call(
        functools.partial(start_kernel, size, tensor_size),
        out_shape=(F32((seqs, width)), column, F32((seqs, rows)), column),
        in_specs=[VMEM_SPEC] * (size + 2),
        out_specs=(VMEM_SPEC,) * 4,
        scratch_shapes=[pltpu.VMEM((size,) + pieces[0].shape, jnp.float32)],
        compiler_params=PARAMS,
        name="cg_start",
    )(*pieces, *prior_pieces)


def diagonal(shape):
    return lax.broadcasted_iota(jnp.int32, shape, 0) == lax.broadcasted_iota(jnp.int32, shape, 1)


def on_lanes(column):
    here = diagonal((column.shape[0], LANES))
    return jnp.sum(jnp.where(here, column, 0.0), axis=0, keepdims=True)


def step_kernel(sizes, first, last, *refs):
    blocks_ref, upper_ref, lower_ref, vectors_ref, scale_ref, norm_ref, fisher_direction_ref = refs[:7]
    refs = refs[7:]
    if not first:
        fisher_residual_ref, direction_ref, residual_ref, solution_ref = refs[:4]
        refs = refs[4:]
    if last:
        queries_ref, curvature_out, norm_out, solved_out, along_out, held = refs
    else:
        fisher_direction_out, norm_out, fisher_residual_out, direction_out, residual_out, solution_out, held = refs
    me = flat_index(sizes[1])
    rows = blocks_ref.shape[2]
    for i, k in enumerate(group_order(sizes)):
        held[:, k * rows : (k + 1) * rows] = blocks_ref[i]
    applied = held[...]
    scale = scale_ref[...][:, :1]
    twice = apply_fisher(scale * applied, vectors_ref, upper_ref, lower_ref, me)
    direction = vectors_ref[...] if first else direction_ref[...]
    residual = direction if first else residual_ref[...]
    norm = norm_ref[...][:, :1]
    step = norm / row_sum(direction * applied)
    solution = step * direction
    if not first:
        solution = solution_ref[...] + solution
    residual = residual - step * applied
    norm_next = row_sum(residual * residual)
    share = norm_next / norm
    direction = residual + share * direction
    fisher_direction = fisher_direction_ref[...]
    fisher_residual = (fisher_direction if first else fisher_residual_ref[...]) - (step / scale) * twice
    fisher_direction = fisher_residual + share * fisher_direction
    norm_out[...] = on_lanes(norm_next) if last else jnp.broadcast_to(norm_next, norm_out.shape)
    if last:
        held[...] = direction
        own = own_columns(held, me, rows)
        curvature_out[...] = on_lanes(row_sum(own * fisher_direction))
        seqs = direction.shape[0]
        solved = jnp.concatenate([solution, direction], axis=0)
        parts = jnp.dot(pieces_of(solved, 3), queries_ref[...], preferred_element_type=jnp.float32)
        scores = parts[: 2 * seqs] + parts[2 * seqs : 4 * seqs] + parts[4 * seqs :]
        solved_out[...] = scores[:seqs]
        along_out[...] = scores[seqs:]
    else:
        fisher_direction_out[...] = fisher_direction
        fisher_residual_out[...] = fisher_residual
        residual_out[...] = residual
        direction_out[...] = direction
        solution_out[...] = solution


def step_cg(blocks, fixed, norm, state, queries, sizes):
    first, last = len(state) == 1, queries is not None
    whole, rows = F32(fixed[2].shape), F32(state[0].shape)
    column = F32(norm.shape)
    operands = [blocks, *fixed, norm, *state]
    out_shape = (rows, column, rows, whole, whole, whole)
    if last:
        operands.append(queries)
        scores = F32((whole.shape[0], queries.shape[1]))
        out_shape = (F32((1, LANES)), F32((1, LANES)), scores, scores)
    return pl.pallas_call(
        functools.partial(step_kernel, sizes, first, last),
        out_shape=out_shape,
        in_specs=[VMEM_SPEC] * len(operands),
        out_specs=(VMEM_SPEC,) * len(out_shape),
        scratch_shapes=[pltpu.VMEM(whole.shape, jnp.float32)],
        compiler_params=PARAMS,
        name="cg_step",
    )(*operands)


def combine_kernel(curvature_ref, norm_ref, solved_ref, along_ref, scores_ref):
    step = norm_ref[...] / jnp.sum(curvature_ref[...], axis=0)
    here = diagonal((solved_ref.shape[0], LANES))
    step = row_sum(jnp.where(here, step, 0.0))
    scores_ref[...] = solved_ref[...] + step * along_ref[...]


def combine(curvature, norm, solved, along):
    return pl.pallas_call(
        combine_kernel,
        out_shape=F32(solved.shape),
        in_specs=[VMEM_SPEC] * 4,
        out_specs=VMEM_SPEC,
        compiler_params=PARAMS,
        name="combine",
    )(curvature, norm, solved, along)


def on_device(dp_size, tensor_size, inputs, in_proj, out_grads, out_proj, prior, queries):
    width = R_IN * R_OUT
    sizes = dp_size, tensor_size
    in_blocks = direct(features(inputs, in_proj, LANES, False, 20, "in_features"), "tensor", tensor_size, order_of(tensor_size))
    out_local = features(out_grads, out_proj, LANES, True, 44, "out_features")
    partial = partial_vectors(in_blocks, out_local).reshape(-1, width)
    prior, partial = lax.optimization_barrier((prior, partial))
    own_vectors = sum_over(partial, "tensor", tensor_size)
    own_vectors, prior_pieces = lax.optimization_barrier((own_vectors, split_prior(prior, queries)))
    pieces = direct(own_vectors, "dp", dp_size, range(dp_size))
    *prior_pieces, queries = [in_vmem(piece) for piece in prior_pieces]
    vectors, scale, applied_rows, norm = start_cg(pieces, prior_pieces, tensor_size)
    fixed = (*prior_pieces, vectors, scale)
    state = [applied_rows]
    for iteration in range(1, ITERS - 1):
        blocks = gather(state[0], sizes)
        applied_rows, norm, *others = step_cg(blocks, fixed, norm, state, None, sizes)
        state = [applied_rows, *others]
    blocks = gather(state[0], sizes)
    curvature, norm, solved, along = step_cg(blocks, fixed, norm, state, queries, sizes)
    return combine(gather(curvature, sizes), norm, solved, along)


def solution(mesh):
    return jax.shard_map(
        functools.partial(on_device, mesh.shape["dp"], mesh.shape["tensor"]),
        mesh=mesh,
        in_specs=(
            P(("groups", "dp", "tensor"), None),
            P(),
            P(("groups", "dp"), "tensor"),
            P(None, "tensor"),
            P(("groups", "dp", "tensor"), None),
            P(("groups", "dp", "tensor"), None),
        ),
        out_specs=P("groups", ("dp", "tensor")),
        check_vma=False,
    )
```

```python
import functools

import jax
import jax.numpy as jnp
from jax import lax
from jax.experimental import pallas as pl
from jax.experimental.pallas import tpu as pltpu
from jax.sharding import PartitionSpec as P

R_IN = 64
R_OUT = 64
SEQ = 1024
ITERS = 4
LANES = 128
FEW = 4
DEPTH = 3
NT = (((1,), (1,)), ((), ()))
HIGHEST = lax.Precision.HIGHEST
ANY_SPEC = pl.BlockSpec(memory_space=pl.ANY)
VMEM_SPEC = pl.BlockSpec(memory_space=pltpu.VMEM)
PARAMS = pltpu.CompilerParams(vmem_limit_bytes=16 * 2**20)
F32 = functools.partial(jax.ShapeDtypeStruct, dtype=jnp.float32)


def swap(value, axis, size, bit):
    return lax.ppermute(value, axis, [(i, i ^ bit) for i in range(size)])


def bits(size):
    return [1 << b for b in reversed(range(size.bit_length() - 1))]


def group_order(sizes):
    dp_size, tensor_size = sizes
    first = (dp_size - 1) * tensor_size + (tensor_size - 1) // 2
    return [first] + [i for i in range(dp_size * tensor_size) if i != first]


def gather(value, sizes):
    order = group_order(sizes)
    value = jnp.broadcast_to(value[None], (len(order),) + value.shape)
    return lax.all_to_all(value, ("dp", "tensor"), 0, 0, axis_index_groups=[order])


def order_of(size):
    return (0, 2, 3, 1) if size == 4 else tuple(range(size))


def direct(value, axis, size, order):
    return [value] + [swap(value, axis, size, k) for k in order[1:]]


def sum_over(value, axis, size):
    if size > FEW:
        for bit in bits(size):
            value = value + swap(value, axis, size, bit)
        return value
    blocks = direct(value, axis, size, range(size))
    while len(blocks) > 1:
        blocks = [a + b for a, b in zip(blocks[::2], blocks[1::2])]
    return blocks[0]


def in_hbm(value):
    return pltpu.with_memory_space_constraint(value, pltpu.HBM)


def in_vmem(value):
    return pltpu.with_memory_space_constraint(value, pltpu.VMEM)


def dot_nt(a, b):
    return lax.dot_general(a, b, NT, precision=HIGHEST, preferred_element_type=jnp.float32)


def row_sum(values):
    return jnp.sum(values, axis=1, keepdims=True)


def stream_kernel(block, by_row, rows_ref, proj_ref, feats_ref, held, proj, turned, sems):
    count, half = proj_ref.shape[0], proj.shape[1]
    steps = held.shape[0] // block
    firsts = [
        pltpu.make_async_copy(
            proj_ref.at[:, pl.ds(h * half, half)], proj.at[pl.ds(h * count, count)], sems.at[steps + h]
        )
        for h in range(2)
    ]

    def fetch(step):
        span = pl.ds(pl.multiple_of(step * block, block), block)
        return pltpu.make_async_copy(rows_ref.at[span], held.at[span], sems.at[step])

    for copy in firsts:
        copy.start()
    for step in range(min(DEPTH, steps)):
        fetch(step).start()
    for copy in firsts:
        copy.wait()
    turned[...] = proj[...].T

    @pl.loop(0, steps)
    def _(step):
        fetch(step).wait()

        @pl.when(step + DEPTH < steps)
        def _():
            fetch(step + DEPTH).start()

        span = pl.ds(pl.multiple_of(step * block, block), block)
        left = jnp.dot(held[span, :half], turned[...], preferred_element_type=jnp.float32)
        right = jnp.dot(held[span, half:], turned[...], preferred_element_type=jnp.float32)
        lane = lax.broadcasted_iota(jnp.int32, left.shape, 1)
        both = jnp.where(lane < count, left, right)
        if by_row:
            feats_ref[span, :] = both
        else:
            both = both.T
            feats_ref[:, span] = both[:count] + both[count:]


def features(rows, proj, block, by_row, limit, name):
    count, width = proj.shape
    shape = (rows.shape[0], 2 * count) if by_row else (count, rows.shape[0])
    return pl.pallas_call(
        functools.partial(stream_kernel, block, by_row),
        out_shape=pltpu.VMEM(shape, jnp.float32),
        in_specs=[ANY_SPEC] * 2,
        out_specs=VMEM_SPEC,
        scratch_shapes=[
            pltpu.VMEM(rows.shape, jnp.bfloat16),
            pltpu.VMEM((2 * count, width // 2), jnp.bfloat16),
            pltpu.VMEM((width // 2, 2 * count), jnp.bfloat16),
            pltpu.SemaphoreType.DMA((rows.shape[0] // block + 2,)),
        ],
        compiler_params=pltpu.CompilerParams(vmem_limit_bytes=limit * 2**20),
        name=name,
    )(in_hbm(rows), in_hbm(proj))


def split_kernel(prior_ref, queries_ref, upper_ref, lower_ref, turned_ref, held, sems):
    chunk = held.shape[1] // sems.shape[0]
    spans = [pl.ds(c * chunk, chunk) for c in range(sems.shape[0])]
    copies = [
        pltpu.make_async_copy(prior_ref.at[:, span], held.at[:, span], sems.at[c])
        for c, span in enumerate(spans)
    ]
    for copy in copies:
        copy.start()
    turned_ref[...] = queries_ref[...].T
    for copy, span in zip(copies, spans):
        copy.wait()
        block = held[:, span]
        upper = block.astype(jnp.bfloat16)
        upper_ref[:, span] = upper
        lower_ref[:, span] = (block - upper.astype(jnp.float32)).astype(jnp.bfloat16)


def split_prior(prior, queries):
    return pl.pallas_call(
        split_kernel,
        out_shape=(
            pltpu.VMEM(prior.shape, jnp.bfloat16),
            pltpu.VMEM(prior.shape, jnp.bfloat16),
            pltpu.VMEM(queries.shape[::-1], jnp.bfloat16),
        ),
        in_specs=[ANY_SPEC, VMEM_SPEC],
        out_specs=(VMEM_SPEC,) * 3,
        scratch_shapes=[pltpu.VMEM(prior.shape, jnp.float32), pltpu.SemaphoreType.DMA((8,))],
        compiler_params=PARAMS,
        name="split_prior",
    )(in_hbm(prior), queries)


def partial_kernel(size, *refs):
    blocks, (out_ref, part_ref, held) = refs[:size], refs[size:]
    me = lax.axis_index("tensor")
    tokens = blocks[0].shape[1]
    for k, block in zip(order_of(size), blocks):
        start = pl.multiple_of((me ^ k) * tokens, LANES)
        held[:, pl.ds(start, tokens)] = block[...]
    for s in range(part_ref.shape[0]):
        span = slice(s * SEQ, (s + 1) * SEQ)
        ins, sums = pieces_of(held[:, span], 2), 0.0
        outs = out_ref[span, :]
        for _ in range(2):
            piece = outs.astype(jnp.bfloat16)
            outs = outs - piece.astype(jnp.float32)
            sums = sums + jnp.dot(ins, piece, preferred_element_type=jnp.float32)
        sums = sums[:R_IN] + sums[R_IN:]
        part_ref[s] = (sums[:, :R_OUT] + sums[:, R_OUT:]) * (1.0 / SEQ)


def partial_vectors(blocks, out_local):
    seq_count = out_local.shape[0] // SEQ
    return pl.pallas_call(
        functools.partial(partial_kernel, len(blocks)),
        out_shape=F32((seq_count, R_IN, R_OUT)),
        in_specs=[VMEM_SPEC] * (len(blocks) + 1),
        out_specs=VMEM_SPEC,
        scratch_shapes=[pltpu.VMEM((R_IN, out_local.shape[0]), jnp.float32)],
        compiler_params=PARAMS,
        name="partial_vectors",
    )(*blocks, out_local)


def own_columns(ref, me, count):
    if count % LANES == 0:
        return ref[:, pl.ds(pl.multiple_of(me * count, LANES), count)]
    per = LANES // count
    held = ref[:, pl.ds(pl.multiple_of((me // per) * LANES, LANES), LANES)]
    return pltpu.roll(held, LANES - (me % per) * count, 1)[:, :count]


def pieces_of(values, count):
    held = []
    for _ in range(count):
        piece = values.astype(jnp.bfloat16)
        held.append(piece)
        values = values - piece.astype(jnp.float32)
    return jnp.concatenate(held, axis=0)


def dot_pieces(a, b, seqs):
    held = lax.dot_general(a, b, NT, preferred_element_type=jnp.float32)
    total = held[:seqs]
    for start in range(seqs, held.shape[0], seqs):
        total = total + held[start : start + seqs]
    return total


def apply_fisher(x, vectors_ref, upper_ref, lower_ref, me):
    seqs = vectors_ref.shape[0]
    pieces = pieces_of(x, 3)
    applied = dot_pieces(pieces, upper_ref[...], seqs)
    applied = applied + dot_pieces(pieces[: 2 * seqs], lower_ref[...], seqs)
    own = own_columns(vectors_ref, me, upper_ref.shape[0])
    for s in range(seqs):
        weight = row_sum(x * vectors_ref[s : s + 1, :]) * (1.0 / seqs)
        applied = applied + weight * own[s : s + 1, :]
    return applied


def flat_index(tensor_size):
    return lax.axis_index("dp") * tensor_size + lax.axis_index("tensor")


def start_kernel(size, tensor_size, *refs):
    pieces, refs = refs[:size], refs[size:]
    upper_ref, lower_ref, vectors_ref, scale_ref, applied_ref, norm_ref, held = refs
    dp = lax.axis_index("dp")
    for k, piece in enumerate(pieces):
        held[dp ^ k] = piece[...]
    vectors = jnp.concatenate([held[k] for k in range(size)], axis=0)
    vectors_ref[...] = vectors
    norm = jnp.broadcast_to(row_sum(vectors * vectors), norm_ref.shape)
    norm_ref[...] = norm
    spread = jnp.sum(norm, axis=0, keepdims=True) * (1.0 / vectors.shape[0])
    scale_ref[...] = jnp.broadcast_to(1.0 / (1.0 + spread), scale_ref.shape)
    me = flat_index(tensor_size)
    applied_ref[...] = apply_fisher(vectors, vectors_ref, upper_ref, lower_ref, me)


def start_cg(pieces, prior_pieces, tensor_size):
    size, seqs = len(pieces), len(pieces) * pieces[0].shape[0]
    rows, width = prior_pieces[0].shape
    column = F32((seqs, LANES))
    return pl.pallas_call(
        functools.partial(start_kernel, size, tensor_size),
        out_shape=(F32((seqs, width)), column, F32((seqs, rows)), column),
        in_specs=[VMEM_SPEC] * (size + 2),
        out_specs=(VMEM_SPEC,) * 4,
        scratch_shapes=[pltpu.VMEM((size,) + pieces[0].shape, jnp.float32)],
        compiler_params=PARAMS,
        name="cg_start",
    )(*pieces, *prior_pieces)


def diagonal(shape):
    return lax.broadcasted_iota(jnp.int32, shape, 0) == lax.broadcasted_iota(jnp.int32, shape, 1)


def on_lanes(column):
    here = diagonal((column.shape[0], LANES))
    return jnp.sum(jnp.where(here, column, 0.0), axis=0, keepdims=True)


def step_kernel(sizes, first, last, *refs):
    blocks_ref, upper_ref, lower_ref, vectors_ref, scale_ref, norm_ref, fisher_direction_ref = refs[:7]
    refs = refs[7:]
    if not first:
        fisher_residual_ref, direction_ref, residual_ref, solution_ref = refs[:4]
        refs = refs[4:]
    if last:
        queries_ref, curvature_out, norm_out, solved_out, along_out, held = refs
    else:
        fisher_direction_out, norm_out, fisher_residual_out, direction_out, residual_out, solution_out, held = refs
    me = flat_index(sizes[1])
    rows = blocks_ref.shape[2]
    for i, k in enumerate(group_order(sizes)):
        held[:, k * rows : (k + 1) * rows] = blocks_ref[i]
    applied = held[...]
    scale = scale_ref[...][:, :1]
    twice = apply_fisher(scale * applied, vectors_ref, upper_ref, lower_ref, me)
    direction = vectors_ref[...] if first else direction_ref[...]
    residual = direction if first else residual_ref[...]
    norm = norm_ref[...][:, :1]
    step = norm / row_sum(direction * applied)
    solution = step * direction
    if not first:
        solution = solution_ref[...] + solution
    residual = residual - step * applied
    norm_next = row_sum(residual * residual)
    share = norm_next / norm
    direction = residual + share * direction
    fisher_direction = fisher_direction_ref[...]
    fisher_residual = (fisher_direction if first else fisher_residual_ref[...]) - (step / scale) * twice
    fisher_direction = fisher_residual + share * fisher_direction
    norm_out[...] = on_lanes(norm_next) if last else jnp.broadcast_to(norm_next, norm_out.shape)
    if last:
        held[...] = direction
        own = own_columns(held, me, rows)
        curvature_out[...] = on_lanes(row_sum(own * fisher_direction))
        seqs = direction.shape[0]
        solved = jnp.concatenate([solution, direction], axis=0)
        parts = jnp.dot(pieces_of(solved, 3), queries_ref[...], preferred_element_type=jnp.float32)
        scores = parts[: 2 * seqs] + parts[2 * seqs : 4 * seqs] + parts[4 * seqs :]
        solved_out[...] = scores[:seqs]
        along_out[...] = scores[seqs:]
    else:
        fisher_direction_out[...] = fisher_direction
        fisher_residual_out[...] = fisher_residual
        residual_out[...] = residual
        direction_out[...] = direction
        solution_out[...] = solution


def step_cg(blocks, fixed, norm, state, queries, sizes):
    first, last = len(state) == 1, queries is not None
    whole, rows = F32(fixed[2].shape), F32(state[0].shape)
    column = F32(norm.shape)
    operands = [blocks, *fixed, norm, *state]
    out_shape = (rows, column, rows, whole, whole, whole)
    if last:
        operands.append(queries)
        scores = F32((whole.shape[0], queries.shape[1]))
        out_shape = (F32((1, LANES)), F32((1, LANES)), scores, scores)
    return pl.pallas_call(
        functools.partial(step_kernel, sizes, first, last),
        out_shape=out_shape,
        in_specs=[VMEM_SPEC] * len(operands),
        out_specs=(VMEM_SPEC,) * len(out_shape),
        scratch_shapes=[pltpu.VMEM(whole.shape, jnp.float32)],
        compiler_params=PARAMS,
        name="cg_step",
    )(*operands)


def combine_kernel(curvature_ref, norm_ref, solved_ref, along_ref, scores_ref):
    step = norm_ref[...] / jnp.sum(curvature_ref[...], axis=0)
    here = diagonal((solved_ref.shape[0], LANES))
    step = row_sum(jnp.where(here, step, 0.0))
    scores_ref[...] = solved_ref[...] + step * along_ref[...]


def combine(curvature, norm, solved, along):
    return pl.pallas_call(
        combine_kernel,
        out_shape=F32(solved.shape),
        in_specs=[VMEM_SPEC] * 4,
        out_specs=VMEM_SPEC,
        compiler_params=PARAMS,
        name="combine",
    )(curvature, norm, solved, along)


def on_device(dp_size, tensor_size, inputs, in_proj, out_grads, out_proj, prior, queries):
    width = R_IN * R_OUT
    sizes = dp_size, tensor_size
    in_blocks = direct(features(inputs, in_proj, LANES, False, 20, "in_features"), "tensor", tensor_size, order_of(tensor_size))
    out_local = features(out_grads, out_proj, 2 * LANES, True, 44, "out_features")
    partial = partial_vectors(in_blocks, out_local).reshape(-1, width)
    prior, partial = lax.optimization_barrier((prior, partial))
    own_vectors = sum_over(partial, "tensor", tensor_size)
    own_vectors, prior_pieces = lax.optimization_barrier((own_vectors, split_prior(prior, queries)))
    pieces = direct(own_vectors, "dp", dp_size, range(dp_size))
    *prior_pieces, queries = [in_vmem(piece) for piece in prior_pieces]
    vectors, scale, applied_rows, norm = start_cg(pieces, prior_pieces, tensor_size)
    fixed = (*prior_pieces, vectors, scale)
    state = [applied_rows]
    for iteration in range(1, ITERS - 1):
        blocks = gather(state[0], sizes)
        applied_rows, norm, *others = step_cg(blocks, fixed, norm, state, None, sizes)
        state = [applied_rows, *others]
    blocks = gather(state[0], sizes)
    curvature, norm, solved, along = step_cg(blocks, fixed, norm, state, queries, sizes)
    return combine(gather(curvature, sizes), norm, solved, along)


def solution(mesh):
    return jax.shard_map(
        functools.partial(on_device, mesh.shape["dp"], mesh.shape["tensor"]),
        mesh=mesh,
        in_specs=(
            P(("groups", "dp", "tensor"), None),
            P(),
            P(("groups", "dp"), "tensor"),
            P(None, "tensor"),
            P(("groups", "dp", "tensor"), None),
            P(("groups", "dp", "tensor"), None),
        ),
        out_specs=P("groups", ("dp", "tensor")),
        check_vma=False,
    )
```

```python
import functools

import jax
import jax.numpy as jnp
from jax import lax
from jax.experimental import pallas as pl
from jax.experimental.pallas import tpu as pltpu
from jax.sharding import PartitionSpec as P

R_IN = 64
R_OUT = 64
SEQ = 1024
ITERS = 4
LANES = 128
FEW = 4
DEPTH = 3
NT = (((1,), (1,)), ((), ()))
HIGHEST = lax.Precision.HIGHEST
ANY_SPEC = pl.BlockSpec(memory_space=pl.ANY)
VMEM_SPEC = pl.BlockSpec(memory_space=pltpu.VMEM)
PARAMS = pltpu.CompilerParams(vmem_limit_bytes=16 * 2**20)
F32 = functools.partial(jax.ShapeDtypeStruct, dtype=jnp.float32)


def swap(value, axis, size, bit):
    return lax.ppermute(value, axis, [(i, i ^ bit) for i in range(size)])


def bits(size):
    return [1 << b for b in reversed(range(size.bit_length() - 1))]


def group_order(sizes):
    dp_size, tensor_size = sizes
    first = (dp_size - 1) * tensor_size + tensor_size // 2
    return [first] + [i for i in range(dp_size * tensor_size) if i != first]


def gather(value, sizes):
    order = group_order(sizes)
    value = jnp.broadcast_to(value[None], (len(order),) + value.shape)
    return lax.all_to_all(value, ("dp", "tensor"), 0, 0, axis_index_groups=[order])


def order_of(size):
    return (0, 2, 3, 1) if size == 4 else tuple(range(size))


def direct(value, axis, size, order):
    return [value] + [swap(value, axis, size, k) for k in order[1:]]


def sum_over(value, axis, size):
    if size > FEW:
        for bit in bits(size):
            value = value + swap(value, axis, size, bit)
        return value
    blocks = direct(value, axis, size, range(size))
    while len(blocks) > 1:
        blocks = [a + b for a, b in zip(blocks[::2], blocks[1::2])]
    return blocks[0]


def in_hbm(value):
    return pltpu.with_memory_space_constraint(value, pltpu.HBM)


def in_vmem(value):
    return pltpu.with_memory_space_constraint(value, pltpu.VMEM)


def dot_nt(a, b):
    return lax.dot_general(a, b, NT, precision=HIGHEST, preferred_element_type=jnp.float32)


def row_sum(values):
    return jnp.sum(values, axis=1, keepdims=True)


def stream_kernel(block, by_row, rows_ref, proj_ref, feats_ref, held, proj, turned, sems):
    count, half = proj_ref.shape[0], proj.shape[1]
    steps = held.shape[0] // block
    firsts = [
        pltpu.make_async_copy(
            proj_ref.at[:, pl.ds(h * half, half)], proj.at[pl.ds(h * count, count)], sems.at[steps + h]
        )
        for h in range(2)
    ]

    def fetch(step):
        span = pl.ds(pl.multiple_of(step * block, block), block)
        return pltpu.make_async_copy(rows_ref.at[span], held.at[span], sems.at[step])

    for copy in firsts:
        copy.start()
    for step in range(min(DEPTH, steps)):
        fetch(step).start()
    for copy in firsts:
        copy.wait()
    turned[...] = proj[...].T

    @pl.loop(0, steps)
    def _(step):
        fetch(step).wait()

        @pl.when(step + DEPTH < steps)
        def _():
            fetch(step + DEPTH).start()

        span = pl.ds(pl.multiple_of(step * block, block), block)
        left = jnp.dot(held[span, :half], turned[...], preferred_element_type=jnp.float32)
        right = jnp.dot(held[span, half:], turned[...], preferred_element_type=jnp.float32)
        lane = lax.broadcasted_iota(jnp.int32, left.shape, 1)
        both = jnp.where(lane < count, left, right)
        if by_row:
            feats_ref[span, :] = both
        else:
            both = both.T
            feats_ref[:, span] = both[:count] + both[count:]


def features(rows, proj, block, by_row, limit, name):
    count, width = proj.shape
    shape = (rows.shape[0], 2 * count) if by_row else (count, rows.shape[0])
    return pl.pallas_call(
        functools.partial(stream_kernel, block, by_row),
        out_shape=pltpu.VMEM(shape, jnp.float32),
        in_specs=[ANY_SPEC] * 2,
        out_specs=VMEM_SPEC,
        scratch_shapes=[
            pltpu.VMEM(rows.shape, jnp.bfloat16),
            pltpu.VMEM((2 * count, width // 2), jnp.bfloat16),
            pltpu.VMEM((width // 2, 2 * count), jnp.bfloat16),
            pltpu.SemaphoreType.DMA((rows.shape[0] // block + 2,)),
        ],
        compiler_params=pltpu.CompilerParams(vmem_limit_bytes=limit * 2**20),
        name=name,
    )(in_hbm(rows), in_hbm(proj))


def split_kernel(prior_ref, queries_ref, upper_ref, lower_ref, turned_ref, held, sems):
    chunk = held.shape[1] // sems.shape[0]
    spans = [pl.ds(c * chunk, chunk) for c in range(sems.shape[0])]
    copies = [
        pltpu.make_async_copy(prior_ref.at[:, span], held.at[:, span], sems.at[c])
        for c, span in enumerate(spans)
    ]
    for copy in copies:
        copy.start()
    turned_ref[...] = queries_ref[...].T
    for copy, span in zip(copies, spans):
        copy.wait()
        block = held[:, span]
        upper = block.astype(jnp.bfloat16)
        upper_ref[:, span] = upper
        lower_ref[:, span] = (block - upper.astype(jnp.float32)).astype(jnp.bfloat16)


def split_prior(prior, queries):
    return pl.pallas_call(
        split_kernel,
        out_shape=(
            pltpu.VMEM(prior.shape, jnp.bfloat16),
            pltpu.VMEM(prior.shape, jnp.bfloat16),
            pltpu.VMEM(queries.shape[::-1], jnp.bfloat16),
        ),
        in_specs=[ANY_SPEC, VMEM_SPEC],
        out_specs=(VMEM_SPEC,) * 3,
        scratch_shapes=[pltpu.VMEM(prior.shape, jnp.float32), pltpu.SemaphoreType.DMA((8,))],
        compiler_params=PARAMS,
        name="split_prior",
    )(in_hbm(prior), queries)


def partial_kernel(size, *refs):
    blocks, (out_ref, part_ref, held) = refs[:size], refs[size:]
    me = lax.axis_index("tensor")
    tokens = blocks[0].shape[1]
    for k, block in zip(order_of(size), blocks):
        start = pl.multiple_of((me ^ k) * tokens, LANES)
        held[:, pl.ds(start, tokens)] = block[...]
    for s in range(part_ref.shape[0]):
        span = slice(s * SEQ, (s + 1) * SEQ)
        ins, sums = pieces_of(held[:, span], 2), 0.0
        outs = out_ref[span, :]
        for _ in range(2):
            piece = outs.astype(jnp.bfloat16)
            outs = outs - piece.astype(jnp.float32)
            sums = sums + jnp.dot(ins, piece, preferred_element_type=jnp.float32)
        sums = sums[:R_IN] + sums[R_IN:]
        part_ref[s] = (sums[:, :R_OUT] + sums[:, R_OUT:]) * (1.0 / SEQ)


def partial_vectors(blocks, out_local):
    seq_count = out_local.shape[0] // SEQ
    return pl.pallas_call(
        functools.partial(partial_kernel, len(blocks)),
        out_shape=F32((seq_count, R_IN, R_OUT)),
        in_specs=[VMEM_SPEC] * (len(blocks) + 1),
        out_specs=VMEM_SPEC,
        scratch_shapes=[pltpu.VMEM((R_IN, out_local.shape[0]), jnp.float32)],
        compiler_params=PARAMS,
        name="partial_vectors",
    )(*blocks, out_local)


def own_columns(ref, me, count):
    if count % LANES == 0:
        return ref[:, pl.ds(pl.multiple_of(me * count, LANES), count)]
    per = LANES // count
    held = ref[:, pl.ds(pl.multiple_of((me // per) * LANES, LANES), LANES)]
    return pltpu.roll(held, LANES - (me % per) * count, 1)[:, :count]


def pieces_of(values, count):
    held = []
    for _ in range(count):
        piece = values.astype(jnp.bfloat16)
        held.append(piece)
        values = values - piece.astype(jnp.float32)
    return jnp.concatenate(held, axis=0)


def dot_pieces(a, b, seqs):
    held = lax.dot_general(a, b, NT, preferred_element_type=jnp.float32)
    total = held[:seqs]
    for start in range(seqs, held.shape[0], seqs):
        total = total + held[start : start + seqs]
    return total


def apply_fisher(x, vectors_ref, upper_ref, lower_ref, me):
    seqs = vectors_ref.shape[0]
    pieces = pieces_of(x, 3)
    applied = dot_pieces(pieces, upper_ref[...], seqs)
    applied = applied + dot_pieces(pieces[: 2 * seqs], lower_ref[...], seqs)
    own = own_columns(vectors_ref, me, upper_ref.shape[0])
    for s in range(seqs):
        weight = row_sum(x * vectors_ref[s : s + 1, :]) * (1.0 / seqs)
        applied = applied + weight * own[s : s + 1, :]
    return applied


def flat_index(tensor_size):
    return lax.axis_index("dp") * tensor_size + lax.axis_index("tensor")


def start_kernel(size, tensor_size, *refs):
    pieces, refs = refs[:size], refs[size:]
    upper_ref, lower_ref, vectors_ref, scale_ref, applied_ref, norm_ref, held = refs
    dp = lax.axis_index("dp")
    for k, piece in enumerate(pieces):
        held[dp ^ k] = piece[...]
    vectors = jnp.concatenate([held[k] for k in range(size)], axis=0)
    vectors_ref[...] = vectors
    norm = jnp.broadcast_to(row_sum(vectors * vectors), norm_ref.shape)
    norm_ref[...] = norm
    spread = jnp.sum(norm, axis=0, keepdims=True) * (1.0 / vectors.shape[0])
    scale_ref[...] = jnp.broadcast_to(1.0 / (1.0 + spread), scale_ref.shape)
    me = flat_index(tensor_size)
    applied_ref[...] = apply_fisher(vectors, vectors_ref, upper_ref, lower_ref, me)


def start_cg(pieces, prior_pieces, tensor_size):
    size, seqs = len(pieces), len(pieces) * pieces[0].shape[0]
    rows, width = prior_pieces[0].shape
    column = F32((seqs, LANES))
    return pl.pallas_call(
        functools.partial(start_kernel, size, tensor_size),
        out_shape=(F32((seqs, width)), column, F32((seqs, rows)), column),
        in_specs=[VMEM_SPEC] * (size + 2),
        out_specs=(VMEM_SPEC,) * 4,
        scratch_shapes=[pltpu.VMEM((size,) + pieces[0].shape, jnp.float32)],
        compiler_params=PARAMS,
        name="cg_start",
    )(*pieces, *prior_pieces)


def diagonal(shape):
    return lax.broadcasted_iota(jnp.int32, shape, 0) == lax.broadcasted_iota(jnp.int32, shape, 1)


def on_lanes(column):
    here = diagonal((column.shape[0], LANES))
    return jnp.sum(jnp.where(here, column, 0.0), axis=0, keepdims=True)


def step_kernel(sizes, first, last, *refs):
    blocks_ref, upper_ref, lower_ref, vectors_ref, scale_ref, norm_ref, fisher_direction_ref = refs[:7]
    refs = refs[7:]
    if not first:
        fisher_residual_ref, direction_ref, residual_ref, solution_ref = refs[:4]
        refs = refs[4:]
    if last:
        queries_ref, curvature_out, norm_out, solved_out, along_out, held = refs
    else:
        fisher_direction_out, norm_out, fisher_residual_out, direction_out, residual_out, solution_out, held = refs
    me = flat_index(sizes[1])
    rows = blocks_ref.shape[2]
    for i, k in enumerate(group_order(sizes)):
        held[:, k * rows : (k + 1) * rows] = blocks_ref[i]
    applied = held[...]
    scale = scale_ref[...][:, :1]
    twice = apply_fisher(scale * applied, vectors_ref, upper_ref, lower_ref, me)
    direction = vectors_ref[...] if first else direction_ref[...]
    residual = direction if first else residual_ref[...]
    norm = norm_ref[...][:, :1]
    step = norm / row_sum(direction * applied)
    solution = step * direction
    if not first:
        solution = solution_ref[...] + solution
    residual = residual - step * applied
    norm_next = row_sum(residual * residual)
    share = norm_next / norm
    direction = residual + share * direction
    fisher_direction = fisher_direction_ref[...]
    fisher_residual = (fisher_direction if first else fisher_residual_ref[...]) - (step / scale) * twice
    fisher_direction = fisher_residual + share * fisher_direction
    norm_out[...] = on_lanes(norm_next) if last else jnp.broadcast_to(norm_next, norm_out.shape)
    if last:
        held[...] = direction
        own = own_columns(held, me, rows)
        curvature_out[...] = on_lanes(row_sum(own * fisher_direction))
        seqs = direction.shape[0]
        solved = jnp.concatenate([solution, direction], axis=0)
        parts = jnp.dot(pieces_of(solved, 3), queries_ref[...], preferred_element_type=jnp.float32)
        scores = parts[: 2 * seqs] + parts[2 * seqs : 4 * seqs] + parts[4 * seqs :]
        solved_out[...] = scores[:seqs]
        along_out[...] = scores[seqs:]
    else:
        fisher_direction_out[...] = fisher_direction
        fisher_residual_out[...] = fisher_residual
        residual_out[...] = residual
        direction_out[...] = direction
        solution_out[...] = solution


def step_cg(blocks, fixed, norm, state, queries, sizes):
    first, last = len(state) == 1, queries is not None
    whole, rows = F32(fixed[2].shape), F32(state[0].shape)
    column = F32(norm.shape)
    operands = [blocks, *fixed, norm, *state]
    out_shape = (rows, column, rows, whole, whole, whole)
    if last:
        operands.append(queries)
        scores = F32((whole.shape[0], queries.shape[1]))
        out_shape = (F32((1, LANES)), F32((1, LANES)), scores, scores)
    return pl.pallas_call(
        functools.partial(step_kernel, sizes, first, last),
        out_shape=out_shape,
        in_specs=[VMEM_SPEC] * len(operands),
        out_specs=(VMEM_SPEC,) * len(out_shape),
        scratch_shapes=[pltpu.VMEM(whole.shape, jnp.float32)],
        compiler_params=PARAMS,
        name="cg_step",
    )(*operands)


def combine_kernel(curvature_ref, norm_ref, solved_ref, along_ref, scores_ref):
    step = norm_ref[...] / jnp.sum(curvature_ref[...], axis=0)
    here = diagonal((solved_ref.shape[0], LANES))
    step = row_sum(jnp.where(here, step, 0.0))
    scores_ref[...] = solved_ref[...] + step * along_ref[...]


def combine(curvature, norm, solved, along):
    return pl.pallas_call(
        combine_kernel,
        out_shape=F32(solved.shape),
        in_specs=[VMEM_SPEC] * 4,
        out_specs=VMEM_SPEC,
        compiler_params=PARAMS,
        name="combine",
    )(curvature, norm, solved, along)


def on_device(dp_size, tensor_size, inputs, in_proj, out_grads, out_proj, prior, queries):
    width = R_IN * R_OUT
    sizes = dp_size, tensor_size
    in_blocks = direct(features(inputs, in_proj, LANES, False, 20, "in_features"), "tensor", tensor_size, order_of(tensor_size))
    out_local = features(out_grads, out_proj, 2 * LANES, True, 44, "out_features")
    partial = partial_vectors(in_blocks, out_local).reshape(-1, width)
    prior, partial = lax.optimization_barrier((prior, partial))
    own_vectors = sum_over(partial, "tensor", tensor_size)
    own_vectors, prior_pieces = lax.optimization_barrier((own_vectors, split_prior(prior, queries)))
    pieces = direct(own_vectors, "dp", dp_size, range(dp_size))
    *prior_pieces, queries = [in_vmem(piece) for piece in prior_pieces]
    vectors, scale, applied_rows, norm = start_cg(pieces, prior_pieces, tensor_size)
    fixed = (*prior_pieces, vectors, scale)
    state = [applied_rows]
    for iteration in range(1, ITERS - 1):
        blocks = gather(state[0], sizes)
        applied_rows, norm, *others = step_cg(blocks, fixed, norm, state, None, sizes)
        state = [applied_rows, *others]
    blocks = gather(state[0], sizes)
    curvature, norm, solved, along = step_cg(blocks, fixed, norm, state, queries, sizes)
    return combine(gather(curvature, sizes), norm, solved, along)


def solution(mesh):
    return jax.shard_map(
        functools.partial(on_device, mesh.shape["dp"], mesh.shape["tensor"]),
        mesh=mesh,
        in_specs=(
            P(("groups", "dp", "tensor"), None),
            P(),
            P(("groups", "dp"), "tensor"),
            P(None, "tensor"),
            P(("groups", "dp", "tensor"), None),
            P(("groups", "dp", "tensor"), None),
        ),
        out_specs=P("groups", ("dp", "tensor")),
        check_vma=False,
    )
```

```python
import functools

import jax
import jax.numpy as jnp
from jax import lax
from jax.experimental import pallas as pl
from jax.experimental.pallas import tpu as pltpu
from jax.sharding import PartitionSpec as P

R_IN = 64
R_OUT = 64
SEQ = 1024
ITERS = 4
LANES = 128
FEW = 4
DEPTH = 3
NT = (((1,), (1,)), ((), ()))
HIGHEST = lax.Precision.HIGHEST
ANY_SPEC = pl.BlockSpec(memory_space=pl.ANY)
VMEM_SPEC = pl.BlockSpec(memory_space=pltpu.VMEM)
PARAMS = pltpu.CompilerParams(vmem_limit_bytes=16 * 2**20)
F32 = functools.partial(jax.ShapeDtypeStruct, dtype=jnp.float32)


def swap(value, axis, size, bit):
    return lax.ppermute(value, axis, [(i, i ^ bit) for i in range(size)])


def bits(size):
    return [1 << b for b in reversed(range(size.bit_length() - 1))]


def group_order(sizes):
    dp_size, tensor_size = sizes
    first = (dp_size - 1) * tensor_size + tensor_size // 2
    return [first] + [i for i in range(dp_size * tensor_size) if i != first]


def gather(value, sizes):
    order = group_order(sizes)
    value = jnp.broadcast_to(value[None], (len(order),) + value.shape)
    return lax.all_to_all(value, ("dp", "tensor"), 0, 0, axis_index_groups=[order])


def order_of(size):
    return (0, 2, 3, 1) if size == 4 else tuple(range(size))


def direct(value, axis, size, order):
    return [value] + [swap(value, axis, size, k) for k in order[1:]]


def sum_over(value, axis, size):
    if size > FEW:
        for bit in bits(size):
            value = value + swap(value, axis, size, bit)
        return value
    blocks = direct(value, axis, size, range(size))
    while len(blocks) > 1:
        blocks = [a + b for a, b in zip(blocks[::2], blocks[1::2])]
    return blocks[0]


def in_hbm(value):
    return pltpu.with_memory_space_constraint(value, pltpu.HBM)


def in_vmem(value):
    return pltpu.with_memory_space_constraint(value, pltpu.VMEM)


def dot_nt(a, b):
    return lax.dot_general(a, b, NT, precision=HIGHEST, preferred_element_type=jnp.float32)


def row_sum(values):
    return jnp.sum(values, axis=1, keepdims=True)


def stream_kernel(block, by_row, rows_ref, proj_ref, feats_ref, held, proj, turned, sems):
    count, half = proj_ref.shape[0], proj.shape[1]
    steps = held.shape[0] // block
    firsts = [
        pltpu.make_async_copy(
            proj_ref.at[:, pl.ds(h * half, half)], proj.at[pl.ds(h * count, count)], sems.at[steps + h]
        )
        for h in range(2)
    ]

    def fetch(step):
        span = pl.ds(pl.multiple_of(step * block, block), block)
        return pltpu.make_async_copy(rows_ref.at[span], held.at[span], sems.at[step])

    for copy in firsts:
        copy.start()
    for step in range(min(DEPTH, steps)):
        fetch(step).start()
    for copy in firsts:
        copy.wait()
    turned[...] = proj[...].T

    @pl.loop(0, steps)
    def _(step):
        fetch(step).wait()

        @pl.when(step + DEPTH < steps)
        def _():
            fetch(step + DEPTH).start()

        span = pl.ds(pl.multiple_of(step * block, block), block)
        left = jnp.dot(held[span, :half], turned[...], preferred_element_type=jnp.float32)
        right = jnp.dot(held[span, half:], turned[...], preferred_element_type=jnp.float32)
        lane = lax.broadcasted_iota(jnp.int32, left.shape, 1)
        both = jnp.where(lane < count, left, right)
        if by_row:
            feats_ref[span, :] = both
        else:
            both = both.T
            feats_ref[:, span] = both[:count] + both[count:]


def features(rows, proj, block, by_row, limit, name):
    count, width = proj.shape
    shape = (rows.shape[0], 2 * count) if by_row else (count, rows.shape[0])
    return pl.pallas_call(
        functools.partial(stream_kernel, block, by_row),
        out_shape=pltpu.VMEM(shape, jnp.float32),
        in_specs=[ANY_SPEC] * 2,
        out_specs=VMEM_SPEC,
        scratch_shapes=[
            pltpu.VMEM(rows.shape, jnp.bfloat16),
            pltpu.VMEM((2 * count, width // 2), jnp.bfloat16),
            pltpu.VMEM((width // 2, 2 * count), jnp.bfloat16),
            pltpu.SemaphoreType.DMA((rows.shape[0] // block + 2,)),
        ],
        compiler_params=pltpu.CompilerParams(vmem_limit_bytes=limit * 2**20),
        name=name,
    )(in_hbm(rows), in_hbm(proj))


def split_kernel(prior_ref, queries_ref, upper_ref, lower_ref, turned_ref, held, sems):
    chunk = held.shape[1] // sems.shape[0]
    spans = [pl.ds(c * chunk, chunk) for c in range(sems.shape[0])]
    copies = [
        pltpu.make_async_copy(prior_ref.at[:, span], held.at[:, span], sems.at[c])
        for c, span in enumerate(spans)
    ]
    for copy in copies:
        copy.start()
    turned_ref[...] = queries_ref[...].T
    for copy, span in zip(copies, spans):
        copy.wait()
        block = held[:, span]
        upper = block.astype(jnp.bfloat16)
        upper_ref[:, span] = upper
        lower_ref[:, span] = (block - upper.astype(jnp.float32)).astype(jnp.bfloat16)


def split_prior(prior, queries):
    return pl.pallas_call(
        split_kernel,
        out_shape=(
            pltpu.VMEM(prior.shape, jnp.bfloat16),
            pltpu.VMEM(prior.shape, jnp.bfloat16),
            pltpu.VMEM(queries.shape[::-1], jnp.bfloat16),
        ),
        in_specs=[ANY_SPEC, VMEM_SPEC],
        out_specs=(VMEM_SPEC,) * 3,
        scratch_shapes=[pltpu.VMEM(prior.shape, jnp.float32), pltpu.SemaphoreType.DMA((8,))],
        compiler_params=PARAMS,
        name="split_prior",
    )(prior, queries)


def partial_kernel(size, *refs):
    blocks, (out_ref, part_ref, held) = refs[:size], refs[size:]
    me = lax.axis_index("tensor")
    tokens = blocks[0].shape[1]
    for k, block in zip(order_of(size), blocks):
        start = pl.multiple_of((me ^ k) * tokens, LANES)
        held[:, pl.ds(start, tokens)] = block[...]
    for s in range(part_ref.shape[0]):
        span = slice(s * SEQ, (s + 1) * SEQ)
        ins, sums = pieces_of(held[:, span], 2), 0.0
        outs = out_ref[span, :]
        for _ in range(2):
            piece = outs.astype(jnp.bfloat16)
            outs = outs - piece.astype(jnp.float32)
            sums = sums + jnp.dot(ins, piece, preferred_element_type=jnp.float32)
        sums = sums[:R_IN] + sums[R_IN:]
        part_ref[s] = (sums[:, :R_OUT] + sums[:, R_OUT:]) * (1.0 / SEQ)


def partial_vectors(blocks, out_local):
    seq_count = out_local.shape[0] // SEQ
    return pl.pallas_call(
        functools.partial(partial_kernel, len(blocks)),
        out_shape=F32((seq_count, R_IN, R_OUT)),
        in_specs=[VMEM_SPEC] * (len(blocks) + 1),
        out_specs=VMEM_SPEC,
        scratch_shapes=[pltpu.VMEM((R_IN, out_local.shape[0]), jnp.float32)],
        compiler_params=PARAMS,
        name="partial_vectors",
    )(*blocks, out_local)


def own_columns(ref, me, count):
    if count % LANES == 0:
        return ref[:, pl.ds(pl.multiple_of(me * count, LANES), count)]
    per = LANES // count
    held = ref[:, pl.ds(pl.multiple_of((me // per) * LANES, LANES), LANES)]
    return pltpu.roll(held, LANES - (me % per) * count, 1)[:, :count]


def pieces_of(values, count):
    held = []
    for _ in range(count):
        piece = values.astype(jnp.bfloat16)
        held.append(piece)
        values = values - piece.astype(jnp.float32)
    return jnp.concatenate(held, axis=0)


def dot_pieces(a, b, seqs):
    held = lax.dot_general(a, b, NT, preferred_element_type=jnp.float32)
    total = held[:seqs]
    for start in range(seqs, held.shape[0], seqs):
        total = total + held[start : start + seqs]
    return total


def apply_fisher(x, vectors_ref, upper_ref, lower_ref, me):
    seqs = vectors_ref.shape[0]
    pieces = pieces_of(x, 3)
    applied = dot_pieces(pieces, upper_ref[...], seqs)
    applied = applied + dot_pieces(pieces[: 2 * seqs], lower_ref[...], seqs)
    own = own_columns(vectors_ref, me, upper_ref.shape[0])
    for s in range(seqs):
        weight = row_sum(x * vectors_ref[s : s + 1, :]) * (1.0 / seqs)
        applied = applied + weight * own[s : s + 1, :]
    return applied


def flat_index(tensor_size):
    return lax.axis_index("dp") * tensor_size + lax.axis_index("tensor")


def start_kernel(size, tensor_size, *refs):
    pieces, refs = refs[:size], refs[size:]
    upper_ref, lower_ref, vectors_ref, scale_ref, applied_ref, norm_ref, held = refs
    dp = lax.axis_index("dp")
    for k, piece in enumerate(pieces):
        held[dp ^ k] = piece[...]
    vectors = jnp.concatenate([held[k] for k in range(size)], axis=0)
    vectors_ref[...] = vectors
    norm = jnp.broadcast_to(row_sum(vectors * vectors), norm_ref.shape)
    norm_ref[...] = norm
    spread = jnp.sum(norm, axis=0, keepdims=True) * (1.0 / vectors.shape[0])
    scale_ref[...] = jnp.broadcast_to(1.0 / (1.0 + spread), scale_ref.shape)
    me = flat_index(tensor_size)
    applied_ref[...] = apply_fisher(vectors, vectors_ref, upper_ref, lower_ref, me)


def start_cg(pieces, prior_pieces, tensor_size):
    size, seqs = len(pieces), len(pieces) * pieces[0].shape[0]
    rows, width = prior_pieces[0].shape
    column = F32((seqs, LANES))
    return pl.pallas_call(
        functools.partial(start_kernel, size, tensor_size),
        out_shape=(F32((seqs, width)), column, F32((seqs, rows)), column),
        in_specs=[VMEM_SPEC] * (size + 2),
        out_specs=(VMEM_SPEC,) * 4,
        scratch_shapes=[pltpu.VMEM((size,) + pieces[0].shape, jnp.float32)],
        compiler_params=PARAMS,
        name="cg_start",
    )(*pieces, *prior_pieces)


def diagonal(shape):
    return lax.broadcasted_iota(jnp.int32, shape, 0) == lax.broadcasted_iota(jnp.int32, shape, 1)


def on_lanes(column):
    here = diagonal((column.shape[0], LANES))
    return jnp.sum(jnp.where(here, column, 0.0), axis=0, keepdims=True)


def step_kernel(sizes, first, last, *refs):
    blocks_ref, upper_ref, lower_ref, vectors_ref, scale_ref, norm_ref, fisher_direction_ref = refs[:7]
    refs = refs[7:]
    if not first:
        fisher_residual_ref, direction_ref, residual_ref, solution_ref = refs[:4]
        refs = refs[4:]
    if last:
        queries_ref, curvature_out, norm_out, solved_out, along_out, held = refs
    else:
        fisher_direction_out, norm_out, fisher_residual_out, direction_out, residual_out, solution_out, held = refs
    me = flat_index(sizes[1])
    rows = blocks_ref.shape[2]
    for i, k in enumerate(group_order(sizes)):
        held[:, k * rows : (k + 1) * rows] = blocks_ref[i]
    applied = held[...]
    scale = scale_ref[...][:, :1]
    twice = apply_fisher(scale * applied, vectors_ref, upper_ref, lower_ref, me)
    direction = vectors_ref[...] if first else direction_ref[...]
    residual = direction if first else residual_ref[...]
    norm = norm_ref[...][:, :1]
    step = norm / row_sum(direction * applied)
    solution = step * direction
    if not first:
        solution = solution_ref[...] + solution
    residual = residual - step * applied
    norm_next = row_sum(residual * residual)
    share = norm_next / norm
    direction = residual + share * direction
    fisher_direction = fisher_direction_ref[...]
    fisher_residual = (fisher_direction if first else fisher_residual_ref[...]) - (step / scale) * twice
    fisher_direction = fisher_residual + share * fisher_direction
    norm_out[...] = on_lanes(norm_next) if last else jnp.broadcast_to(norm_next, norm_out.shape)
    if last:
        held[...] = direction
        own = own_columns(held, me, rows)
        curvature_out[...] = on_lanes(row_sum(own * fisher_direction))
        seqs = direction.shape[0]
        solved = jnp.concatenate([solution, direction], axis=0)
        parts = jnp.dot(pieces_of(solved, 3), queries_ref[...], preferred_element_type=jnp.float32)
        scores = parts[: 2 * seqs] + parts[2 * seqs : 4 * seqs] + parts[4 * seqs :]
        solved_out[...] = scores[:seqs]
        along_out[...] = scores[seqs:]
    else:
        fisher_direction_out[...] = fisher_direction
        fisher_residual_out[...] = fisher_residual
        residual_out[...] = residual
        direction_out[...] = direction
        solution_out[...] = solution


def step_cg(blocks, fixed, norm, state, queries, sizes):
    first, last = len(state) == 1, queries is not None
    whole, rows = F32(fixed[2].shape), F32(state[0].shape)
    column = F32(norm.shape)
    operands = [blocks, *fixed, norm, *state]
    out_shape = (rows, column, rows, whole, whole, whole)
    if last:
        operands.append(queries)
        scores = F32((whole.shape[0], queries.shape[1]))
        out_shape = (F32((1, LANES)), F32((1, LANES)), scores, scores)
    return pl.pallas_call(
        functools.partial(step_kernel, sizes, first, last),
        out_shape=out_shape,
        in_specs=[VMEM_SPEC] * len(operands),
        out_specs=(VMEM_SPEC,) * len(out_shape),
        scratch_shapes=[pltpu.VMEM(whole.shape, jnp.float32)],
        compiler_params=PARAMS,
        name="cg_step",
    )(*operands)


def combine_kernel(curvature_ref, norm_ref, solved_ref, along_ref, scores_ref):
    step = norm_ref[...] / jnp.sum(curvature_ref[...], axis=0)
    here = diagonal((solved_ref.shape[0], LANES))
    step = row_sum(jnp.where(here, step, 0.0))
    scores_ref[...] = solved_ref[...] + step * along_ref[...]


def combine(curvature, norm, solved, along):
    return pl.pallas_call(
        combine_kernel,
        out_shape=F32(solved.shape),
        in_specs=[VMEM_SPEC] * 4,
        out_specs=VMEM_SPEC,
        compiler_params=PARAMS,
        name="combine",
    )(curvature, norm, solved, along)


def on_device(dp_size, tensor_size, inputs, in_proj, out_grads, out_proj, prior, queries):
    width = R_IN * R_OUT
    sizes = dp_size, tensor_size
    in_blocks = direct(features(inputs, in_proj, LANES, False, 20, "in_features"), "tensor", tensor_size, order_of(tensor_size))
    out_local = features(out_grads, out_proj, 2 * LANES, True, 44, "out_features")
    partial = partial_vectors(in_blocks, out_local).reshape(-1, width)
    prior, partial = lax.optimization_barrier((prior, partial))
    own_vectors = sum_over(partial, "tensor", tensor_size)
    own_vectors, prior_pieces = lax.optimization_barrier((own_vectors, split_prior(prior, queries)))
    pieces = direct(own_vectors, "dp", dp_size, range(dp_size))
    *prior_pieces, queries = [in_vmem(piece) for piece in prior_pieces]
    vectors, scale, applied_rows, norm = start_cg(pieces, prior_pieces, tensor_size)
    fixed = (*prior_pieces, vectors, scale)
    state = [applied_rows]
    for iteration in range(1, ITERS - 1):
        blocks = gather(state[0], sizes)
        applied_rows, norm, *others = step_cg(blocks, fixed, norm, state, None, sizes)
        state = [applied_rows, *others]
    blocks = gather(state[0], sizes)
    curvature, norm, solved, along = step_cg(blocks, fixed, norm, state, queries, sizes)
    return combine(gather(curvature, sizes), norm, solved, along)


def solution(mesh):
    return jax.shard_map(
        functools.partial(on_device, mesh.shape["dp"], mesh.shape["tensor"]),
        mesh=mesh,
        in_specs=(
            P(("groups", "dp", "tensor"), None),
            P(),
            P(("groups", "dp"), "tensor"),
            P(None, "tensor"),
            P(("groups", "dp", "tensor"), None),
            P(("groups", "dp", "tensor"), None),
        ),
        out_specs=P("groups", ("dp", "tensor")),
        check_vma=False,
    )
```
